32 devices in a mesh: dp: 8 (over y, x, core), expert: 4 (over z).
Axes of the slice: x: 2, y: 2, z: 4, core: 2. Of those that a mesh axis runs over, the one named last changes fastest.
Arguments:
- tokens: bfloat16 [5120, 1536], P(('dp', 'expert')), may hold values from -6 to 6
- cotangent: bfloat16 [5120, 1536], P(('dp', 'expert')), may hold values from -6 to 6
- gain_attn: bfloat16 [1536], P('dp'), may hold values from 0.5 to 1.5
- gain_ffn: bfloat16 [1536], P('dp'), may hold values from 0.5 to 1.5
- w_query: bfloat16 [1536, 1536], P('dp'), may hold values from -0.4375 to 0.4375
- key_weight: bfloat16 [1536, 512], P('dp'), may hold values from -0.4375 to 0.4375
- value_weight: bfloat16 [1536, 512], P('dp'), may hold values from -0.15625 to 0.15625
- w_out: bfloat16 [1536, 1536], P('dp'), may hold values from -6 to 6
- expert_gate: bfloat16 [1536, 20, 512], P('dp', 'expert'), may hold values from -0.15625 to 0.15625
- expert_up: bfloat16 [1536, 20, 512], P('dp', 'expert'), may hold values from -0.15625 to 0.15625
- expert_down: bfloat16 [1536, 20, 512], P('dp', 'expert'), may hold values from -4 to 4
- expert_ids: int32 [5120, 8], P(('dp', 'expert')), may hold values from 0 to 19, all different within a row; in each aligned block of 80 rows (0 to 79, 80 to 159, ...) at most 64 rows name the same one
- gates: float32 [5120, 8], P(('dp', 'expert')), as said below
- lengths: int32 [8, 3], P('dp'), may hold values from 1 to 638, as said below
- order: int32 [8, 3], P('dp'), may hold values from 0 to 2, each once within a row
Outputs:
- output: bfloat16 [5120, 1536], P(('dp', 'expert'))
- grad_tokens: float32 [5120, 1536], P(('dp', 'expert'))
- grad_gain_attn: float32 [1536], P('dp')
- grad_gain_ffn: float32 [1536], P('dp')
- grad_w_query: float32 [1536, 1536], P('dp')
- grad_w_key: float32 [1536, 512], P('dp')
- grad_w_value: float32 [1536, 512], P('dp')
- grad_w_out: float32 [1536, 1536], P('dp')
- grad_expert_gate: float32 [1536, 20, 512], P('dp', 'expert')
- grad_expert_up: float32 [1536, 20, 512], P('dp', 'expert')
- grad_expert_down: float32 [1536, 20, 512], P('dp', 'expert')
The draws below stay inside these ranges and needn't reach their ends.
Inputs may be any that keep to these rules, and one draw needn't show every extreme that they name: lengths[g, :] are the lengths of the 3 sequences of index g of dp; a row sums to at most 640. Each row of order is a permutation. `expert_ids`: each row names 8 different experts; in each aligned block of 80 rows no expert is named by more than 64 rows. Each row of gates is positive and sums to one.
All inputs are finite; a program needn't handle non-finite values.
Results may differ from the reference program's by a relative error of at most 0.02.
Values may be sent and summed in bfloat16 or wider, within the bound.
A program may use at most 256 MiB of HBM per device.

```python
import math
import jax
import jax.numpy as jnp
import numpy as np
from jax import lax

MODEL_WIDTH = 1536
QUERY_HEADS = 24
KEY_VALUE_HEADS = 8
HEAD_SIZE = 64
FF = 512
TOP = 8
SEQS = 3
TOK_DEV = 160
EXPERTS = 20
TOKEN_SLOTS = 5120
CAP = 256
MOST = 128
N_DP = 8
N_EXPERT = 4


def draw_lengths(key, part):
    key = jax.random.fold_in(key, 11)
    key_short, key_pick, key_spare, key_row = jax.random.split(key, 4)
    sequence_span_rows = N_EXPERT * TOK_DEV
    short_lens = jax.random.randint(key_short, (N_DP, SEQS), 1, TOK_DEV // 8 + 1)
    long_pick = jax.random.randint(key_pick, (N_DP, 1), 0, SEQS)
    spare_slots = jax.random.randint(key_spare, (N_DP, 1), 0, TOK_DEV * 8 // 10 + 1)
    full_row = jax.random.randint(key_row, (1, 1), 0, N_DP)
    is_full = jnp.arange(N_DP)[:, None] == full_row
    short_lens = jnp.where(is_full, 1, short_lens)
    spare_slots = jnp.where(is_full, 0, spare_slots)
    is_long = jnp.arange(SEQS)[None, :] == long_pick
    short_sum = jnp.sum(jnp.where(is_long, 0, short_lens), axis=1, keepdims=True)
    longest = sequence_span_rows - spare_slots - short_sum
    return jnp.where(is_long, longest, short_lens).astype(jnp.int32)


def draw_gates(key, part):
    key = jax.random.fold_in(key, 23)
    logits = 0.5 * jax.random.normal(key, (TOKEN_SLOTS, TOP), jnp.float32)
    return jax.nn.softmax(logits, axis=-1).astype(jnp.float32)


def steps_of(key, shape, pieces, smallest, high):
    gain, own = 1.0, jax.random.fold_in(key, 6)
    for dim, parts in pieces:
        steps = jnp.exp(jax.random.uniform(jax.random.fold_in(own, dim), (parts,), jnp.float32, smallest / len(pieces), high / len(pieces)))
        gain = gain * jnp.repeat(steps, shape[dim] // parts).reshape([-1 if axis == dim else 1 for axis in range(len(shape))])
    return gain


def routed_block(stream_key, own, number, rows, number_of, top, most, slope):
    order = jax.random.permutation(stream_key, number_of)
    crowded, usual = portions_of(number_of, rows * top, most, slope, True), portions_of(number_of, rows * top, most, slope, False)
    places = jnp.arange(number_of)

    def named(sizes, offset_by):
        used = int((sizes > 0).sum())
        fixed = max(1, used // 4)
        moved = fixed + (places - fixed + offset_by * (used - fixed)) % max(1, number_of - fixed)
        return jnp.zeros((number_of,), jnp.int32).at[order[jnp.where(places < fixed, places, moved)]].set(jnp.asarray(sizes, jnp.int32))

    sizes = jnp.where(number % 4 == 0, named(crowded, number // 4), named(usual, number - number // 4 - 1))
    mixed = jax.random.permutation(jax.random.fold_in(own, 3), number_of)
    source_of, receiver = mixed[0:number_of // 2 * 2:2], mixed[1:number_of // 2 * 2:2]
    room = jnp.minimum(sizes[source_of] - 1, most - sizes[receiver]) // 2
    room = jnp.where((source_of == order[0]) | (receiver == order[0]) | (sizes[receiver] == 0), 0, jnp.maximum(room, 0))
    moved = jax.random.randint(jax.random.fold_in(own, 4), (number_of // 2,), 0, 1 << 20) % (room + 1)
    sizes = sizes.at[source_of].add(-moved).at[receiver].add(moved)
    items = jnp.searchsorted(jnp.cumsum(sizes), jnp.arange(rows * top), side="right").astype(jnp.int32)
    grid = items.reshape(top, rows).T
    grid = grid[jax.random.permutation(jax.random.fold_in(own, 1), rows)]
    offset_by = jax.random.randint(jax.random.fold_in(own, 2), (rows, 1), 0, top)
    return jnp.take_along_axis(grid, (jnp.arange(top)[None, :] + offset_by) % top, axis=1)


def portions_of(amount, total, most, skew, full):
    loads = [(1 << 20) // math.isqrt(grade ** skew) + 1 for grade in range(1, amount + 1)]
    largest = most if full else min(most, max(-(-total // amount), total * loads[0] // sum(loads)))
    least = 1 if total - largest >= amount - 1 else 0
    counts, surplus = [largest] + [least] * (amount - 1), total - largest - least * (amount - 1)
    while surplus > 0:
        movable = [i for i in range(1, amount) if counts[i] < largest] or [i for i in range(1, amount) if counts[i] < most]
        pool, remaining = sum([loads[i] for i in movable]), surplus
        for i in movable:
            more = min(most - counts[i], max(1, remaining * loads[i] // pool), surplus)
            counts[i] = counts[i] + more
            surplus = surplus - more
    return np.array(counts)


def centred(key, dims, scale, most, shards=(), kind=jnp.bfloat16):
    entries = scale * jax.random.normal(key, dims, jnp.float32)
    if shards:
        entries = entries * steps_of(key, dims, shards, -0.22, 0.18)
    return jnp.clip(entries, -most, most).astype(kind)


def setup_inputs(seed: int = 0) -> dict:
    splits = jax.random.split(jax.random.key(seed), 16)
    tokens = centred(splits[0], (TOKEN_SLOTS, MODEL_WIDTH), 1.0, 6.0, ((0, 32),))
    cotangent = centred(splits[1], (TOKEN_SLOTS, MODEL_WIDTH), 1.0, 6.0, ((0, 32),))
    gain_attn = jnp.clip(1.0 + 0.1 * jax.random.normal(splits[2], (MODEL_WIDTH,), jnp.float32), 0.5, 1.5).astype(jnp.bfloat16)
    gain_ffn = jnp.clip(1.0 + 0.1 * jax.random.normal(splits[3], (MODEL_WIDTH,), jnp.float32), 0.5, 1.5).astype(jnp.bfloat16)
    w_query = centred(splits[4], (MODEL_WIDTH, QUERY_HEADS * HEAD_SIZE), (MODEL_WIDTH // 8) ** -0.5, 0.4375, ((0, 8),))
    key_weight = centred(splits[5], (MODEL_WIDTH, KEY_VALUE_HEADS * HEAD_SIZE), (MODEL_WIDTH // 8) ** -0.5, 0.4375, ((0, 8),))
    value_weight = centred(splits[6], (MODEL_WIDTH, KEY_VALUE_HEADS * HEAD_SIZE), MODEL_WIDTH ** -0.5, 0.15625, ((0, 8),))
    w_out = centred(splits[7], (MODEL_WIDTH, QUERY_HEADS * HEAD_SIZE), 1 ** -0.5, 6.0, ((0, 8),))
    expert_gate = centred(splits[8], (MODEL_WIDTH, EXPERTS, FF), MODEL_WIDTH ** -0.5, 0.15625, ((0, 8), (1, 4)))
    expert_up = centred(splits[9], (MODEL_WIDTH, EXPERTS, FF), MODEL_WIDTH ** -0.5, 0.15625, ((0, 8), (1, 4)))
    expert_down = centred(splits[10], (MODEL_WIDTH, EXPERTS, FF), (max(1, FF // 256)) ** -0.5, 4.0, ((0, 8), (1, 4)))
    expert_ids_keys = jax.random.split(jax.random.fold_in(splits[11], 1), TOKEN_SLOTS // (TOK_DEV // 2))
    expert_ids_turns = jax.random.permutation(jax.random.fold_in(splits[11], 3), TOKEN_SLOTS // (TOK_DEV // 2))
    expert_ids = jax.vmap(lambda own, number: routed_block(jax.random.fold_in(splits[11], 2), own, number, TOK_DEV // 2, EXPERTS, TOP, MOST // 2, 1))(expert_ids_keys, expert_ids_turns).reshape((TOKEN_SLOTS, TOP))
    gates = draw_gates(jax.random.fold_in(splits[15], 71), 0)
    lengths = draw_lengths(jax.random.fold_in(splits[15], 71), 0)
    order = jax.vmap(lambda own: jax.random.permutation(own, SEQS))(jax.random.split(splits[14], N_DP)).reshape((N_DP, SEQS)).astype(jnp.int32)
    return dict(tokens=tokens, cotangent=cotangent, gain_attn=gain_attn, gain_ffn=gain_ffn, w_query=w_query, key_weight=key_weight, value_weight=value_weight, w_out=w_out, expert_gate=expert_gate, expert_up=expert_up, expert_down=expert_down, expert_ids=expert_ids, gates=gates, lengths=lengths, order=order)


epsilon = 1e-06
rope_base = 10000.0
score_scale = 0.015625
branch_scale = 0.22

@jax.custom_vjp
def reduced_precision(v):
    return lax.optimization_barrier(v.astype(jnp.bfloat16)).astype(jnp.float32)

@jax.custom_vjp
def reduced_backward(v):
    return v

def low_keep(v):
    return (reduced_precision(v), None)

def low_pass(kept, grad):
    return (grad,)

def back_keep(v):
    return (v, None)

def back_low(kept, grad):
    return (reduced_precision(grad),)
reduced_precision.defvjp(low_keep, low_pass)
reduced_backward.defvjp(back_keep, back_low)

def layout(lengths_row, order_row, sequence_span_rows):
    slot_ids = jnp.arange(lengths_row.shape[0], dtype=jnp.int32)
    picked = lax.optimization_barrier(jnp.sum(jnp.where(order_row[:, None] == slot_ids[None, :], lengths_row[None, :], 0), axis=1)).astype(jnp.int32)
    seq_ends = jnp.cumsum(picked).astype(jnp.int32)
    key_place = jnp.arange(sequence_span_rows, dtype=jnp.int32)
    passed = key_place[:, None] >= seq_ends[None, :]
    segment = lax.optimization_barrier(jnp.sum(passed.astype(jnp.int32), axis=1)).astype(jnp.int32)
    seq_start = lax.optimization_barrier(jnp.sum(jnp.where(passed, picked[None, :], 0), axis=1)).astype(jnp.int32)
    return (segment, (key_place - seq_start).astype(jnp.float32))

def rotation(position, head_dim):
    half_dim = head_dim // 2
    frequency = rope_base ** (-(jnp.arange(half_dim, dtype=jnp.float32) * (2.0 / head_dim)))
    angles = position[:, None] * frequency[None, :]
    return (jnp.cos(angles), jnp.sin(angles))

def apply_rotary(vector, cosine_table, sine_table):
    half_dim = vector.shape[-1] // 2
    leading = vector[..., :half_dim]
    trailing = vector[..., half_dim:]
    cos_part = cosine_table[:, None, :]
    sin_part = sine_table[:, None, :]
    return jnp.concatenate([leading * cos_part - trailing * sin_part, trailing * cos_part + leading * sin_part], axis=-1)

def normalize(field_in, gain_in):
    return field_in * lax.rsqrt(lax.optimization_barrier(jnp.mean(field_in * field_in, axis=-1, keepdims=True)) + epsilon) * gain_in

def attend_group(packed):
    query_rows, keys_here, values_here, segment = packed
    sequence_span_rows = segment.shape[0]
    key_place = jnp.arange(sequence_span_rows, dtype=jnp.int32)
    allowed = (segment[:, None] == segment[None, :]) & (key_place[None, :] <= key_place[:, None])
    exact_result = lax.Precision.HIGHEST

    def one_head(inner):
        head_q, head_k, head_v = inner
        scores = jnp.einsum('irh,jh->rij', head_q, head_k, precision=exact_result) * score_scale
        scores = reduced_backward(jnp.where(allowed[None], scores, -1e+30))
        probs = reduced_precision(jax.nn.softmax(scores, axis=-1))
        return jnp.einsum('rij,jh->irh', probs, head_v, precision=exact_result)
    result = lax.map(jax.checkpoint(one_head), (jnp.moveaxis(query_rows, 1, 0), jnp.moveaxis(keys_here, 1, 0), jnp.moveaxis(values_here, 1, 0)))
    return jnp.moveaxis(result, 0, 1).reshape(sequence_span_rows, -1)

def reference(tokens, cotangent, gain_attn, gain_ffn, w_query, key_weight, value_weight, w_out, expert_gate, expert_up, expert_down, expert_ids, gates, lengths, order):
    sequence_span_rows = N_EXPERT * TOK_DEV
    repeat_heads = QUERY_HEADS // KEY_VALUE_HEADS
    pair_count = TOKEN_SLOTS * TOP
    segment, position = jax.vmap(lambda lens_row, ord_row: layout(lens_row, ord_row, sequence_span_rows))(lengths, order)
    cosine_table, sine_table = rotation(position.reshape(-1), HEAD_SIZE)
    chosen = expert_ids.reshape(N_DP, sequence_span_rows * TOP)
    onehot = (chosen[:, :, None] == jnp.arange(EXPERTS, dtype=jnp.int32)[None, None, :]).astype(jnp.int32)
    pair_slot = (lax.optimization_barrier(jnp.sum(jnp.cumsum(onehot, axis=1).astype(jnp.int32) * onehot, axis=2)) - 1).astype(jnp.int32)
    dummy = N_DP * EXPERTS * CAP
    row_index = jnp.arange(N_DP, dtype=jnp.int32)[:, None]
    slot_target = jnp.where(pair_slot < CAP, (row_index * EXPERTS + chosen) * CAP + pair_slot, dummy).reshape(-1).astype(jnp.int32)
    pair_table = jnp.full((dummy + 1,), pair_count, jnp.int32).at[slot_target].set(jnp.arange(pair_count, dtype=jnp.int32))[:dummy]
    slot_tokens = jnp.where(pair_table < pair_count, pair_table // TOP, TOKEN_SLOTS).astype(jnp.int32)
    slot_tokens = jnp.moveaxis(slot_tokens.reshape(N_DP, EXPERTS, CAP), 1, 0).reshape(EXPERTS, N_DP * CAP)
    gate_flat = jnp.concatenate([gates.astype(jnp.float32).reshape(-1), jnp.zeros((1,), jnp.float32)])
    slot_weight = jnp.moveaxis(gate_flat[pair_table].reshape(N_DP, EXPERTS, CAP), 1, 0).reshape(EXPERTS, N_DP * CAP)

    def forward(inputs, gain_one, gain_two, wq_full, full_key_weight, full_value_weight, wo_full, gate_full, up_full, down_full):
        exact_result = lax.Precision.HIGHEST
        normalized_input = reduced_precision(normalize(inputs, gain_one))
        query_rows = reduced_backward(jnp.dot(normalized_input, wq_full, precision=exact_result)).reshape(TOKEN_SLOTS, QUERY_HEADS, HEAD_SIZE)
        every_key = reduced_backward(jnp.dot(normalized_input, full_key_weight, precision=exact_result)).reshape(TOKEN_SLOTS, KEY_VALUE_HEADS, HEAD_SIZE)
        every_value = reduced_precision(reduced_backward(jnp.dot(normalized_input, full_value_weight, precision=exact_result))).reshape(N_DP, sequence_span_rows, KEY_VALUE_HEADS, HEAD_SIZE)
        query_rows = reduced_precision(apply_rotary(query_rows, cosine_table, sine_table)).reshape(N_DP, sequence_span_rows, KEY_VALUE_HEADS, repeat_heads, HEAD_SIZE)
        every_key = reduced_precision(apply_rotary(every_key, cosine_table, sine_table)).reshape(N_DP, sequence_span_rows, KEY_VALUE_HEADS, HEAD_SIZE)
        attended = lax.map(jax.checkpoint(attend_group), (query_rows, every_key, every_value, segment)).reshape(TOKEN_SLOTS, QUERY_HEADS * HEAD_SIZE)
        attended = reduced_precision(reduced_backward(attended))
        residual = inputs + branch_scale * reduced_backward(jnp.dot(attended, wo_full.T, precision=exact_result))
        normed_ffn = reduced_precision(normalize(residual, gain_two))
        padded = jnp.concatenate([normed_ffn, jnp.zeros((1, MODEL_WIDTH), normed_ffn.dtype)], axis=0)

        def expert_step(running_sum, packed):
            slot_ids, weight, w_gate, w_up, w_down = packed
            rows_in = reduced_backward(padded[slot_ids])
            pre_gate = reduced_backward(jnp.dot(rows_in, w_gate, precision=exact_result))
            pre_up = reduced_backward(jnp.dot(rows_in, w_up, precision=exact_result))
            activ = reduced_precision(jax.nn.silu(pre_gate) * pre_up)
            produced = reduced_precision(reduced_backward(jnp.dot(activ, w_down.T, precision=exact_result)))
            return (running_sum.at[slot_ids].add(weight[:, None] * produced), None)
        start_sum = jnp.zeros((TOKEN_SLOTS + 1, MODEL_WIDTH), normed_ffn.dtype)
        mixture, unused = lax.scan(jax.checkpoint(expert_step), start_sum, (slot_tokens, slot_weight, jnp.moveaxis(gate_full, 1, 0), jnp.moveaxis(up_full, 1, 0), jnp.moveaxis(down_full, 1, 0)))
        return residual + branch_scale * mixture[:TOKEN_SLOTS]
    floats = [value.astype(jnp.float32) for value in (tokens, gain_attn, gain_ffn, w_query, key_weight, value_weight, w_out, expert_gate, expert_up, expert_down)]
    result, pullback = jax.vjp(forward, *floats)
    gradients = pullback(cotangent.astype(jnp.float32))
    return (result.astype(jnp.bfloat16), gradients[0], gradients[1], gradients[2], gradients[3], gradients[4], gradients[5], gradients[6], gradients[7], gradients[8], gradients[9])
```

```python
import functools

import jax
import jax.numpy as jnp
from jax import lax
from jax.sharding import PartitionSpec as P

QUERY_HEADS = 24
KEY_VALUE_HEADS = 8
HEAD_SIZE = 64
TOP = 8

epsilon = 1e-06
rope_base = 10000.0
score_scale = 0.015625
branch_scale = 0.22
F32 = jnp.float32
BF16 = jnp.bfloat16


def layout(lengths_row, order_row, span):
    seqs = lengths_row.shape[0]
    slot_ids = jnp.arange(seqs, dtype=jnp.int32)
    picked = jnp.sum(
        jnp.where(order_row[:, None] == slot_ids[None, :], lengths_row[None, :], 0), axis=1
    )
    before = slot_ids[:, None] >= slot_ids[None, :]
    seq_ends = jnp.sum(jnp.where(before, picked[None, :], 0), axis=1)
    place = jnp.arange(span, dtype=jnp.int32)
    passed = place[:, None] >= seq_ends[None, :]
    segment = jnp.sum(passed.astype(jnp.int32), axis=1)
    start = jnp.sum(jnp.where(passed, picked[None, :], 0), axis=1)
    return segment, (place - start).astype(F32)


def rotation(position):
    half = HEAD_SIZE // 2
    frequency = rope_base ** (-(jnp.arange(half, dtype=F32) * (2.0 / HEAD_SIZE)))
    angles = position[:, None] * frequency[None, :]
    return jnp.cos(angles), jnp.sin(angles)


def rotate(rows, cosine, sine, back=False):
    t = rows.shape[0]
    heads = rows.reshape(t, -1, 2, HEAD_SIZE // 2)
    a, b = heads[:, :, 0], heads[:, :, 1]
    c, s = cosine[:, None, :], sine[:, None, :]
    if back:
        s = -s
    return jnp.stack([a * c - b * s, b * c + a * s], axis=2).reshape(t, -1)


def dot(a, b):
    return jnp.dot(a, b, preferred_element_type=F32)


def dot_nt(a, b):
    return jnp.einsum("tc,dc->td", a, b, preferred_element_type=F32)


def dot_tn(a, b):
    return jnp.einsum("td,tc->dc", a, b, preferred_element_type=F32)


def rms_factor(rows):
    return lax.rsqrt(jnp.mean(rows * rows, axis=-1, keepdims=True) + epsilon)


def norm_back(rows, factor, gain, grad):
    scaled = gain * grad
    return factor * scaled - rows * (factor * factor * factor) * jnp.mean(
        scaled * rows, axis=-1, keepdims=True
    )


def gather(x, axis):
    return lax.all_gather(x, axis, axis=0, tiled=True)


def scatter(x, axis):
    return lax.psum_scatter(x.astype(BF16), axis, scatter_dimension=0, tiled=True).astype(F32)


def attend_forward(q, k, v, allowed):
    scores = jnp.einsum("irh,jh->rij", q, k, preferred_element_type=F32) * score_scale
    scores = jnp.where(allowed[None], scores, -1e30)
    peak = jnp.max(scores, axis=-1, keepdims=True)
    exponent = jnp.exp(scores - peak)
    total = jnp.sum(exponent, axis=-1, keepdims=True)
    probs = exponent / total
    return jnp.einsum("rij,jh->irh", probs.astype(BF16), v, preferred_element_type=F32), probs


def attend_backward(q, k, v, probs, grad, allowed):
    grad_probs = jnp.einsum("irh,jh->rij", grad, v, preferred_element_type=F32)
    inner = jnp.sum(probs * grad_probs, axis=-1, keepdims=True)
    grad_scores = (probs * (grad_probs - inner)).astype(BF16)
    grad_q = jnp.einsum("rij,jh->irh", grad_scores, k, preferred_element_type=F32) * score_scale
    grad_k = jnp.einsum("rij,irh->jh", grad_scores, q, preferred_element_type=F32) * score_scale
    grad_v = jnp.einsum("rij,irh->jh", probs.astype(BF16), grad, preferred_element_type=F32)
    return grad_q, grad_k, grad_v


def shards(
    tokens,
    cotangent,
    gain_attn,
    gain_ffn,
    w_query,
    key_weight,
    value_weight,
    w_out,
    expert_gate,
    expert_up,
    expert_down,
    expert_ids,
    gates,
    lengths,
    order,
):
    rows, width = tokens.shape
    members = lax.axis_size("expert")
    member = lax.axis_index("expert")
    span = rows * members
    own_experts, ff = expert_gate.shape[1], expert_gate.shape[2]
    capacity = rows * TOP // own_experts
    q_cols = w_query.shape[1] // members
    kv_cols = key_weight.shape[1] // members
    kv_heads = kv_cols // HEAD_SIZE
    repeat = QUERY_HEADS // KEY_VALUE_HEADS

    def mine(weight, cols):
        return lax.dynamic_slice_in_dim(weight, member * cols, cols, axis=1)

    tokens_all = gather(tokens, "expert").astype(F32)
    packed = jnp.concatenate(
        [
            mine(w_query, q_cols),
            mine(key_weight, kv_cols),
            mine(value_weight, kv_cols),
            mine(w_out, q_cols),
            gain_attn[:, None],
            gain_ffn[:, None],
            jnp.zeros((gain_attn.shape[0], 126), BF16),
        ],
        axis=1,
    )
    packed_all = gather(packed, "dp")
    qkv_cols = q_cols + 2 * kv_cols
    w_qkv = packed_all[:, :qkv_cols]
    wo = packed_all[:, qkv_cols : qkv_cols + q_cols]
    gain_one = packed_all[:, qkv_cols + q_cols].astype(F32)
    gain_two = packed_all[:, qkv_cols + q_cols + 1].astype(F32)
    gate_all = gather(expert_gate.reshape(-1, own_experts * ff), "dp")
    up_all = gather(expert_up.reshape(-1, own_experts * ff), "dp")
    down_all = gather(expert_down.reshape(-1, own_experts * ff), "dp")
    ids_all = gather(expert_ids, "expert")
    gates_all = gather(gates, "expert")
    cot_all = gather(cotangent, "expert")

    segment, position = layout(lengths[0], order[0], span)
    cosine, sine = rotation(position)
    place = jnp.arange(span, dtype=jnp.int32)
    allowed = (segment[:, None] == segment[None, :]) & (place[None, :] <= place[:, None])
    factor_one = rms_factor(tokens_all)
    normed_attn = (tokens_all * factor_one * gain_one).astype(BF16)
    qkv = dot(normed_attn, w_qkv)
    qk = rotate(qkv[:, : q_cols + kv_cols], cosine, sine).astype(BF16)
    v = qkv[:, q_cols + kv_cols :].astype(BF16)
    q_heads = jnp.moveaxis(qk[:, :q_cols].reshape(span, kv_heads, repeat, HEAD_SIZE), 1, 0)
    k_heads = jnp.moveaxis(qk[:, q_cols:].reshape(span, kv_heads, HEAD_SIZE), 1, 0)
    v_heads = jnp.moveaxis(v.reshape(span, kv_heads, HEAD_SIZE), 1, 0)
    attended, probs = jax.vmap(functools.partial(attend_forward, allowed=allowed))(
        q_heads, k_heads, v_heads
    )
    attended = jnp.moveaxis(attended, 0, 1).reshape(span, q_cols).astype(BF16)
    attn_out = scatter(dot_nt(attended, wo), "expert")
    residual = tokens.astype(F32) + branch_scale * attn_out
    factor_two = rms_factor(residual)
    normed_all = gather((residual * factor_two * gain_two).astype(BF16), "expert")

    expert_of = member * own_experts + jnp.arange(own_experts, dtype=jnp.int32)
    named = ids_all[None, :, :] == expert_of[:, None, None]
    chosen = jnp.any(named, axis=2)
    weight = jnp.sum(jnp.where(named, gates_all[None], 0.0), axis=2)
    upto = (place[:, None] <= place[None, :]).astype(BF16)
    slot = dot(chosen.astype(BF16), upto).astype(jnp.int32) - 1
    slots = jnp.arange(capacity, dtype=jnp.int32)
    picks = chosen[:, None, :] & (slot[:, None, :] == slots[None, :, None])
    pick = picks.astype(BF16)
    slot_weight = jnp.sum(jnp.where(picks, weight[:, None, :], 0.0), axis=2)
    mixture = jnp.zeros((span, width), F32)
    grad_normed = jnp.zeros((span, width), F32)
    expert_grads = []
    for e in range(own_experts):
        cols = slice(e * ff, (e + 1) * ff)
        w_gate, w_up, w_down = gate_all[:, cols], up_all[:, cols], down_all[:, cols]
        here = pick[e]
        gate_col = slot_weight[e][:, None]
        received = dot(here, normed_all).astype(BF16)
        pre_gate, pre_up = dot(received, w_gate), dot(received, w_up)
        sig = jax.nn.sigmoid(pre_gate)
        silu = pre_gate * sig
        activ = (silu * pre_up).astype(BF16)
        produced = (gate_col * dot_nt(activ, w_down)).astype(BF16)
        mixture = mixture + dot_tn(here, produced)
        grad_out = (gate_col * (branch_scale * dot(here, cot_all))).astype(BF16)
        grad_activ = dot(grad_out, w_down)
        grad_gate = (grad_activ * pre_up * sig * (1.0 + pre_gate * (1.0 - sig))).astype(BF16)
        grad_up = (grad_activ * silu).astype(BF16)
        grad_pair = (dot_nt(grad_gate, w_gate) + dot_nt(grad_up, w_up)).astype(BF16)
        grad_normed = grad_normed + dot_tn(here, grad_pair)
        expert_grads.append(
            (dot_tn(received, grad_gate), dot_tn(received, grad_up), dot_tn(grad_out, activ))
        )
    output = (residual + branch_scale * scatter(mixture, "expert")).astype(BF16)
    summed = [
        scatter(jnp.stack([one[i] for one in expert_grads], axis=1), "dp") for i in range(3)
    ]

    grad_norm_own = scatter(grad_normed, "expert")
    gain_two_part = jnp.sum(grad_norm_own * residual * factor_two, axis=0)
    grad_residual = cotangent.astype(F32) + norm_back(
        residual, factor_two, gain_two, grad_norm_own
    )
    grad_attn_out = gather((branch_scale * grad_residual).astype(BF16), "expert")
    term_out = dot_tn(grad_attn_out, attended)
    grad_attended = dot(grad_attn_out, wo).astype(BF16)
    grad_heads = jnp.moveaxis(grad_attended.reshape(span, kv_heads, repeat, HEAD_SIZE), 1, 0)
    grad_q, grad_k, grad_v = jax.vmap(functools.partial(attend_backward, allowed=allowed))(
        q_heads, k_heads, v_heads, probs, grad_heads
    )
    grad_qk = jnp.concatenate(
        [
            jnp.moveaxis(grad_q, 0, 1).reshape(span, q_cols),
            jnp.moveaxis(grad_k, 0, 1).reshape(span, kv_cols),
        ],
        axis=1,
    )
    grad_qkv = jnp.concatenate(
        [
            rotate(grad_qk, cosine, sine, back=True).astype(BF16),
            jnp.moveaxis(grad_v, 0, 1).reshape(span, kv_cols).astype(BF16),
        ],
        axis=1,
    )
    grad_norm_part = dot_nt(grad_qkv, w_qkv)
    gain_one_part = jnp.sum(grad_norm_part * tokens_all * factor_one, axis=0)
    term_qkv = dot_tn(normed_attn, grad_qkv)
    packed_grads = jnp.concatenate(
        [
            term_qkv,
            term_out,
            gain_one_part[:, None],
            gain_two_part[:, None],
            jnp.zeros((width, 126), F32),
        ],
        axis=1,
    )
    packed_own = scatter(packed_grads, "dp").astype(BF16)
    per_member = lax.all_gather(packed_own, "expert", axis=0).astype(F32)

    def columns(first, cols):
        part = per_member[:, :, first : first + cols]
        return jnp.moveaxis(part, 0, 1).reshape(part.shape[1], -1)

    grad_norm_attn = scatter(grad_norm_part, "expert")
    own_tokens = tokens.astype(F32)
    grad_tokens = grad_residual + norm_back(
        own_tokens, rms_factor(own_tokens), gain_one, grad_norm_attn
    )
    gains = jnp.sum(per_member[:, :, qkv_cols + q_cols :], axis=0)
    return (
        output,
        grad_tokens,
        gains[:, 0],
        gains[:, 1],
        columns(0, q_cols),
        columns(q_cols, kv_cols),
        columns(q_cols + kv_cols, kv_cols),
        columns(qkv_cols, q_cols),
        summed[0],
        summed[1],
        summed[2],
    )


def solution(mesh):
    both = P(("dp", "expert"), None)
    row, rows = P("dp"), P("dp", None)
    experts = P("dp", "expert", None)
    return jax.shard_map(
        shards,
        mesh=mesh,
        in_specs=(both, both, row, row, rows, rows, rows, rows)
        + (experts, experts, experts, both, both, rows, rows),
        out_specs=(both, both, row, row, rows, rows, rows, rows, experts, experts, experts),
        check_vma=False,
    )
```

```python
import functools

import jax
import jax.numpy as jnp
from jax import lax
from jax.experimental import pallas as pl
from jax.experimental.pallas import tpu as pltpu
from jax.sharding import PartitionSpec as P

QUERY_HEADS = 24
KEY_VALUE_HEADS = 8
HEAD_SIZE = 64
TOP = 8

epsilon = 1e-06
rope_base = 10000.0
score_scale = 0.015625
branch_scale = 0.22
F32 = jnp.float32
BF16 = jnp.bfloat16
MESH = pl.DeviceIdType.MESH
VMEM_LIMIT = 58 * 2**20


def layout(lengths_row, order_row, span):
    seqs = lengths_row.shape[0]
    slot_ids = jnp.arange(seqs, dtype=jnp.int32)
    picked = jnp.sum(
        jnp.where(order_row[:, None] == slot_ids[None, :], lengths_row[None, :], 0), axis=1
    )
    before = slot_ids[:, None] >= slot_ids[None, :]
    seq_ends = jnp.sum(jnp.where(before, picked[None, :], 0), axis=1)
    place = jnp.arange(span, dtype=jnp.int32)
    passed = place[:, None] >= seq_ends[None, :]
    segment = jnp.sum(passed.astype(jnp.int32), axis=1)
    start = jnp.sum(jnp.where(passed, picked[None, :], 0), axis=1)
    return segment, (place - start).astype(F32)


def rotation(position):
    half = HEAD_SIZE // 2
    frequency = rope_base ** (-(jnp.arange(half, dtype=F32) * (2.0 / HEAD_SIZE)))
    angles = position[:, None] * frequency[None, :]
    return jnp.cos(angles), jnp.sin(angles)


def rotate(rows, cosine, sine, back=False):
    t = rows.shape[0]
    heads = rows.reshape(t, -1, 2, HEAD_SIZE // 2)
    a, b = heads[:, :, 0], heads[:, :, 1]
    c, s = cosine[:, None, :], sine[:, None, :]
    if back:
        s = -s
    return jnp.stack([a * c - b * s, b * c + a * s], axis=2).reshape(t, -1)


def dot(a, b):
    return jnp.dot(a, b, preferred_element_type=F32)


def dot_nt(a, b):
    return jnp.einsum("tc,dc->td", a, b, preferred_element_type=F32)


def dot_tn(a, b):
    return jnp.einsum("td,tc->dc", a, b, preferred_element_type=F32)


def rms_factor(rows):
    return lax.rsqrt(jnp.mean(rows * rows, axis=-1, keepdims=True) + epsilon)


def norm_back(rows, factor, gain, grad):
    scaled = gain * grad
    return factor * scaled - rows * (factor * factor * factor) * jnp.mean(
        scaled * rows, axis=-1, keepdims=True
    )


def gather(x, axis):
    return lax.all_gather(x, axis, axis=0, tiled=True)


def scatter(x, axis):
    return lax.psum_scatter(x.astype(BF16), axis, scatter_dimension=0, tiled=True).astype(F32)


class Links:
    def __init__(self, send, recv, local, members):
        self.send, self.recv, self.local = send, recv, local
        self.remotes = self.locals = 0
        self.members = members
        self.d, self.z = lax.axis_index("dp"), lax.axis_index("expert")
        d = self.d
        core, x, y = d % 2, (d // 2) % 2, d // 4
        self.core = core
        self.sib = d + 1 - 2 * core
        self.x = d + 2 - 4 * x
        self.y = d + 4 - 8 * y
        self.diag = self.x + 4 - 8 * y
        self.waiting = []

    def other(self, d):
        return d + 1 - 2 * self.core

    def greet(self):
        barrier = pltpu.get_barrier_semaphore()
        last = self.members - 1

        def hello(d, z):
            pl.semaphore_signal(barrier, inc=1, device_id=(d, z), device_id_type=MESH)

        for d in (self.sib, self.x, self.y):
            hello(d, self.z)
        pl.when(self.z > 0)(lambda: hello(self.d, self.z - 1))
        pl.when(self.z < last)(lambda: hello(self.d, self.z + 1))
        ends = (self.z == 0).astype(jnp.int32) + (self.z == last).astype(jnp.int32)
        pl.semaphore_wait(barrier, 5 - ends)

    def remote(self, src, dst, to):
        k = self.remotes
        self.remotes += 1
        return pltpu.make_async_remote_copy(
            src_ref=src,
            dst_ref=dst,
            send_sem=self.send.at[k],
            recv_sem=self.recv.at[k],
            device_id=to,
            device_id_type=MESH,
        )

    def push(self, src, dst, d):
        copy = self.remote(src, dst, (d, self.z))
        copy.start()
        self.waiting.append(copy.wait_send)
        return copy

    def move(self, src, dst):
        k = self.locals
        self.locals += 1
        copy = pltpu.make_async_copy(src, dst, self.local.at[k])
        copy.start()
        return copy

    def finish(self):
        for wait in self.waiting:
            wait()


def run(order, **chains):
    for name in order:
        next(chains[name], None)
    chains = list(chains.values())
    while chains:
        for chain in list(chains):
            try:
                next(chain)
            except StopIteration:
                chains.remove(chain)


def line_gather(links, own, full):
    z, last = links.z, links.members - 1
    local = links.move(own, full.at[z])
    right, left = (links.d, z + 1), (links.d, z - 1)
    to_right, to_left = [], []
    for s in range(last):
        at_r, at_l = jnp.maximum(z - s, 0), jnp.minimum(z + s, last)
        to_right.append(links.remote(own if s == 0 else full.at[at_r], full.at[at_r], right))
        to_left.append(links.remote(own if s == 0 else full.at[at_l], full.at[at_l], left))
    for s in range(last):
        send_r, send_l = (z < last) & (z >= s), (z > 0) & (z + s <= last)
        pl.when(send_r)(to_right[s].start)
        pl.when(send_l)(to_left[s].start)
        yield
        pl.when((z > 0) & (z - 1 >= s))(to_right[s].wait_recv)
        pl.when((z < last) & (z + 1 + s <= last))(to_left[s].wait_recv)
    for s in range(last):
        send_r, send_l = (z < last) & (z >= s), (z > 0) & (z + s <= last)
        pl.when(send_r)(to_right[s].wait_send)
        pl.when(send_l)(to_left[s].wait_send)
    local.wait()


def add_rows(target, other, step=16):
    rows = target.shape[0]

    @pl.loop(0, rows // step)
    def _(i):
        at = pl.ds(pl.multiple_of(i * step, step), step)
        target[at] = (target[at].astype(F32) + other[at].astype(F32)).astype(target.dtype)


def line_scatter(links, part, acc, from_left, from_right):
    z, last = links.z, links.members - 1
    links.move(part, acc).wait()
    to_right = {o: links.remote(acc.at[o], from_left.at[o], (links.d, z + 1)) for o in range(1, last + 1)}
    to_left = {o: links.remote(acc.at[o], from_right.at[o], (links.d, z - 1)) for o in range(last)}

    def pass_right(o):
        @pl.when(z > 0)
        def _():
            to_right[o].wait_recv()
            add_rows(acc.at[o], from_left.at[o])

        to_right[o].start()

    def pass_left(o):
        @pl.when(z < last)
        def _():
            to_left[o].wait_recv()
            add_rows(acc.at[o], from_right.at[o])

        to_left[o].start()

    @pl.when(z == 0)
    def _():
        from_left[0] = jnp.zeros(from_left.shape[1:], from_left.dtype)

    @pl.when(z == last)
    def _():
        from_right[last] = jnp.zeros(from_right.shape[1:], from_right.dtype)

    for j in range(last):
        pl.when(z < last - j)(functools.partial(pass_right, last - j))
        pl.when(z > j)(functools.partial(pass_left, j))
        yield
    for o in range(last + 1):

        @pl.when(z == o)
        def _(o=o):
            if o > 0:
                to_right[o].wait_recv()
            if o < last:
                to_left[o].wait_recv()

    for o in range(last + 1):
        if o > 0:
            pl.when(z < o)(to_right[o].wait_send)
        if o < last:
            pl.when(z > o)(to_left[o].wait_send)


def plane_gather(links, own, full):
    half = own.shape[0] // 2
    first, second = pl.ds(0, half), pl.ds(half, half)
    me = links.d
    local = links.move(own, full.at[me])
    by_x, by_y = {}, {}
    for by, d, h in ((by_y, links.y, first), (by_x, links.x, second), (by_x, links.x, first), (by_y, links.y, second)):
        by[h.start // half] = links.push(own.at[h], full.at[me, h], d)
    to_sib = [links.push(own, full.at[me], links.sib)]

    def share(d, h):
        to_sib.append(links.push(full.at[d, h], full.at[d, h], links.sib))

    yield
    by_y[0].wait_recv()
    over_x = links.push(full.at[links.y, first], full.at[links.y, first], links.x)
    share(links.y, first)
    by_x[1].wait_recv()
    over_y = links.push(full.at[links.x, second], full.at[links.x, second], links.y)
    share(links.x, second)
    yield
    by_x[0].wait_recv()
    share(links.x, first)
    by_y[1].wait_recv()
    share(links.y, second)
    yield
    over_x.wait_recv()
    share(links.diag, first)
    over_y.wait_recv()
    share(links.diag, second)
    yield
    for copy in to_sib:
        copy.wait_recv()
    local.wait()


def plane_scatter(links, part, mine, theirs, mid_x, mid_y, end_x, end_y):
    half = part.shape[1] // 2
    first, second = pl.ds(0, half), pl.ds(half, half)
    chips = (links.d, links.x, links.y, links.diag)
    from_sib, load = {}, {}
    for k in (3, 1, 2, 0):
        from_sib[k] = links.push(part.at[links.other(chips[k])], theirs.at[k], links.sib)
        load[k] = links.move(part.at[chips[k]], mine.at[k])
    yield
    for k in (3, 1, 2):
        load[k].wait()
        from_sib[k].wait_recv()
        add_rows(mine.at[k], theirs.at[k])
        if k == 3:
            to_mid_x = links.push(mine.at[3, first], mid_x, links.x)
            to_mid_y = links.push(mine.at[3, second], mid_y, links.y)
        if k == 1:
            to_end_x = links.push(mine.at[1, first], end_x.at[first], links.x)
        if k == 2:
            to_end_y = links.push(mine.at[2, second], end_y.at[second], links.y)
    yield
    to_mid_y.wait_recv()
    add_rows(mine.at[1, second], mid_y)
    rest_x = links.push(mine.at[1, second], end_x.at[second], links.x)
    to_mid_x.wait_recv()
    add_rows(mine.at[2, first], mid_x)
    rest_y = links.push(mine.at[2, first], end_y.at[first], links.y)
    yield
    load[0].wait()
    from_sib[0].wait_recv()
    to_end_x.wait_recv()
    to_end_y.wait_recv()
    rest_x.wait_recv()
    rest_y.wait_recv()


def plane_scratch(rows, cols):
    return [
        pltpu.VMEM((4, rows, cols), BF16),
        pltpu.VMEM((4, rows, cols), BF16),
        pltpu.VMEM((rows // 2, cols), BF16),
        pltpu.VMEM((rows // 2, cols), BF16),
        pltpu.VMEM((rows, cols), BF16),
        pltpu.VMEM((rows, cols), BF16),
    ]


def plane_result(mine, theirs, end_x, end_y, out, step=16):
    @pl.loop(0, out.shape[0] // step)
    def _(i):
        at = pl.ds(pl.multiple_of(i * step, step), step)
        own = mine[0, at].astype(F32) + theirs[0, at].astype(F32)
        out[at] = (own + end_x[at].astype(F32) + end_y[at].astype(F32)).astype(out.dtype)


def line_result(z, acc, from_left, from_right, at):
    return (
        acc[z, at].astype(F32) + from_left[z, at].astype(F32) + from_right[z, at].astype(F32)
    )


ANY = pl.BlockSpec(memory_space=pl.ANY)
VMEM = pl.BlockSpec(memory_space=pltpu.VMEM)


def comm_call(kernel, name, number, members, remotes, locals_, in_specs, out_specs, out_shape, scratch):
    return pl.pallas_call(
        functools.partial(kernel, members),
        out_shape=out_shape,
        in_specs=in_specs,
        out_specs=out_specs,
        scratch_shapes=[
            pltpu.SemaphoreType.DMA((remotes,)),
            pltpu.SemaphoreType.DMA((remotes,)),
            pltpu.SemaphoreType.DMA((locals_,)),
            *scratch,
        ],
        compiler_params=pltpu.CompilerParams(
            collective_id=number, has_side_effects=True, vmem_limit_bytes=VMEM_LIMIT
        ),
        name=name,
    )


def sds(shape, dtype):
    return jax.ShapeDtypeStruct(shape, dtype)


def first_kernel(members, tokens, cot, route, pack, gate, tokens_all, cot_all, route_all, pack_all, gate_all, send, recv, local):
    links = Links(send, recv, local, members)
    links.greet()
    run(
        "trpgtrptrtrgcpgcpgcpc",
        t=line_gather(links, tokens, tokens_all),
        r=line_gather(links, route, route_all),
        p=plane_gather(links, pack, pack_all),
        g=plane_gather(links, gate, gate_all),
        c=line_gather(links, cot, cot_all),
    )
    links.finish()


def first_phase(members, tokens, cot, route, pack, gate):
    many = lambda a, n: sds((n, *a.shape), a.dtype)
    return comm_call(
        first_kernel, "phase_one", 1, members, 60, 8, [ANY] * 5, [ANY] * 5,
        [many(tokens, members), many(cot, members), many(route, members), many(pack, 8), many(gate, 8)], [],
    )(tokens, cot, route, pack, gate)


def second_kernel(members, part, tokens, gain, up, down, residual, normed_all, up_all, down_all, send, recv, local, acc, from_left, from_right, normed):
    links = Links(send, recv, local, members)
    links.greet()

    def chain():
        yield from line_scatter(links, part, acc, from_left, from_right)

        @pl.loop(0, tokens.shape[0] // 16)
        def _(i):
            at = pl.ds(pl.multiple_of(i * 16, 16), 16)
            here = tokens[at].astype(F32) + branch_scale * line_result(links.z, acc, from_left, from_right, at)
            residual[at] = here
            normed[at] = (here * rms_factor(here) * gain[...]).astype(BF16)

        yield from line_gather(links, normed, normed_all)

    run(
        "zudzzzzudududzud",
        z=chain(),
        u=plane_gather(links, up, up_all),
        d=plane_gather(links, down, down_all),
    )
    links.finish()


def second_phase(members, part, tokens, gain, up, down):
    rows, width = tokens.shape
    blocks = pltpu.VMEM((members, rows, width), BF16)
    return comm_call(
        second_kernel, "phase_two", 2, members, 60, 8,
        [ANY, VMEM, VMEM, ANY, ANY], [VMEM, ANY, ANY, ANY],
        [
            sds((rows, width), F32),
            sds((members, rows, width), BF16),
            sds((8, *up.shape), BF16),
            sds((8, *down.shape), BF16),
        ],
        [blocks, blocks, blocks, pltpu.VMEM((rows, width), BF16)],
    )(part, tokens, gain, up, down)


def third_kernel(members, part, residual, cot, gain, gate, up, grad_residual, gain_part, out_all, gate_out, up_out, send, recv, local, acc, from_left, from_right, grad_out, *rest):
    links = Links(send, recv, local, members)
    links.greet()
    for_gate, for_up = rest[:6], rest[6:]

    def chain():
        yield from line_scatter(links, part, acc, from_left, from_right)
        gain_part[...] = jnp.zeros(gain_part.shape, F32)

        @pl.loop(0, residual.shape[0] // 16)
        def _(i):
            at = pl.ds(pl.multiple_of(i * 16, 16), 16)
            grad = line_result(links.z, acc, from_left, from_right, at)
            here = residual[at]
            factor = rms_factor(here)
            gain_part[...] += jnp.sum(grad * here * factor, axis=0, keepdims=True)
            total = cot[at].astype(F32) + norm_back(here, factor, gain[...], grad)
            grad_residual[at] = total
            grad_out[at] = (branch_scale * total).astype(BF16)

        yield from line_gather(links, grad_out, out_all)

    run(
        "zguguzzzguzgu",
        z=chain(),
        g=plane_scatter(links, gate, *for_gate),
        u=plane_scatter(links, up, *for_up),
    )
    plane_result(for_gate[0], for_gate[1], for_gate[4], for_gate[5], gate_out)
    plane_result(for_up[0], for_up[1], for_up[4], for_up[5], up_out)
    links.finish()


def third_phase(members, part, residual, cot, gain, gate, up):
    rows, width = cot.shape
    blocks = pltpu.VMEM((members, rows, width), BF16)
    return comm_call(
        third_kernel, "phase_three", 3, members, 60, 16,
        [ANY, VMEM, VMEM, VMEM, ANY, ANY], [VMEM, VMEM, ANY, VMEM, VMEM],
        [
            sds((rows, width), F32),
            sds((1, width), F32),
            sds((members, rows, width), BF16),
            sds(gate.shape[1:], F32),
            sds(up.shape[1:], F32),
        ],
        [blocks, blocks, blocks, pltpu.VMEM((rows, width), BF16)]
        + plane_scratch(*gate.shape[1:])
        + plane_scratch(*up.shape[1:]),
    )(part, residual, cot, gain, gate, up)


def fourth_kernel(members, part, grad_residual, tokens, gain, pack, down, grad_tokens, pack_all, down_out, send, recv, local, acc, from_left, from_right, pack_own, *rest):
    links = Links(send, recv, local, members)
    links.greet()
    for_pack, for_down = rest[:6], rest[6:]

    def pack_chain():
        yield from plane_scatter(links, pack, *for_pack)
        plane_result(for_pack[0], for_pack[1], for_pack[4], for_pack[5], pack_own)
        yield from line_gather(links, pack_own, pack_all)

    run(
        "zpdpdzppppzdpppd",
        p=pack_chain(),
        z=line_scatter(links, part, acc, from_left, from_right),
        d=plane_scatter(links, down, *for_down),
    )

    @pl.loop(0, tokens.shape[0] // 16)
    def _(i):
        at = pl.ds(pl.multiple_of(i * 16, 16), 16)
        grad = line_result(links.z, acc, from_left, from_right, at)
        here = tokens[at].astype(F32)
        grad_tokens[at] = grad_residual[at] + norm_back(here, rms_factor(here), gain[...], grad)

    plane_result(for_down[0], for_down[1], for_down[4], for_down[5], down_out)
    links.finish()


def fourth_phase(members, part, grad_residual, tokens, gain, pack, down):
    rows, width = tokens.shape
    blocks = pltpu.VMEM((members, rows, width), BF16)
    return comm_call(
        fourth_kernel, "phase_four", 4, members, 60, 16,
        [ANY, VMEM, VMEM, VMEM, ANY, ANY], [VMEM, ANY, VMEM],
        [
            sds((rows, width), F32),
            sds((members, *pack.shape[1:]), BF16),
            sds(down.shape[1:], F32),
        ],
        [blocks, blocks, blocks, pltpu.VMEM(pack.shape[1:], BF16)]
        + plane_scratch(*pack.shape[1:])
        + plane_scratch(*down.shape[1:]),
    )(part, grad_residual, tokens, gain, pack, down)


def all_blocks(x, axis):
    return lax.all_gather(x, axis, axis=0)


def plain_first(members, tokens, cot, route, pack, gate):
    return (
        all_blocks(tokens, "expert"),
        all_blocks(cot, "expert"),
        all_blocks(route, "expert"),
        all_blocks(pack, "dp"),
        all_blocks(gate, "dp"),
    )


def line_sum(part):
    return scatter(part.reshape(-1, part.shape[2]), "expert")


def plain_second(members, part, tokens, gain, up, down):
    residual = tokens.astype(F32) + branch_scale * line_sum(part)
    normed = (residual * rms_factor(residual) * gain).astype(BF16)
    return residual, all_blocks(normed, "expert"), all_blocks(up, "dp"), all_blocks(down, "dp")


def plane_sum(part):
    return scatter(part.reshape(-1, part.shape[2]), "dp")


def plain_third(members, part, residual, cot, gain, gate, up):
    grad = line_sum(part)
    factor = rms_factor(residual)
    gain_part = jnp.sum(grad * residual * factor, axis=0, keepdims=True)
    total = cot.astype(F32) + norm_back(residual, factor, gain, grad)
    out_all = all_blocks((branch_scale * total).astype(BF16), "expert")
    return total, gain_part, out_all, plane_sum(gate), plane_sum(up)


def plain_fourth(members, part, grad_residual, tokens, gain, pack, down):
    here = tokens.astype(F32)
    grad_tokens = grad_residual + norm_back(here, rms_factor(here), gain, line_sum(part))
    return grad_tokens, all_blocks(plane_sum(pack).astype(BF16), "expert"), plane_sum(down)


def attend_forward(q, k, v, allowed):
    scores = jnp.einsum("irh,jh->rij", q, k, preferred_element_type=F32) * score_scale
    scores = jnp.where(allowed[None], scores, -1e30)
    peak = jnp.max(scores, axis=-1, keepdims=True)
    exponent = jnp.exp(scores - peak)
    total = jnp.sum(exponent, axis=-1, keepdims=True)
    probs = exponent / total
    return jnp.einsum("rij,jh->irh", probs.astype(BF16), v, preferred_element_type=F32), probs


def attend_backward(q, k, v, probs, grad, allowed):
    grad_probs = jnp.einsum("irh,jh->rij", grad, v, preferred_element_type=F32)
    inner = jnp.sum(probs * grad_probs, axis=-1, keepdims=True)
    grad_scores = (probs * (grad_probs - inner)).astype(BF16)
    grad_q = jnp.einsum("rij,jh->irh", grad_scores, k, preferred_element_type=F32) * score_scale
    grad_k = jnp.einsum("rij,irh->jh", grad_scores, q, preferred_element_type=F32) * score_scale
    grad_v = jnp.einsum("rij,irh->jh", probs.astype(BF16), grad, preferred_element_type=F32)
    return grad_q, grad_k, grad_v


def shards(
    tokens,
    cotangent,
    gain_attn,
    gain_ffn,
    w_query,
    key_weight,
    value_weight,
    w_out,
    expert_gate,
    expert_up,
    expert_down,
    expert_ids,
    gates,
    lengths,
    order,
):
    rows, width = tokens.shape
    members = lax.axis_size("expert")
    member = lax.axis_index("expert")
    span = rows * members
    own_experts, ff = expert_gate.shape[1], expert_gate.shape[2]
    capacity = rows * TOP // own_experts
    q_cols = w_query.shape[1] // members
    kv_cols = key_weight.shape[1] // members
    kv_heads = kv_cols // HEAD_SIZE
    repeat = QUERY_HEADS // KEY_VALUE_HEADS

    def mine(weight, cols):
        return lax.dynamic_slice_in_dim(weight, member * cols, cols, axis=1)

    devices = lax.axis_size("dp")
    phases = (plain_first, plain_second, plain_third, plain_fourth)
    if devices == 8 and rows % 16 == 0 and width % (32 * devices) == 0:
        phases = (first_phase, second_phase, third_phase, fourth_phase)
    phases = [functools.partial(phase, members) for phase in phases]

    pack = jnp.concatenate(
        [
            mine(w_query, q_cols),
            mine(key_weight, kv_cols),
            mine(value_weight, kv_cols),
            mine(w_out, q_cols),
            gain_attn[:, None],
            gain_ffn[:, None],
            jnp.zeros((gain_attn.shape[0], 126), BF16),
        ],
        axis=1,
    )
    route = jnp.concatenate([expert_ids.astype(F32), gates], axis=1)
    tokens_all, cot_all, route_all, pack_all, gate_all = phases[0](
        tokens, cotangent, route, pack, expert_gate.reshape(-1, own_experts * ff)
    )
    tokens_all = tokens_all.reshape(span, width).astype(F32)
    cot_all = cot_all.reshape(span, width)
    route_all = route_all.reshape(span, 2 * TOP)
    ids_all, gates_all = route_all[:, :TOP].astype(jnp.int32), route_all[:, TOP:]
    pack_all = pack_all.reshape(width, -1)
    gate_all = gate_all.reshape(width, -1)
    qkv_cols = q_cols + 2 * kv_cols
    w_qkv = pack_all[:, :qkv_cols]
    wo = pack_all[:, qkv_cols : qkv_cols + q_cols]
    gain_one = pack_all[:, qkv_cols + q_cols].astype(F32)[None]
    gain_two = pack_all[:, qkv_cols + q_cols + 1].astype(F32)[None]

    segment, position = layout(lengths[0], order[0], span)
    cosine, sine = rotation(position)
    place = jnp.arange(span, dtype=jnp.int32)
    allowed = (segment[:, None] == segment[None, :]) & (place[None, :] <= place[:, None])
    factor_one = rms_factor(tokens_all)
    normed_attn = (tokens_all * factor_one * gain_one).astype(BF16)
    qkv = dot(normed_attn, w_qkv)
    qk = rotate(qkv[:, : q_cols + kv_cols], cosine, sine).astype(BF16)
    v = qkv[:, q_cols + kv_cols :].astype(BF16)
    q_heads = jnp.moveaxis(qk[:, :q_cols].reshape(span, kv_heads, repeat, HEAD_SIZE), 1, 0)
    k_heads = jnp.moveaxis(qk[:, q_cols:].reshape(span, kv_heads, HEAD_SIZE), 1, 0)
    v_heads = jnp.moveaxis(v.reshape(span, kv_heads, HEAD_SIZE), 1, 0)
    attended, probs = jax.vmap(functools.partial(attend_forward, allowed=allowed))(
        q_heads, k_heads, v_heads
    )
    attended = jnp.moveaxis(attended, 0, 1).reshape(span, q_cols).astype(BF16)
    attn_part = dot_nt(attended, wo).astype(BF16).reshape(members, rows, width)
    residual, normed_all, up_all, down_all = phases[1](
        attn_part,
        tokens,
        gain_two,
        expert_up.reshape(-1, own_experts * ff),
        expert_down.reshape(-1, own_experts * ff),
    )
    normed_all = normed_all.reshape(span, width)
    up_all, down_all = up_all.reshape(width, -1), down_all.reshape(width, -1)

    expert_of = member * own_experts + jnp.arange(own_experts, dtype=jnp.int32)
    named = ids_all[None, :, :] == expert_of[:, None, None]
    chosen = jnp.any(named, axis=2)
    weight = jnp.sum(jnp.where(named, gates_all[None], 0.0), axis=2)
    upto = (place[:, None] <= place[None, :]).astype(BF16)
    slot = dot(chosen.astype(BF16), upto).astype(jnp.int32) - 1
    slots = jnp.arange(capacity, dtype=jnp.int32)
    picks = chosen[:, None, :] & (slot[:, None, :] == slots[None, :, None])
    pick = picks.astype(BF16)
    slot_weight = jnp.sum(jnp.where(picks, weight[:, None, :], 0.0), axis=2)
    mixture = jnp.zeros((span, width), F32)
    grad_normed = jnp.zeros((span, width), F32)
    expert_grads = []
    for e in range(own_experts):
        cols = slice(e * ff, (e + 1) * ff)
        w_gate, w_up, w_down = gate_all[:, cols], up_all[:, cols], down_all[:, cols]
        here = pick[e]
        gate_col = slot_weight[e][:, None]
        received = dot(here, normed_all).astype(BF16)
        pre_gate, pre_up = dot(received, w_gate), dot(received, w_up)
        sig = jax.nn.sigmoid(pre_gate)
        silu = pre_gate * sig
        activ = (silu * pre_up).astype(BF16)
        produced = (gate_col * dot_nt(activ, w_down)).astype(BF16)
        mixture = mixture + dot_tn(here, produced)
        grad_out = (gate_col * (branch_scale * dot(here, cot_all))).astype(BF16)
        grad_activ = dot(grad_out, w_down)
        grad_gate = (grad_activ * pre_up * sig * (1.0 + pre_gate * (1.0 - sig))).astype(BF16)
        grad_up = (grad_activ * silu).astype(BF16)
        grad_pair = (dot_nt(grad_gate, w_gate) + dot_nt(grad_up, w_up)).astype(BF16)
        grad_normed = grad_normed + dot_tn(here, grad_pair)
        expert_grads.append(
            (dot_tn(received, grad_gate), dot_tn(received, grad_up), dot_tn(grad_out, activ))
        )
    output = (residual + branch_scale * scatter(mixture, "expert")).astype(BF16)
    by_kind = [
        jnp.concatenate([one[i].astype(BF16) for one in expert_grads], axis=1).reshape(
            devices, -1, own_experts * ff
        )
        for i in range(3)
    ]

    grad_residual, gain_two_part, grad_attn_out, sum_gate, sum_up = phases[2](
        grad_normed.astype(BF16).reshape(members, rows, width),
        residual,
        cotangent,
        gain_two,
        by_kind[0],
        by_kind[1],
    )
    grad_attn_out = grad_attn_out.reshape(span, width)
    term_out = dot_tn(grad_attn_out, attended)
    grad_attended = dot(grad_attn_out, wo).astype(BF16)
    grad_heads = jnp.moveaxis(grad_attended.reshape(span, kv_heads, repeat, HEAD_SIZE), 1, 0)
    grad_q, grad_k, grad_v = jax.vmap(functools.partial(attend_backward, allowed=allowed))(
        q_heads, k_heads, v_heads, probs, grad_heads
    )
    grad_qk = jnp.concatenate(
        [
            jnp.moveaxis(grad_q, 0, 1).reshape(span, q_cols),
            jnp.moveaxis(grad_k, 0, 1).reshape(span, kv_cols),
        ],
        axis=1,
    )
    grad_qkv = jnp.concatenate(
        [
            rotate(grad_qk, cosine, sine, back=True).astype(BF16),
            jnp.moveaxis(grad_v, 0, 1).reshape(span, kv_cols).astype(BF16),
        ],
        axis=1,
    )
    grad_norm_part = dot_nt(grad_qkv, w_qkv)
    gain_one_part = jnp.sum(grad_norm_part * tokens_all * factor_one, axis=0)
    term_qkv = dot_tn(normed_attn, grad_qkv)
    packed_grads = jnp.concatenate(
        [
            term_qkv,
            term_out,
            gain_one_part[:, None],
            gain_two_part.reshape(-1, 1),
            jnp.zeros((width, 126), F32),
        ],
        axis=1,
    )
    grad_tokens, per_member, sum_down = phases[3](
        grad_norm_part.astype(BF16).reshape(members, rows, width),
        grad_residual,
        tokens,
        gain_one,
        packed_grads.astype(BF16).reshape(devices, -1, packed_grads.shape[1]),
        by_kind[2],
    )
    per_member = per_member.astype(F32)

    def columns(first, cols):
        part = per_member[:, :, first : first + cols]
        return jnp.moveaxis(part, 0, 1).reshape(part.shape[1], -1)

    gains = jnp.sum(per_member[:, :, qkv_cols + q_cols :], axis=0)
    return (
        output,
        grad_tokens,
        gains[:, 0],
        gains[:, 1],
        columns(0, q_cols),
        columns(q_cols, kv_cols),
        columns(q_cols + kv_cols, kv_cols),
        columns(qkv_cols, q_cols),
        sum_gate.reshape(-1, own_experts, ff),
        sum_up.reshape(-1, own_experts, ff),
        sum_down.reshape(-1, own_experts, ff),
    )


def solution(mesh):
    both = P(("dp", "expert"), None)
    row, rows = P("dp"), P("dp", None)
    experts = P("dp", "expert", None)
    return jax.shard_map(
        shards,
        mesh=mesh,
        in_specs=(both, both, row, row, rows, rows, rows, rows)
        + (experts, experts, experts, both, both, rows, rows),
        out_specs=(both, both, row, row, rows, rows, rows, rows, experts, experts, experts),
        check_vma=False,
    )
```

```python
import functools

import jax
import jax.numpy as jnp
from jax import lax
from jax.experimental import pallas as pl
from jax.experimental.pallas import tpu as pltpu
from jax.sharding import PartitionSpec as P

QUERY_HEADS = 24
KEY_VALUE_HEADS = 8
HEAD_SIZE = 64
TOP = 8

epsilon = 1e-06
rope_base = 10000.0
score_scale = 0.015625
branch_scale = 0.22
F32 = jnp.float32
BF16 = jnp.bfloat16
MESH = pl.DeviceIdType.MESH
VMEM_LIMIT = 58 * 2**20


def layout(lengths_row, order_row, span):
    seqs = lengths_row.shape[0]
    slot_ids = jnp.arange(seqs, dtype=jnp.int32)
    picked = jnp.sum(
        jnp.where(order_row[:, None] == slot_ids[None, :], lengths_row[None, :], 0), axis=1
    )
    before = slot_ids[:, None] >= slot_ids[None, :]
    seq_ends = jnp.sum(jnp.where(before, picked[None, :], 0), axis=1)
    place = jnp.arange(span, dtype=jnp.int32)
    passed = place[:, None] >= seq_ends[None, :]
    segment = jnp.sum(passed.astype(jnp.int32), axis=1)
    start = jnp.sum(jnp.where(passed, picked[None, :], 0), axis=1)
    return segment, (place - start).astype(F32)


def rotation(position):
    half = HEAD_SIZE // 2
    frequency = rope_base ** (-(jnp.arange(half, dtype=F32) * (2.0 / HEAD_SIZE)))
    angles = position[:, None] * frequency[None, :]
    return jnp.cos(angles), jnp.sin(angles)


def rotate(rows, cosine, sine, back=False):
    t = rows.shape[0]
    heads = rows.reshape(t, -1, 2, HEAD_SIZE // 2)
    a, b = heads[:, :, 0], heads[:, :, 1]
    c, s = cosine[:, None, :], sine[:, None, :]
    if back:
        s = -s
    return jnp.stack([a * c - b * s, b * c + a * s], axis=2).reshape(t, -1)


def dot(a, b):
    return jnp.dot(a, b, preferred_element_type=F32)


def dot_nt(a, b):
    return jnp.einsum("tc,dc->td", a, b, preferred_element_type=F32)


def dot_tn(a, b):
    return jnp.einsum("td,tc->dc", a, b, preferred_element_type=F32)


def rms_factor(rows):
    return lax.rsqrt(jnp.mean(rows * rows, axis=-1, keepdims=True) + epsilon)


def norm_back(rows, factor, gain, grad):
    scaled = gain * grad
    return factor * scaled - rows * (factor * factor * factor) * jnp.mean(
        scaled * rows, axis=-1, keepdims=True
    )


def gather(x, axis):
    return lax.all_gather(x, axis, axis=0, tiled=True)


def scatter(x, axis):
    return lax.psum_scatter(x.astype(BF16), axis, scatter_dimension=0, tiled=True).astype(F32)


class Links:
    def __init__(self, send, recv, local, members):
        self.send, self.recv, self.local = send, recv, local
        self.remotes = self.locals = 0
        self.members = members
        self.d, self.z = lax.axis_index("dp"), lax.axis_index("expert")
        d = self.d
        core, x, y = d % 2, (d // 2) % 2, d // 4
        self.core = core
        self.sib = d + 1 - 2 * core
        self.x = d + 2 - 4 * x
        self.y = d + 4 - 8 * y
        self.diag = self.x + 4 - 8 * y
        self.waiting = []

    def other(self, d):
        return d + 1 - 2 * self.core

    def greet(self):
        barrier = pltpu.get_barrier_semaphore()
        last = self.members - 1

        def hello(d, z):
            pl.semaphore_signal(barrier, inc=1, device_id=(d, z), device_id_type=MESH)

        for d in (self.sib, self.x, self.y):
            hello(d, self.z)
        pl.when(self.z > 0)(lambda: hello(self.d, self.z - 1))
        pl.when(self.z < last)(lambda: hello(self.d, self.z + 1))
        ends = (self.z == 0).astype(jnp.int32) + (self.z == last).astype(jnp.int32)
        pl.semaphore_wait(barrier, 5 - ends)

    def remote(self, src, dst, to):
        k = self.remotes
        self.remotes += 1
        return pltpu.make_async_remote_copy(
            src_ref=src,
            dst_ref=dst,
            send_sem=self.send.at[k],
            recv_sem=self.recv.at[k],
            device_id=to,
            device_id_type=MESH,
        )

    def push(self, src, dst, d):
        copy = self.remote(src, dst, (d, self.z))
        copy.start()
        self.waiting.append(copy.wait_send)
        return copy

    def move(self, src, dst):
        k = self.locals
        self.locals += 1
        copy = pltpu.make_async_copy(src, dst, self.local.at[k])
        copy.start()
        return copy

    def finish(self):
        for wait in self.waiting:
            wait()


def run(order, **chains):
    for name in order:
        next(chains[name], None)
    chains = list(chains.values())
    while chains:
        for chain in list(chains):
            try:
                next(chain)
            except StopIteration:
                chains.remove(chain)


def line_gather(links, own, full):
    z, last = links.z, links.members - 1
    local = links.move(own, full.at[z])
    right, left = (links.d, z + 1), (links.d, z - 1)
    to_right, to_left = [], []
    for s in range(last):
        at_r, at_l = jnp.maximum(z - s, 0), jnp.minimum(z + s, last)
        to_right.append(links.remote(own if s == 0 else full.at[at_r], full.at[at_r], right))
        to_left.append(links.remote(own if s == 0 else full.at[at_l], full.at[at_l], left))
    for s in range(last):
        send_r, send_l = (z < last) & (z >= s), (z > 0) & (z + s <= last)
        pl.when(send_r)(to_right[s].start)
        pl.when(send_l)(to_left[s].start)
        yield
        pl.when((z > 0) & (z - 1 >= s))(to_right[s].wait_recv)
        pl.when((z < last) & (z + 1 + s <= last))(to_left[s].wait_recv)
    for s in range(last):
        send_r, send_l = (z < last) & (z >= s), (z > 0) & (z + s <= last)
        pl.when(send_r)(to_right[s].wait_send)
        pl.when(send_l)(to_left[s].wait_send)
    local.wait()


def add_rows(target, other, step=16):
    rows = target.shape[0]

    @pl.loop(0, rows // step)
    def _(i):
        at = pl.ds(pl.multiple_of(i * step, step), step)
        target[at] = (target[at].astype(F32) + other[at].astype(F32)).astype(target.dtype)


def line_scatter(links, part, acc, from_left, from_right):
    z, last = links.z, links.members - 1
    made = set()

    def make(o):
        if o not in made:
            made.add(o)
            part(o)

    to_right = {o: links.remote(acc.at[o], from_left.at[o], (links.d, z + 1)) for o in range(1, last + 1)}
    to_left = {o: links.remote(acc.at[o], from_right.at[o], (links.d, z - 1)) for o in range(last)}

    def pass_right(o):
        @pl.when(z > 0)
        def _():
            to_right[o].wait_recv()
            add_rows(acc.at[o], from_left.at[o])

        to_right[o].start()

    def pass_left(o):
        @pl.when(z < last)
        def _():
            to_left[o].wait_recv()
            add_rows(acc.at[o], from_right.at[o])

        to_left[o].start()

    @pl.when(z == 0)
    def _():
        from_left[0] = jnp.zeros(from_left.shape[1:], from_left.dtype)

    @pl.when(z == last)
    def _():
        from_right[last] = jnp.zeros(from_right.shape[1:], from_right.dtype)

    for j in range(last):
        make(last - j)
        make(j)
        pl.when((z < last - j) & (2 * z < last))(functools.partial(pass_right, last - j))
        pl.when(z > j)(functools.partial(pass_left, j))
        pl.when((z < last - j) & (2 * z >= last))(functools.partial(pass_right, last - j))
        yield
    for o in range(last + 1):

        @pl.when(z == o)
        def _(o=o):
            if o > 0:
                to_right[o].wait_recv()
            if o < last:
                to_left[o].wait_recv()

    for o in range(last + 1):
        if o > 0:
            pl.when(z < o)(to_right[o].wait_send)
        if o < last:
            pl.when(z > o)(to_left[o].wait_send)


def plane_gather(links, own, full):
    half = own.shape[0] // 2
    first, second = pl.ds(0, half), pl.ds(half, half)
    me = links.d
    local = links.move(own, full.at[me])
    by_x, by_y = {}, {}
    for by, d, h in ((by_y, links.y, first), (by_x, links.x, second), (by_x, links.x, first), (by_y, links.y, second)):
        by[h.start // half] = links.push(own.at[h], full.at[me, h], d)
    to_sib = [links.push(own, full.at[me], links.sib)]

    def share(d, h):
        to_sib.append(links.push(full.at[d, h], full.at[d, h], links.sib))

    yield
    by_y[0].wait_recv()
    over_x = links.push(full.at[links.y, first], full.at[links.y, first], links.x)
    share(links.y, first)
    by_x[1].wait_recv()
    over_y = links.push(full.at[links.x, second], full.at[links.x, second], links.y)
    share(links.x, second)
    yield
    by_x[0].wait_recv()
    share(links.x, first)
    by_y[1].wait_recv()
    share(links.y, second)
    yield
    over_x.wait_recv()
    share(links.diag, first)
    over_y.wait_recv()
    share(links.diag, second)
    yield
    for copy in to_sib:
        copy.wait_recv()
    local.wait()


def plane_scatter(links, part, mine, theirs, mid_x, mid_y, end_x, end_y):
    half = part.shape[1] // 2
    first, second = pl.ds(0, half), pl.ds(half, half)
    chips = (links.d, links.x, links.y, links.diag)
    from_sib, load = {}, {}
    for k in (3, 1, 2, 0):
        from_sib[k] = links.push(part.at[links.other(chips[k])], theirs.at[k], links.sib)
        load[k] = links.move(part.at[chips[k]], mine.at[k])
    yield
    for k in (3, 1, 2):
        load[k].wait()
        from_sib[k].wait_recv()
        add_rows(mine.at[k], theirs.at[k])
        if k == 3:
            to_mid_x = links.push(mine.at[3, first], mid_x, links.x)
            to_mid_y = links.push(mine.at[3, second], mid_y, links.y)
        if k == 1:
            to_end_x = links.push(mine.at[1, first], end_x.at[first], links.x)
        if k == 2:
            to_end_y = links.push(mine.at[2, second], end_y.at[second], links.y)
    yield
    to_mid_y.wait_recv()
    add_rows(mine.at[1, second], mid_y)
    rest_x = links.push(mine.at[1, second], end_x.at[second], links.x)
    to_mid_x.wait_recv()
    add_rows(mine.at[2, first], mid_x)
    rest_y = links.push(mine.at[2, first], end_y.at[first], links.y)
    yield
    load[0].wait()
    from_sib[0].wait_recv()
    to_end_x.wait_recv()
    to_end_y.wait_recv()
    rest_x.wait_recv()
    rest_y.wait_recv()


def plane_scratch(rows, cols):
    return [
        pltpu.VMEM((4, rows, cols), BF16),
        pltpu.VMEM((4, rows, cols), BF16),
        pltpu.VMEM((rows // 2, cols), BF16),
        pltpu.VMEM((rows // 2, cols), BF16),
        pltpu.VMEM((rows, cols), BF16),
        pltpu.VMEM((rows, cols), BF16),
    ]


def plane_result(mine, theirs, end_x, end_y, out, step=16):
    @pl.loop(0, out.shape[0] // step)
    def _(i):
        at = pl.ds(pl.multiple_of(i * step, step), step)
        own = mine[0, at].astype(F32) + theirs[0, at].astype(F32)
        out[at] = (own + end_x[at].astype(F32) + end_y[at].astype(F32)).astype(out.dtype)


def line_result(z, acc, from_left, from_right, at):
    return (
        acc[z, at].astype(F32) + from_left[z, at].astype(F32) + from_right[z, at].astype(F32)
    )


ANY = pl.BlockSpec(memory_space=pl.ANY)
VMEM = pl.BlockSpec(memory_space=pltpu.VMEM)


def comm_call(kernel, name, number, members, remotes, locals_, in_specs, out_specs, out_shape, scratch):
    return pl.pallas_call(
        functools.partial(kernel, members),
        out_shape=out_shape,
        in_specs=in_specs,
        out_specs=out_specs,
        scratch_shapes=[
            pltpu.SemaphoreType.DMA((remotes,)),
            pltpu.SemaphoreType.DMA((remotes,)),
            pltpu.SemaphoreType.DMA((locals_,)),
            *scratch,
        ],
        compiler_params=pltpu.CompilerParams(
            collective_id=number, has_side_effects=True, vmem_limit_bytes=VMEM_LIMIT
        ),
        name=name,
    )


def sds(shape, dtype):
    return jax.ShapeDtypeStruct(shape, dtype)


def third_kernel(members, part, residual, cot, gain, gate, up, grad_residual, gain_part, out_all, gate_out, up_out, send, recv, local, acc, from_left, from_right, grad_out, *rest):
    links = Links(send, recv, local, members)
    links.greet()
    for_gate, for_up = rest[:6], rest[6:]

    def chain():
        links.move(part, acc).wait()
        yield from line_scatter(links, lambda o: None, acc, from_left, from_right)
        gain_part[...] = jnp.zeros(gain_part.shape, F32)

        @pl.loop(0, residual.shape[0] // 16)
        def _(i):
            at = pl.ds(pl.multiple_of(i * 16, 16), 16)
            grad = line_result(links.z, acc, from_left, from_right, at)
            here = residual[at]
            factor = rms_factor(here)
            gain_part[...] += jnp.sum(grad * here * factor, axis=0, keepdims=True)
            total = cot[at].astype(F32) + norm_back(here, factor, gain[...], grad)
            grad_residual[at] = total
            grad_out[at] = (branch_scale * total).astype(BF16)

        yield from line_gather(links, grad_out, out_all)

    run(
        "zguguzzzguzgu",
        z=chain(),
        g=plane_scatter(links, gate, *for_gate),
        u=plane_scatter(links, up, *for_up),
    )
    plane_result(for_gate[0], for_gate[1], for_gate[4], for_gate[5], gate_out)
    plane_result(for_up[0], for_up[1], for_up[4], for_up[5], up_out)
    links.finish()


def third_phase(members, part, residual, cot, gain, gate, up):
    rows, width = cot.shape
    blocks = pltpu.VMEM((members, rows, width), BF16)
    return comm_call(
        third_kernel, "phase_three", 3, members, 60, 16,
        [ANY, VMEM, VMEM, VMEM, ANY, ANY], [VMEM, VMEM, ANY, VMEM, VMEM],
        [
            sds((rows, width), F32),
            sds((1, width), F32),
            sds((members, rows, width), BF16),
            sds(gate.shape[1:], F32),
            sds(up.shape[1:], F32),
        ],
        [blocks, blocks, blocks, pltpu.VMEM((rows, width), BF16)]
        + plane_scratch(*gate.shape[1:])
        + plane_scratch(*up.shape[1:]),
    )(part, residual, cot, gain, gate, up)


def fourth_kernel(members, part, grad_residual, tokens, gain, pack, down, grad_tokens, pack_all, down_out, send, recv, local, acc, from_left, from_right, pack_own, *rest):
    links = Links(send, recv, local, members)
    links.greet()
    for_pack, for_down = rest[:6], rest[6:]

    def pack_chain():
        yield from plane_scatter(links, pack, *for_pack)
        plane_result(for_pack[0], for_pack[1], for_pack[4], for_pack[5], pack_own)
        yield from line_gather(links, pack_own, pack_all)

    links.move(part, acc).wait()
    run(
        "zpdpdzppppzdpppd",
        p=pack_chain(),
        z=line_scatter(links, lambda o: None, acc, from_left, from_right),
        d=plane_scatter(links, down, *for_down),
    )

    @pl.loop(0, tokens.shape[0] // 16)
    def _(i):
        at = pl.ds(pl.multiple_of(i * 16, 16), 16)
        grad = line_result(links.z, acc, from_left, from_right, at)
        here = tokens[at].astype(F32)
        grad_tokens[at] = grad_residual[at] + norm_back(here, rms_factor(here), gain[...], grad)

    plane_result(for_down[0], for_down[1], for_down[4], for_down[5], down_out)
    links.finish()


def fourth_phase(members, part, grad_residual, tokens, gain, pack, down):
    rows, width = tokens.shape
    blocks = pltpu.VMEM((members, rows, width), BF16)
    return comm_call(
        fourth_kernel, "phase_four", 4, members, 60, 16,
        [ANY, VMEM, VMEM, VMEM, ANY, ANY], [VMEM, ANY, VMEM],
        [
            sds((rows, width), F32),
            sds((members, *pack.shape[1:]), BF16),
            sds(down.shape[1:], F32),
        ],
        [blocks, blocks, blocks, pltpu.VMEM(pack.shape[1:], BF16)]
        + plane_scratch(*pack.shape[1:])
        + plane_scratch(*down.shape[1:]),
    )(part, grad_residual, tokens, gain, pack, down)


def dims(a, b):
    return (((a,), (b,)), ((), ()))


def mm(a, b):
    return lax.dot_general(a, b, dims(1, 0), preferred_element_type=F32)


def mm_nt(a, b):
    return lax.dot_general(a, b, dims(1, 1), preferred_element_type=F32)


def mm_tn(a, b):
    return lax.dot_general(a, b, dims(0, 0), preferred_element_type=F32)


def expert_kernel(capacity, slot_row, slot_col, weight_row, normed, cot, w_gate, w_up, w_down, mixture, grad_normed, d_gate, d_up, d_down, mix_sum, grad_sum):
    e = pl.program_id(0)
    span = normed.shape[0]

    @pl.when(e == 0)
    def _():
        mix_sum[...] = jnp.zeros(mix_sum.shape, F32)
        grad_sum[...] = jnp.zeros(grad_sum.shape, F32)

    slots = slot_row[0]
    picks = slots == lax.broadcasted_iota(jnp.int32, (capacity, span), 0)
    pick = picks.astype(BF16)
    gate_col = jnp.sum(jnp.where(picks, weight_row[0], 0.0), axis=1, keepdims=True)
    put = (slot_col[0] == lax.broadcasted_iota(jnp.int32, (span, capacity), 1)).astype(BF16)
    received = mm(pick, normed[...]).astype(BF16)
    pre_gate, pre_up = mm(received, w_gate[...]), mm(received, w_up[...])
    sig = 1.0 / (1.0 + jnp.exp(-pre_gate))
    silu = pre_gate * sig
    activ = (silu * pre_up).astype(BF16)
    produced = (gate_col * mm_nt(activ, w_down[...])).astype(BF16)
    mix_sum[...] += mm(put, produced)
    grad_out = (gate_col * (branch_scale * mm(pick, cot[...]))).astype(BF16)
    grad_activ = mm(grad_out, w_down[...])
    grad_gate = (grad_activ * pre_up * (sig * (1.0 + pre_gate * (1.0 - sig)))).astype(BF16)
    grad_up = (grad_activ * silu).astype(BF16)
    grad_pair = (mm_nt(grad_gate, w_gate[...]) + mm_nt(grad_up, w_up[...])).astype(BF16)
    grad_sum[...] += mm(put, grad_pair)
    d_gate[...] = mm_tn(received, grad_gate).astype(BF16)
    d_up[...] = mm_tn(received, grad_up).astype(BF16)
    d_down[...] = mm_tn(grad_out, activ).astype(BF16)

    @pl.when(e == pl.num_programs(0) - 1)
    def _():
        mixture[...] = mix_sum[...].astype(BF16)
        grad_normed[...] = grad_sum[...].astype(BF16)


def experts(slot, weight, normed, cot, w_gate, w_up, w_down, ff, capacity):
    own_experts, span = slot.shape
    width = normed.shape[1]
    whole = pl.BlockSpec((span, width), lambda e: (0, 0))
    column = pl.BlockSpec((width, ff), lambda e: (0, e))
    row = pl.BlockSpec((1, 1, span), lambda e: (e, 0, 0))
    grads = jax.ShapeDtypeStruct(w_gate.shape, BF16)
    rows = jax.ShapeDtypeStruct((span, width), BF16)
    return pl.pallas_call(
        functools.partial(expert_kernel, capacity),
        grid=(own_experts,),
        in_specs=[row, pl.BlockSpec((1, span, 1), lambda e: (e, 0, 0)), row, whole, whole, column, column, column],
        out_specs=[whole, whole, column, column, column],
        out_shape=[rows, rows, grads, grads, grads],
        scratch_shapes=[pltpu.VMEM((span, width), F32), pltpu.VMEM((span, width), F32)],
        compiler_params=pltpu.CompilerParams(vmem_limit_bytes=VMEM_LIMIT),
        name="experts",
    )(slot[:, None, :], slot[:, :, None], weight[:, None, :], normed, cot, w_gate, w_up, w_down)


LANES = 128


def lane_ids(rows):
    return lax.broadcasted_iota(jnp.int32, (rows, LANES), 1)


def turn(x, cosine, sine):
    half = HEAD_SIZE // 2
    ahead, behind = pltpu.roll(x, LANES - half, axis=1), pltpu.roll(x, half, axis=1)
    partner = jnp.where(lane_ids(x.shape[0]) % HEAD_SIZE < half, ahead, behind)
    return x * cosine + partner * sine


def spread(block, at, out):
    low = lane_ids(block.shape[0]) < HEAD_SIZE
    other = pltpu.roll(block, HEAD_SIZE, axis=1)
    zero = jnp.zeros_like(block)
    out[0, 0, at] = jnp.where(low, block, zero).astype(BF16)
    out[0, 1, at] = jnp.where(low, zero, other).astype(BF16)
    out[1, 0, at] = jnp.where(low, other, zero).astype(BF16)
    out[1, 1, at] = jnp.where(low, zero, block).astype(BF16)


def attention_setup(seg_row, seg_col, bias):
    span = bias.shape[0]
    for b in range(span // LANES):
        at = pl.ds(b * LANES, LANES)
        row = b * LANES + lax.broadcasted_iota(jnp.int32, (LANES, span), 0)
        col = lax.broadcasted_iota(jnp.int32, (LANES, span), 1)
        ok = (seg_col[at] == seg_row[...]) & (col <= row)
        bias[at] = jnp.where(ok, 0.0, -1e30)


def weight_columns(pack_all, first, cols):
    return pack_all[:, :, first : first + cols].reshape(-1, cols)


def gain_rows(pack_all, first):
    pick = lax.broadcasted_iota(jnp.int32, (16, LANES), 0) == lax.broadcasted_iota(jnp.int32, (16, LANES), 1)
    return mm_nt(pick.astype(BF16), weight_columns(pack_all, first, LANES))


def attend_steps(qkv, kx, vx, bias, probs, attended):
    span, blocks = qkv.shape[0], attended.shape[1] // LANES
    repeat = QUERY_HEADS // KEY_VALUE_HEADS
    for j in range(blocks):
        for b in range(span // LANES):
            at, keys = pl.ds(b * LANES, LANES), (b + 1) * LANES
            q = qkv[at, j * LANES : (j + 1) * LANES]
            total = jnp.zeros((LANES, LANES), F32)
            for half in range(2):
                h = 2 * j + half
                kv = h // repeat
                scores = mm_nt(q, kx[kv, half, :keys]) + bias[at, :keys]
                peak = jnp.max(scores, axis=1, keepdims=True)
                exponent = jnp.exp(scores - peak)
                share = 1.0 / jnp.sum(exponent, axis=1, keepdims=True)
                low = (exponent * share).astype(BF16)
                probs[h, at, :keys] = low
                total += mm(low, vx[kv, half, :keys])
            attended[at, j * LANES : (j + 1) * LANES] = total.astype(BF16)
        yield


def forward_kernel(
    members, tokens, cot, route, pack, gate, up, down, seg_row, seg_col, cosine, sine,
    cot_all, route_all, pack_all, gate_all, up_all, down_all, normed_attn, qkv, kx, vx, probs, attended, residual, normed_all,
    send, recv, local, tokens_all, bias, acc, from_left, from_right, normed,
):
    links = Links(send, recv, local, members)
    links.greet()
    rows, width = tokens.shape
    span = rows * members
    q_cols = attended.shape[1]
    qkv_cols = qkv.shape[1]

    def produce(o):
        acc[o] = mm_nt(attended[o * rows : (o + 1) * rows], weight_columns(pack_all, qkv_cols, q_cols)).astype(BF16)

    def chain():
        attention_setup(seg_row, seg_col, bias)
        yield
        gains = gain_rows(pack_all, qkv_cols + q_cols)

        @pl.loop(0, span // 16)
        def _(i):
            here = tokens_all[i // (rows // 16), pl.ds(pl.multiple_of(i % (rows // 16) * 16, 16), 16)].astype(F32)
            normed_attn[pl.ds(pl.multiple_of(i * 16, 16), 16)] = (here * rms_factor(here) * gains[0:1]).astype(BF16)

        @pl.loop(0, span // LANES)
        def _(i):
            at = pl.ds(pl.multiple_of(i * LANES, LANES), LANES)
            here = mm(normed_attn[at], weight_columns(pack_all, 0, qkv_cols))
            c, s = cosine[at], sine[at]
            for j in range(q_cols // LANES):
                lanes = slice(j * LANES, (j + 1) * LANES)
                qkv[at, lanes] = (turn(here[:, lanes], c, s).astype(BF16).astype(F32) * score_scale).astype(BF16)
            key = turn(here[:, q_cols : q_cols + LANES], c, s)
            value = here[:, q_cols + LANES :]
            qkv[at, q_cols : q_cols + LANES] = key.astype(BF16)
            qkv[at, q_cols + LANES :] = value.astype(BF16)
            spread(key, at, kx)
            spread(value, at, vx)

        yield
        yield from attend_steps(qkv, kx, vx, bias, probs, attended)
        yield from line_scatter(links, produce, acc, from_left, from_right)

        @pl.loop(0, rows // 16)
        def _(i):
            at = pl.ds(pl.multiple_of(i * 16, 16), 16)
            here = tokens[at].astype(F32) + branch_scale * line_result(links.z, acc, from_left, from_right, at)
            residual[at] = here
            normed[at] = (here * rms_factor(here) * gains[1:2]).astype(BF16)

        yield from line_gather(links, normed, normed_all)

    run(
        FORWARD_ORDER,
        t=line_gather(links, tokens, tokens_all),
        r=line_gather(links, route, route_all),
        c=line_gather(links, cot, cot_all),
        p=plane_gather(links, pack, pack_all),
        g=plane_gather(links, gate, gate_all),
        u=plane_gather(links, up, up_all),
        d=plane_gather(links, down, down_all),
        a=chain(),
    )
    links.finish()


FORWARD_ORDER = "trpgatrputrpppdtrcaggacguaucaudcauaddacadada"


def forward_phase(members, tokens, cot, route, pack, gate, up, down, seg_row, seg_col, cosine, sine, q_cols, qkv_cols):
    rows, width = tokens.shape
    span = rows * members
    blocks = pltpu.VMEM((members, rows, width), BF16)
    heads = q_cols // HEAD_SIZE
    return comm_call(
        forward_kernel, "forward", 1, members, 100, 16,
        [VMEM, ANY, ANY, ANY, ANY, ANY, ANY, VMEM, VMEM, VMEM, VMEM],
        [ANY, ANY, VMEM, ANY, ANY, ANY, VMEM, VMEM, VMEM, VMEM, VMEM, VMEM, VMEM, ANY],
        [
            sds((members, rows, width), BF16),
            sds((members, *route.shape), F32),
            sds((8, *pack.shape), BF16),
            sds((8, *gate.shape), BF16),
            sds((8, *up.shape), BF16),
            sds((8, *down.shape), BF16),
            sds((span, width), BF16),
            sds((span, qkv_cols), BF16),
            sds((2, 2, span, LANES), BF16),
            sds((2, 2, span, LANES), BF16),
            sds((heads, span, span), BF16),
            sds((span, q_cols), BF16),
            sds((rows, width), F32),
            sds((members, rows, width), BF16),
        ],
        [
            blocks,
            pltpu.VMEM((span, span), F32),
            blocks,
            blocks,
            blocks,
            pltpu.VMEM((rows, width), BF16),
        ],
    )(tokens, cot, route, pack, gate, up, down, seg_row, seg_col, cosine, sine)


def all_blocks(x, axis):
    return lax.all_gather(x, axis, axis=0)


def plain_first(members, tokens, cot, route, pack, gate):
    return (
        all_blocks(tokens, "expert"),
        all_blocks(cot, "expert"),
        all_blocks(route, "expert"),
        all_blocks(pack, "dp"),
        all_blocks(gate, "dp"),
    )


def line_sum(part):
    return scatter(part.reshape(-1, part.shape[2]), "expert")


def plain_second(members, part, tokens, gain, up, down):
    residual = tokens.astype(F32) + branch_scale * line_sum(part)
    normed = (residual * rms_factor(residual) * gain).astype(BF16)
    return residual, all_blocks(normed, "expert"), all_blocks(up, "dp"), all_blocks(down, "dp")


def plane_sum(part):
    return scatter(part.reshape(-1, part.shape[2]), "dp")


def plain_third(members, part, residual, cot, gain, gate, up):
    grad = line_sum(part)
    factor = rms_factor(residual)
    gain_part = jnp.sum(grad * residual * factor, axis=0, keepdims=True)
    total = cot.astype(F32) + norm_back(residual, factor, gain, grad)
    out_all = all_blocks((branch_scale * total).astype(BF16), "expert")
    return total, gain_part, out_all, plane_sum(gate), plane_sum(up)


def plain_fourth(members, part, grad_residual, tokens, gain, pack, down):
    here = tokens.astype(F32)
    grad_tokens = grad_residual + norm_back(here, rms_factor(here), gain, line_sum(part))
    return grad_tokens, all_blocks(plane_sum(pack).astype(BF16), "expert"), plane_sum(down)


def attend_forward(q, k, v, allowed):
    scores = jnp.einsum("irh,jh->rij", q, k, preferred_element_type=F32) * score_scale
    scores = jnp.where(allowed[None], scores, -1e30)
    peak = jnp.max(scores, axis=-1, keepdims=True)
    exponent = jnp.exp(scores - peak)
    total = jnp.sum(exponent, axis=-1, keepdims=True)
    probs = exponent / total
    return jnp.einsum("rij,jh->irh", probs.astype(BF16), v, preferred_element_type=F32), probs


def attend_backward(q, k, v, probs, grad, allowed):
    grad_probs = jnp.einsum("irh,jh->rij", grad, v, preferred_element_type=F32)
    inner = jnp.sum(probs * grad_probs, axis=-1, keepdims=True)
    grad_scores = (probs * (grad_probs - inner)).astype(BF16)
    grad_q = jnp.einsum("rij,jh->irh", grad_scores, k, preferred_element_type=F32) * score_scale
    grad_k = jnp.einsum("rij,irh->jh", grad_scores, q, preferred_element_type=F32) * score_scale
    grad_v = jnp.einsum("rij,irh->jh", probs.astype(BF16), grad, preferred_element_type=F32)
    return grad_q, grad_k, grad_v


def shards_plain(
    tokens,
    cotangent,
    gain_attn,
    gain_ffn,
    w_query,
    key_weight,
    value_weight,
    w_out,
    expert_gate,
    expert_up,
    expert_down,
    expert_ids,
    gates,
    lengths,
    order,
):
    rows, width = tokens.shape
    members = lax.axis_size("expert")
    member = lax.axis_index("expert")
    span = rows * members
    own_experts, ff = expert_gate.shape[1], expert_gate.shape[2]
    capacity = rows * TOP // own_experts
    q_cols = w_query.shape[1] // members
    kv_cols = key_weight.shape[1] // members
    kv_heads = kv_cols // HEAD_SIZE
    repeat = QUERY_HEADS // KEY_VALUE_HEADS

    def mine(weight, cols):
        return lax.dynamic_slice_in_dim(weight, member * cols, cols, axis=1)

    devices = lax.axis_size("dp")
    phases = [
        functools.partial(phase, members)
        for phase in (plain_first, plain_second, plain_third, plain_fourth)
    ]

    pack = jnp.concatenate(
        [
            mine(w_query, q_cols),
            mine(key_weight, kv_cols),
            mine(value_weight, kv_cols),
            mine(w_out, q_cols),
            gain_attn[:, None],
            gain_ffn[:, None],
            jnp.zeros((gain_attn.shape[0], 126), BF16),
        ],
        axis=1,
    )
    route = jnp.concatenate([expert_ids.astype(F32), gates], axis=1)
    tokens_all, cot_all, route_all, pack_all, gate_all = phases[0](
        tokens, cotangent, route, pack, expert_gate.reshape(-1, own_experts * ff)
    )
    tokens_all = tokens_all.reshape(span, width).astype(F32)
    cot_all = cot_all.reshape(span, width)
    route_all = route_all.reshape(span, 2 * TOP)
    ids_all, gates_all = route_all[:, :TOP].astype(jnp.int32), route_all[:, TOP:]
    pack_all = pack_all.reshape(width, -1)
    gate_all = gate_all.reshape(width, -1)
    qkv_cols = q_cols + 2 * kv_cols
    w_qkv = pack_all[:, :qkv_cols]
    wo = pack_all[:, qkv_cols : qkv_cols + q_cols]
    gain_one = pack_all[:, qkv_cols + q_cols].astype(F32)[None]
    gain_two = pack_all[:, qkv_cols + q_cols + 1].astype(F32)[None]

    segment, position = layout(lengths[0], order[0], span)
    cosine, sine = rotation(position)
    place = jnp.arange(span, dtype=jnp.int32)
    allowed = (segment[:, None] == segment[None, :]) & (place[None, :] <= place[:, None])
    factor_one = rms_factor(tokens_all)
    normed_attn = (tokens_all * factor_one * gain_one).astype(BF16)
    qkv = dot(normed_attn, w_qkv)
    qk = rotate(qkv[:, : q_cols + kv_cols], cosine, sine).astype(BF16)
    v = qkv[:, q_cols + kv_cols :].astype(BF16)
    q_heads = jnp.moveaxis(qk[:, :q_cols].reshape(span, kv_heads, repeat, HEAD_SIZE), 1, 0)
    k_heads = jnp.moveaxis(qk[:, q_cols:].reshape(span, kv_heads, HEAD_SIZE), 1, 0)
    v_heads = jnp.moveaxis(v.reshape(span, kv_heads, HEAD_SIZE), 1, 0)
    attended, probs = jax.vmap(functools.partial(attend_forward, allowed=allowed))(
        q_heads, k_heads, v_heads
    )
    attended = jnp.moveaxis(attended, 0, 1).reshape(span, q_cols).astype(BF16)
    attn_part = dot_nt(attended, wo).astype(BF16).reshape(members, rows, width)
    residual, normed_all, up_all, down_all = phases[1](
        attn_part,
        tokens,
        gain_two,
        expert_up.reshape(-1, own_experts * ff),
        expert_down.reshape(-1, own_experts * ff),
    )
    normed_all = normed_all.reshape(span, width)
    up_all, down_all = up_all.reshape(width, -1), down_all.reshape(width, -1)

    expert_of = member * own_experts + jnp.arange(own_experts, dtype=jnp.int32)
    named = ids_all[None, :, :] == expert_of[:, None, None]
    chosen = jnp.any(named, axis=2)
    weight = jnp.sum(jnp.where(named, gates_all[None], 0.0), axis=2)
    upto = (place[:, None] <= place[None, :]).astype(BF16)
    slot = dot(chosen.astype(BF16), upto).astype(jnp.int32) - 1
    slot = jnp.where(chosen & (slot < capacity), slot, -1)
    mixture, grad_normed, *by_kind = experts(
        slot, weight, normed_all, cot_all, gate_all, up_all, down_all, ff, capacity
    )
    output = (residual + branch_scale * scatter(mixture, "expert")).astype(BF16)
    by_kind = [one.reshape(devices, -1, own_experts * ff) for one in by_kind]

    grad_residual, gain_two_part, grad_attn_out, sum_gate, sum_up = phases[2](
        grad_normed.reshape(members, rows, width),
        residual,
        cotangent,
        gain_two,
        by_kind[0],
        by_kind[1],
    )
    grad_attn_out = grad_attn_out.reshape(span, width)
    term_out = dot_tn(grad_attn_out, attended)
    grad_attended = dot(grad_attn_out, wo).astype(BF16)
    grad_heads = jnp.moveaxis(grad_attended.reshape(span, kv_heads, repeat, HEAD_SIZE), 1, 0)
    grad_q, grad_k, grad_v = jax.vmap(functools.partial(attend_backward, allowed=allowed))(
        q_heads, k_heads, v_heads, probs, grad_heads
    )
    grad_qk = jnp.concatenate(
        [
            jnp.moveaxis(grad_q, 0, 1).reshape(span, q_cols),
            jnp.moveaxis(grad_k, 0, 1).reshape(span, kv_cols),
        ],
        axis=1,
    )
    grad_qkv = jnp.concatenate(
        [
            rotate(grad_qk, cosine, sine, back=True).astype(BF16),
            jnp.moveaxis(grad_v, 0, 1).reshape(span, kv_cols).astype(BF16),
        ],
        axis=1,
    )
    grad_norm_part = dot_nt(grad_qkv, w_qkv)
    gain_one_part = jnp.sum(grad_norm_part * tokens_all * factor_one, axis=0)
    term_qkv = dot_tn(normed_attn, grad_qkv)
    packed_grads = jnp.concatenate(
        [
            term_qkv,
            term_out,
            gain_one_part[:, None],
            gain_two_part.reshape(-1, 1),
            jnp.zeros((width, 126), F32),
        ],
        axis=1,
    )
    grad_tokens, per_member, sum_down = phases[3](
        grad_norm_part.astype(BF16).reshape(members, rows, width),
        grad_residual,
        tokens,
        gain_one,
        packed_grads.astype(BF16).reshape(devices, -1, packed_grads.shape[1]),
        by_kind[2],
    )
    per_member = per_member.astype(F32)

    def columns(first, cols):
        part = per_member[:, :, first : first + cols]
        return jnp.moveaxis(part, 0, 1).reshape(part.shape[1], -1)

    gains = jnp.sum(per_member[:, :, qkv_cols + q_cols :], axis=0)
    return (
        output,
        grad_tokens,
        gains[:, 0],
        gains[:, 1],
        columns(0, q_cols),
        columns(q_cols, kv_cols),
        columns(q_cols + kv_cols, kv_cols),
        columns(qkv_cols, q_cols),
        sum_gate.reshape(-1, own_experts, ff),
        sum_up.reshape(-1, own_experts, ff),
        sum_down.reshape(-1, own_experts, ff),
    )


def shards_fast(
    tokens,
    cotangent,
    gain_attn,
    gain_ffn,
    w_query,
    key_weight,
    value_weight,
    w_out,
    expert_gate,
    expert_up,
    expert_down,
    expert_ids,
    gates,
    lengths,
    order,
):
    rows, width = tokens.shape
    members, devices = lax.axis_size("expert"), lax.axis_size("dp")
    member = lax.axis_index("expert")
    span = rows * members
    own_experts, ff = expert_gate.shape[1], expert_gate.shape[2]
    capacity = rows * TOP // own_experts
    q_cols = w_query.shape[1] // members
    kv_cols = key_weight.shape[1] // members
    qkv_cols = q_cols + 2 * kv_cols
    kv_heads = kv_cols // HEAD_SIZE
    repeat = QUERY_HEADS // KEY_VALUE_HEADS

    def mine(weight, cols):
        return lax.dynamic_slice_in_dim(weight, member * cols, cols, axis=1)

    pack = jnp.concatenate(
        [
            mine(w_query, q_cols),
            mine(key_weight, kv_cols),
            mine(value_weight, kv_cols),
            mine(w_out, q_cols),
            gain_attn[:, None],
            gain_ffn[:, None],
            jnp.zeros((gain_attn.shape[0], 126), BF16),
        ],
        axis=1,
    )
    route = jnp.concatenate([expert_ids.astype(F32), gates], axis=1)
    segment, position = layout(lengths[0], order[0], span)
    cosine, sine = rotation(position)
    place = jnp.arange(span, dtype=jnp.int32)
    (
        cot_all, route_all, pack_all, gate_all, up_all, down_all,
        normed_attn, qkv, kx, vx, probs, attended, residual, normed_all,
    ) = forward_phase(
        members, tokens, cotangent, route, pack,
        expert_gate.reshape(-1, own_experts * ff),
        expert_up.reshape(-1, own_experts * ff),
        expert_down.reshape(-1, own_experts * ff),
        segment[None, :], segment[:, None],
        jnp.tile(cosine, (1, 4)),
        jnp.tile(jnp.concatenate([-sine, sine], axis=1), (1, 2)),
        q_cols, qkv_cols,
    )
    cot_all = cot_all.reshape(span, width)
    normed_all = normed_all.reshape(span, width)
    route_all = route_all.reshape(span, 2 * TOP)
    ids_all, gates_all = route_all[:, :TOP].astype(jnp.int32), route_all[:, TOP:]
    pack_all = pack_all.reshape(width, -1)
    gate_all, up_all, down_all = (w.reshape(width, -1) for w in (gate_all, up_all, down_all))
    w_qkv = pack_all[:, :qkv_cols]
    wo = pack_all[:, qkv_cols : qkv_cols + q_cols]
    gain_one = pack_all[:, qkv_cols + q_cols].astype(F32)[None]
    gain_two = pack_all[:, qkv_cols + q_cols + 1].astype(F32)[None]

    expert_of = member * own_experts + jnp.arange(own_experts, dtype=jnp.int32)
    named = ids_all[None, :, :] == expert_of[:, None, None]
    chosen = jnp.any(named, axis=2)
    weight = jnp.sum(jnp.where(named, gates_all[None], 0.0), axis=2)
    upto = (place[:, None] <= place[None, :]).astype(BF16)
    slot = dot(chosen.astype(BF16), upto).astype(jnp.int32) - 1
    slot = jnp.where(chosen & (slot < capacity), slot, -1)
    mixture, grad_normed, *by_kind = experts(
        slot, weight, normed_all, cot_all, gate_all, up_all, down_all, ff, capacity
    )
    output = (residual + branch_scale * scatter(mixture, "expert")).astype(BF16)
    by_kind = [one.reshape(devices, -1, own_experts * ff) for one in by_kind]

    grad_residual, gain_two_part, grad_attn_out, sum_gate, sum_up = third_phase(
        members,
        grad_normed.reshape(members, rows, width),
        residual,
        cotangent,
        gain_two,
        by_kind[0],
        by_kind[1],
    )
    grad_attn_out = grad_attn_out.reshape(span, width)
    term_out = dot_tn(grad_attn_out, attended)
    grad_attended = dot(grad_attn_out, wo).astype(BF16)
    grad_heads = jnp.moveaxis(grad_attended.reshape(span, kv_heads, repeat, HEAD_SIZE), 1, 0)
    allowed = (segment[:, None] == segment[None, :]) & (place[None, :] <= place[:, None])
    probs = jnp.where(allowed, probs.astype(F32), 0.0).reshape(kv_heads, repeat, span, span)
    q_heads = jnp.moveaxis(qkv[:, :q_cols].reshape(span, kv_heads, repeat, HEAD_SIZE), 1, 0) * BF16(64.0)
    k_heads = jnp.moveaxis(qkv[:, q_cols : q_cols + kv_cols].reshape(span, kv_heads, HEAD_SIZE), 1, 0)
    v_heads = jnp.moveaxis(qkv[:, q_cols + kv_cols :].reshape(span, kv_heads, HEAD_SIZE), 1, 0)
    grad_q, grad_k, grad_v = jax.vmap(functools.partial(attend_backward, allowed=allowed))(
        q_heads, k_heads, v_heads, probs, grad_heads
    )
    grad_qk = jnp.concatenate(
        [
            jnp.moveaxis(grad_q, 0, 1).reshape(span, q_cols),
            jnp.moveaxis(grad_k, 0, 1).reshape(span, kv_cols),
        ],
        axis=1,
    )
    grad_qkv = jnp.concatenate(
        [
            rotate(grad_qk, cosine, sine, back=True).astype(BF16),
            jnp.moveaxis(grad_v, 0, 1).reshape(span, kv_cols).astype(BF16),
        ],
        axis=1,
    )
    grad_norm_part = dot_nt(grad_qkv, w_qkv)
    gain_one_part = jnp.sum(grad_norm_part * normed_attn.astype(F32), axis=0) / gain_one[0]
    term_qkv = dot_tn(normed_attn, grad_qkv)
    packed_grads = jnp.concatenate(
        [
            term_qkv,
            term_out,
            gain_one_part[:, None],
            gain_two_part.reshape(-1, 1),
            jnp.zeros((width, 126), F32),
        ],
        axis=1,
    )
    grad_tokens, per_member, sum_down = fourth_phase(
        members,
        grad_norm_part.astype(BF16).reshape(members, rows, width),
        grad_residual,
        tokens,
        gain_one,
        packed_grads.astype(BF16).reshape(devices, -1, packed_grads.shape[1]),
        by_kind[2],
    )
    per_member = per_member.astype(F32)

    def columns(first, cols):
        part = per_member[:, :, first : first + cols]
        return jnp.moveaxis(part, 0, 1).reshape(part.shape[1], -1)

    gains = jnp.sum(per_member[:, :, qkv_cols + q_cols :], axis=0)
    return (
        output,
        grad_tokens,
        gains[:, 0],
        gains[:, 1],
        columns(0, q_cols),
        columns(q_cols, kv_cols),
        columns(q_cols + kv_cols, kv_cols),
        columns(qkv_cols, q_cols),
        sum_gate.reshape(-1, own_experts, ff),
        sum_up.reshape(-1, own_experts, ff),
        sum_down.reshape(-1, own_experts, ff),
    )


def solution(mesh):
    both = P(("dp", "expert"), None)
    row, rows = P("dp"), P("dp", None)
    experts = P("dp", "expert", None)
    fast = mesh.shape["dp"] == 8 and mesh.shape["expert"] == 4
    return jax.shard_map(
        shards_fast if fast else shards_plain,
        mesh=mesh,
        in_specs=(both, both, row, row, rows, rows, rows, rows)
        + (experts, experts, experts, both, both, rows, rows),
        out_specs=(both, both, row, row, rows, rows, rows, rows, experts, experts, experts),
        check_vma=False,
    )
```

```python
import functools

import jax
import jax.numpy as jnp
from jax import lax
from jax.experimental import pallas as pl
from jax.experimental.pallas import tpu as pltpu
from jax.sharding import PartitionSpec as P

QUERY_HEADS = 24
KEY_VALUE_HEADS = 8
HEAD_SIZE = 64
TOP = 8

epsilon = 1e-06
rope_base = 10000.0
score_scale = 0.015625
branch_scale = 0.22
F32 = jnp.float32
BF16 = jnp.bfloat16
MESH = pl.DeviceIdType.MESH
VMEM_LIMIT = 60 * 2**20


def layout(lengths_row, order_row, span):
    seqs = lengths_row.shape[0]
    slot_ids = jnp.arange(seqs, dtype=jnp.int32)
    picked = jnp.sum(
        jnp.where(order_row[:, None] == slot_ids[None, :], lengths_row[None, :], 0), axis=1
    )
    before = slot_ids[:, None] >= slot_ids[None, :]
    seq_ends = jnp.sum(jnp.where(before, picked[None, :], 0), axis=1)
    place = jnp.arange(span, dtype=jnp.int32)
    passed = place[:, None] >= seq_ends[None, :]
    segment = jnp.sum(passed.astype(jnp.int32), axis=1)
    start = jnp.sum(jnp.where(passed, picked[None, :], 0), axis=1)
    return segment, (place - start).astype(F32)


def rotation(position):
    half = HEAD_SIZE // 2
    frequency = rope_base ** (-(jnp.arange(half, dtype=F32) * (2.0 / HEAD_SIZE)))
    angles = position[:, None] * frequency[None, :]
    return jnp.cos(angles), jnp.sin(angles)


def rotate(rows, cosine, sine, back=False):
    t = rows.shape[0]
    heads = rows.reshape(t, -1, 2, HEAD_SIZE // 2)
    a, b = heads[:, :, 0], heads[:, :, 1]
    c, s = cosine[:, None, :], sine[:, None, :]
    if back:
        s = -s
    return jnp.stack([a * c - b * s, b * c + a * s], axis=2).reshape(t, -1)


def dot(a, b):
    return jnp.dot(a, b, preferred_element_type=F32)


def dot_nt(a, b):
    return jnp.einsum("tc,dc->td", a, b, preferred_element_type=F32)


def dot_tn(a, b):
    return jnp.einsum("td,tc->dc", a, b, preferred_element_type=F32)


def rms_factor(rows):
    return lax.rsqrt(jnp.mean(rows * rows, axis=-1, keepdims=True) + epsilon)


def norm_back(rows, factor, gain, grad):
    scaled = gain * grad
    return factor * scaled - rows * (factor * factor * factor) * jnp.mean(
        scaled * rows, axis=-1, keepdims=True
    )


def gather(x, axis):
    return lax.all_gather(x, axis, axis=0, tiled=True)


def scatter(x, axis):
    return lax.psum_scatter(x.astype(BF16), axis, scatter_dimension=0, tiled=True).astype(F32)


class Links:
    def __init__(self, send, recv, local, members):
        self.send, self.recv, self.local = send, recv, local
        self.remotes = self.locals = 0
        self.members = members
        self.d, self.z = lax.axis_index("dp"), lax.axis_index("expert")
        d = self.d
        core, x, y = d % 2, (d // 2) % 2, d // 4
        self.core = core
        self.sib = d + 1 - 2 * core
        self.x = d + 2 - 4 * x
        self.y = d + 4 - 8 * y
        self.diag = self.x + 4 - 8 * y
        self.waiting = []

    def other(self, d):
        return d + 1 - 2 * self.core

    def greet(self):
        barrier = pltpu.get_barrier_semaphore()
        last = self.members - 1

        def hello(d, z):
            pl.semaphore_signal(barrier, inc=1, device_id=(d, z), device_id_type=MESH)

        for d in (self.sib, self.x, self.y):
            hello(d, self.z)
        pl.when(self.z > 0)(lambda: hello(self.d, self.z - 1))
        pl.when(self.z < last)(lambda: hello(self.d, self.z + 1))
        ends = (self.z == 0).astype(jnp.int32) + (self.z == last).astype(jnp.int32)
        pl.semaphore_wait(barrier, 5 - ends)

    def remote(self, src, dst, to):
        k = self.remotes
        self.remotes += 1
        return pltpu.make_async_remote_copy(
            src_ref=src,
            dst_ref=dst,
            send_sem=self.send.at[k],
            recv_sem=self.recv.at[k],
            device_id=to,
            device_id_type=MESH,
        )

    def push(self, src, dst, d):
        copy = self.remote(src, dst, (d, self.z))
        copy.start()
        self.waiting.append(copy.wait_send)
        return copy

    def move(self, src, dst):
        k = self.locals
        self.locals += 1
        copy = pltpu.make_async_copy(src, dst, self.local.at[k])
        copy.start()
        return copy

    def finish(self):
        for wait in self.waiting:
            wait()


def run(order, **chains):
    for name in order:
        next(chains[name], None)
    chains = list(chains.values())
    while chains:
        for chain in list(chains):
            try:
                next(chain)
            except StopIteration:
                chains.remove(chain)


def line_gather(links, own, full):
    z, last = links.z, links.members - 1
    local = links.move(own, full.at[z])
    right, left = (links.d, z + 1), (links.d, z - 1)
    to_right, to_left = [], []
    for s in range(last):
        at_r, at_l = jnp.maximum(z - s, 0), jnp.minimum(z + s, last)
        to_right.append(links.remote(own if s == 0 else full.at[at_r], full.at[at_r], right))
        to_left.append(links.remote(own if s == 0 else full.at[at_l], full.at[at_l], left))
    for s in range(last):
        send_r, send_l = (z < last) & (z >= s), (z > 0) & (z + s <= last)
        pl.when(send_r)(to_right[s].start)
        pl.when(send_l)(to_left[s].start)
        yield
        pl.when((z > 0) & (z - 1 >= s))(to_right[s].wait_recv)
        pl.when((z < last) & (z + 1 + s <= last))(to_left[s].wait_recv)
    for s in range(last):
        send_r, send_l = (z < last) & (z >= s), (z > 0) & (z + s <= last)
        pl.when(send_r)(to_right[s].wait_send)
        pl.when(send_l)(to_left[s].wait_send)
    local.wait()


def add_rows(target, other, step=16):
    rows = target.shape[0]

    @pl.loop(0, rows // step)
    def _(i):
        at = pl.ds(pl.multiple_of(i * step, step), step)
        target[at] = (target[at].astype(F32) + other[at].astype(F32)).astype(target.dtype)


def line_scatter(links, part, acc, from_left, from_right):
    z, last = links.z, links.members - 1
    made = set()

    def make(o):
        if o not in made:
            made.add(o)
            part(o)

    to_right = {o: links.remote(acc.at[o], from_left.at[o], (links.d, z + 1)) for o in range(1, last + 1)}
    to_left = {o: links.remote(acc.at[o], from_right.at[o], (links.d, z - 1)) for o in range(last)}

    def pass_right(o):
        @pl.when(z > 0)
        def _():
            to_right[o].wait_recv()
            add_rows(acc.at[o], from_left.at[o])

        to_right[o].start()

    def pass_left(o):
        @pl.when(z < last)
        def _():
            to_left[o].wait_recv()
            add_rows(acc.at[o], from_right.at[o])

        to_left[o].start()

    @pl.when(z == 0)
    def _():
        from_left[0] = jnp.zeros(from_left.shape[1:], from_left.dtype)

    @pl.when(z == last)
    def _():
        from_right[last] = jnp.zeros(from_right.shape[1:], from_right.dtype)

    for j in range(last):
        make(last - j)
        make(j)
        pl.when((z < last - j) & (2 * z < last))(functools.partial(pass_right, last - j))
        pl.when(z > j)(functools.partial(pass_left, j))
        pl.when((z < last - j) & (2 * z >= last))(functools.partial(pass_right, last - j))
        yield
    for o in range(last + 1):

        @pl.when(z == o)
        def _(o=o):
            if o > 0:
                to_right[o].wait_recv()
            if o < last:
                to_left[o].wait_recv()

    for o in range(last + 1):
        if o > 0:
            pl.when(z < o)(to_right[o].wait_send)
        if o < last:
            pl.when(z > o)(to_left[o].wait_send)


def plane_gather(links, own, full):
    half = own.shape[0] // 2
    first, second = pl.ds(0, half), pl.ds(half, half)
    me = links.d
    local = links.move(own, full.at[me])
    by_x, by_y = {}, {}
    for by, d, h in ((by_y, links.y, first), (by_x, links.x, second), (by_x, links.x, first), (by_y, links.y, second)):
        by[h.start // half] = links.push(own.at[h], full.at[me, h], d)
    to_sib = [links.push(own, full.at[me], links.sib)]

    def share(d, h):
        to_sib.append(links.push(full.at[d, h], full.at[d, h], links.sib))

    yield
    by_y[0].wait_recv()
    over_x = links.push(full.at[links.y, first], full.at[links.y, first], links.x)
    share(links.y, first)
    by_x[1].wait_recv()
    over_y = links.push(full.at[links.x, second], full.at[links.x, second], links.y)
    share(links.x, second)
    yield
    by_x[0].wait_recv()
    share(links.x, first)
    by_y[1].wait_recv()
    share(links.y, second)
    yield
    over_x.wait_recv()
    share(links.diag, first)
    over_y.wait_recv()
    share(links.diag, second)
    yield
    for copy in to_sib:
        copy.wait_recv()
    local.wait()


def plane_scatter(links, part, mine, theirs, mid_x, mid_y, end_x, end_y):
    half = part.shape[1] // 2
    first, second = pl.ds(0, half), pl.ds(half, half)
    chips = (links.d, links.x, links.y, links.diag)
    from_sib, load = {}, {}
    held = [part.at[chip] if mine is None else mine.at[k] for k, chip in enumerate(chips)]
    for k in (3, 1, 2, 0):
        from_sib[k] = links.push(part.at[links.other(chips[k])], theirs.at[k], links.sib)
        if mine is not None:
            load[k] = links.move(part.at[chips[k]], held[k])
    yield
    for k in (3, 1, 2):
        if load:
            load[k].wait()
        from_sib[k].wait_recv()
        add_rows(held[k], theirs.at[k])
        if k == 3:
            to_mid_x = links.push(held[3].at[first], mid_x, links.x)
            to_mid_y = links.push(held[3].at[second], mid_y, links.y)
        if k == 1:
            to_end_x = links.push(held[1].at[first], end_x.at[first], links.x)
        if k == 2:
            to_end_y = links.push(held[2].at[second], end_y.at[second], links.y)
    yield
    to_mid_y.wait_recv()
    add_rows(held[1].at[second], mid_y)
    rest_x = links.push(held[1].at[second], end_x.at[second], links.x)
    to_mid_x.wait_recv()
    add_rows(held[2].at[first], mid_x)
    rest_y = links.push(held[2].at[first], end_y.at[first], links.y)
    yield
    if load:
        load[0].wait()
    from_sib[0].wait_recv()
    to_end_x.wait_recv()
    to_end_y.wait_recv()
    rest_x.wait_recv()
    rest_y.wait_recv()


def plane_scratch(rows, cols, mine=True):
    return [pltpu.VMEM((4, rows, cols), BF16)] * mine + [
        pltpu.VMEM((4, rows, cols), BF16),
        pltpu.VMEM((rows // 2, cols), BF16),
        pltpu.VMEM((rows // 2, cols), BF16),
        pltpu.VMEM((rows, cols), BF16),
        pltpu.VMEM((rows, cols), BF16),
    ]


def plane_result(mine, theirs, end_x, end_y, out, step=16):
    @pl.loop(0, out.shape[0] // step)
    def _(i):
        at = pl.ds(pl.multiple_of(i * step, step), step)
        own = mine[at].astype(F32) + theirs[0, at].astype(F32)
        out[at] = (own + end_x[at].astype(F32) + end_y[at].astype(F32)).astype(out.dtype)


def line_result(z, acc, from_left, from_right, at):
    return (
        acc[z, at].astype(F32) + from_left[z, at].astype(F32) + from_right[z, at].astype(F32)
    )


ANY = pl.BlockSpec(memory_space=pl.ANY)
VMEM = pl.BlockSpec(memory_space=pltpu.VMEM)


def comm_call(kernel, name, number, members, remotes, locals_, in_specs, out_specs, out_shape, scratch):
    return pl.pallas_call(
        functools.partial(kernel, members),
        out_shape=out_shape,
        in_specs=in_specs,
        out_specs=out_specs,
        scratch_shapes=[
            pltpu.SemaphoreType.DMA((remotes,)),
            pltpu.SemaphoreType.DMA((remotes,)),
            pltpu.SemaphoreType.DMA((locals_,)),
            *scratch,
        ],
        compiler_params=pltpu.CompilerParams(
            collective_id=number, has_side_effects=True, vmem_limit_bytes=VMEM_LIMIT
        ),
        name=name,
    )


def sds(shape, dtype):
    return jax.ShapeDtypeStruct(shape, dtype)


def third_kernel(members, part, residual, cot, gain, gate, up, grad_residual, gain_part, out_all, gate_out, up_out, send, recv, local, acc, from_left, from_right, grad_out, *rest):
    links = Links(send, recv, local, members)
    links.greet()
    for_gate, for_up = rest[:6], rest[6:]

    def chain():
        links.move(part, acc).wait()
        yield from line_scatter(links, lambda o: None, acc, from_left, from_right)
        gain_part[...] = jnp.zeros(gain_part.shape, F32)

        @pl.loop(0, residual.shape[0] // 16)
        def _(i):
            at = pl.ds(pl.multiple_of(i * 16, 16), 16)
            grad = line_result(links.z, acc, from_left, from_right, at)
            here = residual[at]
            factor = rms_factor(here)
            gain_part[...] += jnp.sum(grad * here * factor, axis=0, keepdims=True)
            total = cot[at].astype(F32) + norm_back(here, factor, gain[...], grad)
            grad_residual[at] = total
            grad_out[at] = (branch_scale * total).astype(BF16)

        yield from line_gather(links, grad_out, out_all)

    run(
        "zguguzzzguzgu",
        z=chain(),
        g=plane_scatter(links, gate, *for_gate),
        u=plane_scatter(links, up, *for_up),
    )
    plane_result(for_gate[0].at[0], for_gate[1], for_gate[4], for_gate[5], gate_out)
    plane_result(for_up[0].at[0], for_up[1], for_up[4], for_up[5], up_out)
    links.finish()


def third_phase(members, part, residual, cot, gain, gate, up):
    rows, width = cot.shape
    blocks = pltpu.VMEM((members, rows, width), BF16)
    return comm_call(
        third_kernel, "phase_three", 3, members, 60, 16,
        [ANY, VMEM, VMEM, VMEM, ANY, ANY], [VMEM, VMEM, ANY, VMEM, VMEM],
        [
            sds((rows, width), F32),
            sds((1, width), F32),
            sds((members, rows, width), BF16),
            sds(gate.shape[1:], F32),
            sds(up.shape[1:], F32),
        ],
        [blocks, blocks, blocks, pltpu.VMEM((rows, width), BF16)]
        + plane_scratch(*gate.shape[1:])
        + plane_scratch(*up.shape[1:]),
    )(part, residual, cot, gain, gate, up)


def dims(a, b):
    return (((a,), (b,)), ((), ()))


def mm(a, b):
    return lax.dot_general(a, b, dims(1, 0), preferred_element_type=F32)


def mm_nt(a, b):
    return lax.dot_general(a, b, dims(1, 1), preferred_element_type=F32)


def mm_tn(a, b):
    return lax.dot_general(a, b, dims(0, 0), preferred_element_type=F32)


def expert_kernel(capacity, slot_row, slot_col, weight_row, normed, cot, w_gate, w_up, w_down, mixture, grad_normed, d_gate, d_up, d_down, mix_sum, grad_sum):
    e = pl.program_id(0)
    span = normed.shape[0]

    @pl.when(e == 0)
    def _():
        mix_sum[...] = jnp.zeros(mix_sum.shape, F32)
        grad_sum[...] = jnp.zeros(grad_sum.shape, F32)

    slots = slot_row[0]
    picks = slots == lax.broadcasted_iota(jnp.int32, (capacity, span), 0)
    pick = picks.astype(BF16)
    gate_col = jnp.sum(jnp.where(picks, weight_row[0], 0.0), axis=1, keepdims=True)
    put = (slot_col[0] == lax.broadcasted_iota(jnp.int32, (span, capacity), 1)).astype(BF16)
    received = mm(pick, normed[...]).astype(BF16)
    pre_gate, pre_up = mm(received, w_gate[...]), mm(received, w_up[...])
    sig = 1.0 / (1.0 + jnp.exp(-pre_gate))
    silu = pre_gate * sig
    activ = (silu * pre_up).astype(BF16)
    produced = (gate_col * mm_nt(activ, w_down[...])).astype(BF16)
    mix_sum[...] += mm(put, produced)
    grad_out = (gate_col * (branch_scale * mm(pick, cot[...]))).astype(BF16)
    grad_activ = mm(grad_out, w_down[...])
    grad_gate = (grad_activ * pre_up * (sig * (1.0 + pre_gate * (1.0 - sig)))).astype(BF16)
    grad_up = (grad_activ * silu).astype(BF16)
    grad_pair = (mm_nt(grad_gate, w_gate[...]) + mm_nt(grad_up, w_up[...])).astype(BF16)
    grad_sum[...] += mm(put, grad_pair)
    d_gate[...] = mm_tn(received, grad_gate).astype(BF16)
    d_up[...] = mm_tn(received, grad_up).astype(BF16)
    d_down[...] = mm_tn(grad_out, activ).astype(BF16)

    @pl.when(e == pl.num_programs(0) - 1)
    def _():
        mixture[...] = mix_sum[...].astype(BF16)
        grad_normed[...] = grad_sum[...].astype(BF16)


def experts(slot, weight, normed, cot, w_gate, w_up, w_down, ff, capacity):
    own_experts, span = slot.shape
    width = normed.shape[1]
    whole = pl.BlockSpec((span, width), lambda e: (0, 0))
    column = pl.BlockSpec((width, ff), lambda e: (0, e))
    row = pl.BlockSpec((1, 1, span), lambda e: (e, 0, 0))
    grads = jax.ShapeDtypeStruct(w_gate.shape, BF16)
    rows = jax.ShapeDtypeStruct((span, width), BF16)
    return pl.pallas_call(
        functools.partial(expert_kernel, capacity),
        grid=(own_experts,),
        in_specs=[row, pl.BlockSpec((1, span, 1), lambda e: (e, 0, 0)), row, whole, whole, column, column, column],
        out_specs=[whole, whole, column, column, column],
        out_shape=[rows, rows, grads, grads, grads],
        scratch_shapes=[pltpu.VMEM((span, width), F32), pltpu.VMEM((span, width), F32)],
        compiler_params=pltpu.CompilerParams(vmem_limit_bytes=VMEM_LIMIT),
        name="experts",
    )(slot[:, None, :], slot[:, :, None], weight[:, None, :], normed, cot, w_gate, w_up, w_down)


LANES = 128


def lane_ids(rows):
    return lax.broadcasted_iota(jnp.int32, (rows, LANES), 1)


def turn(x, cosine, sine):
    half = HEAD_SIZE // 2
    ahead, behind = pltpu.roll(x, LANES - half, axis=1), pltpu.roll(x, half, axis=1)
    partner = jnp.where(lane_ids(x.shape[0]) % HEAD_SIZE < half, ahead, behind)
    return x * cosine + partner * sine


def spread(block, at, out):
    low = lane_ids(block.shape[0]) < HEAD_SIZE
    other = pltpu.roll(block, HEAD_SIZE, axis=1)
    zero = jnp.zeros_like(block)
    out[0, 0, at] = jnp.where(low, block, zero).astype(BF16)
    out[0, 1, at] = jnp.where(low, zero, other).astype(BF16)
    out[1, 0, at] = jnp.where(low, other, zero).astype(BF16)
    out[1, 1, at] = jnp.where(low, zero, block).astype(BF16)


def attention_setup(seg_row, seg_col, bias):
    span = bias.shape[0]
    for b in range(span // LANES):
        at = pl.ds(b * LANES, LANES)
        row = b * LANES + lax.broadcasted_iota(jnp.int32, (LANES, span), 0)
        col = lax.broadcasted_iota(jnp.int32, (LANES, span), 1)
        ok = (seg_col[at] == seg_row[...]) & (col <= row)
        bias[at] = jnp.where(ok, 0.0, -1e30)


def weight_columns(pack_all, first, cols):
    return pack_all[:, :, first : first + cols].reshape(-1, cols)


def gain_rows(pack_all, first):
    pick = lax.broadcasted_iota(jnp.int32, (16, LANES), 0) == lax.broadcasted_iota(jnp.int32, (16, LANES), 1)
    return mm_nt(pick.astype(BF16), weight_columns(pack_all, first, LANES))


def attend_steps(qkv, kx, vx, bias, probs, attended):
    span, blocks = qkv.shape[0], attended.shape[1] // LANES
    repeat = QUERY_HEADS // KEY_VALUE_HEADS
    for j in range(blocks):
        for b in range(span // LANES):
            at, keys = pl.ds(b * LANES, LANES), (b + 1) * LANES
            q = qkv[at, j * LANES : (j + 1) * LANES]
            total = jnp.zeros((LANES, LANES), F32)
            for half in range(2):
                h = 2 * j + half
                kv = h // repeat
                scores = mm_nt(q, kx[kv, half, :keys]) + bias[at, :keys]
                peak = jnp.max(scores, axis=1, keepdims=True)
                exponent = jnp.exp(scores - peak)
                share = 1.0 / jnp.sum(exponent, axis=1, keepdims=True)
                low = (exponent * share).astype(BF16)
                probs[h, at, :keys] = low
                total += mm(low, vx[kv, half, :keys])
            attended[at, j * LANES : (j + 1) * LANES] = total.astype(BF16)
        yield


def forward_kernel(
    members, tokens, cot, route, pack, gate, up, down, seg_row, seg_col, cosine, sine,
    cot_all, route_all, pack_all, gate_all, up_all, down_all, normed_attn, qkv, kx, vx, probs, attended, residual, normed_all,
    send, recv, local, tokens_all, bias, acc, from_left, from_right, normed,
):
    links = Links(send, recv, local, members)
    links.greet()
    rows, width = tokens.shape
    span = rows * members
    q_cols = attended.shape[1]
    qkv_cols = qkv.shape[1]

    def produce(o):
        acc[o] = mm_nt(attended[o * rows : (o + 1) * rows], weight_columns(pack_all, qkv_cols, q_cols)).astype(BF16)

    def chain():
        attention_setup(seg_row, seg_col, bias)
        yield
        gains = gain_rows(pack_all, qkv_cols + q_cols)

        @pl.loop(0, span // 16)
        def _(i):
            here = tokens_all[i // (rows // 16), pl.ds(pl.multiple_of(i % (rows // 16) * 16, 16), 16)].astype(F32)
            normed_attn[pl.ds(pl.multiple_of(i * 16, 16), 16)] = (here * rms_factor(here) * gains[0:1]).astype(BF16)

        @pl.loop(0, span // LANES)
        def _(i):
            at = pl.ds(pl.multiple_of(i * LANES, LANES), LANES)
            here = mm(normed_attn[at], weight_columns(pack_all, 0, qkv_cols))
            c, s = cosine[at], sine[at]
            for j in range(q_cols // LANES):
                lanes = slice(j * LANES, (j + 1) * LANES)
                qkv[at, lanes] = (turn(here[:, lanes], c, s).astype(BF16).astype(F32) * score_scale).astype(BF16)
            key = turn(here[:, q_cols : q_cols + LANES], c, s)
            value = here[:, q_cols + LANES :]
            qkv[at, q_cols : q_cols + LANES] = key.astype(BF16)
            qkv[at, q_cols + LANES :] = value.astype(BF16)
            spread(key, at, kx)
            spread(value, at, vx)

        yield
        yield from attend_steps(qkv, kx, vx, bias, probs, attended)
        yield from line_scatter(links, produce, acc, from_left, from_right)

        @pl.loop(0, rows // 16)
        def _(i):
            at = pl.ds(pl.multiple_of(i * 16, 16), 16)
            here = tokens[at].astype(F32) + branch_scale * line_result(links.z, acc, from_left, from_right, at)
            residual[at] = here
            normed[at] = (here * rms_factor(here) * gains[1:2]).astype(BF16)

        yield from line_gather(links, normed, normed_all)

    run(
        FORWARD_ORDER,
        t=line_gather(links, tokens, tokens_all),
        r=line_gather(links, route, route_all),
        c=line_gather(links, cot, cot_all),
        p=plane_gather(links, pack, pack_all),
        g=plane_gather(links, gate, gate_all),
        u=plane_gather(links, up, up_all),
        d=plane_gather(links, down, down_all),
        a=chain(),
    )
    links.finish()


FORWARD_ORDER = "trpgatrputrpppdtrcaggacguaucaudcauaddacadada"


def forward_phase(members, tokens, cot, route, pack, gate, up, down, seg_row, seg_col, cosine, sine, q_cols, qkv_cols):
    rows, width = tokens.shape
    span = rows * members
    blocks = pltpu.VMEM((members, rows, width), BF16)
    heads = q_cols // HEAD_SIZE
    return comm_call(
        forward_kernel, "forward", 1, members, 100, 16,
        [VMEM, ANY, ANY, ANY, ANY, ANY, ANY, VMEM, VMEM, VMEM, VMEM],
        [ANY, ANY, VMEM, ANY, ANY, ANY, VMEM, VMEM, VMEM, VMEM, VMEM, VMEM, VMEM, ANY],
        [
            sds((members, rows, width), BF16),
            sds((members, *route.shape), F32),
            sds((8, *pack.shape), BF16),
            sds((8, *gate.shape), BF16),
            sds((8, *up.shape), BF16),
            sds((8, *down.shape), BF16),
            sds((span, width), BF16),
            sds((span, qkv_cols), BF16),
            sds((2, 2, span, LANES), BF16),
            sds((2, 2, span, LANES), BF16),
            sds((heads, span, span), BF16),
            sds((span, q_cols), BF16),
            sds((rows, width), F32),
            sds((members, rows, width), BF16),
        ],
        [
            blocks,
            pltpu.VMEM((span, span), F32),
            blocks,
            blocks,
            blocks,
            pltpu.VMEM((rows, width), BF16),
        ],
    )(tokens, cot, route, pack, gate, up, down, seg_row, seg_col, cosine, sine)


def attend_back_steps(qkv, kx, vx, probs, grad_attended, cosine, sine, grad_k, grad_v, grad_qkv):
    span = qkv.shape[0]
    blocks = grad_attended.shape[1] // LANES
    repeat = QUERY_HEADS // KEY_VALUE_HEADS
    grad_k[...] = jnp.zeros(grad_k.shape, F32)
    grad_v[...] = jnp.zeros(grad_v.shape, F32)
    for j in range(blocks):
        lanes = slice(j * LANES, (j + 1) * LANES)
        for b in range(span // LANES):
            at, keys = pl.ds(b * LANES, LANES), (b + 1) * LANES
            q, grad = qkv[at, lanes], grad_attended[at, lanes]
            total = jnp.zeros((LANES, LANES), F32)
            for half in range(2):
                h = 2 * j + half
                kv = h // repeat
                low = probs[h, at, :keys]
                share = low.astype(F32)
                grad_probs = mm_nt(grad, vx[kv, half, :keys])
                inner = jnp.sum(share * grad_probs, axis=1, keepdims=True)
                grad_scores = (share * (grad_probs - inner)).astype(BF16)
                total += mm(grad_scores, kx[kv, half, :keys])
                grad_k[kv, half, :keys] += mm_tn(grad_scores, q)
                grad_v[kv, half, :keys] += mm_tn(low, grad)
            grad_qkv[at, lanes] = turn(total * score_scale, cosine[at], -sine[at]).astype(BF16)
        yield
    first = blocks * LANES

    def fold(parts, at):
        low = lane_ids(LANES) < HEAD_SIZE
        same = jnp.where(low, parts[0, 0, at], parts[1, 1, at])
        crossed = jnp.where(low, parts[1, 0, at], parts[0, 1, at])
        return same + pltpu.roll(crossed, HEAD_SIZE, axis=1)

    for b in range(span // LANES):
        at = pl.ds(b * LANES, LANES)
        grad_qkv[at, first : first + LANES] = turn(fold(grad_k, at), cosine[at], -sine[at]).astype(BF16)
        grad_qkv[at, first + LANES :] = fold(grad_v, at).astype(BF16)


def backward_kernel(
    members, mixture, residual, grad_out_all, grad_residual, gain_ffn_part, tokens, down, pack_all, normed_attn, qkv, kx, vx, probs, attended, cosine, sine,
    output, grad_tokens, gains, d_query, d_key, d_value, d_out, d_down,
    send, recv, local, acc_m, left_m, right_m, acc, from_left, from_right, grad_attended, grad_k, grad_v, grad_qkv, gain_part,
    for_w_out, for_w_qkv, own_out, own_qkv, all_out, all_qkv, *rest,
):
    links = Links(send, recv, local, members)
    links.greet()
    rows, width = tokens.shape
    q_cols, qkv_cols = attended.shape[1], qkv.shape[1]
    kv_cols = (qkv_cols - q_cols) // 2
    with_out, with_qkv, with_down = rest[:5], rest[5:10], rest[10:]
    pairs = for_w_out.shape[0] // 2
    step = width // pairs
    row_gains = gain_rows(pack_all, qkv_cols + q_cols)

    def out_chain():
        for i in range(pairs):
            term = mm_tn(grad_out_all[:, i * step : (i + 1) * step], attended[...])
            for_w_out[2 * i : 2 * i + 2] = term.astype(BF16).reshape(2, step // 2, q_cols)
        yield from plane_scatter(links, for_w_out, None, *with_out)
        plane_result(for_w_out.at[links.d], with_out[0], with_out[3], with_out[4], own_out)
        yield from line_gather(links, own_out, all_out)

    def produce(o):
        at = slice(o * rows, (o + 1) * rows)
        part = mm_nt(grad_qkv[at], weight_columns(pack_all, 0, qkv_cols))
        gain_part[...] += jnp.sum(part * normed_attn[at].astype(F32), axis=0, keepdims=True)
        acc[o] = part.astype(BF16)

    def chain():
        wo = weight_columns(pack_all, qkv_cols, q_cols)

        @pl.loop(0, grad_attended.shape[0] // LANES)
        def _(i):
            at = pl.ds(pl.multiple_of(i * LANES, LANES), LANES)
            grad_attended[at] = mm(grad_out_all[at], wo).astype(BF16)

        yield
        yield from attend_back_steps(qkv, kx, vx, probs, grad_attended, cosine, sine, grad_k, grad_v, grad_qkv)
        gain_part[...] = jnp.zeros(gain_part.shape, F32)
        yield from line_scatter(links, produce, acc, from_left, from_right)

        @pl.loop(0, rows // 16)
        def _(i):
            at = pl.ds(pl.multiple_of(i * 16, 16), 16)
            grad = line_result(links.z, acc, from_left, from_right, at)
            here = tokens[at].astype(F32)
            grad_tokens[at] = grad_residual[at] + norm_back(here, rms_factor(here), row_gains[0:1], grad)

    def qkv_chain():
        for i in range(pairs):
            term = mm_tn(normed_attn[:, i * step : (i + 1) * step], grad_qkv[...])
            for_w_qkv[2 * i : 2 * i + 2, :, :qkv_cols] = term.astype(BF16).reshape(2, step // 2, qkv_cols)
        which = lax.broadcasted_iota(jnp.int32, (16, width), 0)
        both = jnp.where(which == 0, gain_part[...] / row_gains[0:1], jnp.where(which == 1, gain_ffn_part[...], 0.0))
        pick = lax.broadcasted_iota(jnp.int32, (16, LANES), 0) == lax.broadcasted_iota(jnp.int32, (16, LANES), 1)
        columns = mm_tn(both.astype(BF16), pick.astype(BF16))
        for_w_qkv[:, :, qkv_cols:] = columns.astype(BF16).reshape(2 * pairs, step // 2, LANES)
        yield from plane_scatter(links, for_w_qkv, None, *with_qkv)
        plane_result(for_w_qkv.at[links.d], with_qkv[0], with_qkv[3], with_qkv[4], own_qkv)
        yield from line_gather(links, own_qkv, all_qkv)

    def mixture_chain():
        links.move(mixture, acc_m).wait()
        yield from line_scatter(links, lambda o: None, acc_m, left_m, right_m)

        @pl.loop(0, rows // 16)
        def _(i):
            at = pl.ds(pl.multiple_of(i * 16, 16), 16)
            here = residual[at] + branch_scale * line_result(links.z, acc_m, left_m, right_m, at)
            output[at] = here.astype(BF16)

    run(
        BACKWARD_ORDER,
        m=mixture_chain(),
        d=plane_scatter(links, down, *with_down),
        o=out_chain(),
        a=chain(),
        q=qkv_chain(),
    )
    plane_result(with_down[0].at[0], with_down[1], with_down[4], with_down[5], d_down)
    for m in range(members):
        d_out[:, m * q_cols : (m + 1) * q_cols] = all_out[m].astype(F32)
        d_query[:, m * q_cols : (m + 1) * q_cols] = all_qkv[m, :, :q_cols].astype(F32)
        d_key[:, m * kv_cols : (m + 1) * kv_cols] = all_qkv[m, :, q_cols : q_cols + kv_cols].astype(F32)
        d_value[:, m * kv_cols : (m + 1) * kv_cols] = all_qkv[m, :, q_cols + kv_cols : qkv_cols].astype(F32)
    gains[...] = sum(all_qkv[m, :, qkv_cols:].astype(F32) for m in range(members))
    links.finish()


BACKWARD_ORDER = "mododmaoaomaodmaodaoaqaqaoqaq"


def backward_phase(members, mixture, residual, grad_out_all, grad_residual, gain_ffn_part, tokens, down, pack_all, normed_attn, qkv, kx, vx, probs, attended, cosine, sine):
    rows, width = tokens.shape
    span, q_cols = attended.shape
    qkv_cols = qkv.shape[1]
    kv_cols = (qkv_cols - q_cols) // 2
    devices, own = down.shape[:2]
    line = [pltpu.VMEM((members, rows, width), BF16)] * 3
    return comm_call(
        backward_kernel, "backward", 4, members, 100, 32,
        [ANY, VMEM, VMEM, VMEM, VMEM, VMEM, ANY] + [VMEM] * 9,
        [VMEM] * 8,
        [
            sds((rows, width), BF16),
            sds((rows, width), F32),
            sds((own, LANES), F32),
            sds((own, members * q_cols), F32),
            sds((own, members * kv_cols), F32),
            sds((own, members * kv_cols), F32),
            sds((own, members * q_cols), F32),
            sds(down.shape[1:], F32),
        ],
        [
            *line,
            *line,
            pltpu.VMEM((span, q_cols), BF16),
            pltpu.VMEM((2, 2, span, LANES), F32),
            pltpu.VMEM((2, 2, span, LANES), F32),
            pltpu.VMEM((span, qkv_cols), BF16),
            pltpu.VMEM((1, width), F32),
            pltpu.VMEM((devices, own, q_cols), BF16),
            pltpu.VMEM((devices, own, qkv_cols + LANES), BF16),
            pltpu.VMEM((own, q_cols), BF16),
            pltpu.VMEM((own, qkv_cols + LANES), BF16),
            pltpu.VMEM((members, own, q_cols), BF16),
            pltpu.VMEM((members, own, qkv_cols + LANES), BF16),
            *plane_scratch(own, q_cols, False),
            *plane_scratch(own, qkv_cols + LANES, False),
            *plane_scratch(*down.shape[1:]),
        ],
    )(mixture, residual, grad_out_all, grad_residual, gain_ffn_part, tokens, down, pack_all, normed_attn, qkv, kx, vx, probs, attended, cosine, sine)


def all_blocks(x, axis):
    return lax.all_gather(x, axis, axis=0)


def plain_first(members, tokens, cot, route, pack, gate):
    return (
        all_blocks(tokens, "expert"),
        all_blocks(cot, "expert"),
        all_blocks(route, "expert"),
        all_blocks(pack, "dp"),
        all_blocks(gate, "dp"),
    )


def line_sum(part):
    return scatter(part.reshape(-1, part.shape[2]), "expert")


def plain_second(members, part, tokens, gain, up, down):
    residual = tokens.astype(F32) + branch_scale * line_sum(part)
    normed = (residual * rms_factor(residual) * gain).astype(BF16)
    return residual, all_blocks(normed, "expert"), all_blocks(up, "dp"), all_blocks(down, "dp")


def plane_sum(part):
    return scatter(part.reshape(-1, part.shape[2]), "dp")


def plain_third(members, part, residual, cot, gain, gate, up):
    grad = line_sum(part)
    factor = rms_factor(residual)
    gain_part = jnp.sum(grad * residual * factor, axis=0, keepdims=True)
    total = cot.astype(F32) + norm_back(residual, factor, gain, grad)
    out_all = all_blocks((branch_scale * total).astype(BF16), "expert")
    return total, gain_part, out_all, plane_sum(gate), plane_sum(up)


def plain_fourth(members, part, grad_residual, tokens, gain, pack, down):
    here = tokens.astype(F32)
    grad_tokens = grad_residual + norm_back(here, rms_factor(here), gain, line_sum(part))
    return grad_tokens, all_blocks(plane_sum(pack).astype(BF16), "expert"), plane_sum(down)


def attend_forward(q, k, v, allowed):
    scores = jnp.einsum("irh,jh->rij", q, k, preferred_element_type=F32) * score_scale
    scores = jnp.where(allowed[None], scores, -1e30)
    peak = jnp.max(scores, axis=-1, keepdims=True)
    exponent = jnp.exp(scores - peak)
    total = jnp.sum(exponent, axis=-1, keepdims=True)
    probs = exponent / total
    return jnp.einsum("rij,jh->irh", probs.astype(BF16), v, preferred_element_type=F32), probs


def attend_backward(q, k, v, probs, grad, allowed):
    grad_probs = jnp.einsum("irh,jh->rij", grad, v, preferred_element_type=F32)
    inner = jnp.sum(probs * grad_probs, axis=-1, keepdims=True)
    grad_scores = (probs * (grad_probs - inner)).astype(BF16)
    grad_q = jnp.einsum("rij,jh->irh", grad_scores, k, preferred_element_type=F32) * score_scale
    grad_k = jnp.einsum("rij,irh->jh", grad_scores, q, preferred_element_type=F32) * score_scale
    grad_v = jnp.einsum("rij,irh->jh", probs.astype(BF16), grad, preferred_element_type=F32)
    return grad_q, grad_k, grad_v


def shards_plain(
    tokens,
    cotangent,
    gain_attn,
    gain_ffn,
    w_query,
    key_weight,
    value_weight,
    w_out,
    expert_gate,
    expert_up,
    expert_down,
    expert_ids,
    gates,
    lengths,
    order,
):
    rows, width = tokens.shape
    members = lax.axis_size("expert")
    member = lax.axis_index("expert")
    span = rows * members
    own_experts, ff = expert_gate.shape[1], expert_gate.shape[2]
    capacity = rows * TOP // own_experts
    q_cols = w_query.shape[1] // members
    kv_cols = key_weight.shape[1] // members
    kv_heads = kv_cols // HEAD_SIZE
    repeat = QUERY_HEADS // KEY_VALUE_HEADS

    def mine(weight, cols):
        return lax.dynamic_slice_in_dim(weight, member * cols, cols, axis=1)

    devices = lax.axis_size("dp")
    phases = [
        functools.partial(phase, members)
        for phase in (plain_first, plain_second, plain_third, plain_fourth)
    ]

    pack = jnp.concatenate(
        [
            mine(w_query, q_cols),
            mine(key_weight, kv_cols),
            mine(value_weight, kv_cols),
            mine(w_out, q_cols),
            gain_attn[:, None],
            gain_ffn[:, None],
            jnp.zeros((gain_attn.shape[0], 126), BF16),
        ],
        axis=1,
    )
    route = jnp.concatenate([expert_ids.astype(F32), gates], axis=1)
    tokens_all, cot_all, route_all, pack_all, gate_all = phases[0](
        tokens, cotangent, route, pack, expert_gate.reshape(-1, own_experts * ff)
    )
    tokens_all = tokens_all.reshape(span, width).astype(F32)
    cot_all = cot_all.reshape(span, width)
    route_all = route_all.reshape(span, 2 * TOP)
    ids_all, gates_all = route_all[:, :TOP].astype(jnp.int32), route_all[:, TOP:]
    pack_all = pack_all.reshape(width, -1)
    gate_all = gate_all.reshape(width, -1)
    qkv_cols = q_cols + 2 * kv_cols
    w_qkv = pack_all[:, :qkv_cols]
    wo = pack_all[:, qkv_cols : qkv_cols + q_cols]
    gain_one = pack_all[:, qkv_cols + q_cols].astype(F32)[None]
    gain_two = pack_all[:, qkv_cols + q_cols + 1].astype(F32)[None]

    segment, position = layout(lengths[0], order[0], span)
    cosine, sine = rotation(position)
    place = jnp.arange(span, dtype=jnp.int32)
    allowed = (segment[:, None] == segment[None, :]) & (place[None, :] <= place[:, None])
    factor_one = rms_factor(tokens_all)
    normed_attn = (tokens_all * factor_one * gain_one).astype(BF16)
    qkv = dot(normed_attn, w_qkv)
    qk = rotate(qkv[:, : q_cols + kv_cols], cosine, sine).astype(BF16)
    v = qkv[:, q_cols + kv_cols :].astype(BF16)
    q_heads = jnp.moveaxis(qk[:, :q_cols].reshape(span, kv_heads, repeat, HEAD_SIZE), 1, 0)
    k_heads = jnp.moveaxis(qk[:, q_cols:].reshape(span, kv_heads, HEAD_SIZE), 1, 0)
    v_heads = jnp.moveaxis(v.reshape(span, kv_heads, HEAD_SIZE), 1, 0)
    attended, probs = jax.vmap(functools.partial(attend_forward, allowed=allowed))(
        q_heads, k_heads, v_heads
    )
    attended = jnp.moveaxis(attended, 0, 1).reshape(span, q_cols).astype(BF16)
    attn_part = dot_nt(attended, wo).astype(BF16).reshape(members, rows, width)
    residual, normed_all, up_all, down_all = phases[1](
        attn_part,
        tokens,
        gain_two,
        expert_up.reshape(-1, own_experts * ff),
        expert_down.reshape(-1, own_experts * ff),
    )
    normed_all = normed_all.reshape(span, width)
    up_all, down_all = up_all.reshape(width, -1), down_all.reshape(width, -1)

    expert_of = member * own_experts + jnp.arange(own_experts, dtype=jnp.int32)
    named = ids_all[None, :, :] == expert_of[:, None, None]
    chosen = jnp.any(named, axis=2)
    weight = jnp.sum(jnp.where(named, gates_all[None], 0.0), axis=2)
    upto = (place[:, None] <= place[None, :]).astype(BF16)
    slot = dot(chosen.astype(BF16), upto).astype(jnp.int32) - 1
    slot = jnp.where(chosen & (slot < capacity), slot, -1)
    mixture, grad_normed, *by_kind = experts(
        slot, weight, normed_all, cot_all, gate_all, up_all, down_all, ff, capacity
    )
    output = (residual + branch_scale * scatter(mixture, "expert")).astype(BF16)
    by_kind = [one.reshape(devices, -1, own_experts * ff) for one in by_kind]

    grad_residual, gain_two_part, grad_attn_out, sum_gate, sum_up = phases[2](
        grad_normed.reshape(members, rows, width),
        residual,
        cotangent,
        gain_two,
        by_kind[0],
        by_kind[1],
    )
    grad_attn_out = grad_attn_out.reshape(span, width)
    term_out = dot_tn(grad_attn_out, attended)
    grad_attended = dot(grad_attn_out, wo).astype(BF16)
    grad_heads = jnp.moveaxis(grad_attended.reshape(span, kv_heads, repeat, HEAD_SIZE), 1, 0)
    grad_q, grad_k, grad_v = jax.vmap(functools.partial(attend_backward, allowed=allowed))(
        q_heads, k_heads, v_heads, probs, grad_heads
    )
    grad_qk = jnp.concatenate(
        [
            jnp.moveaxis(grad_q, 0, 1).reshape(span, q_cols),
            jnp.moveaxis(grad_k, 0, 1).reshape(span, kv_cols),
        ],
        axis=1,
    )
    grad_qkv = jnp.concatenate(
        [
            rotate(grad_qk, cosine, sine, back=True).astype(BF16),
            jnp.moveaxis(grad_v, 0, 1).reshape(span, kv_cols).astype(BF16),
        ],
        axis=1,
    )
    grad_norm_part = dot_nt(grad_qkv, w_qkv)
    gain_one_part = jnp.sum(grad_norm_part * tokens_all * factor_one, axis=0)
    term_qkv = dot_tn(normed_attn, grad_qkv)
    packed_grads = jnp.concatenate(
        [
            term_qkv,
            term_out,
            gain_one_part[:, None],
            gain_two_part.reshape(-1, 1),
            jnp.zeros((width, 126), F32),
        ],
        axis=1,
    )
    grad_tokens, per_member, sum_down = phases[3](
        grad_norm_part.astype(BF16).reshape(members, rows, width),
        grad_residual,
        tokens,
        gain_one,
        packed_grads.astype(BF16).reshape(devices, -1, packed_grads.shape[1]),
        by_kind[2],
    )
    per_member = per_member.astype(F32)

    def columns(first, cols):
        part = per_member[:, :, first : first + cols]
        return jnp.moveaxis(part, 0, 1).reshape(part.shape[1], -1)

    gains = jnp.sum(per_member[:, :, qkv_cols + q_cols :], axis=0)
    return (
        output,
        grad_tokens,
        gains[:, 0],
        gains[:, 1],
        columns(0, q_cols),
        columns(q_cols, kv_cols),
        columns(q_cols + kv_cols, kv_cols),
        columns(qkv_cols, q_cols),
        sum_gate.reshape(-1, own_experts, ff),
        sum_up.reshape(-1, own_experts, ff),
        sum_down.reshape(-1, own_experts, ff),
    )


def shards_fast(
    tokens,
    cotangent,
    gain_attn,
    gain_ffn,
    w_query,
    key_weight,
    value_weight,
    w_out,
    expert_gate,
    expert_up,
    expert_down,
    expert_ids,
    gates,
    lengths,
    order,
):
    rows, width = tokens.shape
    members, devices = lax.axis_size("expert"), lax.axis_size("dp")
    member = lax.axis_index("expert")
    span = rows * members
    own_experts, ff = expert_gate.shape[1], expert_gate.shape[2]
    capacity = rows * TOP // own_experts
    q_cols = w_query.shape[1] // members
    kv_cols = key_weight.shape[1] // members
    qkv_cols = q_cols + 2 * kv_cols

    def mine(weight, cols):
        return lax.dynamic_slice_in_dim(weight, member * cols, cols, axis=1)

    pack = jnp.concatenate(
        [
            mine(w_query, q_cols),
            mine(key_weight, kv_cols),
            mine(value_weight, kv_cols),
            mine(w_out, q_cols),
            gain_attn[:, None],
            gain_ffn[:, None],
            jnp.zeros((gain_attn.shape[0], 126), BF16),
        ],
        axis=1,
    )
    route = jnp.concatenate([expert_ids.astype(F32), gates], axis=1)
    segment, position = layout(lengths[0], order[0], span)
    cosine, sine = rotation(position)
    cosine = jnp.tile(cosine, (1, 4))
    sine = jnp.tile(jnp.concatenate([-sine, sine], axis=1), (1, 2))
    place = jnp.arange(span, dtype=jnp.int32)
    (
        cot_all, route_all, pack_all, gate_all, up_all, down_all,
        normed_attn, qkv, kx, vx, probs, attended, residual, normed_all,
    ) = forward_phase(
        members, tokens, cotangent, route, pack,
        expert_gate.reshape(-1, own_experts * ff),
        expert_up.reshape(-1, own_experts * ff),
        expert_down.reshape(-1, own_experts * ff),
        segment[None, :], segment[:, None],
        cosine, sine,
        q_cols, qkv_cols,
    )
    cot_all = cot_all.reshape(span, width)
    normed_all = normed_all.reshape(span, width)
    route_all = route_all.reshape(span, 2 * TOP)
    ids_all, gates_all = route_all[:, :TOP].astype(jnp.int32), route_all[:, TOP:]
    gate_all, up_all, down_all = (w.reshape(width, -1) for w in (gate_all, up_all, down_all))
    gain_two = pack_all[:, :, qkv_cols + q_cols + 1].astype(F32).reshape(1, width)

    expert_of = member * own_experts + jnp.arange(own_experts, dtype=jnp.int32)
    named = ids_all[None, :, :] == expert_of[:, None, None]
    chosen = jnp.any(named, axis=2)
    weight = jnp.sum(jnp.where(named, gates_all[None], 0.0), axis=2)
    upto = (place[:, None] <= place[None, :]).astype(BF16)
    slot = dot(chosen.astype(BF16), upto).astype(jnp.int32) - 1
    slot = jnp.where(chosen & (slot < capacity), slot, -1)
    mixture, grad_normed, *by_kind = experts(
        slot, weight, normed_all, cot_all, gate_all, up_all, down_all, ff, capacity
    )
    by_kind = [one.reshape(devices, -1, own_experts * ff) for one in by_kind]

    grad_residual, gain_two_part, grad_attn_out, sum_gate, sum_up = third_phase(
        members,
        grad_normed.reshape(members, rows, width),
        residual,
        cotangent,
        gain_two,
        by_kind[0],
        by_kind[1],
    )
    (
        output, grad_tokens, gains, d_query, d_key, d_value, d_out, d_down,
    ) = backward_phase(
        members,
        mixture.reshape(members, rows, width),
        residual,
        grad_attn_out.reshape(span, width),
        grad_residual,
        gain_two_part,
        tokens,
        by_kind[2],
        pack_all,
        normed_attn, qkv, kx, vx, probs, attended, cosine, sine,
    )
    return (
        output,
        grad_tokens,
        gains[:, 0],
        gains[:, 1],
        d_query,
        d_key,
        d_value,
        d_out,
        sum_gate.reshape(-1, own_experts, ff),
        sum_up.reshape(-1, own_experts, ff),
        d_down.reshape(-1, own_experts, ff),
    )


def solution(mesh):
    both = P(("dp", "expert"), None)
    row, rows = P("dp"), P("dp", None)
    experts = P("dp", "expert", None)
    fast = mesh.shape["dp"] == 8 and mesh.shape["expert"] == 4
    return jax.shard_map(
        shards_fast if fast else shards_plain,
        mesh=mesh,
        in_specs=(both, both, row, row, rows, rows, rows, rows)
        + (experts, experts, experts, both, both, rows, rows),
        out_specs=(both, both, row, row, rows, rows, rows, rows, experts, experts, experts),
        check_vma=False,
    )
```

```python
import functools

import jax
import jax.numpy as jnp
from jax import lax
from jax.experimental import pallas as pl
from jax.experimental.pallas import tpu as pltpu
from jax.sharding import PartitionSpec as P

QUERY_HEADS = 24
KEY_VALUE_HEADS = 8
HEAD_SIZE = 64
TOP = 8

epsilon = 1e-06
rope_base = 10000.0
score_scale = 0.015625
branch_scale = 0.22
F32 = jnp.float32
BF16 = jnp.bfloat16
MESH = pl.DeviceIdType.MESH
VMEM_LIMIT = 60 * 2**20


def layout(lengths_row, order_row, span):
    seqs = lengths_row.shape[0]
    slot_ids = jnp.arange(seqs, dtype=jnp.int32)
    picked = jnp.sum(
        jnp.where(order_row[:, None] == slot_ids[None, :], lengths_row[None, :], 0), axis=1
    )
    before = slot_ids[:, None] >= slot_ids[None, :]
    seq_ends = jnp.sum(jnp.where(before, picked[None, :], 0), axis=1)
    place = jnp.arange(span, dtype=jnp.int32)
    passed = place[:, None] >= seq_ends[None, :]
    segment = jnp.sum(passed.astype(jnp.int32), axis=1)
    start = jnp.sum(jnp.where(passed, picked[None, :], 0), axis=1)
    return segment, (place - start).astype(F32)


def rotation(position):
    half = HEAD_SIZE // 2
    frequency = rope_base ** (-(jnp.arange(half, dtype=F32) * (2.0 / HEAD_SIZE)))
    angles = position[:, None] * frequency[None, :]
    return jnp.cos(angles), jnp.sin(angles)


def rotate(rows, cosine, sine, back=False):
    t = rows.shape[0]
    heads = rows.reshape(t, -1, 2, HEAD_SIZE // 2)
    a, b = heads[:, :, 0], heads[:, :, 1]
    c, s = cosine[:, None, :], sine[:, None, :]
    if back:
        s = -s
    return jnp.stack([a * c - b * s, b * c + a * s], axis=2).reshape(t, -1)


def dot(a, b):
    return jnp.dot(a, b, preferred_element_type=F32)


def dot_nt(a, b):
    return jnp.einsum("tc,dc->td", a, b, preferred_element_type=F32)


def dot_tn(a, b):
    return jnp.einsum("td,tc->dc", a, b, preferred_element_type=F32)


def rms_factor(rows):
    return lax.rsqrt(jnp.mean(rows * rows, axis=-1, keepdims=True) + epsilon)


def norm_back(rows, factor, gain, grad):
    scaled = gain * grad
    return factor * scaled - rows * (factor * factor * factor) * jnp.mean(
        scaled * rows, axis=-1, keepdims=True
    )


def gather(x, axis):
    return lax.all_gather(x, axis, axis=0, tiled=True)


def scatter(x, axis):
    return lax.psum_scatter(x.astype(BF16), axis, scatter_dimension=0, tiled=True).astype(F32)


class Links:
    def __init__(self, send, recv, local, members):
        self.send, self.recv, self.local = send, recv, local
        self.remotes = self.locals = 0
        self.members = members
        self.d, self.z = lax.axis_index("dp"), lax.axis_index("expert")
        d = self.d
        core, x, y = d % 2, (d // 2) % 2, d // 4
        self.core = core
        self.sib = d + 1 - 2 * core
        self.x = d + 2 - 4 * x
        self.y = d + 4 - 8 * y
        self.diag = self.x + 4 - 8 * y
        self.waiting = []

    def other(self, d):
        return d + 1 - 2 * self.core

    def greet(self):
        barrier = pltpu.get_barrier_semaphore()
        last = self.members - 1

        def hello(d, z):
            pl.semaphore_signal(barrier, inc=1, device_id=(d, z), device_id_type=MESH)

        for d in (self.sib, self.x, self.y):
            hello(d, self.z)
        pl.when(self.z > 0)(lambda: hello(self.d, self.z - 1))
        pl.when(self.z < last)(lambda: hello(self.d, self.z + 1))
        ends = (self.z == 0).astype(jnp.int32) + (self.z == last).astype(jnp.int32)
        pl.semaphore_wait(barrier, 5 - ends)

    def remote(self, src, dst, to):
        k = self.remotes
        self.remotes += 1
        return pltpu.make_async_remote_copy(
            src_ref=src,
            dst_ref=dst,
            send_sem=self.send.at[k],
            recv_sem=self.recv.at[k],
            device_id=to,
            device_id_type=MESH,
        )

    def push(self, src, dst, d):
        copy = self.remote(src, dst, (d, self.z))
        copy.start()
        self.waiting.append(copy.wait_send)
        return copy

    def move(self, src, dst):
        k = self.locals
        self.locals += 1
        copy = pltpu.make_async_copy(src, dst, self.local.at[k])
        copy.start()
        return copy

    def finish(self):
        for wait in self.waiting:
            wait()


def run(order, **chains):
    for name in order:
        next(chains[name], None)
    chains = list(chains.values())
    while chains:
        for chain in list(chains):
            try:
                next(chain)
            except StopIteration:
                chains.remove(chain)


def line_gather(links, own, full):
    z, last = links.z, links.members - 1
    local = links.move(own, full.at[z])
    right, left = (links.d, z + 1), (links.d, z - 1)
    to_right, to_left = [], []
    for s in range(last):
        at_r, at_l = jnp.maximum(z - s, 0), jnp.minimum(z + s, last)
        to_right.append(links.remote(own if s == 0 else full.at[at_r], full.at[at_r], right))
        to_left.append(links.remote(own if s == 0 else full.at[at_l], full.at[at_l], left))
    for s in range(last):
        send_r, send_l = (z < last) & (z >= s), (z > 0) & (z + s <= last)
        pl.when(send_r)(to_right[s].start)
        pl.when(send_l)(to_left[s].start)
        yield
        pl.when((z > 0) & (z - 1 >= s))(to_right[s].wait_recv)
        pl.when((z < last) & (z + 1 + s <= last))(to_left[s].wait_recv)
    for s in range(last):
        send_r, send_l = (z < last) & (z >= s), (z > 0) & (z + s <= last)
        pl.when(send_r)(to_right[s].wait_send)
        pl.when(send_l)(to_left[s].wait_send)
    local.wait()


def add_rows(target, other, step=16):
    rows = target.shape[0]

    @pl.loop(0, rows // step)
    def _(i):
        at = pl.ds(pl.multiple_of(i * step, step), step)
        target[at] = (target[at].astype(F32) + other[at].astype(F32)).astype(target.dtype)


def line_scatter(links, part, acc, from_left, from_right):
    z, last = links.z, links.members - 1
    made = set()

    def make(o):
        if o not in made:
            made.add(o)
            part(o)

    to_right = {o: links.remote(acc.at[o], from_left.at[o], (links.d, z + 1)) for o in range(1, last + 1)}
    to_left = {o: links.remote(acc.at[o], from_right.at[o], (links.d, z - 1)) for o in range(last)}

    def pass_right(o):
        @pl.when(z > 0)
        def _():
            to_right[o].wait_recv()
            add_rows(acc.at[o], from_left.at[o])

        to_right[o].start()

    def pass_left(o):
        @pl.when(z < last)
        def _():
            to_left[o].wait_recv()
            add_rows(acc.at[o], from_right.at[o])

        to_left[o].start()

    @pl.when(z == 0)
    def _():
        from_left[0] = jnp.zeros(from_left.shape[1:], from_left.dtype)

    @pl.when(z == last)
    def _():
        from_right[last] = jnp.zeros(from_right.shape[1:], from_right.dtype)

    for j in range(last):
        make(last - j)
        make(j)
        pl.when((z < last - j) & (2 * z < last))(functools.partial(pass_right, last - j))
        pl.when(z > j)(functools.partial(pass_left, j))
        pl.when((z < last - j) & (2 * z >= last))(functools.partial(pass_right, last - j))
        yield
    for o in range(last + 1):

        @pl.when(z == o)
        def _(o=o):
            if o > 0:
                to_right[o].wait_recv()
            if o < last:
                to_left[o].wait_recv()

    for o in range(last + 1):
        if o > 0:
            pl.when(z < o)(to_right[o].wait_send)
        if o < last:
            pl.when(z > o)(to_left[o].wait_send)


def plane_gather(links, own, full):
    half = own.shape[0] // 2
    first, second = pl.ds(0, half), pl.ds(half, half)
    me = links.d
    local = links.move(own, full.at[me])
    by_x, by_y = {}, {}
    for by, d, h in ((by_y, links.y, first), (by_x, links.x, second), (by_x, links.x, first), (by_y, links.y, second)):
        by[h.start // half] = links.push(own.at[h], full.at[me, h], d)
    to_sib = [links.push(own, full.at[me], links.sib)]

    def share(d, h):
        to_sib.append(links.push(full.at[d, h], full.at[d, h], links.sib))

    yield
    by_y[0].wait_recv()
    over_x = links.push(full.at[links.y, first], full.at[links.y, first], links.x)
    share(links.y, first)
    by_x[1].wait_recv()
    over_y = links.push(full.at[links.x, second], full.at[links.x, second], links.y)
    share(links.x, second)
    yield
    by_x[0].wait_recv()
    share(links.x, first)
    by_y[1].wait_recv()
    share(links.y, second)
    yield
    over_x.wait_recv()
    share(links.diag, first)
    over_y.wait_recv()
    share(links.diag, second)
    yield
    for copy in to_sib:
        copy.wait_recv()
    local.wait()


def plane_scatter(links, part, mine, theirs, mid_x, mid_y, end_x, end_y):
    half = part.shape[1] // 2
    first, second = pl.ds(0, half), pl.ds(half, half)
    chips = (links.d, links.x, links.y, links.diag)
    from_sib, load = {}, {}
    held = [part.at[chip] if mine is None else mine.at[k] for k, chip in enumerate(chips)]
    for k in (3, 1, 2, 0):
        from_sib[k] = links.push(part.at[links.other(chips[k])], theirs.at[k], links.sib)
        if mine is not None:
            load[k] = links.move(part.at[chips[k]], held[k])
    yield
    for k in (3, 1, 2):
        if load:
            load[k].wait()
        from_sib[k].wait_recv()
        add_rows(held[k], theirs.at[k])
        if k == 3:
            to_mid_x = links.push(held[3].at[first], mid_x, links.x)
            to_mid_y = links.push(held[3].at[second], mid_y, links.y)
        if k == 1:
            to_end_x = links.push(held[1].at[first], end_x.at[first], links.x)
        if k == 2:
            to_end_y = links.push(held[2].at[second], end_y.at[second], links.y)
    yield
    to_mid_y.wait_recv()
    add_rows(held[1].at[second], mid_y)
    rest_x = links.push(held[1].at[second], end_x.at[second], links.x)
    to_mid_x.wait_recv()
    add_rows(held[2].at[first], mid_x)
    rest_y = links.push(held[2].at[first], end_y.at[first], links.y)
    yield
    if load:
        load[0].wait()
    from_sib[0].wait_recv()
    to_end_x.wait_recv()
    to_end_y.wait_recv()
    rest_x.wait_recv()
    rest_y.wait_recv()


def plane_scratch(rows, cols, mine=True):
    return [pltpu.VMEM((4, rows, cols), BF16)] * mine + [
        pltpu.VMEM((4, rows, cols), BF16),
        pltpu.VMEM((rows // 2, cols), BF16),
        pltpu.VMEM((rows // 2, cols), BF16),
        pltpu.VMEM((rows, cols), BF16),
        pltpu.VMEM((rows, cols), BF16),
    ]


def plane_result(mine, theirs, end_x, end_y, out, step=16):
    @pl.loop(0, out.shape[0] // step)
    def _(i):
        at = pl.ds(pl.multiple_of(i * step, step), step)
        own = mine[at].astype(F32) + theirs[0, at].astype(F32)
        out[at] = (own + end_x[at].astype(F32) + end_y[at].astype(F32)).astype(out.dtype)


def line_result(z, acc, from_left, from_right, at):
    return (
        acc[z, at].astype(F32) + from_left[z, at].astype(F32) + from_right[z, at].astype(F32)
    )


ANY = pl.BlockSpec(memory_space=pl.ANY)
VMEM = pl.BlockSpec(memory_space=pltpu.VMEM)


def comm_call(kernel, name, number, members, remotes, locals_, in_specs, out_specs, out_shape, scratch):
    return pl.pallas_call(
        functools.partial(kernel, members),
        out_shape=out_shape,
        in_specs=in_specs,
        out_specs=out_specs,
        scratch_shapes=[
            pltpu.SemaphoreType.DMA((remotes,)),
            pltpu.SemaphoreType.DMA((remotes,)),
            pltpu.SemaphoreType.DMA((locals_,)),
            *scratch,
        ],
        compiler_params=pltpu.CompilerParams(
            collective_id=number, has_side_effects=True, vmem_limit_bytes=VMEM_LIMIT
        ),
        name=name,
    )


def sds(shape, dtype):
    return jax.ShapeDtypeStruct(shape, dtype)


def third_kernel(members, part, residual, cot, gain, gate, up, grad_residual, gain_part, out_all, gate_out, up_out, send, recv, local, acc, from_left, from_right, grad_out, *rest):
    links = Links(send, recv, local, members)
    links.greet()
    for_gate, for_up = rest[:6], rest[6:]

    def chain():
        links.move(part, acc).wait()
        yield from line_scatter(links, lambda o: None, acc, from_left, from_right)
        gain_part[...] = jnp.zeros(gain_part.shape, F32)

        @pl.loop(0, residual.shape[0] // 16)
        def _(i):
            at = pl.ds(pl.multiple_of(i * 16, 16), 16)
            grad = line_result(links.z, acc, from_left, from_right, at)
            here = residual[at]
            factor = rms_factor(here)
            gain_part[...] += jnp.sum(grad * here * factor, axis=0, keepdims=True)
            total = cot[at].astype(F32) + norm_back(here, factor, gain[...], grad)
            grad_residual[at] = total
            grad_out[at] = (branch_scale * total).astype(BF16)

        yield from line_gather(links, grad_out, out_all)

    run(
        "uuzzuzgzgzguz",
        z=chain(),
        g=plane_scatter(links, gate, *for_gate),
        u=plane_scatter(links, up, *for_up),
    )
    plane_result(for_gate[0].at[0], for_gate[1], for_gate[4], for_gate[5], gate_out)
    plane_result(for_up[0].at[0], for_up[1], for_up[4], for_up[5], up_out)
    links.finish()


def third_phase(members, part, residual, cot, gain, gate, up):
    rows, width = cot.shape
    blocks = pltpu.VMEM((members, rows, width), BF16)
    return comm_call(
        third_kernel, "phase_three", 3, members, 60, 16,
        [ANY, VMEM, VMEM, VMEM, ANY, ANY], [VMEM, VMEM, ANY, VMEM, VMEM],
        [
            sds((rows, width), F32),
            sds((1, width), F32),
            sds((members, rows, width), BF16),
            sds(gate.shape[1:], F32),
            sds(up.shape[1:], F32),
        ],
        [blocks, blocks, blocks, pltpu.VMEM((rows, width), BF16)]
        + plane_scratch(*gate.shape[1:])
        + plane_scratch(*up.shape[1:]),
    )(part, residual, cot, gain, gate, up)


def dims(a, b):
    return (((a,), (b,)), ((), ()))


def mm(a, b):
    return lax.dot_general(a, b, dims(1, 0), preferred_element_type=F32)


def mm_nt(a, b):
    return lax.dot_general(a, b, dims(1, 1), preferred_element_type=F32)


def mm_tn(a, b):
    return lax.dot_general(a, b, dims(0, 0), preferred_element_type=F32)


def expert_kernel(capacity, slot_row, slot_col, weight_row, normed, cot, w_gate, w_up, w_down, mixture, grad_normed, d_gate, d_up, d_down, mix_sum, grad_sum):
    e = pl.program_id(0)
    span = normed.shape[0]

    @pl.when(e == 0)
    def _():
        mix_sum[...] = jnp.zeros(mix_sum.shape, F32)
        grad_sum[...] = jnp.zeros(grad_sum.shape, F32)

    slots = slot_row[0]
    picks = slots == lax.broadcasted_iota(jnp.int32, (capacity, span), 0)
    pick = picks.astype(BF16)
    gate_col = jnp.sum(jnp.where(picks, weight_row[0], 0.0), axis=1, keepdims=True)
    put = (slot_col[0] == lax.broadcasted_iota(jnp.int32, (span, capacity), 1)).astype(BF16)
    received = mm(pick, normed[...]).astype(BF16)
    pre_gate, pre_up = mm(received, w_gate[...]), mm(received, w_up[...])
    sig = 1.0 / (1.0 + jnp.exp(-pre_gate))
    silu = pre_gate * sig
    activ = (silu * pre_up).astype(BF16)
    produced = (gate_col * mm_nt(activ, w_down[...])).astype(BF16)
    mix_sum[...] += mm(put, produced)
    grad_out = (gate_col * (branch_scale * mm(pick, cot[...]))).astype(BF16)
    grad_activ = mm(grad_out, w_down[...])
    grad_gate = (grad_activ * pre_up * (sig * (1.0 + pre_gate * (1.0 - sig)))).astype(BF16)
    grad_up = (grad_activ * silu).astype(BF16)
    grad_pair = (mm_nt(grad_gate, w_gate[...]) + mm_nt(grad_up, w_up[...])).astype(BF16)
    grad_sum[...] += mm(put, grad_pair)
    d_gate[...] = mm_tn(received, grad_gate).astype(BF16)
    d_up[...] = mm_tn(received, grad_up).astype(BF16)
    d_down[...] = mm_tn(grad_out, activ).astype(BF16)

    @pl.when(e == pl.num_programs(0) - 1)
    def _():
        mixture[...] = mix_sum[...].astype(BF16)
        grad_normed[...] = grad_sum[...].astype(BF16)


def experts(slot, weight, normed, cot, w_gate, w_up, w_down, ff, capacity):
    own_experts, span = slot.shape
    width = normed.shape[1]
    whole = pl.BlockSpec((span, width), lambda e: (0, 0))
    column = pl.BlockSpec((width, ff), lambda e: (0, e))
    row = pl.BlockSpec((1, 1, span), lambda e: (e, 0, 0))
    grads = jax.ShapeDtypeStruct(w_gate.shape, BF16)
    rows = jax.ShapeDtypeStruct((span, width), BF16)
    return pl.pallas_call(
        functools.partial(expert_kernel, capacity),
        grid=(own_experts,),
        in_specs=[row, pl.BlockSpec((1, span, 1), lambda e: (e, 0, 0)), row, whole, whole, column, column, column],
        out_specs=[whole, whole, column, column, column],
        out_shape=[rows, rows, grads, grads, grads],
        scratch_shapes=[pltpu.VMEM((span, width), F32), pltpu.VMEM((span, width), F32)],
        compiler_params=pltpu.CompilerParams(vmem_limit_bytes=VMEM_LIMIT),
        name="experts",
    )(slot[:, None, :], slot[:, :, None], weight[:, None, :], normed, cot, w_gate, w_up, w_down)


LANES = 128


def lane_ids(rows):
    return lax.broadcasted_iota(jnp.int32, (rows, LANES), 1)


def turn(x, cosine, sine):
    half = HEAD_SIZE // 2
    ahead, behind = pltpu.roll(x, LANES - half, axis=1), pltpu.roll(x, half, axis=1)
    partner = jnp.where(lane_ids(x.shape[0]) % HEAD_SIZE < half, ahead, behind)
    return x * cosine + partner * sine


def spread(block, at, out):
    low = lane_ids(block.shape[0]) < HEAD_SIZE
    other = pltpu.roll(block, HEAD_SIZE, axis=1)
    zero = jnp.zeros_like(block)
    out[0, 0, at] = jnp.where(low, block, zero).astype(BF16)
    out[0, 1, at] = jnp.where(low, zero, other).astype(BF16)
    out[1, 0, at] = jnp.where(low, other, zero).astype(BF16)
    out[1, 1, at] = jnp.where(low, zero, block).astype(BF16)


def attention_setup(seg_row, seg_col, bias):
    span = bias.shape[0]
    for b in range(span // LANES):
        at = pl.ds(b * LANES, LANES)
        row = b * LANES + lax.broadcasted_iota(jnp.int32, (LANES, span), 0)
        col = lax.broadcasted_iota(jnp.int32, (LANES, span), 1)
        ok = (seg_col[at] == seg_row[...]) & (col <= row)
        bias[at] = jnp.where(ok, 0.0, -1e30)


def weight_columns(pack_all, first, cols):
    return pack_all[:, :, first : first + cols].reshape(-1, cols)


def gain_rows(pack_all, first):
    pick = lax.broadcasted_iota(jnp.int32, (16, LANES), 0) == lax.broadcasted_iota(jnp.int32, (16, LANES), 1)
    return mm_nt(pick.astype(BF16), weight_columns(pack_all, first, LANES))


def attend_steps(qkv, kx, vx, bias, probs, attended):
    span, blocks = qkv.shape[0], attended.shape[1] // LANES
    repeat = QUERY_HEADS // KEY_VALUE_HEADS
    for j in range(blocks):
        for b in range(span // LANES):
            at, keys = pl.ds(b * LANES, LANES), (b + 1) * LANES
            q = qkv[at, j * LANES : (j + 1) * LANES]
            total = jnp.zeros((LANES, LANES), F32)
            for half in range(2):
                h = 2 * j + half
                kv = h // repeat
                scores = mm_nt(q, kx[kv, half, :keys]) + bias[at, :keys]
                peak = jnp.max(scores, axis=1, keepdims=True)
                exponent = jnp.exp(scores - peak)
                share = 1.0 / jnp.sum(exponent, axis=1, keepdims=True)
                low = (exponent * share).astype(BF16)
                probs[h, at, :keys] = low
                total += mm(low, vx[kv, half, :keys])
            attended[at, j * LANES : (j + 1) * LANES] = total.astype(BF16)
        yield


def forward_kernel(
    members, tokens, cot, route, pack, gate, up, down, seg_row, seg_col, cosine, sine,
    cot_all, route_all, pack_all, gate_all, up_all, down_all, normed_attn, qkv, kx, vx, probs, attended, residual, normed_all,
    send, recv, local, tokens_all, bias, acc, from_left, from_right, normed,
):
    links = Links(send, recv, local, members)
    links.greet()
    rows, width = tokens.shape
    span = rows * members
    q_cols = attended.shape[1]
    qkv_cols = qkv.shape[1]

    def produce(o):
        acc[o] = mm_nt(attended[o * rows : (o + 1) * rows], weight_columns(pack_all, qkv_cols, q_cols)).astype(BF16)

    def chain():
        attention_setup(seg_row, seg_col, bias)
        yield
        gains = gain_rows(pack_all, qkv_cols + q_cols)

        @pl.loop(0, span // 16)
        def _(i):
            here = tokens_all[i // (rows // 16), pl.ds(pl.multiple_of(i % (rows // 16) * 16, 16), 16)].astype(F32)
            normed_attn[pl.ds(pl.multiple_of(i * 16, 16), 16)] = (here * rms_factor(here) * gains[0:1]).astype(BF16)

        @pl.loop(0, span // LANES)
        def _(i):
            at = pl.ds(pl.multiple_of(i * LANES, LANES), LANES)
            here = mm(normed_attn[at], weight_columns(pack_all, 0, qkv_cols))
            c, s = cosine[at], sine[at]
            for j in range(q_cols // LANES):
                lanes = slice(j * LANES, (j + 1) * LANES)
                qkv[at, lanes] = (turn(here[:, lanes], c, s).astype(BF16).astype(F32) * score_scale).astype(BF16)
            key = turn(here[:, q_cols : q_cols + LANES], c, s)
            value = here[:, q_cols + LANES :]
            qkv[at, q_cols : q_cols + LANES] = key.astype(BF16)
            qkv[at, q_cols + LANES :] = value.astype(BF16)
            spread(key, at, kx)
            spread(value, at, vx)

        yield
        yield from attend_steps(qkv, kx, vx, bias, probs, attended)
        yield from line_scatter(links, produce, acc, from_left, from_right)

        @pl.loop(0, rows // 16)
        def _(i):
            at = pl.ds(pl.multiple_of(i * 16, 16), 16)
            here = tokens[at].astype(F32) + branch_scale * line_result(links.z, acc, from_left, from_right, at)
            residual[at] = here
            normed[at] = (here * rms_factor(here) * gains[1:2]).astype(BF16)

        yield from line_gather(links, normed, normed_all)

    run(
        FORWARD_ORDER,
        t=line_gather(links, tokens, tokens_all),
        r=line_gather(links, route, route_all),
        c=line_gather(links, cot, cot_all),
        p=plane_gather(links, pack, pack_all),
        g=plane_gather(links, gate, gate_all),
        u=plane_gather(links, up, up_all),
        d=plane_gather(links, down, down_all),
        a=chain(),
    )
    links.finish()


FORWARD_ORDER = "tpptdatpppctpatacpadrpgatcaacdparuagrrttcr"


def forward_phase(members, tokens, cot, route, pack, gate, up, down, seg_row, seg_col, cosine, sine, q_cols, qkv_cols):
    rows, width = tokens.shape
    span = rows * members
    blocks = pltpu.VMEM((members, rows, width), BF16)
    heads = q_cols // HEAD_SIZE
    return comm_call(
        forward_kernel, "forward", 1, members, 100, 16,
        [VMEM, ANY, ANY, ANY, ANY, ANY, ANY, VMEM, VMEM, VMEM, VMEM],
        [ANY, ANY, VMEM, ANY, ANY, ANY, VMEM, VMEM, VMEM, VMEM, VMEM, VMEM, VMEM, ANY],
        [
            sds((members, rows, width), BF16),
            sds((members, *route.shape), F32),
            sds((8, *pack.shape), BF16),
            sds((8, *gate.shape), BF16),
            sds((8, *up.shape), BF16),
            sds((8, *down.shape), BF16),
            sds((span, width), BF16),
            sds((span, qkv_cols), BF16),
            sds((2, 2, span, LANES), BF16),
            sds((2, 2, span, LANES), BF16),
            sds((heads, span, span), BF16),
            sds((span, q_cols), BF16),
            sds((rows, width), F32),
            sds((members, rows, width), BF16),
        ],
        [
            blocks,
            pltpu.VMEM((span, span), F32),
            blocks,
            blocks,
            blocks,
            pltpu.VMEM((rows, width), BF16),
        ],
    )(tokens, cot, route, pack, gate, up, down, seg_row, seg_col, cosine, sine)


def attend_back_steps(qkv, kx, vx, probs, grad_attended, cosine, sine, grad_k, grad_v, grad_qkv):
    span = qkv.shape[0]
    blocks = grad_attended.shape[1] // LANES
    repeat = QUERY_HEADS // KEY_VALUE_HEADS
    grad_k[...] = jnp.zeros(grad_k.shape, F32)
    grad_v[...] = jnp.zeros(grad_v.shape, F32)
    for j in range(blocks):
        lanes = slice(j * LANES, (j + 1) * LANES)
        for b in range(span // LANES):
            at, keys = pl.ds(b * LANES, LANES), (b + 1) * LANES
            q, grad = qkv[at, lanes], grad_attended[at, lanes]
            total = jnp.zeros((LANES, LANES), F32)
            for half in range(2):
                h = 2 * j + half
                kv = h // repeat
                low = probs[h, at, :keys]
                share = low.astype(F32)
                grad_probs = mm_nt(grad, vx[kv, half, :keys])
                inner = jnp.sum(share * grad_probs, axis=1, keepdims=True)
                grad_scores = (share * (grad_probs - inner)).astype(BF16)
                total += mm(grad_scores, kx[kv, half, :keys])
                grad_k[kv, half, :keys] += mm_tn(grad_scores, q)
                grad_v[kv, half, :keys] += mm_tn(low, grad)
            grad_qkv[at, lanes] = turn(total * score_scale, cosine[at], -sine[at]).astype(BF16)
        yield
    first = blocks * LANES

    def fold(parts, at):
        low = lane_ids(LANES) < HEAD_SIZE
        same = jnp.where(low, parts[0, 0, at], parts[1, 1, at])
        crossed = jnp.where(low, parts[1, 0, at], parts[0, 1, at])
        return same + pltpu.roll(crossed, HEAD_SIZE, axis=1)

    for b in range(span // LANES):
        at = pl.ds(b * LANES, LANES)
        grad_qkv[at, first : first + LANES] = turn(fold(grad_k, at), cosine[at], -sine[at]).astype(BF16)
        grad_qkv[at, first + LANES :] = fold(grad_v, at).astype(BF16)


def backward_kernel(
    members, mixture, residual, grad_out_all, grad_residual, gain_ffn_part, tokens, down, pack_all, normed_attn, qkv, kx, vx, probs, attended, cosine, sine,
    output, grad_tokens, gains, d_query, d_key, d_value, d_out, d_down,
    send, recv, local, acc_m, left_m, right_m, acc, from_left, from_right, grad_attended, grad_k, grad_v, grad_qkv, gain_part,
    for_w_out, for_w_qkv, own_out, own_qkv, all_out, all_qkv, *rest,
):
    links = Links(send, recv, local, members)
    links.greet()
    rows, width = tokens.shape
    q_cols, qkv_cols = attended.shape[1], qkv.shape[1]
    kv_cols = (qkv_cols - q_cols) // 2
    with_out, with_qkv, with_down = rest[:5], rest[5:10], rest[10:]
    pairs = for_w_out.shape[0] // 2
    step = width // pairs
    row_gains = gain_rows(pack_all, qkv_cols + q_cols)

    def out_chain():
        for i in range(pairs):
            term = mm_tn(grad_out_all[:, i * step : (i + 1) * step], attended[...])
            for_w_out[2 * i : 2 * i + 2] = term.astype(BF16).reshape(2, step // 2, q_cols)
        yield from plane_scatter(links, for_w_out, None, *with_out)
        plane_result(for_w_out.at[links.d], with_out[0], with_out[3], with_out[4], own_out)
        yield from line_gather(links, own_out, all_out)

    def produce(o):
        at = slice(o * rows, (o + 1) * rows)
        part = mm_nt(grad_qkv[at], weight_columns(pack_all, 0, qkv_cols))
        gain_part[...] += jnp.sum(part * normed_attn[at].astype(F32), axis=0, keepdims=True)
        acc[o] = part.astype(BF16)

    def chain():
        wo = weight_columns(pack_all, qkv_cols, q_cols)

        @pl.loop(0, grad_attended.shape[0] // LANES)
        def _(i):
            at = pl.ds(pl.multiple_of(i * LANES, LANES), LANES)
            grad_attended[at] = mm(grad_out_all[at], wo).astype(BF16)

        yield
        yield from attend_back_steps(qkv, kx, vx, probs, grad_attended, cosine, sine, grad_k, grad_v, grad_qkv)
        gain_part[...] = jnp.zeros(gain_part.shape, F32)
        yield from line_scatter(links, produce, acc, from_left, from_right)

        @pl.loop(0, rows // 16)
        def _(i):
            at = pl.ds(pl.multiple_of(i * 16, 16), 16)
            grad = line_result(links.z, acc, from_left, from_right, at)
            here = tokens[at].astype(F32)
            grad_tokens[at] = grad_residual[at] + norm_back(here, rms_factor(here), row_gains[0:1], grad)

    def qkv_chain():
        for i in range(pairs):
            term = mm_tn(normed_attn[:, i * step : (i + 1) * step], grad_qkv[...])
            for_w_qkv[2 * i : 2 * i + 2, :, :qkv_cols] = term.astype(BF16).reshape(2, step // 2, qkv_cols)
        which = lax.broadcasted_iota(jnp.int32, (16, width), 0)
        both = jnp.where(which == 0, gain_part[...] / row_gains[0:1], jnp.where(which == 1, gain_ffn_part[...], 0.0))
        pick = lax.broadcasted_iota(jnp.int32, (16, LANES), 0) == lax.broadcasted_iota(jnp.int32, (16, LANES), 1)
        columns = mm_tn(both.astype(BF16), pick.astype(BF16))
        for_w_qkv[:, :, qkv_cols:] = columns.astype(BF16).reshape(2 * pairs, step // 2, LANES)
        yield from plane_scatter(links, for_w_qkv, None, *with_qkv)
        plane_result(for_w_qkv.at[links.d], with_qkv[0], with_qkv[3], with_qkv[4], own_qkv)
        yield from line_gather(links, own_qkv, all_qkv)

    def mixture_chain():
        links.move(mixture, acc_m).wait()
        yield from line_scatter(links, lambda o: None, acc_m, left_m, right_m)

        @pl.loop(0, rows // 16)
        def _(i):
            at = pl.ds(pl.multiple_of(i * 16, 16), 16)
            here = residual[at] + branch_scale * line_result(links.z, acc_m, left_m, right_m, at)
            output[at] = here.astype(BF16)

    run(
        BACKWARD_ORDER,
        m=mixture_chain(),
        d=plane_scatter(links, down, *with_down),
        o=out_chain(),
        a=chain(),
        q=qkv_chain(),
    )
    plane_result(with_down[0].at[0], with_down[1], with_down[4], with_down[5], d_down)
    for m in range(members):
        d_out[:, m * q_cols : (m + 1) * q_cols] = all_out[m].astype(F32)
        d_query[:, m * q_cols : (m + 1) * q_cols] = all_qkv[m, :, :q_cols].astype(F32)
        d_key[:, m * kv_cols : (m + 1) * kv_cols] = all_qkv[m, :, q_cols : q_cols + kv_cols].astype(F32)
        d_value[:, m * kv_cols : (m + 1) * kv_cols] = all_qkv[m, :, q_cols + kv_cols : qkv_cols].astype(F32)
    gains[...] = sum(all_qkv[m, :, qkv_cols:].astype(F32) for m in range(members))
    links.finish()


BACKWARD_ORDER = "amoadmmadaaaoqoqoqaoaq"


def backward_phase(members, mixture, residual, grad_out_all, grad_residual, gain_ffn_part, tokens, down, pack_all, normed_attn, qkv, kx, vx, probs, attended, cosine, sine):
    rows, width = tokens.shape
    span, q_cols = attended.shape
    qkv_cols = qkv.shape[1]
    kv_cols = (qkv_cols - q_cols) // 2
    devices, own = down.shape[:2]
    line = [pltpu.VMEM((members, rows, width), BF16)] * 3
    return comm_call(
        backward_kernel, "backward", 4, members, 100, 32,
        [ANY, VMEM, VMEM, VMEM, VMEM, VMEM, ANY] + [VMEM] * 9,
        [VMEM] * 8,
        [
            sds((rows, width), BF16),
            sds((rows, width), F32),
            sds((own, LANES), F32),
            sds((own, members * q_cols), F32),
            sds((own, members * kv_cols), F32),
            sds((own, members * kv_cols), F32),
            sds((own, members * q_cols), F32),
            sds(down.shape[1:], F32),
        ],
        [
            *line,
            *line,
            pltpu.VMEM((span, q_cols), BF16),
            pltpu.VMEM((2, 2, span, LANES), F32),
            pltpu.VMEM((2, 2, span, LANES), F32),
            pltpu.VMEM((span, qkv_cols), BF16),
            pltpu.VMEM((1, width), F32),
            pltpu.VMEM((devices, own, q_cols), BF16),
            pltpu.VMEM((devices, own, qkv_cols + LANES), BF16),
            pltpu.VMEM((own, q_cols), BF16),
            pltpu.VMEM((own, qkv_cols + LANES), BF16),
            pltpu.VMEM((members, own, q_cols), BF16),
            pltpu.VMEM((members, own, qkv_cols + LANES), BF16),
            *plane_scratch(own, q_cols, False),
            *plane_scratch(own, qkv_cols + LANES, False),
            *plane_scratch(*down.shape[1:]),
        ],
    )(mixture, residual, grad_out_all, grad_residual, gain_ffn_part, tokens, down, pack_all, normed_attn, qkv, kx, vx, probs, attended, cosine, sine)


def all_blocks(x, axis):
    return lax.all_gather(x, axis, axis=0)


def plain_first(members, tokens, cot, route, pack, gate):
    return (
        all_blocks(tokens, "expert"),
        all_blocks(cot, "expert"),
        all_blocks(route, "expert"),
        all_blocks(pack, "dp"),
        all_blocks(gate, "dp"),
    )


def line_sum(part):
    return scatter(part.reshape(-1, part.shape[2]), "expert")


def plain_second(members, part, tokens, gain, up, down):
    residual = tokens.astype(F32) + branch_scale * line_sum(part)
    normed = (residual * rms_factor(residual) * gain).astype(BF16)
    return residual, all_blocks(normed, "expert"), all_blocks(up, "dp"), all_blocks(down, "dp")


def plane_sum(part):
    return scatter(part.reshape(-1, part.shape[2]), "dp")


def plain_third(members, part, residual, cot, gain, gate, up):
    grad = line_sum(part)
    factor = rms_factor(residual)
    gain_part = jnp.sum(grad * residual * factor, axis=0, keepdims=True)
    total = cot.astype(F32) + norm_back(residual, factor, gain, grad)
    out_all = all_blocks((branch_scale * total).astype(BF16), "expert")
    return total, gain_part, out_all, plane_sum(gate), plane_sum(up)


def plain_fourth(members, part, grad_residual, tokens, gain, pack, down):
    here = tokens.astype(F32)
    grad_tokens = grad_residual + norm_back(here, rms_factor(here), gain, line_sum(part))
    return grad_tokens, all_blocks(plane_sum(pack).astype(BF16), "expert"), plane_sum(down)


def attend_forward(q, k, v, allowed):
    scores = jnp.einsum("irh,jh->rij", q, k, preferred_element_type=F32) * score_scale
    scores = jnp.where(allowed[None], scores, -1e30)
    peak = jnp.max(scores, axis=-1, keepdims=True)
    exponent = jnp.exp(scores - peak)
    total = jnp.sum(exponent, axis=-1, keepdims=True)
    probs = exponent / total
    return jnp.einsum("rij,jh->irh", probs.astype(BF16), v, preferred_element_type=F32), probs


def attend_backward(q, k, v, probs, grad, allowed):
    grad_probs = jnp.einsum("irh,jh->rij", grad, v, preferred_element_type=F32)
    inner = jnp.sum(probs * grad_probs, axis=-1, keepdims=True)
    grad_scores = (probs * (grad_probs - inner)).astype(BF16)
    grad_q = jnp.einsum("rij,jh->irh", grad_scores, k, preferred_element_type=F32) * score_scale
    grad_k = jnp.einsum("rij,irh->jh", grad_scores, q, preferred_element_type=F32) * score_scale
    grad_v = jnp.einsum("rij,irh->jh", probs.astype(BF16), grad, preferred_element_type=F32)
    return grad_q, grad_k, grad_v


def shards_plain(
    tokens,
    cotangent,
    gain_attn,
    gain_ffn,
    w_query,
    key_weight,
    value_weight,
    w_out,
    expert_gate,
    expert_up,
    expert_down,
    expert_ids,
    gates,
    lengths,
    order,
):
    rows, width = tokens.shape
    members = lax.axis_size("expert")
    member = lax.axis_index("expert")
    span = rows * members
    own_experts, ff = expert_gate.shape[1], expert_gate.shape[2]
    capacity = rows * TOP // own_experts
    q_cols = w_query.shape[1] // members
    kv_cols = key_weight.shape[1] // members
    kv_heads = kv_cols // HEAD_SIZE
    repeat = QUERY_HEADS // KEY_VALUE_HEADS

    def mine(weight, cols):
        return lax.dynamic_slice_in_dim(weight, member * cols, cols, axis=1)

    devices = lax.axis_size("dp")
    phases = [
        functools.partial(phase, members)
        for phase in (plain_first, plain_second, plain_third, plain_fourth)
    ]

    pack = jnp.concatenate(
        [
            mine(w_query, q_cols),
            mine(key_weight, kv_cols),
            mine(value_weight, kv_cols),
            mine(w_out, q_cols),
            gain_attn[:, None],
            gain_ffn[:, None],
            jnp.zeros((gain_attn.shape[0], 126), BF16),
        ],
        axis=1,
    )
    route = jnp.concatenate([expert_ids.astype(F32), gates], axis=1)
    tokens_all, cot_all, route_all, pack_all, gate_all = phases[0](
        tokens, cotangent, route, pack, expert_gate.reshape(-1, own_experts * ff)
    )
    tokens_all = tokens_all.reshape(span, width).astype(F32)
    cot_all = cot_all.reshape(span, width)
    route_all = route_all.reshape(span, 2 * TOP)
    ids_all, gates_all = route_all[:, :TOP].astype(jnp.int32), route_all[:, TOP:]
    pack_all = pack_all.reshape(width, -1)
    gate_all = gate_all.reshape(width, -1)
    qkv_cols = q_cols + 2 * kv_cols
    w_qkv = pack_all[:, :qkv_cols]
    wo = pack_all[:, qkv_cols : qkv_cols + q_cols]
    gain_one = pack_all[:, qkv_cols + q_cols].astype(F32)[None]
    gain_two = pack_all[:, qkv_cols + q_cols + 1].astype(F32)[None]

    segment, position = layout(lengths[0], order[0], span)
    cosine, sine = rotation(position)
    place = jnp.arange(span, dtype=jnp.int32)
    allowed = (segment[:, None] == segment[None, :]) & (place[None, :] <= place[:, None])
    factor_one = rms_factor(tokens_all)
    normed_attn = (tokens_all * factor_one * gain_one).astype(BF16)
    qkv = dot(normed_attn, w_qkv)
    qk = rotate(qkv[:, : q_cols + kv_cols], cosine, sine).astype(BF16)
    v = qkv[:, q_cols + kv_cols :].astype(BF16)
    q_heads = jnp.moveaxis(qk[:, :q_cols].reshape(span, kv_heads, repeat, HEAD_SIZE), 1, 0)
    k_heads = jnp.moveaxis(qk[:, q_cols:].reshape(span, kv_heads, HEAD_SIZE), 1, 0)
    v_heads = jnp.moveaxis(v.reshape(span, kv_heads, HEAD_SIZE), 1, 0)
    attended, probs = jax.vmap(functools.partial(attend_forward, allowed=allowed))(
        q_heads, k_heads, v_heads
    )
    attended = jnp.moveaxis(attended, 0, 1).reshape(span, q_cols).astype(BF16)
    attn_part = dot_nt(attended, wo).astype(BF16).reshape(members, rows, width)
    residual, normed_all, up_all, down_all = phases[1](
        attn_part,
        tokens,
        gain_two,
        expert_up.reshape(-1, own_experts * ff),
        expert_down.reshape(-1, own_experts * ff),
    )
    normed_all = normed_all.reshape(span, width)
    up_all, down_all = up_all.reshape(width, -1), down_all.reshape(width, -1)

    expert_of = member * own_experts + jnp.arange(own_experts, dtype=jnp.int32)
    named = ids_all[None, :, :] == expert_of[:, None, None]
    chosen = jnp.any(named, axis=2)
    weight = jnp.sum(jnp.where(named, gates_all[None], 0.0), axis=2)
    upto = (place[:, None] <= place[None, :]).astype(BF16)
    slot = dot(chosen.astype(BF16), upto).astype(jnp.int32) - 1
    slot = jnp.where(chosen & (slot < capacity), slot, -1)
    mixture, grad_normed, *by_kind = experts(
        slot, weight, normed_all, cot_all, gate_all, up_all, down_all, ff, capacity
    )
    output = (residual + branch_scale * scatter(mixture, "expert")).astype(BF16)
    by_kind = [one.reshape(devices, -1, own_experts * ff) for one in by_kind]

    grad_residual, gain_two_part, grad_attn_out, sum_gate, sum_up = phases[2](
        grad_normed.reshape(members, rows, width),
        residual,
        cotangent,
        gain_two,
        by_kind[0],
        by_kind[1],
    )
    grad_attn_out = grad_attn_out.reshape(span, width)
    term_out = dot_tn(grad_attn_out, attended)
    grad_attended = dot(grad_attn_out, wo).astype(BF16)
    grad_heads = jnp.moveaxis(grad_attended.reshape(span, kv_heads, repeat, HEAD_SIZE), 1, 0)
    grad_q, grad_k, grad_v = jax.vmap(functools.partial(attend_backward, allowed=allowed))(
        q_heads, k_heads, v_heads, probs, grad_heads
    )
    grad_qk = jnp.concatenate(
        [
            jnp.moveaxis(grad_q, 0, 1).reshape(span, q_cols),
            jnp.moveaxis(grad_k, 0, 1).reshape(span, kv_cols),
        ],
        axis=1,
    )
    grad_qkv = jnp.concatenate(
        [
            rotate(grad_qk, cosine, sine, back=True).astype(BF16),
            jnp.moveaxis(grad_v, 0, 1).reshape(span, kv_cols).astype(BF16),
        ],
        axis=1,
    )
    grad_norm_part = dot_nt(grad_qkv, w_qkv)
    gain_one_part = jnp.sum(grad_norm_part * tokens_all * factor_one, axis=0)
    term_qkv = dot_tn(normed_attn, grad_qkv)
    packed_grads = jnp.concatenate(
        [
            term_qkv,
            term_out,
            gain_one_part[:, None],
            gain_two_part.reshape(-1, 1),
            jnp.zeros((width, 126), F32),
        ],
        axis=1,
    )
    grad_tokens, per_member, sum_down = phases[3](
        grad_norm_part.astype(BF16).reshape(members, rows, width),
        grad_residual,
        tokens,
        gain_one,
        packed_grads.astype(BF16).reshape(devices, -1, packed_grads.shape[1]),
        by_kind[2],
    )
    per_member = per_member.astype(F32)

    def columns(first, cols):
        part = per_member[:, :, first : first + cols]
        return jnp.moveaxis(part, 0, 1).reshape(part.shape[1], -1)

    gains = jnp.sum(per_member[:, :, qkv_cols + q_cols :], axis=0)
    return (
        output,
        grad_tokens,
        gains[:, 0],
        gains[:, 1],
        columns(0, q_cols),
        columns(q_cols, kv_cols),
        columns(q_cols + kv_cols, kv_cols),
        columns(qkv_cols, q_cols),
        sum_gate.reshape(-1, own_experts, ff),
        sum_up.reshape(-1, own_experts, ff),
        sum_down.reshape(-1, own_experts, ff),
    )


def shards_fast(
    tokens,
    cotangent,
    gain_attn,
    gain_ffn,
    w_query,
    key_weight,
    value_weight,
    w_out,
    expert_gate,
    expert_up,
    expert_down,
    expert_ids,
    gates,
    lengths,
    order,
):
    rows, width = tokens.shape
    members, devices = lax.axis_size("expert"), lax.axis_size("dp")
    member = lax.axis_index("expert")
    span = rows * members
    own_experts, ff = expert_gate.shape[1], expert_gate.shape[2]
    capacity = rows * TOP // own_experts
    q_cols = w_query.shape[1] // members
    kv_cols = key_weight.shape[1] // members
    qkv_cols = q_cols + 2 * kv_cols

    def mine(weight, cols):
        return lax.dynamic_slice_in_dim(weight, member * cols, cols, axis=1)

    pack = jnp.concatenate(
        [
            mine(w_query, q_cols),
            mine(key_weight, kv_cols),
            mine(value_weight, kv_cols),
            mine(w_out, q_cols),
            gain_attn[:, None],
            gain_ffn[:, None],
            jnp.zeros((gain_attn.shape[0], 126), BF16),
        ],
        axis=1,
    )
    route = jnp.concatenate([expert_ids.astype(F32), gates], axis=1)
    segment, position = layout(lengths[0], order[0], span)
    cosine, sine = rotation(position)
    cosine = jnp.tile(cosine, (1, 4))
    sine = jnp.tile(jnp.concatenate([-sine, sine], axis=1), (1, 2))
    place = jnp.arange(span, dtype=jnp.int32)
    (
        cot_all, route_all, pack_all, gate_all, up_all, down_all,
        normed_attn, qkv, kx, vx, probs, attended, residual, normed_all,
    ) = forward_phase(
        members, tokens, cotangent, route, pack,
        expert_gate.reshape(-1, own_experts * ff),
        expert_up.reshape(-1, own_experts * ff),
        expert_down.reshape(-1, own_experts * ff),
        segment[None, :], segment[:, None],
        cosine, sine,
        q_cols, qkv_cols,
    )
    cot_all = cot_all.reshape(span, width)
    normed_all = normed_all.reshape(span, width)
    route_all = route_all.reshape(span, 2 * TOP)
    ids_all, gates_all = route_all[:, :TOP].astype(jnp.int32), route_all[:, TOP:]
    gate_all, up_all, down_all = (w.reshape(width, -1) for w in (gate_all, up_all, down_all))
    gain_two = pack_all[:, :, qkv_cols + q_cols + 1].astype(F32).reshape(1, width)

    expert_of = member * own_experts + jnp.arange(own_experts, dtype=jnp.int32)
    named = ids_all[None, :, :] == expert_of[:, None, None]
    chosen = jnp.any(named, axis=2)
    weight = jnp.sum(jnp.where(named, gates_all[None], 0.0), axis=2)
    upto = (place[:, None] <= place[None, :]).astype(BF16)
    slot = dot(chosen.astype(BF16), upto).astype(jnp.int32) - 1
    slot = jnp.where(chosen & (slot < capacity), slot, -1)
    mixture, grad_normed, *by_kind = experts(
        slot, weight, normed_all, cot_all, gate_all, up_all, down_all, ff, capacity
    )
    by_kind = [one.reshape(devices, -1, own_experts * ff) for one in by_kind]

    grad_residual, gain_two_part, grad_attn_out, sum_gate, sum_up = third_phase(
        members,
        grad_normed.reshape(members, rows, width),
        residual,
        cotangent,
        gain_two,
        by_kind[0],
        by_kind[1],
    )
    (
        output, grad_tokens, gains, d_query, d_key, d_value, d_out, d_down,
    ) = backward_phase(
        members,
        mixture.reshape(members, rows, width),
        residual,
        grad_attn_out.reshape(span, width),
        grad_residual,
        gain_two_part,
        tokens,
        by_kind[2],
        pack_all,
        normed_attn, qkv, kx, vx, probs, attended, cosine, sine,
    )
    return (
        output,
        grad_tokens,
        gains[:, 0],
        gains[:, 1],
        d_query,
        d_key,
        d_value,
        d_out,
        sum_gate.reshape(-1, own_experts, ff),
        sum_up.reshape(-1, own_experts, ff),
        d_down.reshape(-1, own_experts, ff),
    )


def solution(mesh):
    both = P(("dp", "expert"), None)
    row, rows = P("dp"), P("dp", None)
    experts = P("dp", "expert", None)
    fast = mesh.shape["dp"] == 8 and mesh.shape["expert"] == 4
    return jax.shard_map(
        shards_fast if fast else shards_plain,
        mesh=mesh,
        in_specs=(both, both, row, row, rows, rows, rows, rows)
        + (experts, experts, experts, both, both, rows, rows),
        out_specs=(both, both, row, row, rows, rows, rows, rows, experts, experts, experts),
        check_vma=False,
    )
```

```python
import functools

import jax
import jax.numpy as jnp
from jax import lax
from jax.experimental import pallas as pl
from jax.experimental.pallas import tpu as pltpu
from jax.sharding import PartitionSpec as P

QUERY_HEADS = 24
KEY_VALUE_HEADS = 8
HEAD_SIZE = 64
TOP = 8

epsilon = 1e-06
rope_base = 10000.0
score_scale = 0.015625
branch_scale = 0.22
F32 = jnp.float32
BF16 = jnp.bfloat16
MESH = pl.DeviceIdType.MESH
LANES = 128
VMEM_LIMIT = 60 * 2**20


def layout(lengths_row, order_row, span):
    seqs = lengths_row.shape[0]
    slot_ids = jnp.arange(seqs, dtype=jnp.int32)
    picked = jnp.sum(
        jnp.where(order_row[:, None] == slot_ids[None, :], lengths_row[None, :], 0), axis=1
    )
    before = slot_ids[:, None] >= slot_ids[None, :]
    seq_ends = jnp.sum(jnp.where(before, picked[None, :], 0), axis=1)
    place = jnp.arange(span, dtype=jnp.int32)
    passed = place[:, None] >= seq_ends[None, :]
    segment = jnp.sum(passed.astype(jnp.int32), axis=1)
    start = jnp.sum(jnp.where(passed, picked[None, :], 0), axis=1)
    return segment, (place - start).astype(F32)


def rotation(position):
    half = HEAD_SIZE // 2
    frequency = rope_base ** (-(jnp.arange(half, dtype=F32) * (2.0 / HEAD_SIZE)))
    angles = position[:, None] * frequency[None, :]
    return jnp.cos(angles), jnp.sin(angles)


def rotate(rows, cosine, sine, back=False):
    t = rows.shape[0]
    heads = rows.reshape(t, -1, 2, HEAD_SIZE // 2)
    a, b = heads[:, :, 0], heads[:, :, 1]
    c, s = cosine[:, None, :], sine[:, None, :]
    if back:
        s = -s
    return jnp.stack([a * c - b * s, b * c + a * s], axis=2).reshape(t, -1)


def dot(a, b):
    return jnp.dot(a, b, preferred_element_type=F32)


def dot_nt(a, b):
    return jnp.einsum("tc,dc->td", a, b, preferred_element_type=F32)


def dot_tn(a, b):
    return jnp.einsum("td,tc->dc", a, b, preferred_element_type=F32)


def rms_factor(rows):
    return lax.rsqrt(jnp.mean(rows * rows, axis=-1, keepdims=True) + epsilon)


def norm_back(rows, factor, gain, grad):
    scaled = gain * grad
    return factor * scaled - rows * (factor * factor * factor) * jnp.mean(
        scaled * rows, axis=-1, keepdims=True
    )


def gather(x, axis):
    return lax.all_gather(x, axis, axis=0, tiled=True)


def scatter(x, axis):
    return lax.psum_scatter(x.astype(BF16), axis, scatter_dimension=0, tiled=True).astype(F32)


class Links:
    def __init__(self, send, recv, local, members):
        self.send, self.recv, self.local = send, recv, local
        self.remotes = self.locals = 0
        self.members = members
        self.d, self.z = lax.axis_index("dp"), lax.axis_index("expert")
        d = self.d
        core, x, y = d % 2, (d // 2) % 2, d // 4
        self.core = core
        self.sib = d + 1 - 2 * core
        self.x = d + 2 - 4 * x
        self.y = d + 4 - 8 * y
        self.diag = self.x + 4 - 8 * y
        self.waiting = []

    def other(self, d):
        return d + 1 - 2 * self.core

    def greet(self):
        barrier = pltpu.get_barrier_semaphore()
        last = self.members - 1

        def hello(d, z):
            pl.semaphore_signal(barrier, inc=1, device_id=(d, z), device_id_type=MESH)

        for d in (self.sib, self.x, self.y):
            hello(d, self.z)
        pl.when(self.z > 0)(lambda: hello(self.d, self.z - 1))
        pl.when(self.z < last)(lambda: hello(self.d, self.z + 1))
        ends = (self.z == 0).astype(jnp.int32) + (self.z == last).astype(jnp.int32)
        pl.semaphore_wait(barrier, 5 - ends)

    def remote(self, src, dst, to):
        k = self.remotes
        self.remotes += 1
        return pltpu.make_async_remote_copy(
            src_ref=src,
            dst_ref=dst,
            send_sem=self.send.at[k],
            recv_sem=self.recv.at[k],
            device_id=to,
            device_id_type=MESH,
        )

    def push(self, src, dst, d):
        copy = self.remote(src, dst, (d, self.z))
        copy.start()
        self.waiting.append(copy.wait_send)
        return copy

    def move(self, src, dst):
        k = self.locals
        self.locals += 1
        copy = pltpu.make_async_copy(src, dst, self.local.at[k])
        copy.start()
        return copy

    def finish(self):
        for wait in self.waiting:
            wait()


def run(order, **chains):
    for name in order:
        next(chains[name], None)
    chains = list(chains.values())
    while chains:
        for chain in list(chains):
            try:
                next(chain)
            except StopIteration:
                chains.remove(chain)


def line_gather(links, own, full):
    z, last = links.z, links.members - 1
    local = links.move(own, full.at[z])
    right, left = (links.d, z + 1), (links.d, z - 1)
    to_right, to_left = [], []
    for s in range(last):
        at_r, at_l = jnp.maximum(z - s, 0), jnp.minimum(z + s, last)
        to_right.append(links.remote(own if s == 0 else full.at[at_r], full.at[at_r], right))
        to_left.append(links.remote(own if s == 0 else full.at[at_l], full.at[at_l], left))
    for s in range(last):
        send_r, send_l = (z < last) & (z >= s), (z > 0) & (z + s <= last)
        pl.when(send_r)(to_right[s].start)
        pl.when(send_l)(to_left[s].start)
        yield
        pl.when((z > 0) & (z - 1 >= s))(to_right[s].wait_recv)
        pl.when((z < last) & (z + 1 + s <= last))(to_left[s].wait_recv)
    for s in range(last):
        send_r, send_l = (z < last) & (z >= s), (z > 0) & (z + s <= last)
        pl.when(send_r)(to_right[s].wait_send)
        pl.when(send_l)(to_left[s].wait_send)
    local.wait()


def add_rows(target, other, step=16):
    rows = target.shape[0]

    @pl.loop(0, rows // step)
    def _(i):
        at = pl.ds(pl.multiple_of(i * step, step), step)
        target[at] = (target[at].astype(F32) + other[at].astype(F32)).astype(target.dtype)


def line_scatter(links, part, acc, from_left, from_right):
    z, last = links.z, links.members - 1
    made = set()

    def make(o):
        if o not in made:
            made.add(o)
            part(o)

    to_right = {o: links.remote(acc.at[o], from_left.at[o], (links.d, z + 1)) for o in range(1, last + 1)}
    to_left = {o: links.remote(acc.at[o], from_right.at[o], (links.d, z - 1)) for o in range(last)}

    def pass_right(o):
        @pl.when(z > 0)
        def _():
            to_right[o].wait_recv()
            add_rows(acc.at[o], from_left.at[o])

        to_right[o].start()

    def pass_left(o):
        @pl.when(z < last)
        def _():
            to_left[o].wait_recv()
            add_rows(acc.at[o], from_right.at[o])

        to_left[o].start()

    @pl.when(z == 0)
    def _():
        from_left[0] = jnp.zeros(from_left.shape[1:], from_left.dtype)

    @pl.when(z == last)
    def _():
        from_right[last] = jnp.zeros(from_right.shape[1:], from_right.dtype)

    for j in range(last):
        make(last - j)
        make(j)
        pl.when((z < last - j) & (2 * z < last))(functools.partial(pass_right, last - j))
        pl.when(z > j)(functools.partial(pass_left, j))
        pl.when((z < last - j) & (2 * z >= last))(functools.partial(pass_right, last - j))
        yield
    for o in range(last + 1):

        @pl.when(z == o)
        def _(o=o):
            if o > 0:
                to_right[o].wait_recv()
            if o < last:
                to_left[o].wait_recv()

    for o in range(last + 1):
        if o > 0:
            pl.when(z < o)(to_right[o].wait_send)
        if o < last:
            pl.when(z > o)(to_left[o].wait_send)


def line_sum_gather(links, part, acc, from_left, from_right, finish, own, full, parts=2):
    z, last = links.z, links.members - 1
    rows = own.shape[0] // parts
    spans = [pl.ds(h * rows, rows) for h in range(parts)]
    right, left = (links.d, z + 1), (links.d, z - 1)
    sum_r, sum_l, go_r, go_l, local = {}, {}, {}, {}, []
    for h, span in enumerate(spans):
        for o in range(last + 1):
            if o > 0:
                sum_r[h, o] = links.remote(acc.at[o, span], from_left.at[o, span], right)
            if o < last:
                sum_l[h, o] = links.remote(acc.at[o, span], from_right.at[o, span], left)
        for s in range(last):
            at_r, at_l = jnp.maximum(z - s, 0), jnp.minimum(z + s, last)
            here_r, here_l = full.at[at_r, span], full.at[at_l, span]
            go_r[h, s] = links.remote(own.at[span] if s == 0 else here_r, here_r, right)
            go_l[h, s] = links.remote(own.at[span] if s == 0 else here_l, here_l, left)

    def pass_right(h, o):
        @pl.when(z > 0)
        def _():
            sum_r[h, o].wait_recv()
            add_rows(acc.at[o, spans[h]], from_left.at[o, spans[h]])

        sum_r[h, o].start()

    def pass_left(h, o):
        @pl.when(z < last)
        def _():
            sum_l[h, o].wait_recv()
            add_rows(acc.at[o, spans[h]], from_right.at[o, spans[h]])

        sum_l[h, o].start()

    def send(h, s):
        pl.when((z < last) & (z >= s))(go_r[h, s].start)
        pl.when((z > 0) & (z + s <= last))(go_l[h, s].start)

    @pl.when(z == 0)
    def _():
        from_left[0] = jnp.zeros(from_left.shape[1:], from_left.dtype)

    @pl.when(z == last)
    def _():
        from_right[last] = jnp.zeros(from_right.shape[1:], from_right.dtype)

    made = set()
    for j in range(last):
        for o in (last - j, j):
            if o not in made:
                made.add(o)
                part(o)
        for h in range(parts):
            pl.when((z < last - j) & (2 * z < last))(functools.partial(pass_right, h, last - j))
            pl.when(z > j)(functools.partial(pass_left, h, j))
            pl.when((z < last - j) & (2 * z >= last))(functools.partial(pass_right, h, last - j))
            yield
    for h in range(parts):
        for o in range(last + 1):
            if o > 0:
                pl.when(z == o)(sum_r[h, o].wait_recv)
            if o < last:
                pl.when(z == o)(sum_l[h, o].wait_recv)
        finish(h * rows, rows)
        send(h, 0)
        local.append(links.move(own.at[spans[h]], full.at[z, spans[h]]))
        yield
    for s in range(last):
        for h in range(parts):
            pl.when((z > 0) & (z - 1 >= s))(go_r[h, s].wait_recv)
            pl.when((z < last) & (z + 1 + s <= last))(go_l[h, s].wait_recv)
            if s + 1 < last:
                send(h, s + 1)
            yield
    for h in range(parts):
        for o in range(last + 1):
            if o > 0:
                pl.when(z < o)(sum_r[h, o].wait_send)
            if o < last:
                pl.when(z > o)(sum_l[h, o].wait_send)
        for s in range(last):
            pl.when((z < last) & (z >= s))(go_r[h, s].wait_send)
            pl.when((z > 0) & (z + s <= last))(go_l[h, s].wait_send)
    for copy in local:
        copy.wait()


def plane_gather(links, own, full):
    half = own.shape[0] // 2
    first, second = pl.ds(0, half), pl.ds(half, half)
    me = links.d
    local = links.move(own, full.at[me])
    by_x, by_y = {}, {}
    for by, d, h in ((by_y, links.y, first), (by_x, links.x, second), (by_x, links.x, first), (by_y, links.y, second)):
        by[h.start // half] = links.push(own.at[h], full.at[me, h], d)
    to_sib = [links.push(own, full.at[me], links.sib)]

    def share(d, h):
        to_sib.append(links.push(full.at[d, h], full.at[d, h], links.sib))

    yield
    by_y[0].wait_recv()
    over_x = links.push(full.at[links.y, first], full.at[links.y, first], links.x)
    share(links.y, first)
    by_x[1].wait_recv()
    over_y = links.push(full.at[links.x, second], full.at[links.x, second], links.y)
    share(links.x, second)
    yield
    by_x[0].wait_recv()
    share(links.x, first)
    by_y[1].wait_recv()
    share(links.y, second)
    yield
    over_x.wait_recv()
    share(links.diag, first)
    over_y.wait_recv()
    share(links.diag, second)
    yield
    for copy in to_sib:
        copy.wait_recv()
    local.wait()


def plane_scatter(links, part, mine, theirs, mid_x, mid_y, end_x, end_y):
    half = part.shape[1] // 2
    first, second = pl.ds(0, half), pl.ds(half, half)
    chips = (links.d, links.x, links.y, links.diag)
    from_sib, load = {}, {}
    held = [part.at[chip] if mine is None else mine.at[k] for k, chip in enumerate(chips)]
    for k in (3, 1, 2, 0):
        from_sib[k] = links.push(part.at[links.other(chips[k])], theirs.at[k], links.sib)
        if mine is not None:
            load[k] = links.move(part.at[chips[k]], held[k])
    yield
    for k in (3, 1, 2):
        if load:
            load[k].wait()
        from_sib[k].wait_recv()
        add_rows(held[k], theirs.at[k])
        if k == 3:
            to_mid_x = links.push(held[3].at[first], mid_x, links.x)
            to_mid_y = links.push(held[3].at[second], mid_y, links.y)
        if k == 1:
            to_end_x = links.push(held[1].at[first], end_x.at[first], links.x)
        if k == 2:
            to_end_y = links.push(held[2].at[second], end_y.at[second], links.y)
    yield
    to_mid_y.wait_recv()
    add_rows(held[1].at[second], mid_y)
    rest_x = links.push(held[1].at[second], end_x.at[second], links.x)
    to_mid_x.wait_recv()
    add_rows(held[2].at[first], mid_x)
    rest_y = links.push(held[2].at[first], end_y.at[first], links.y)
    yield
    if load:
        load[0].wait()
    from_sib[0].wait_recv()
    to_end_x.wait_recv()
    to_end_y.wait_recv()
    rest_x.wait_recv()
    rest_y.wait_recv()


def plane_scratch(rows, cols, mine=True):
    return [pltpu.VMEM((4, rows, cols), BF16)] * mine + [
        pltpu.VMEM((4, rows, cols), BF16),
        pltpu.VMEM((rows // 2, cols), BF16),
        pltpu.VMEM((rows // 2, cols), BF16),
        pltpu.VMEM((rows, cols), BF16),
        pltpu.VMEM((rows, cols), BF16),
    ]


def plane_result(mine, theirs, end_x, end_y, out, step=16):
    @pl.loop(0, out.shape[-2] // step)
    def _(i):
        at = pl.ds(pl.multiple_of(i * step, step), step)
        own = mine[at].astype(F32) + theirs[0, at].astype(F32)
        total = (own + end_x[at].astype(F32) + end_y[at].astype(F32)).astype(out.dtype)
        if len(out.shape) == 2:
            out[at] = total
        else:
            cols = out.shape[2]
            for e in range(out.shape[0]):
                out[e, at] = total[:, e * cols : (e + 1) * cols]


def line_result(z, acc, from_left, from_right, at):
    return (
        acc[z, at].astype(F32) + from_left[z, at].astype(F32) + from_right[z, at].astype(F32)
    )


ANY = pl.BlockSpec(memory_space=pl.ANY)
VMEM = pl.BlockSpec(memory_space=pltpu.VMEM)


def comm_call(kernel, name, number, members, remotes, locals_, in_specs, out_specs, out_shape, scratch):
    return pl.pallas_call(
        functools.partial(kernel, members),
        out_shape=out_shape,
        in_specs=in_specs,
        out_specs=out_specs,
        scratch_shapes=[
            pltpu.SemaphoreType.DMA((remotes,)),
            pltpu.SemaphoreType.DMA((remotes,)),
            pltpu.SemaphoreType.DMA((locals_,)),
            *scratch,
        ],
        compiler_params=pltpu.CompilerParams(
            collective_id=number, has_side_effects=True, vmem_limit_bytes=VMEM_LIMIT
        ),
        name=name,
    )


def sds(shape, dtype):
    return jax.ShapeDtypeStruct(shape, dtype)


def third_kernel(members, part, residual, cot, gain, gate, up, grad_residual, gain_part, out_all, gate_out, up_out, send, recv, local, acc, from_left, from_right, grad_out, *rest):
    links = Links(send, recv, local, members)
    links.greet()
    for_gate, for_up = rest[:6], rest[6:]

    def finish(first, count):
        @pl.loop(0, count // 16)
        def _(i):
            at = pl.ds(pl.multiple_of(first + i * 16, 16), 16)
            grad = line_result(links.z, acc, from_left, from_right, at)
            here = residual[at]
            factor = rms_factor(here)
            gain_part[...] += jnp.sum(grad * here * factor, axis=0, keepdims=True)
            total = cot[at].astype(F32) + norm_back(here, factor, gain[1:2], grad)
            grad_residual[at] = total
            grad_out[at] = (branch_scale * total).astype(BF16)

    def chain():
        links.move(part, acc).wait()
        gain_part[...] = jnp.zeros(gain_part.shape, F32)
        yield from line_sum_gather(
            links, lambda o: None, acc, from_left, from_right, finish, grad_out, out_all
        )

    run(
        "uuzuzzgzzgzzzzzzg",
        z=chain(),
        g=plane_scatter(links, gate, *for_gate),
        u=plane_scatter(links, up, *for_up),
    )
    plane_result(for_gate[0].at[0], for_gate[1], for_gate[4], for_gate[5], gate_out)
    plane_result(for_up[0].at[0], for_up[1], for_up[4], for_up[5], up_out)
    links.finish()


def third_phase(members, own_experts, part, residual, cot, gain, gate, up):
    rows, width = cot.shape
    blocks = pltpu.VMEM((members, rows, width), BF16)
    return comm_call(
        third_kernel, "phase_three", 3, members, 80, 16,
        [ANY, VMEM, VMEM, VMEM, ANY, ANY], [VMEM, VMEM, ANY, VMEM, VMEM],
        [
            sds((rows, width), F32),
            sds((1, width), F32),
            sds((members, rows, width), BF16),
            sds((own_experts, gate.shape[1], gate.shape[2] // own_experts), F32),
            sds((own_experts, up.shape[1], up.shape[2] // own_experts), F32),
        ],
        [blocks, blocks, blocks, pltpu.VMEM((rows, width), BF16)]
        + plane_scratch(*gate.shape[1:])
        + plane_scratch(*up.shape[1:]),
    )(part, residual, cot, gain, gate, up)


def lane_ids(rows):
    return lax.broadcasted_iota(jnp.int32, (rows, LANES), 1)


def dims(a, b):
    return (((a,), (b,)), ((), ()))


def mm(a, b):
    return lax.dot_general(a, b, dims(1, 0), preferred_element_type=F32)


def mm_nt(a, b):
    return lax.dot_general(a, b, dims(1, 1), preferred_element_type=F32)


def mm_tn(a, b):
    return lax.dot_general(a, b, dims(0, 0), preferred_element_type=F32)


def first_lanes():
    same = lax.broadcasted_iota(jnp.int32, (16, LANES), 0) == lax.broadcasted_iota(jnp.int32, (16, LANES), 1)
    return same.astype(BF16)


def expert_kernel(capacity, own_experts, route, normed, cot, w_gate, w_up, w_down, mixture, grad_normed, d_gate, d_up, d_down, mix_sum, grad_sum, slot_cols, weight_cols, slot_rows):
    e = pl.program_id(0)
    span = normed.shape[0]

    @pl.when(e == 0)
    def _():
        mix_sum[...] = jnp.zeros(mix_sum.shape, F32)
        grad_sum[...] = jnp.zeros(grad_sum.shape, F32)
        lane = lane_ids(LANES)
        name = (lax.axis_index("expert") * own_experts + lane).astype(F32)
        name = jnp.where(lane < own_experts, name, -1.0)
        upto = (lane <= lax.broadcasted_iota(jnp.int32, (LANES, LANES), 0)).astype(BF16)
        before = jnp.zeros((1, LANES), F32)
        for b in range(span // LANES):
            at = pl.ds(b * LANES, LANES)
            chosen, weight = jnp.zeros((LANES, LANES), F32), jnp.zeros((LANES, LANES), F32)
            for k in range(TOP):
                named = route[at, k : k + 1] == name
                chosen = jnp.where(named, 1.0, chosen)
                weight = jnp.where(named, route[at, TOP + k : TOP + k + 1], weight)
            slot = mm(upto, chosen.astype(BF16)) + (before - 1.0)
            slot_cols[at] = jnp.where((chosen > 0.0) & (slot < capacity), slot, -1.0)
            weight_cols[at] = weight
            before = before + jnp.sum(chosen, axis=0, keepdims=True)
        slot_rows[...] = mm_nt(first_lanes(), slot_cols[...].astype(BF16))

    def column(values):
        return jnp.sum(jnp.where(lane_ids(span) == e, values[...], 0.0), axis=1, keepdims=True)

    slots = lax.broadcasted_iota(jnp.int32, (capacity, span), 0).astype(F32)
    pick = (slot_rows[pl.ds(e, 1)] == slots).astype(BF16)
    puts = column(slot_cols) == lax.broadcasted_iota(jnp.int32, (span, capacity), 1).astype(F32)
    put = puts.astype(BF16)
    gate_row = jnp.sum(jnp.where(puts, column(weight_cols), 0.0), axis=0, keepdims=True)
    same = lax.broadcasted_iota(jnp.int32, (capacity, capacity), 0) == lax.broadcasted_iota(jnp.int32, (capacity, capacity), 1)
    gate_col = jnp.sum(jnp.where(same, gate_row, 0.0), axis=1, keepdims=True)
    received = mm(pick, normed[...]).astype(BF16)
    pre_gate, pre_up = mm(received, w_gate[...]), mm(received, w_up[...])
    sig = 1.0 / (1.0 + jnp.exp(-pre_gate))
    silu = pre_gate * sig
    activ = (silu * pre_up).astype(BF16)
    produced = (gate_col * mm_nt(activ, w_down[...])).astype(BF16)
    mix_sum[...] += mm(put, produced)
    grad_out = (gate_col * (branch_scale * mm(pick, cot[...]))).astype(BF16)
    grad_activ = mm(grad_out, w_down[...])
    grad_gate = (grad_activ * pre_up * (sig * (1.0 + pre_gate * (1.0 - sig)))).astype(BF16)
    grad_up = (grad_activ * silu).astype(BF16)
    grad_pair = (mm_nt(grad_gate, w_gate[...]) + mm_nt(grad_up, w_up[...])).astype(BF16)
    grad_sum[...] += mm(put, grad_pair)
    d_gate[...] = mm_tn(received, grad_gate).astype(BF16)
    d_up[...] = mm_tn(received, grad_up).astype(BF16)
    d_down[...] = mm_tn(grad_out, activ).astype(BF16)

    @pl.when(e == pl.num_programs(0) - 1)
    def _():
        mixture[...] = mix_sum[...].astype(BF16)
        grad_normed[...] = grad_sum[...].astype(BF16)


def experts(own_experts, capacity, route, normed, cot, w_gate, w_up, w_down):
    span, width = normed.shape
    ff = w_gate.shape[1] // own_experts
    whole = pl.BlockSpec((span, width), lambda e: (0, 0))
    column = pl.BlockSpec((width, ff), lambda e: (0, e))
    grads = jax.ShapeDtypeStruct(w_gate.shape, BF16)
    rows = jax.ShapeDtypeStruct((span, width), BF16)
    return pl.pallas_call(
        functools.partial(expert_kernel, capacity, own_experts),
        grid=(own_experts,),
        in_specs=[pl.BlockSpec(route.shape, lambda e: (0, 0)), whole, whole, column, column, column],
        out_specs=[whole, whole, column, column, column],
        out_shape=[rows, rows, grads, grads, grads],
        scratch_shapes=[
            pltpu.VMEM((span, width), F32),
            pltpu.VMEM((span, width), F32),
            pltpu.VMEM((span, LANES), F32),
            pltpu.VMEM((span, LANES), F32),
            pltpu.VMEM((16, span), F32),
        ],
        compiler_params=pltpu.CompilerParams(vmem_limit_bytes=VMEM_LIMIT),
        name="experts",
    )(route, normed, cot, w_gate, w_up, w_down)


def turn(x, cosine, sine):
    half = HEAD_SIZE // 2
    ahead, behind = pltpu.roll(x, LANES - half, axis=1), pltpu.roll(x, half, axis=1)
    partner = jnp.where(lane_ids(x.shape[0]) % HEAD_SIZE < half, ahead, behind)
    return x * cosine + partner * sine


def spread(block, at, out):
    low = lane_ids(block.shape[0]) < HEAD_SIZE
    other = pltpu.roll(block, HEAD_SIZE, axis=1)
    zero = jnp.zeros_like(block)
    out[0, 0, at] = jnp.where(low, block, zero).astype(BF16)
    out[0, 1, at] = jnp.where(low, zero, other).astype(BF16)
    out[1, 0, at] = jnp.where(low, other, zero).astype(BF16)
    out[1, 1, at] = jnp.where(low, zero, block).astype(BF16)


def attention_setup(segment, bias):
    span = bias.shape[0]
    same = lax.broadcasted_iota(jnp.int32, (LANES, LANES), 0) == lane_ids(LANES)
    for b in range(span // LANES):
        at = pl.ds(b * LANES, LANES)
        row = b * LANES + lax.broadcasted_iota(jnp.int32, (LANES, span), 0)
        col = lax.broadcasted_iota(jnp.int32, (LANES, span), 1)
        here = segment[:, b * LANES : (b + 1) * LANES]
        here = jnp.sum(jnp.where(same, here, 0.0), axis=1, keepdims=True)
        ok = (here == segment[...]) & (col <= row)
        bias[at] = jnp.where(ok, 0.0, -1e30)


def weight_columns(pack_all, first, cols):
    return pack_all[:, :, first : first + cols].reshape(-1, cols)


def gain_rows(pack_all, first):
    return mm_nt(first_lanes(), weight_columns(pack_all, first, LANES))


def attend_steps(qkv, kx, vx, bias, probs, attended):
    span, blocks = qkv.shape[0], attended.shape[1] // LANES
    repeat = QUERY_HEADS // KEY_VALUE_HEADS
    for j in range(blocks):
        for b in range(span // LANES):
            at, keys = pl.ds(b * LANES, LANES), (b + 1) * LANES
            q = qkv[at, j * LANES : (j + 1) * LANES]
            total = jnp.zeros((LANES, LANES), F32)
            for half in range(2):
                h = 2 * j + half
                kv = h // repeat
                scores = mm_nt(q, kx[kv, half, :keys]) + bias[at, :keys]
                peak = jnp.max(scores, axis=1, keepdims=True)
                exponent = jnp.exp(scores - peak)
                share = 1.0 / jnp.sum(exponent, axis=1, keepdims=True)
                low = (exponent * share).astype(BF16)
                probs[h, at, :keys] = low
                total += mm(low, vx[kv, half, :keys])
            attended[at, j * LANES : (j + 1) * LANES] = total.astype(BF16)
        yield


def forward_kernel(
    members, tokens, cot, route, w_query, w_key, w_value, w_out, gain_attn, gain_ffn, gate, up, down, segment, cosine, sine,
    cot_all, route_all, pack_all, gate_all, up_all, down_all, normed_attn, qkv, kx, vx, probs, attended, residual, normed_all, gains,
    send, recv, local, pack, tokens_all, bias, acc, from_left, from_right, normed,
):
    links = Links(send, recv, local, members)
    links.greet()
    rows, width = tokens.shape
    span = rows * members
    q_cols = attended.shape[1]
    qkv_cols = qkv.shape[1]

    def pack_chain():
        loads, at = [], 0
        for weight in (w_query, w_key, w_value, w_out):
            cols = weight.shape[1] // members
            mine = pl.ds(pl.multiple_of(links.z * cols, LANES), cols)
            loads.append(links.move(weight.at[:, mine], pack.at[:, at : at + cols]))
            at += cols
        which = lax.broadcasted_iota(jnp.int32, (16, pack.shape[0]), 0)
        both = jnp.where(which == 0, gain_attn[...].astype(F32), jnp.where(which == 1, gain_ffn[...].astype(F32), 0.0))
        pack[:, at:] = mm_tn(both.astype(BF16), first_lanes()).astype(BF16)
        for load in loads:
            load.wait()
        yield from plane_gather(links, pack, pack_all)

    def produce(o):
        acc[o] = mm_nt(attended[o * rows : (o + 1) * rows], weight_columns(pack_all, qkv_cols, q_cols)).astype(BF16)

    def chain():
        attention_setup(segment, bias)
        yield
        gains[...] = gain_rows(pack_all, qkv_cols + q_cols)

        @pl.loop(0, span // 16)
        def _(i):
            here = tokens_all[i // (rows // 16), pl.ds(pl.multiple_of(i % (rows // 16) * 16, 16), 16)].astype(F32)
            normed_attn[pl.ds(pl.multiple_of(i * 16, 16), 16)] = (here * rms_factor(here) * gains[0:1]).astype(BF16)

        @pl.loop(0, span // LANES)
        def _(i):
            at = pl.ds(pl.multiple_of(i * LANES, LANES), LANES)
            here = mm(normed_attn[at], weight_columns(pack_all, 0, qkv_cols))
            c, s = cosine[at], sine[at]
            for j in range(q_cols // LANES):
                lanes = slice(j * LANES, (j + 1) * LANES)
                qkv[at, lanes] = (turn(here[:, lanes], c, s).astype(BF16).astype(F32) * score_scale).astype(BF16)
            key = turn(here[:, q_cols : q_cols + LANES], c, s)
            value = here[:, q_cols + LANES :]
            qkv[at, q_cols : q_cols + LANES] = key.astype(BF16)
            qkv[at, q_cols + LANES :] = value.astype(BF16)
            spread(key, at, kx)
            spread(value, at, vx)

        yield
        yield from attend_steps(qkv, kx, vx, bias, probs, attended)

        def finish(first, count):
            @pl.loop(0, count // 16)
            def _(i):
                at = pl.ds(pl.multiple_of(first + i * 16, 16), 16)
                here = tokens[at].astype(F32) + branch_scale * line_result(links.z, acc, from_left, from_right, at)
                residual[at] = here
                normed[at] = (here * rms_factor(here) * gains[1:2]).astype(BF16)

        yield from line_sum_gather(links, produce, acc, from_left, from_right, finish, normed, normed_all)

    run(
        FORWARD_ORDER,
        t=line_gather(links, tokens, tokens_all),
        r=line_gather(links, route, route_all),
        c=line_gather(links, cot, cot_all),
        p=pack_chain(),
        g=plane_gather(links, gate, gate_all),
        u=plane_gather(links, up, up_all),
        d=plane_gather(links, down, down_all),
        a=chain(),
    )
    links.finish()


FORWARD_ORDER = "tptpdptpcaptgaaacdtrgatcaardaagdattpuparparadrpaarrd"


def forward_phase(members, tokens, cot, route, w_query, w_key, w_value, w_out, gain_attn, gain_ffn, gate, up, down, segment, cosine, sine):
    rows, width = tokens.shape
    q_cols = w_query.shape[1] // members
    qkv_cols = q_cols + 2 * w_key.shape[1] // members
    pack = (w_query.shape[0], qkv_cols + q_cols + LANES)
    span = rows * members
    blocks = pltpu.VMEM((members, rows, width), BF16)
    heads = q_cols // HEAD_SIZE
    return comm_call(
        forward_kernel, "forward", 1, members, 120, 16,
        [VMEM, ANY, ANY, ANY, ANY, ANY, ANY, VMEM, VMEM, ANY, ANY, ANY, VMEM, VMEM, VMEM],
        [ANY, ANY, VMEM, ANY, ANY, ANY, VMEM, VMEM, VMEM, VMEM, VMEM, VMEM, VMEM, ANY, VMEM],
        [
            sds((members, rows, width), BF16),
            sds((members, *route.shape), F32),
            sds((8, *pack), BF16),
            sds((8, *gate.shape), BF16),
            sds((8, *up.shape), BF16),
            sds((8, *down.shape), BF16),
            sds((span, width), BF16),
            sds((span, qkv_cols), BF16),
            sds((2, 2, span, LANES), BF16),
            sds((2, 2, span, LANES), BF16),
            sds((heads, span, span), BF16),
            sds((span, q_cols), BF16),
            sds((rows, width), F32),
            sds((members, rows, width), BF16),
            sds((16, width), F32),
        ],
        [
            pltpu.VMEM(pack, BF16),
            blocks,
            pltpu.VMEM((span, span), F32),
            blocks,
            blocks,
            blocks,
            pltpu.VMEM((rows, width), BF16),
        ],
    )(tokens, cot, route, w_query, w_key, w_value, w_out, gain_attn, gain_ffn, gate, up, down, segment, cosine, sine)


def attend_back_steps(qkv, kx, vx, probs, grad_attended, cosine, sine, grad_k, grad_v, grad_qkv):
    span = qkv.shape[0]
    blocks = grad_attended.shape[1] // LANES
    repeat = QUERY_HEADS // KEY_VALUE_HEADS
    grad_k[...] = jnp.zeros(grad_k.shape, F32)
    grad_v[...] = jnp.zeros(grad_v.shape, F32)
    for j in range(blocks):
        lanes = slice(j * LANES, (j + 1) * LANES)
        for b in range(span // LANES):
            at, keys = pl.ds(b * LANES, LANES), (b + 1) * LANES
            q, grad = qkv[at, lanes], grad_attended[at, lanes]
            total = jnp.zeros((LANES, LANES), F32)
            for half in range(2):
                h = 2 * j + half
                kv = h // repeat
                low = probs[h, at, :keys]
                share = low.astype(F32)
                grad_probs = mm_nt(grad, vx[kv, half, :keys])
                inner = jnp.sum(share * grad_probs, axis=1, keepdims=True)
                grad_scores = (share * (grad_probs - inner)).astype(BF16)
                total += mm(grad_scores, kx[kv, half, :keys])
                grad_k[kv, half, :keys] += mm_tn(grad_scores, q)
                grad_v[kv, half, :keys] += mm_tn(low, grad)
            grad_qkv[at, lanes] = turn(total * score_scale, cosine[at], -sine[at]).astype(BF16)
        yield
    first = blocks * LANES

    def fold(parts, at):
        low = lane_ids(LANES) < HEAD_SIZE
        same = jnp.where(low, parts[0, 0, at], parts[1, 1, at])
        crossed = jnp.where(low, parts[1, 0, at], parts[0, 1, at])
        return same + pltpu.roll(crossed, HEAD_SIZE, axis=1)

    for b in range(span // LANES):
        at = pl.ds(b * LANES, LANES)
        grad_qkv[at, first : first + LANES] = turn(fold(grad_k, at), cosine[at], -sine[at]).astype(BF16)
        grad_qkv[at, first + LANES :] = fold(grad_v, at).astype(BF16)


def backward_kernel(
    members, mixture, residual, grad_out_all, grad_residual, gain_ffn_part, tokens, down, row_gains, pack_all, normed_attn, qkv, kx, vx, probs, attended, cosine, sine,
    output, grad_tokens, gains, d_query, d_key, d_value, d_out, d_down,
    send, recv, local, acc_m, left_m, right_m, acc, from_left, from_right, grad_attended, grad_k, grad_v, grad_qkv, gain_part,
    for_w_out, for_w_qkv, own_out, own_qkv, all_out, all_qkv, *rest,
):
    links = Links(send, recv, local, members)
    links.greet()
    rows, width = tokens.shape
    q_cols, qkv_cols = attended.shape[1], qkv.shape[1]
    kv_cols = (qkv_cols - q_cols) // 2
    with_out, with_qkv, with_down = rest[:5], rest[5:10], rest[10:]
    pairs = for_w_out.shape[0] // 2
    step = width // pairs

    def out_chain():
        for i in range(pairs):
            term = mm_tn(grad_out_all[:, i * step : (i + 1) * step], attended[...])
            for_w_out[2 * i : 2 * i + 2] = term.astype(BF16).reshape(2, step // 2, q_cols)
        yield from plane_scatter(links, for_w_out, None, *with_out)
        plane_result(for_w_out.at[links.d], with_out[0], with_out[3], with_out[4], own_out)
        yield from line_gather(links, own_out, all_out)

    def produce(o):
        at = slice(o * rows, (o + 1) * rows)
        part = mm_nt(grad_qkv[at], weight_columns(pack_all, 0, qkv_cols))
        gain_part[...] += jnp.sum(part * normed_attn[at].astype(F32), axis=0, keepdims=True)
        acc[o] = part.astype(BF16)

    def chain():
        wo = weight_columns(pack_all, qkv_cols, q_cols)

        @pl.loop(0, grad_attended.shape[0] // LANES)
        def _(i):
            at = pl.ds(pl.multiple_of(i * LANES, LANES), LANES)
            grad_attended[at] = mm(grad_out_all[at], wo).astype(BF16)

        yield
        yield from attend_back_steps(qkv, kx, vx, probs, grad_attended, cosine, sine, grad_k, grad_v, grad_qkv)
        gain_part[...] = jnp.zeros(gain_part.shape, F32)
        yield from line_scatter(links, produce, acc, from_left, from_right)

        @pl.loop(0, rows // 16)
        def _(i):
            at = pl.ds(pl.multiple_of(i * 16, 16), 16)
            grad = line_result(links.z, acc, from_left, from_right, at)
            here = tokens[at].astype(F32)
            grad_tokens[at] = grad_residual[at] + norm_back(here, rms_factor(here), row_gains[0:1], grad)

    def qkv_chain():
        for i in range(pairs):
            term = mm_tn(normed_attn[:, i * step : (i + 1) * step], grad_qkv[...])
            for_w_qkv[2 * i : 2 * i + 2, :, :qkv_cols] = term.astype(BF16).reshape(2, step // 2, qkv_cols)
        which = lax.broadcasted_iota(jnp.int32, (16, width), 0)
        both = jnp.where(which == 0, gain_part[...] / row_gains[0:1], jnp.where(which == 1, gain_ffn_part[...], 0.0))
        columns = mm_tn(both.astype(BF16), first_lanes())
        for_w_qkv[:, :, qkv_cols:] = columns.astype(BF16).reshape(2 * pairs, step // 2, LANES)
        yield from plane_scatter(links, for_w_qkv, None, *with_qkv)
        plane_result(for_w_qkv.at[links.d], with_qkv[0], with_qkv[3], with_qkv[4], own_qkv)
        yield from line_gather(links, own_qkv, all_qkv)

    def mixture_chain():
        links.move(mixture, acc_m).wait()
        yield from line_scatter(links, lambda o: None, acc_m, left_m, right_m)

        @pl.loop(0, rows // 16)
        def _(i):
            at = pl.ds(pl.multiple_of(i * 16, 16), 16)
            here = residual[at] + branch_scale * line_result(links.z, acc_m, left_m, right_m, at)
            output[at] = here.astype(BF16)

    run(
        BACKWARD_ORDER,
        m=mixture_chain(),
        d=plane_scatter(links, down, *with_down),
        o=out_chain(),
        a=chain(),
        q=qkv_chain(),
    )
    plane_result(with_down[0].at[0], with_down[1], with_down[4], with_down[5], d_down)
    for m in range(members):
        d_out[:, m * q_cols : (m + 1) * q_cols] = all_out[m].astype(F32)
        d_query[:, m * q_cols : (m + 1) * q_cols] = all_qkv[m, :, :q_cols].astype(F32)
        d_key[:, m * kv_cols : (m + 1) * kv_cols] = all_qkv[m, :, q_cols : q_cols + kv_cols].astype(F32)
        d_value[:, m * kv_cols : (m + 1) * kv_cols] = all_qkv[m, :, q_cols + kv_cols : qkv_cols].astype(F32)
    gains[...] = sum(all_qkv[m, :, qkv_cols:].astype(F32) for m in range(members))
    links.finish()


BACKWARD_ORDER = "amoadmmadaaaoqoqoqaoaq"


def backward_phase(members, own_experts, mixture, residual, grad_out_all, grad_residual, gain_ffn_part, tokens, down, row_gains, pack_all, normed_attn, qkv, kx, vx, probs, attended, cosine, sine):
    rows, width = tokens.shape
    span, q_cols = attended.shape
    qkv_cols = qkv.shape[1]
    kv_cols = (qkv_cols - q_cols) // 2
    devices, own = down.shape[:2]
    line = [pltpu.VMEM((members, rows, width), BF16)] * 3
    return comm_call(
        backward_kernel, "backward", 4, members, 100, 32,
        [ANY, VMEM, VMEM, VMEM, VMEM, VMEM, ANY] + [VMEM] * 10,
        [VMEM] * 8,
        [
            sds((rows, width), BF16),
            sds((rows, width), F32),
            sds((own, LANES), F32),
            sds((own, members * q_cols), F32),
            sds((own, members * kv_cols), F32),
            sds((own, members * kv_cols), F32),
            sds((own, members * q_cols), F32),
            sds((own_experts, own, down.shape[2] // own_experts), F32),
        ],
        [
            *line,
            *line,
            pltpu.VMEM((span, q_cols), BF16),
            pltpu.VMEM((2, 2, span, LANES), F32),
            pltpu.VMEM((2, 2, span, LANES), F32),
            pltpu.VMEM((span, qkv_cols), BF16),
            pltpu.VMEM((1, width), F32),
            pltpu.VMEM((devices, own, q_cols), BF16),
            pltpu.VMEM((devices, own, qkv_cols + LANES), BF16),
            pltpu.VMEM((own, q_cols), BF16),
            pltpu.VMEM((own, qkv_cols + LANES), BF16),
            pltpu.VMEM((members, own, q_cols), BF16),
            pltpu.VMEM((members, own, qkv_cols + LANES), BF16),
            *plane_scratch(own, q_cols, False),
            *plane_scratch(own, qkv_cols + LANES, False),
            *plane_scratch(*down.shape[1:]),
        ],
    )(mixture, residual, grad_out_all, grad_residual, gain_ffn_part, tokens, down, row_gains, pack_all, normed_attn, qkv, kx, vx, probs, attended, cosine, sine)


def all_blocks(x, axis):
    return lax.all_gather(x, axis, axis=0)


def plain_first(members, tokens, cot, route, pack, gate):
    return (
        all_blocks(tokens, "expert"),
        all_blocks(cot, "expert"),
        all_blocks(route, "expert"),
        all_blocks(pack, "dp"),
        all_blocks(gate, "dp"),
    )


def line_sum(part):
    return scatter(part.reshape(-1, part.shape[2]), "expert")


def plain_second(members, part, tokens, gain, up, down):
    residual = tokens.astype(F32) + branch_scale * line_sum(part)
    normed = (residual * rms_factor(residual) * gain).astype(BF16)
    return residual, all_blocks(normed, "expert"), all_blocks(up, "dp"), all_blocks(down, "dp")


def plane_sum(part):
    return scatter(part.reshape(-1, part.shape[2]), "dp")


def plain_third(members, part, residual, cot, gain, gate, up):
    grad = line_sum(part)
    factor = rms_factor(residual)
    gain_part = jnp.sum(grad * residual * factor, axis=0, keepdims=True)
    total = cot.astype(F32) + norm_back(residual, factor, gain, grad)
    out_all = all_blocks((branch_scale * total).astype(BF16), "expert")
    return total, gain_part, out_all, plane_sum(gate), plane_sum(up)


def plain_fourth(members, part, grad_residual, tokens, gain, pack, down):
    here = tokens.astype(F32)
    grad_tokens = grad_residual + norm_back(here, rms_factor(here), gain, line_sum(part))
    return grad_tokens, all_blocks(plane_sum(pack).astype(BF16), "expert"), plane_sum(down)


def attend_forward(q, k, v, allowed):
    scores = jnp.einsum("irh,jh->rij", q, k, preferred_element_type=F32) * score_scale
    scores = jnp.where(allowed[None], scores, -1e30)
    peak = jnp.max(scores, axis=-1, keepdims=True)
    exponent = jnp.exp(scores - peak)
    total = jnp.sum(exponent, axis=-1, keepdims=True)
    probs = exponent / total
    return jnp.einsum("rij,jh->irh", probs.astype(BF16), v, preferred_element_type=F32), probs


def attend_backward(q, k, v, probs, grad, allowed):
    grad_probs = jnp.einsum("irh,jh->rij", grad, v, preferred_element_type=F32)
    inner = jnp.sum(probs * grad_probs, axis=-1, keepdims=True)
    grad_scores = (probs * (grad_probs - inner)).astype(BF16)
    grad_q = jnp.einsum("rij,jh->irh", grad_scores, k, preferred_element_type=F32) * score_scale
    grad_k = jnp.einsum("rij,irh->jh", grad_scores, q, preferred_element_type=F32) * score_scale
    grad_v = jnp.einsum("rij,irh->jh", probs.astype(BF16), grad, preferred_element_type=F32)
    return grad_q, grad_k, grad_v


def shards_plain(
    tokens,
    cotangent,
    gain_attn,
    gain_ffn,
    w_query,
    key_weight,
    value_weight,
    w_out,
    expert_gate,
    expert_up,
    expert_down,
    expert_ids,
    gates,
    lengths,
    order,
):
    rows, width = tokens.shape
    members = lax.axis_size("expert")
    member = lax.axis_index("expert")
    span = rows * members
    own_experts, ff = expert_gate.shape[1], expert_gate.shape[2]
    capacity = rows * TOP // own_experts
    q_cols = w_query.shape[1] // members
    kv_cols = key_weight.shape[1] // members
    kv_heads = kv_cols // HEAD_SIZE
    repeat = QUERY_HEADS // KEY_VALUE_HEADS

    def mine(weight, cols):
        return lax.dynamic_slice_in_dim(weight, member * cols, cols, axis=1)

    devices = lax.axis_size("dp")
    phases = [
        functools.partial(phase, members)
        for phase in (plain_first, plain_second, plain_third, plain_fourth)
    ]

    pack = jnp.concatenate(
        [
            mine(w_query, q_cols),
            mine(key_weight, kv_cols),
            mine(value_weight, kv_cols),
            mine(w_out, q_cols),
            gain_attn[:, None],
            gain_ffn[:, None],
            jnp.zeros((gain_attn.shape[0], 126), BF16),
        ],
        axis=1,
    )
    route = jnp.concatenate([expert_ids.astype(F32), gates], axis=1)
    tokens_all, cot_all, route_all, pack_all, gate_all = phases[0](
        tokens, cotangent, route, pack, expert_gate.reshape(-1, own_experts * ff)
    )
    tokens_all = tokens_all.reshape(span, width).astype(F32)
    cot_all = cot_all.reshape(span, width)
    route_all = route_all.reshape(span, 2 * TOP)
    pack_all = pack_all.reshape(width, -1)
    gate_all = gate_all.reshape(width, -1)
    qkv_cols = q_cols + 2 * kv_cols
    w_qkv = pack_all[:, :qkv_cols]
    wo = pack_all[:, qkv_cols : qkv_cols + q_cols]
    gain_one = pack_all[:, qkv_cols + q_cols].astype(F32)[None]
    gain_two = pack_all[:, qkv_cols + q_cols + 1].astype(F32)[None]

    segment, position = layout(lengths[0], order[0], span)
    cosine, sine = rotation(position)
    place = jnp.arange(span, dtype=jnp.int32)
    allowed = (segment[:, None] == segment[None, :]) & (place[None, :] <= place[:, None])
    factor_one = rms_factor(tokens_all)
    normed_attn = (tokens_all * factor_one * gain_one).astype(BF16)
    qkv = dot(normed_attn, w_qkv)
    qk = rotate(qkv[:, : q_cols + kv_cols], cosine, sine).astype(BF16)
    v = qkv[:, q_cols + kv_cols :].astype(BF16)
    q_heads = jnp.moveaxis(qk[:, :q_cols].reshape(span, kv_heads, repeat, HEAD_SIZE), 1, 0)
    k_heads = jnp.moveaxis(qk[:, q_cols:].reshape(span, kv_heads, HEAD_SIZE), 1, 0)
    v_heads = jnp.moveaxis(v.reshape(span, kv_heads, HEAD_SIZE), 1, 0)
    attended, probs = jax.vmap(functools.partial(attend_forward, allowed=allowed))(
        q_heads, k_heads, v_heads
    )
    attended = jnp.moveaxis(attended, 0, 1).reshape(span, q_cols).astype(BF16)
    attn_part = dot_nt(attended, wo).astype(BF16).reshape(members, rows, width)
    residual, normed_all, up_all, down_all = phases[1](
        attn_part,
        tokens,
        gain_two,
        expert_up.reshape(-1, own_experts * ff),
        expert_down.reshape(-1, own_experts * ff),
    )
    normed_all = normed_all.reshape(span, width)
    up_all, down_all = up_all.reshape(width, -1), down_all.reshape(width, -1)

    mixture, grad_normed, *by_kind = experts(
        own_experts, capacity, route_all, normed_all, cot_all, gate_all, up_all, down_all
    )
    output = (residual + branch_scale * scatter(mixture, "expert")).astype(BF16)
    by_kind = [one.reshape(devices, -1, own_experts * ff) for one in by_kind]

    grad_residual, gain_two_part, grad_attn_out, sum_gate, sum_up = phases[2](
        grad_normed.reshape(members, rows, width),
        residual,
        cotangent,
        gain_two,
        by_kind[0],
        by_kind[1],
    )
    grad_attn_out = grad_attn_out.reshape(span, width)
    term_out = dot_tn(grad_attn_out, attended)
    grad_attended = dot(grad_attn_out, wo).astype(BF16)
    grad_heads = jnp.moveaxis(grad_attended.reshape(span, kv_heads, repeat, HEAD_SIZE), 1, 0)
    grad_q, grad_k, grad_v = jax.vmap(functools.partial(attend_backward, allowed=allowed))(
        q_heads, k_heads, v_heads, probs, grad_heads
    )
    grad_qk = jnp.concatenate(
        [
            jnp.moveaxis(grad_q, 0, 1).reshape(span, q_cols),
            jnp.moveaxis(grad_k, 0, 1).reshape(span, kv_cols),
        ],
        axis=1,
    )
    grad_qkv = jnp.concatenate(
        [
            rotate(grad_qk, cosine, sine, back=True).astype(BF16),
            jnp.moveaxis(grad_v, 0, 1).reshape(span, kv_cols).astype(BF16),
        ],
        axis=1,
    )
    grad_norm_part = dot_nt(grad_qkv, w_qkv)
    gain_one_part = jnp.sum(grad_norm_part * tokens_all * factor_one, axis=0)
    term_qkv = dot_tn(normed_attn, grad_qkv)
    packed_grads = jnp.concatenate(
        [
            term_qkv,
            term_out,
            gain_one_part[:, None],
            gain_two_part.reshape(-1, 1),
            jnp.zeros((width, 126), F32),
        ],
        axis=1,
    )
    grad_tokens, per_member, sum_down = phases[3](
        grad_norm_part.astype(BF16).reshape(members, rows, width),
        grad_residual,
        tokens,
        gain_one,
        packed_grads.astype(BF16).reshape(devices, -1, packed_grads.shape[1]),
        by_kind[2],
    )
    per_member = per_member.astype(F32)

    def columns(first, cols):
        part = per_member[:, :, first : first + cols]
        return jnp.moveaxis(part, 0, 1).reshape(part.shape[1], -1)

    gains = jnp.sum(per_member[:, :, qkv_cols + q_cols :], axis=0)
    return (
        output,
        grad_tokens,
        gains[:, 0],
        gains[:, 1],
        columns(0, q_cols),
        columns(q_cols, kv_cols),
        columns(q_cols + kv_cols, kv_cols),
        columns(qkv_cols, q_cols),
        sum_gate.reshape(-1, own_experts, ff),
        sum_up.reshape(-1, own_experts, ff),
        sum_down.reshape(-1, own_experts, ff),
    )


def shards_fast(
    tokens,
    cotangent,
    gain_attn,
    gain_ffn,
    w_query,
    key_weight,
    value_weight,
    w_out,
    expert_gate,
    expert_up,
    expert_down,
    expert_ids,
    gates,
    lengths,
    order,
):
    rows, width = tokens.shape
    members, devices = lax.axis_size("expert"), lax.axis_size("dp")
    span = rows * members
    own_experts, ff = expert_gate.shape[1], expert_gate.shape[2]
    capacity = rows * TOP // own_experts
    route = jnp.concatenate([expert_ids.astype(F32), gates], axis=1)
    segment, position = layout(lengths[0], order[0], span)
    lane = jnp.arange(LANES, dtype=jnp.int32) % HEAD_SIZE
    half = HEAD_SIZE // 2
    frequency = rope_base ** (-((lane % half).astype(F32) * (2.0 / HEAD_SIZE)))
    angles = position[:, None] * frequency[None, :]
    cosine, sine = jnp.cos(angles), jnp.where(lane < half, -1.0, 1.0) * jnp.sin(angles)
    (
        cot_all, route_all, pack_all, gate_all, up_all, down_all,
        normed_attn, qkv, kx, vx, probs, attended, residual, normed_all, gains,
    ) = forward_phase(
        members, tokens, cotangent, route, w_query, key_weight, value_weight, w_out,
        gain_attn[None], gain_ffn[None],
        expert_gate.reshape(-1, own_experts * ff),
        expert_up.reshape(-1, own_experts * ff),
        expert_down.reshape(-1, own_experts * ff),
        segment.astype(F32)[None], cosine, sine,
    )
    cot_all = cot_all.reshape(span, width)
    normed_all = normed_all.reshape(span, width)
    route_all = route_all.reshape(span, 2 * TOP)
    gate_all, up_all, down_all = (w.reshape(width, -1) for w in (gate_all, up_all, down_all))
    mixture, grad_normed, *by_kind = experts(
        own_experts, capacity, route_all, normed_all, cot_all, gate_all, up_all, down_all
    )
    by_kind = [one.reshape(devices, -1, own_experts * ff) for one in by_kind]

    grad_residual, gain_two_part, grad_attn_out, sum_gate, sum_up = third_phase(
        members, own_experts,
        grad_normed.reshape(members, rows, width),
        residual,
        cotangent,
        gains,
        by_kind[0],
        by_kind[1],
    )
    (
        output, grad_tokens, grad_gains, d_query, d_key, d_value, d_out, d_down,
    ) = backward_phase(
        members, own_experts,
        mixture.reshape(members, rows, width),
        residual,
        grad_attn_out.reshape(span, width),
        grad_residual,
        gain_two_part,
        tokens,
        by_kind[2],
        gains,
        pack_all,
        normed_attn, qkv, kx, vx, probs, attended, cosine, sine,
    )
    return (
        output,
        grad_tokens,
        grad_gains[:, 0],
        grad_gains[:, 1],
        d_query,
        d_key,
        d_value,
        d_out,
        sum_gate.transpose(1, 0, 2),
        sum_up.transpose(1, 0, 2),
        d_down.transpose(1, 0, 2),
    )


def solution(mesh):
    both = P(("dp", "expert"), None)
    row, rows = P("dp"), P("dp", None)
    experts = P("dp", "expert", None)
    fast = mesh.shape["dp"] == 8 and mesh.shape["expert"] == 4
    return jax.shard_map(
        shards_fast if fast else shards_plain,
        mesh=mesh,
        in_specs=(both, both, row, row, rows, rows, rows, rows)
        + (experts, experts, experts, both, both, rows, rows),
        out_specs=(both, both, row, row, rows, rows, rows, rows, experts, experts, experts),
        check_vma=False,
    )
```

```python
import functools

import jax
import jax.numpy as jnp
from jax import lax
from jax.experimental import pallas as pl
from jax.experimental.pallas import tpu as pltpu
from jax.sharding import PartitionSpec as P

QUERY_HEADS = 24
KEY_VALUE_HEADS = 8
HEAD_SIZE = 64
TOP = 8

epsilon = 1e-06
rope_base = 10000.0
score_scale = 0.015625
branch_scale = 0.22
F32 = jnp.float32
BF16 = jnp.bfloat16
MESH = pl.DeviceIdType.MESH
LANES = 128
VMEM_LIMIT = 60 * 2**20


def layout(lengths_row, order_row, span):
    seqs = lengths_row.shape[0]
    slot_ids = jnp.arange(seqs, dtype=jnp.int32)
    picked = jnp.sum(
        jnp.where(order_row[:, None] == slot_ids[None, :], lengths_row[None, :], 0), axis=1
    )
    before = slot_ids[:, None] >= slot_ids[None, :]
    seq_ends = jnp.sum(jnp.where(before, picked[None, :], 0), axis=1)
    place = jnp.arange(span, dtype=jnp.int32)
    passed = place[:, None] >= seq_ends[None, :]
    segment = jnp.sum(passed.astype(jnp.int32), axis=1)
    start = jnp.sum(jnp.where(passed, picked[None, :], 0), axis=1)
    return segment, (place - start).astype(F32)


def rotation(position):
    half = HEAD_SIZE // 2
    frequency = rope_base ** (-(jnp.arange(half, dtype=F32) * (2.0 / HEAD_SIZE)))
    angles = position[:, None] * frequency[None, :]
    return jnp.cos(angles), jnp.sin(angles)


def rotate(rows, cosine, sine, back=False):
    t = rows.shape[0]
    heads = rows.reshape(t, -1, 2, HEAD_SIZE // 2)
    a, b = heads[:, :, 0], heads[:, :, 1]
    c, s = cosine[:, None, :], sine[:, None, :]
    if back:
        s = -s
    return jnp.stack([a * c - b * s, b * c + a * s], axis=2).reshape(t, -1)


def dot(a, b):
    return jnp.dot(a, b, preferred_element_type=F32)


def dot_nt(a, b):
    return jnp.einsum("tc,dc->td", a, b, preferred_element_type=F32)


def dot_tn(a, b):
    return jnp.einsum("td,tc->dc", a, b, preferred_element_type=F32)


def rms_factor(rows):
    return lax.rsqrt(jnp.mean(rows * rows, axis=-1, keepdims=True) + epsilon)


def norm_back(rows, factor, gain, grad):
    scaled = gain * grad
    return factor * scaled - rows * (factor * factor * factor) * jnp.mean(
        scaled * rows, axis=-1, keepdims=True
    )


def gather(x, axis):
    return lax.all_gather(x, axis, axis=0, tiled=True)


def scatter(x, axis):
    return lax.psum_scatter(x.astype(BF16), axis, scatter_dimension=0, tiled=True).astype(F32)


class Links:
    def __init__(self, send, recv, local, members):
        self.send, self.recv, self.local = send, recv, local
        self.remotes = self.locals = 0
        self.members = members
        self.d, self.z = lax.axis_index("dp"), lax.axis_index("expert")
        d = self.d
        core, x, y = d % 2, (d // 2) % 2, d // 4
        self.core = core
        self.sib = d + 1 - 2 * core
        self.x = d + 2 - 4 * x
        self.y = d + 4 - 8 * y
        self.diag = self.x + 4 - 8 * y
        self.waiting = []

    def other(self, d):
        return d + 1 - 2 * self.core

    def greet(self):
        barrier = pltpu.get_barrier_semaphore()
        last = self.members - 1

        def hello(d, z):
            pl.semaphore_signal(barrier, inc=1, device_id=(d, z), device_id_type=MESH)

        for d in (self.sib, self.x, self.y):
            hello(d, self.z)
        pl.when(self.z > 0)(lambda: hello(self.d, self.z - 1))
        pl.when(self.z < last)(lambda: hello(self.d, self.z + 1))
        ends = (self.z == 0).astype(jnp.int32) + (self.z == last).astype(jnp.int32)
        pl.semaphore_wait(barrier, 5 - ends)

    def remote(self, src, dst, to):
        k = self.remotes
        self.remotes += 1
        return pltpu.make_async_remote_copy(
            src_ref=src,
            dst_ref=dst,
            send_sem=self.send.at[k],
            recv_sem=self.recv.at[k],
            device_id=to,
            device_id_type=MESH,
        )

    def push(self, src, dst, d):
        copy = self.remote(src, dst, (d, self.z))
        copy.start()
        self.waiting.append(copy.wait_send)
        return copy

    def move(self, src, dst):
        k = self.locals
        self.locals += 1
        copy = pltpu.make_async_copy(src, dst, self.local.at[k])
        copy.start()
        return copy

    def finish(self):
        for wait in self.waiting:
            wait()


def run(order, **chains):
    for name in order:
        next(chains[name], None)
    chains = list(chains.values())
    while chains:
        for chain in list(chains):
            try:
                next(chain)
            except StopIteration:
                chains.remove(chain)


def line_gather(links, own, full):
    z, last = links.z, links.members - 1
    local = links.move(own, full.at[z])
    right, left = (links.d, z + 1), (links.d, z - 1)
    to_right, to_left = [], []
    for s in range(last):
        at_r, at_l = jnp.maximum(z - s, 0), jnp.minimum(z + s, last)
        to_right.append(links.remote(own if s == 0 else full.at[at_r], full.at[at_r], right))
        to_left.append(links.remote(own if s == 0 else full.at[at_l], full.at[at_l], left))
    for s in range(last):
        send_r, send_l = (z < last) & (z >= s), (z > 0) & (z + s <= last)
        pl.when(send_r)(to_right[s].start)
        pl.when(send_l)(to_left[s].start)
        yield
        pl.when((z > 0) & (z - 1 >= s))(to_right[s].wait_recv)
        pl.when((z < last) & (z + 1 + s <= last))(to_left[s].wait_recv)
    for s in range(last):
        send_r, send_l = (z < last) & (z >= s), (z > 0) & (z + s <= last)
        pl.when(send_r)(to_right[s].wait_send)
        pl.when(send_l)(to_left[s].wait_send)
    local.wait()


def add_rows(target, other, step=16):
    rows = target.shape[0]

    @pl.loop(0, rows // step)
    def _(i):
        at = pl.ds(pl.multiple_of(i * step, step), step)
        target[at] = (target[at].astype(F32) + other[at].astype(F32)).astype(target.dtype)


def line_sum(links, part, acc, from_left, from_right, finish, own=None, full=None, parts=2):
    z, last = links.z, links.members - 1
    rows = acc.shape[1] // parts
    spans = [pl.ds(h * rows, rows) for h in range(parts)]
    right, left = (links.d, z + 1), (links.d, z - 1)
    sum_r, sum_l, go_r, go_l, local = {}, {}, {}, {}, []
    for h, span in enumerate(spans):
        for o in range(last + 1):
            if o > 0:
                sum_r[h, o] = links.remote(acc.at[o, span], from_left.at[o, span], right)
            if o < last:
                sum_l[h, o] = links.remote(acc.at[o, span], from_right.at[o, span], left)
        for s in range(last if own is not None else 0):
            at_r, at_l = jnp.maximum(z - s, 0), jnp.minimum(z + s, last)
            here_r, here_l = full.at[at_r, span], full.at[at_l, span]
            go_r[h, s] = links.remote(own.at[span] if s == 0 else here_r, here_r, right)
            go_l[h, s] = links.remote(own.at[span] if s == 0 else here_l, here_l, left)

    def pass_right(h, o):
        @pl.when(z > 0)
        def _():
            sum_r[h, o].wait_recv()
            add_rows(acc.at[o, spans[h]], from_left.at[o, spans[h]])

        sum_r[h, o].start()

    def pass_left(h, o):
        @pl.when(z < last)
        def _():
            sum_l[h, o].wait_recv()
            add_rows(acc.at[o, spans[h]], from_right.at[o, spans[h]])

        sum_l[h, o].start()

    def send(h, s):
        pl.when((z < last) & (z >= s))(go_r[h, s].start)
        pl.when((z > 0) & (z + s <= last))(go_l[h, s].start)

    @pl.when(z == 0)
    def _():
        from_left[0] = jnp.zeros(from_left.shape[1:], from_left.dtype)

    @pl.when(z == last)
    def _():
        from_right[last] = jnp.zeros(from_right.shape[1:], from_right.dtype)

    made = set()
    for j in range(last):
        for o in (last - j, j):
            if o not in made:
                made.add(o)
                part(o)
        for h in range(parts):
            pl.when((z < last - j) & (2 * z < last))(functools.partial(pass_right, h, last - j))
            pl.when(z > j)(functools.partial(pass_left, h, j))
            pl.when((z < last - j) & (2 * z >= last))(functools.partial(pass_right, h, last - j))
            yield
    for h in range(parts):
        for o in range(last + 1):
            if o > 0:
                pl.when(z == o)(sum_r[h, o].wait_recv)
            if o < last:
                pl.when(z == o)(sum_l[h, o].wait_recv)
        finish(h * rows, rows)
        if own is None:
            continue
        send(h, 0)
        local.append(links.move(own.at[spans[h]], full.at[z, spans[h]]))
        yield
    for s in range(last if own is not None else 0):
        for h in range(parts):
            pl.when((z > 0) & (z - 1 >= s))(go_r[h, s].wait_recv)
            pl.when((z < last) & (z + 1 + s <= last))(go_l[h, s].wait_recv)
            if s + 1 < last:
                send(h, s + 1)
            yield
    for h in range(parts):
        for o in range(last + 1):
            if o > 0:
                pl.when(z < o)(sum_r[h, o].wait_send)
            if o < last:
                pl.when(z > o)(sum_l[h, o].wait_send)
        for s in range(last if own is not None else 0):
            pl.when((z < last) & (z >= s))(go_r[h, s].wait_send)
            pl.when((z > 0) & (z + s <= last))(go_l[h, s].wait_send)
    for copy in local:
        copy.wait()


def plane_gather(links, own, full):
    half = own.shape[0] // 2
    first, second = pl.ds(0, half), pl.ds(half, half)
    me = links.d
    local = links.move(own, full.at[me])
    by_x, by_y = {}, {}
    for by, d, h in ((by_y, links.y, first), (by_x, links.x, second), (by_x, links.x, first), (by_y, links.y, second)):
        by[h.start // half] = links.push(own.at[h], full.at[me, h], d)
    to_sib = [links.push(own, full.at[me], links.sib)]

    def share(d, h):
        to_sib.append(links.push(full.at[d, h], full.at[d, h], links.sib))

    yield
    by_y[0].wait_recv()
    over_x = links.push(full.at[links.y, first], full.at[links.y, first], links.x)
    share(links.y, first)
    by_x[1].wait_recv()
    over_y = links.push(full.at[links.x, second], full.at[links.x, second], links.y)
    share(links.x, second)
    yield
    by_x[0].wait_recv()
    share(links.x, first)
    by_y[1].wait_recv()
    share(links.y, second)
    yield
    over_x.wait_recv()
    share(links.diag, first)
    over_y.wait_recv()
    share(links.diag, second)
    yield
    for copy in to_sib:
        copy.wait_recv()
    local.wait()


def plane_scatter(links, part, mine, theirs, mid_x, mid_y, end_x, end_y):
    half = part.shape[1] // 2
    first, second = pl.ds(0, half), pl.ds(half, half)
    chips = (links.d, links.x, links.y, links.diag)
    from_sib, load = {}, {}
    held = [part.at[chip] if mine is None else mine.at[k] for k, chip in enumerate(chips)]
    for k in (3, 1, 2, 0):
        from_sib[k] = links.push(part.at[links.other(chips[k])], theirs.at[k], links.sib)
        if mine is not None:
            load[k] = links.move(part.at[chips[k]], held[k])
    yield
    for k in (3, 1, 2):
        if load:
            load[k].wait()
        from_sib[k].wait_recv()
        add_rows(held[k], theirs.at[k])
        if k == 3:
            to_mid_x = links.push(held[3].at[first], mid_x, links.x)
            to_mid_y = links.push(held[3].at[second], mid_y, links.y)
        if k == 1:
            to_end_x = links.push(held[1].at[first], end_x.at[first], links.x)
        if k == 2:
            to_end_y = links.push(held[2].at[second], end_y.at[second], links.y)
        if k != 1:
            yield
    to_mid_y.wait_recv()
    add_rows(held[1].at[second], mid_y)
    rest_x = links.push(held[1].at[second], end_x.at[second], links.x)
    to_mid_x.wait_recv()
    add_rows(held[2].at[first], mid_x)
    rest_y = links.push(held[2].at[first], end_y.at[first], links.y)
    yield
    if load:
        load[0].wait()
    from_sib[0].wait_recv()
    to_end_x.wait_recv()
    to_end_y.wait_recv()
    rest_x.wait_recv()
    rest_y.wait_recv()
    yield


def plane_scratch(rows, cols, mine=True):
    return [pltpu.VMEM((4, rows, cols), BF16)] * mine + [
        pltpu.VMEM((4, rows, cols), BF16),
        pltpu.VMEM((rows // 2, cols), BF16),
        pltpu.VMEM((rows // 2, cols), BF16),
        pltpu.VMEM((rows, cols), BF16),
        pltpu.VMEM((rows, cols), BF16),
    ]


def plane_result(mine, theirs, end_x, end_y, out, step=16):
    @pl.loop(0, out.shape[-2] // step)
    def _(i):
        at = pl.ds(pl.multiple_of(i * step, step), step)
        own = mine[at].astype(F32) + theirs[0, at].astype(F32)
        total = (own + end_x[at].astype(F32) + end_y[at].astype(F32)).astype(out.dtype)
        if len(out.shape) == 2:
            out[at] = total
        else:
            cols = out.shape[2]
            for e in range(out.shape[0]):
                out[e, at] = total[:, e * cols : (e + 1) * cols]


def line_result(z, acc, from_left, from_right, at):
    return (
        acc[z, at].astype(F32) + from_left[z, at].astype(F32) + from_right[z, at].astype(F32)
    )


ANY = pl.BlockSpec(memory_space=pl.ANY)
VMEM = pl.BlockSpec(memory_space=pltpu.VMEM)


def comm_call(kernel, name, number, members, remotes, locals_, in_specs, out_specs, out_shape, scratch):
    return pl.pallas_call(
        functools.partial(kernel, members),
        out_shape=out_shape,
        in_specs=in_specs,
        out_specs=out_specs,
        scratch_shapes=[
            pltpu.SemaphoreType.DMA((remotes,)),
            pltpu.SemaphoreType.DMA((remotes,)),
            pltpu.SemaphoreType.DMA((locals_,)),
            *scratch,
        ],
        compiler_params=pltpu.CompilerParams(
            collective_id=number, has_side_effects=True, vmem_limit_bytes=VMEM_LIMIT
        ),
        name=name,
    )


def sds(shape, dtype):
    return jax.ShapeDtypeStruct(shape, dtype)


def third_kernel(members, part, mixture, residual, cot, gain, gate, up, output, grad_residual, gain_part, out_all, gate_out, up_out, send, recv, local, acc, from_left, from_right, acc_m, left_m, right_m, grad_out, *rest):
    links = Links(send, recv, local, members)
    links.greet()
    for_gate, for_up = rest[:6], rest[6:]

    def finish(first, count):
        @pl.loop(0, count // 16)
        def _(i):
            at = pl.ds(pl.multiple_of(first + i * 16, 16), 16)
            grad = line_result(links.z, acc, from_left, from_right, at)
            here = residual[at]
            factor = rms_factor(here)
            gain_part[...] += jnp.sum(grad * here * factor, axis=0, keepdims=True)
            total = cot[at].astype(F32) + norm_back(here, factor, gain[1:2], grad)
            grad_residual[at] = total
            grad_out[at] = (branch_scale * total).astype(BF16)

    def chain():
        links.move(part, acc).wait()
        gain_part[...] = jnp.zeros(gain_part.shape, F32)
        yield from line_sum(
            links, lambda o: None, acc, from_left, from_right, finish, grad_out, out_all
        )

    def finish_mixture(first, count):
        @pl.loop(0, count // 16)
        def _(i):
            at = pl.ds(pl.multiple_of(first + i * 16, 16), 16)
            here = residual[at] + branch_scale * line_result(links.z, acc_m, left_m, right_m, at)
            output[at] = here.astype(BF16)

    def mixture_chain():
        links.move(mixture, acc_m).wait()
        yield from line_sum(links, lambda o: None, acc_m, left_m, right_m, finish_mixture)

    run(
        THIRD_ORDER,
        m=mixture_chain(),
        z=chain(),
        g=plane_scatter(links, gate, *for_gate),
        u=plane_scatter(links, up, *for_up),
    )
    plane_result(for_gate[0].at[0], for_gate[1], for_gate[4], for_gate[5], gate_out)
    plane_result(for_up[0].at[0], for_up[1], for_up[4], for_up[5], up_out)
    links.finish()


THIRD_ORDER = "uzuzzgugmmzzguzzzgzmzmzmmzmugguuzm"


def third_phase(members, own_experts, part, mixture, residual, cot, gain, gate, up):
    rows, width = cot.shape
    blocks = pltpu.VMEM((members, rows, width), BF16)
    return comm_call(
        third_kernel, "phase_three", 3, members, 80, 16,
        [ANY, ANY, VMEM, VMEM, VMEM, ANY, ANY], [VMEM, VMEM, VMEM, ANY, VMEM, VMEM],
        [
            sds((rows, width), BF16),
            sds((rows, width), F32),
            sds((1, width), F32),
            sds((members, rows, width), BF16),
            sds((own_experts, gate.shape[1], gate.shape[2] // own_experts), F32),
            sds((own_experts, up.shape[1], up.shape[2] // own_experts), F32),
        ],
        [blocks] * 6
        + [pltpu.VMEM((rows, width), BF16)]
        + plane_scratch(*gate.shape[1:])
        + plane_scratch(*up.shape[1:]),
    )(part, mixture, residual, cot, gain, gate, up)


def lane_ids(rows):
    return lax.broadcasted_iota(jnp.int32, (rows, LANES), 1)


def dims(a, b):
    return (((a,), (b,)), ((), ()))


def mm(a, b):
    return lax.dot_general(a, b, dims(1, 0), preferred_element_type=F32)


def mm_nt(a, b):
    return lax.dot_general(a, b, dims(1, 1), preferred_element_type=F32)


def mm_tn(a, b):
    return lax.dot_general(a, b, dims(0, 0), preferred_element_type=F32)


def first_lanes():
    same = lax.broadcasted_iota(jnp.int32, (16, LANES), 0) == lax.broadcasted_iota(jnp.int32, (16, LANES), 1)
    return same.astype(BF16)


def expert_kernel(capacity, own_experts, route, normed, cot, w_gate, w_up, w_down, mixture, grad_normed, d_gate, d_up, d_down, mix_sum, grad_sum, slot_cols, weight_cols, slot_rows):
    e = pl.program_id(0)
    span = normed.shape[0]

    @pl.when(e == 0)
    def _():
        mix_sum[...] = jnp.zeros(mix_sum.shape, F32)
        grad_sum[...] = jnp.zeros(grad_sum.shape, F32)
        lane = lane_ids(LANES)
        name = (lax.axis_index("expert") * own_experts + lane).astype(F32)
        name = jnp.where(lane < own_experts, name, -1.0)
        upto = (lane <= lax.broadcasted_iota(jnp.int32, (LANES, LANES), 0)).astype(BF16)
        before = jnp.zeros((1, LANES), F32)
        for b in range(span // LANES):
            at = pl.ds(b * LANES, LANES)
            chosen, weight = jnp.zeros((LANES, LANES), F32), jnp.zeros((LANES, LANES), F32)
            for k in range(TOP):
                named = route[at, k : k + 1] == name
                chosen = jnp.where(named, 1.0, chosen)
                weight = jnp.where(named, route[at, TOP + k : TOP + k + 1], weight)
            slot = mm(upto, chosen.astype(BF16)) + (before - 1.0)
            slot_cols[at] = jnp.where((chosen > 0.0) & (slot < capacity), slot, -1.0)
            weight_cols[at] = weight
            before = before + jnp.sum(chosen, axis=0, keepdims=True)
        slot_rows[...] = mm_nt(first_lanes(), slot_cols[...].astype(BF16))

    def column(values):
        return jnp.sum(jnp.where(lane_ids(span) == e, values[...], 0.0), axis=1, keepdims=True)

    slots = lax.broadcasted_iota(jnp.int32, (capacity, span), 0).astype(F32)
    pick = (slot_rows[pl.ds(e, 1)] == slots).astype(BF16)
    puts = column(slot_cols) == lax.broadcasted_iota(jnp.int32, (span, capacity), 1).astype(F32)
    put = puts.astype(BF16)
    gate_row = jnp.sum(jnp.where(puts, column(weight_cols), 0.0), axis=0, keepdims=True)
    same = lax.broadcasted_iota(jnp.int32, (capacity, capacity), 0) == lax.broadcasted_iota(jnp.int32, (capacity, capacity), 1)
    gate_col = jnp.sum(jnp.where(same, gate_row, 0.0), axis=1, keepdims=True)
    received = mm(pick, normed[...]).astype(BF16)
    pre_gate, pre_up = mm(received, w_gate[...]), mm(received, w_up[...])
    sig = 1.0 / (1.0 + jnp.exp(-pre_gate))
    silu = pre_gate * sig
    activ = (silu * pre_up).astype(BF16)
    produced = (gate_col * mm_nt(activ, w_down[...])).astype(BF16)
    mix_sum[...] += mm(put, produced)
    grad_out = (gate_col * (branch_scale * mm(pick, cot[...]))).astype(BF16)
    grad_activ = mm(grad_out, w_down[...])
    grad_gate = (grad_activ * pre_up * (sig * (1.0 + pre_gate * (1.0 - sig)))).astype(BF16)
    grad_up = (grad_activ * silu).astype(BF16)
    grad_pair = (mm_nt(grad_gate, w_gate[...]) + mm_nt(grad_up, w_up[...])).astype(BF16)
    grad_sum[...] += mm(put, grad_pair)
    d_gate[...] = mm_tn(received, grad_gate).astype(BF16)
    d_up[...] = mm_tn(received, grad_up).astype(BF16)
    d_down[...] = mm_tn(grad_out, activ).astype(BF16)

    @pl.when(e == pl.num_programs(0) - 1)
    def _():
        mixture[...] = mix_sum[...].astype(BF16)
        grad_normed[...] = grad_sum[...].astype(BF16)


def experts(own_experts, capacity, route, normed, cot, w_gate, w_up, w_down):
    span, width = normed.shape
    ff = w_gate.shape[1] // own_experts
    whole = pl.BlockSpec((span, width), lambda e: (0, 0))
    column = pl.BlockSpec((width, ff), lambda e: (0, e))
    grads = jax.ShapeDtypeStruct(w_gate.shape, BF16)
    rows = jax.ShapeDtypeStruct((span, width), BF16)
    return pl.pallas_call(
        functools.partial(expert_kernel, capacity, own_experts),
        grid=(own_experts,),
        in_specs=[pl.BlockSpec(route.shape, lambda e: (0, 0)), whole, whole, column, column, column],
        out_specs=[whole, whole, column, column, column],
        out_shape=[rows, rows, grads, grads, grads],
        scratch_shapes=[
            pltpu.VMEM((span, width), F32),
            pltpu.VMEM((span, width), F32),
            pltpu.VMEM((span, LANES), F32),
            pltpu.VMEM((span, LANES), F32),
            pltpu.VMEM((16, span), F32),
        ],
        compiler_params=pltpu.CompilerParams(vmem_limit_bytes=VMEM_LIMIT),
        name="experts",
    )(route, normed, cot, w_gate, w_up, w_down)


def turn(x, cosine, sine):
    half = HEAD_SIZE // 2
    ahead, behind = pltpu.roll(x, LANES - half, axis=1), pltpu.roll(x, half, axis=1)
    partner = jnp.where(lane_ids(x.shape[0]) % HEAD_SIZE < half, ahead, behind)
    return x * cosine + partner * sine


def spread(block, at, out):
    low = lane_ids(block.shape[0]) < HEAD_SIZE
    other = pltpu.roll(block, HEAD_SIZE, axis=1)
    zero = jnp.zeros_like(block)
    out[0, 0, at] = jnp.where(low, block, zero).astype(BF16)
    out[0, 1, at] = jnp.where(low, zero, other).astype(BF16)
    out[1, 0, at] = jnp.where(low, other, zero).astype(BF16)
    out[1, 1, at] = jnp.where(low, zero, block).astype(BF16)


def attention_setup(segment, bias):
    span = bias.shape[0]
    same = lax.broadcasted_iota(jnp.int32, (LANES, LANES), 0) == lane_ids(LANES)
    for b in range(span // LANES):
        at = pl.ds(b * LANES, LANES)
        row = b * LANES + lax.broadcasted_iota(jnp.int32, (LANES, span), 0)
        col = lax.broadcasted_iota(jnp.int32, (LANES, span), 1)
        here = segment[:, b * LANES : (b + 1) * LANES]
        here = jnp.sum(jnp.where(same, here, 0.0), axis=1, keepdims=True)
        ok = (here == segment[...]) & (col <= row)
        bias[at] = jnp.where(ok, 0.0, -1e30)


def weight_columns(pack_all, first, cols):
    return pack_all[:, :, first : first + cols].reshape(-1, cols)


def gain_rows(pack_all, first):
    return mm_nt(first_lanes(), weight_columns(pack_all, first, LANES))


def attend_steps(qkv, kx, vx, bias, probs, attended):
    span, blocks = qkv.shape[0], attended.shape[1] // LANES
    repeat = QUERY_HEADS // KEY_VALUE_HEADS
    for j in range(blocks):
        for b in range(span // LANES):
            at, keys = pl.ds(b * LANES, LANES), (b + 1) * LANES
            q = qkv[at, j * LANES : (j + 1) * LANES]
            total = jnp.zeros((LANES, LANES), F32)
            for half in range(2):
                h = 2 * j + half
                kv = h // repeat
                scores = mm_nt(q, kx[kv, half, :keys]) + bias[at, :keys]
                peak = jnp.max(scores, axis=1, keepdims=True)
                exponent = jnp.exp(scores - peak)
                share = 1.0 / jnp.sum(exponent, axis=1, keepdims=True)
                low = (exponent * share).astype(BF16)
                probs[h, at, :keys] = low
                total += mm(low, vx[kv, half, :keys])
            attended[at, j * LANES : (j + 1) * LANES] = total.astype(BF16)
        yield


def forward_kernel(
    members, tokens, cot, route, w_query, w_key, w_value, w_out, gain_attn, gain_ffn, gate, up, down, segment, cosine, sine,
    cot_all, route_all, pack_all, gate_all, up_all, down_all, normed_attn, qkv, kx, vx, probs, attended, residual, normed_all, gains,
    send, recv, local, pack, tokens_all, bias, acc, from_left, from_right, normed,
):
    links = Links(send, recv, local, members)
    links.greet()
    rows, width = tokens.shape
    span = rows * members
    q_cols = attended.shape[1]
    qkv_cols = qkv.shape[1]

    def pack_chain():
        loads, at = [], 0
        for weight in (w_query, w_key, w_value, w_out):
            cols = weight.shape[1] // members
            mine = pl.ds(pl.multiple_of(links.z * cols, LANES), cols)
            loads.append(links.move(weight.at[:, mine], pack.at[:, at : at + cols]))
            at += cols
        which = lax.broadcasted_iota(jnp.int32, (16, pack.shape[0]), 0)
        both = jnp.where(which == 0, gain_attn[...].astype(F32), jnp.where(which == 1, gain_ffn[...].astype(F32), 0.0))
        pack[:, at:] = mm_tn(both.astype(BF16), first_lanes()).astype(BF16)
        for load in loads:
            load.wait()
        yield from plane_gather(links, pack, pack_all)

    def produce(o):
        acc[o] = mm_nt(attended[o * rows : (o + 1) * rows], weight_columns(pack_all, qkv_cols, q_cols)).astype(BF16)

    def chain():
        attention_setup(segment, bias)
        yield
        gains[...] = gain_rows(pack_all, qkv_cols + q_cols)

        @pl.loop(0, span // 16)
        def _(i):
            here = tokens_all[i // (rows // 16), pl.ds(pl.multiple_of(i % (rows // 16) * 16, 16), 16)].astype(F32)
            normed_attn[pl.ds(pl.multiple_of(i * 16, 16), 16)] = (here * rms_factor(here) * gains[0:1]).astype(BF16)

        @pl.loop(0, span // LANES)
        def _(i):
            at = pl.ds(pl.multiple_of(i * LANES, LANES), LANES)
            here = mm(normed_attn[at], weight_columns(pack_all, 0, qkv_cols))
            c, s = cosine[at], sine[at]
            for j in range(q_cols // LANES):
                lanes = slice(j * LANES, (j + 1) * LANES)
                qkv[at, lanes] = (turn(here[:, lanes], c, s).astype(BF16).astype(F32) * score_scale).astype(BF16)
            key = turn(here[:, q_cols : q_cols + LANES], c, s)
            value = here[:, q_cols + LANES :]
            qkv[at, q_cols : q_cols + LANES] = key.astype(BF16)
            qkv[at, q_cols + LANES :] = value.astype(BF16)
            spread(key, at, kx)
            spread(value, at, vx)

        yield
        yield from attend_steps(qkv, kx, vx, bias, probs, attended)

        def finish(first, count):
            @pl.loop(0, count // 16)
            def _(i):
                at = pl.ds(pl.multiple_of(first + i * 16, 16), 16)
                here = tokens[at].astype(F32) + branch_scale * line_result(links.z, acc, from_left, from_right, at)
                residual[at] = here
                normed[at] = (here * rms_factor(here) * gains[1:2]).astype(BF16)

        yield from line_sum(links, produce, acc, from_left, from_right, finish, normed, normed_all)

    run(
        FORWARD_ORDER,
        t=line_gather(links, tokens, tokens_all),
        r=line_gather(links, route, route_all),
        c=line_gather(links, cot, cot_all),
        p=pack_chain(),
        g=plane_gather(links, gate, gate_all),
        u=plane_gather(links, up, up_all),
        d=plane_gather(links, down, down_all),
        a=chain(),
    )
    links.finish()


FORWARD_ORDER = "tptpdptpcaptgaaacdtrgatcaardaagdattpuparparadrpaarrd"


def forward_phase(members, tokens, cot, route, w_query, w_key, w_value, w_out, gain_attn, gain_ffn, gate, up, down, segment, cosine, sine):
    rows, width = tokens.shape
    q_cols = w_query.shape[1] // members
    qkv_cols = q_cols + 2 * w_key.shape[1] // members
    pack = (w_query.shape[0], qkv_cols + q_cols + LANES)
    span = rows * members
    blocks = pltpu.VMEM((members, rows, width), BF16)
    heads = q_cols // HEAD_SIZE
    return comm_call(
        forward_kernel, "forward", 1, members, 120, 16,
        [VMEM, ANY, ANY, ANY, ANY, ANY, ANY, VMEM, VMEM, ANY, ANY, ANY, VMEM, VMEM, VMEM],
        [ANY, ANY, VMEM, ANY, ANY, ANY, VMEM, VMEM, VMEM, VMEM, VMEM, VMEM, VMEM, ANY, VMEM],
        [
            sds((members, rows, width), BF16),
            sds((members, *route.shape), F32),
            sds((8, *pack), BF16),
            sds((8, *gate.shape), BF16),
            sds((8, *up.shape), BF16),
            sds((8, *down.shape), BF16),
            sds((span, width), BF16),
            sds((span, qkv_cols), BF16),
            sds((2, 2, span, LANES), BF16),
            sds((2, 2, span, LANES), BF16),
            sds((heads, span, span), BF16),
            sds((span, q_cols), BF16),
            sds((rows, width), F32),
            sds((members, rows, width), BF16),
            sds((16, width), F32),
        ],
        [
            pltpu.VMEM(pack, BF16),
            blocks,
            pltpu.VMEM((span, span), F32),
            blocks,
            blocks,
            blocks,
            pltpu.VMEM((rows, width), BF16),
        ],
    )(tokens, cot, route, w_query, w_key, w_value, w_out, gain_attn, gain_ffn, gate, up, down, segment, cosine, sine)


def attend_back_steps(qkv, kx, vx, probs, grad_attended, cosine, sine, grad_k, grad_v, grad_qkv):
    span = qkv.shape[0]
    blocks = grad_attended.shape[1] // LANES
    repeat = QUERY_HEADS // KEY_VALUE_HEADS
    grad_k[...] = jnp.zeros(grad_k.shape, F32)
    grad_v[...] = jnp.zeros(grad_v.shape, F32)
    for j in range(blocks):
        lanes = slice(j * LANES, (j + 1) * LANES)
        for b in range(span // LANES):
            at, keys = pl.ds(b * LANES, LANES), (b + 1) * LANES
            q, grad = qkv[at, lanes], grad_attended[at, lanes]
            total = jnp.zeros((LANES, LANES), F32)
            for half in range(2):
                h = 2 * j + half
                kv = h // repeat
                low = probs[h, at, :keys]
                share = low.astype(F32)
                grad_probs = mm_nt(grad, vx[kv, half, :keys])
                inner = jnp.sum(share * grad_probs, axis=1, keepdims=True)
                grad_scores = (share * (grad_probs - inner)).astype(BF16)
                total += mm(grad_scores, kx[kv, half, :keys])
                grad_k[kv, half, :keys] += mm_tn(grad_scores, q)
                grad_v[kv, half, :keys] += mm_tn(low, grad)
            grad_qkv[at, lanes] = turn(total * score_scale, cosine[at], -sine[at]).astype(BF16)
        yield
    first = blocks * LANES

    def fold(parts, at):
        low = lane_ids(LANES) < HEAD_SIZE
        same = jnp.where(low, parts[0, 0, at], parts[1, 1, at])
        crossed = jnp.where(low, parts[1, 0, at], parts[0, 1, at])
        return same + pltpu.roll(crossed, HEAD_SIZE, axis=1)

    for b in range(span // LANES):
        at = pl.ds(b * LANES, LANES)
        grad_qkv[at, first : first + LANES] = turn(fold(grad_k, at), cosine[at], -sine[at]).astype(BF16)
        grad_qkv[at, first + LANES :] = fold(grad_v, at).astype(BF16)


def backward_kernel(
    members, grad_out_all, grad_residual, gain_ffn_part, tokens, down, row_gains, pack_all, normed_attn, qkv, kx, vx, probs, attended, cosine, sine,
    grad_tokens, gains, d_query, d_key, d_value, d_out, d_down,
    send, recv, local, acc, from_left, from_right, grad_attended, grad_k, grad_v, grad_qkv, gain_part,
    for_w_out, for_w_query, for_rest, own_out, own_query, own_rest, all_out, all_query, all_rest, *rest,
):
    links = Links(send, recv, local, members)
    links.greet()
    rows, width = tokens.shape
    q_cols, qkv_cols = attended.shape[1], qkv.shape[1]
    kv_cols = (qkv_cols - q_cols) // 2
    with_out, with_query, with_rest, with_down = rest[:5], rest[5:10], rest[10:15], rest[15:]
    pairs = for_w_out.shape[0] // 2
    step = width // pairs

    def weight_term(rows_of, grads, out, cols):
        for i in range(pairs):
            term = mm_tn(rows_of[:, i * step : (i + 1) * step], grads)
            out[2 * i : 2 * i + 2, :, :cols] = term.astype(BF16).reshape(2, step // 2, cols)

    def weight_chain(fill, part, mine, full, scratch):
        fill()
        yield from plane_scatter(links, part, None, *scratch)
        plane_result(part.at[links.d], scratch[0], scratch[3], scratch[4], mine)
        yield from line_gather(links, mine, full)

    def fill_out():
        weight_term(grad_out_all, attended[...], for_w_out, q_cols)

    def fill_query():
        weight_term(normed_attn, grad_qkv[:, :q_cols], for_w_query, q_cols)

    def fill_rest():
        weight_term(normed_attn, grad_qkv[:, q_cols:], for_rest, 2 * kv_cols)
        which = lax.broadcasted_iota(jnp.int32, (16, width), 0)
        both = jnp.where(which == 0, gain_part[...] / row_gains[0:1], jnp.where(which == 1, gain_ffn_part[...], 0.0))
        columns = mm_tn(both.astype(BF16), first_lanes())
        for_rest[:, :, 2 * kv_cols :] = columns.astype(BF16).reshape(2 * pairs, step // 2, LANES)

    def produce(o):
        at = slice(o * rows, (o + 1) * rows)
        part = mm_nt(grad_qkv[at], weight_columns(pack_all, 0, qkv_cols))
        gain_part[...] += jnp.sum(part * normed_attn[at].astype(F32), axis=0, keepdims=True)
        acc[o] = part.astype(BF16)

    def chain():
        wo = weight_columns(pack_all, qkv_cols, q_cols)

        @pl.loop(0, grad_attended.shape[0] // LANES)
        def _(i):
            at = pl.ds(pl.multiple_of(i * LANES, LANES), LANES)
            grad_attended[at] = mm(grad_out_all[at], wo).astype(BF16)

        yield
        yield from attend_back_steps(qkv, kx, vx, probs, grad_attended, cosine, sine, grad_k, grad_v, grad_qkv)
        gain_part[...] = jnp.zeros(gain_part.shape, F32)
        yield

        def finish(first, count):
            @pl.loop(0, count // 16)
            def _(i):
                at = pl.ds(pl.multiple_of(first + i * 16, 16), 16)
                grad = line_result(links.z, acc, from_left, from_right, at)
                here = tokens[at].astype(F32)
                grad_tokens[at] = grad_residual[at] + norm_back(here, rms_factor(here), row_gains[0:1], grad)

        yield from line_sum(links, produce, acc, from_left, from_right, finish)

    run(
        BACKWARD_ORDER,
        d=plane_scatter(links, down, *with_down),
        o=weight_chain(fill_out, for_w_out, own_out, all_out, with_out),
        a=chain(),
        q=weight_chain(fill_query, for_w_query, own_query, all_query, with_query),
        r=weight_chain(fill_rest, for_rest, own_rest, all_rest, with_rest),
    )
    plane_result(with_down[0].at[0], with_down[1], with_down[4], with_down[5], d_down)
    for m in range(members):
        d_out[:, m * q_cols : (m + 1) * q_cols] = all_out[m].astype(F32)
        d_query[:, m * q_cols : (m + 1) * q_cols] = all_query[m].astype(F32)
        d_key[:, m * kv_cols : (m + 1) * kv_cols] = all_rest[m, :, :kv_cols].astype(F32)
        d_value[:, m * kv_cols : (m + 1) * kv_cols] = all_rest[m, :, kv_cols : 2 * kv_cols].astype(F32)
    gains[...] = sum(all_rest[m, :, 2 * kv_cols :].astype(F32) for m in range(members))
    links.finish()


BACKWARD_ORDER = "oadoaoaoaooqaqqdoaqdaqqarorarradrraqrqdaoodaaqdrddrr"


def backward_phase(members, own_experts, grad_out_all, grad_residual, gain_ffn_part, tokens, down, row_gains, pack_all, normed_attn, qkv, kx, vx, probs, attended, cosine, sine):
    rows, width = tokens.shape
    span, q_cols = attended.shape
    qkv_cols = qkv.shape[1]
    kv_cols = (qkv_cols - q_cols) // 2
    devices, own = down.shape[:2]
    line = [pltpu.VMEM((members, rows, width), BF16)] * 3
    three = (q_cols, q_cols, 2 * kv_cols + LANES)
    return comm_call(
        backward_kernel, "backward", 4, members, 100, 32,
        [VMEM, VMEM, VMEM, VMEM, ANY] + [VMEM] * 10,
        [VMEM] * 7,
        [
            sds((rows, width), F32),
            sds((own, LANES), F32),
            sds((own, members * q_cols), F32),
            sds((own, members * kv_cols), F32),
            sds((own, members * kv_cols), F32),
            sds((own, members * q_cols), F32),
            sds((own_experts, own, down.shape[2] // own_experts), F32),
        ],
        [
            *line,
            pltpu.VMEM((span, q_cols), BF16),
            pltpu.VMEM((2, 2, span, LANES), F32),
            pltpu.VMEM((2, 2, span, LANES), F32),
            pltpu.VMEM((span, qkv_cols), BF16),
            pltpu.VMEM((1, width), F32),
            *[pltpu.VMEM((devices, own, cols), BF16) for cols in three],
            *[pltpu.VMEM((own, cols), BF16) for cols in three],
            *[pltpu.VMEM((members, own, cols), BF16) for cols in three],
            *[one for cols in three for one in plane_scratch(own, cols, False)],
            *plane_scratch(*down.shape[1:]),
        ],
    )(grad_out_all, grad_residual, gain_ffn_part, tokens, down, row_gains, pack_all, normed_attn, qkv, kx, vx, probs, attended, cosine, sine)


def all_blocks(x, axis):
    return lax.all_gather(x, axis, axis=0)


def plain_first(members, tokens, cot, route, pack, gate):
    return (
        all_blocks(tokens, "expert"),
        all_blocks(cot, "expert"),
        all_blocks(route, "expert"),
        all_blocks(pack, "dp"),
        all_blocks(gate, "dp"),
    )


def line_total(part):
    return scatter(part.reshape(-1, part.shape[2]), "expert")


def plain_second(members, part, tokens, gain, up, down):
    residual = tokens.astype(F32) + branch_scale * line_total(part)
    normed = (residual * rms_factor(residual) * gain).astype(BF16)
    return residual, all_blocks(normed, "expert"), all_blocks(up, "dp"), all_blocks(down, "dp")


def plane_sum(part):
    return scatter(part.reshape(-1, part.shape[2]), "dp")


def plain_third(members, part, residual, cot, gain, gate, up):
    grad = line_total(part)
    factor = rms_factor(residual)
    gain_part = jnp.sum(grad * residual * factor, axis=0, keepdims=True)
    total = cot.astype(F32) + norm_back(residual, factor, gain, grad)
    out_all = all_blocks((branch_scale * total).astype(BF16), "expert")
    return total, gain_part, out_all, plane_sum(gate), plane_sum(up)


def plain_fourth(members, part, grad_residual, tokens, gain, pack, down):
    here = tokens.astype(F32)
    grad_tokens = grad_residual + norm_back(here, rms_factor(here), gain, line_total(part))
    return grad_tokens, all_blocks(plane_sum(pack).astype(BF16), "expert"), plane_sum(down)


def attend_forward(q, k, v, allowed):
    scores = jnp.einsum("irh,jh->rij", q, k, preferred_element_type=F32) * score_scale
    scores = jnp.where(allowed[None], scores, -1e30)
    peak = jnp.max(scores, axis=-1, keepdims=True)
    exponent = jnp.exp(scores - peak)
    total = jnp.sum(exponent, axis=-1, keepdims=True)
    probs = exponent / total
    return jnp.einsum("rij,jh->irh", probs.astype(BF16), v, preferred_element_type=F32), probs


def attend_backward(q, k, v, probs, grad, allowed):
    grad_probs = jnp.einsum("irh,jh->rij", grad, v, preferred_element_type=F32)
    inner = jnp.sum(probs * grad_probs, axis=-1, keepdims=True)
    grad_scores = (probs * (grad_probs - inner)).astype(BF16)
    grad_q = jnp.einsum("rij,jh->irh", grad_scores, k, preferred_element_type=F32) * score_scale
    grad_k = jnp.einsum("rij,irh->jh", grad_scores, q, preferred_element_type=F32) * score_scale
    grad_v = jnp.einsum("rij,irh->jh", probs.astype(BF16), grad, preferred_element_type=F32)
    return grad_q, grad_k, grad_v


def shards_plain(
    tokens,
    cotangent,
    gain_attn,
    gain_ffn,
    w_query,
    key_weight,
    value_weight,
    w_out,
    expert_gate,
    expert_up,
    expert_down,
    expert_ids,
    gates,
    lengths,
    order,
):
    rows, width = tokens.shape
    members = lax.axis_size("expert")
    member = lax.axis_index("expert")
    span = rows * members
    own_experts, ff = expert_gate.shape[1], expert_gate.shape[2]
    capacity = rows * TOP // own_experts
    q_cols = w_query.shape[1] // members
    kv_cols = key_weight.shape[1] // members
    kv_heads = kv_cols // HEAD_SIZE
    repeat = QUERY_HEADS // KEY_VALUE_HEADS

    def mine(weight, cols):
        return lax.dynamic_slice_in_dim(weight, member * cols, cols, axis=1)

    devices = lax.axis_size("dp")
    phases = [
        functools.partial(phase, members)
        for phase in (plain_first, plain_second, plain_third, plain_fourth)
    ]

    pack = jnp.concatenate(
        [
            mine(w_query, q_cols),
            mine(key_weight, kv_cols),
            mine(value_weight, kv_cols),
            mine(w_out, q_cols),
            gain_attn[:, None],
            gain_ffn[:, None],
            jnp.zeros((gain_attn.shape[0], 126), BF16),
        ],
        axis=1,
    )
    route = jnp.concatenate([expert_ids.astype(F32), gates], axis=1)
    tokens_all, cot_all, route_all, pack_all, gate_all = phases[0](
        tokens, cotangent, route, pack, expert_gate.reshape(-1, own_experts * ff)
    )
    tokens_all = tokens_all.reshape(span, width).astype(F32)
    cot_all = cot_all.reshape(span, width)
    route_all = route_all.reshape(span, 2 * TOP)
    pack_all = pack_all.reshape(width, -1)
    gate_all = gate_all.reshape(width, -1)
    qkv_cols = q_cols + 2 * kv_cols
    w_qkv = pack_all[:, :qkv_cols]
    wo = pack_all[:, qkv_cols : qkv_cols + q_cols]
    gain_one = pack_all[:, qkv_cols + q_cols].astype(F32)[None]
    gain_two = pack_all[:, qkv_cols + q_cols + 1].astype(F32)[None]

    segment, position = layout(lengths[0], order[0], span)
    cosine, sine = rotation(position)
    place = jnp.arange(span, dtype=jnp.int32)
    allowed = (segment[:, None] == segment[None, :]) & (place[None, :] <= place[:, None])
    factor_one = rms_factor(tokens_all)
    normed_attn = (tokens_all * factor_one * gain_one).astype(BF16)
    qkv = dot(normed_attn, w_qkv)
    qk = rotate(qkv[:, : q_cols + kv_cols], cosine, sine).astype(BF16)
    v = qkv[:, q_cols + kv_cols :].astype(BF16)
    q_heads = jnp.moveaxis(qk[:, :q_cols].reshape(span, kv_heads, repeat, HEAD_SIZE), 1, 0)
    k_heads = jnp.moveaxis(qk[:, q_cols:].reshape(span, kv_heads, HEAD_SIZE), 1, 0)
    v_heads = jnp.moveaxis(v.reshape(span, kv_heads, HEAD_SIZE), 1, 0)
    attended, probs = jax.vmap(functools.partial(attend_forward, allowed=allowed))(
        q_heads, k_heads, v_heads
    )
    attended = jnp.moveaxis(attended, 0, 1).reshape(span, q_cols).astype(BF16)
    attn_part = dot_nt(attended, wo).astype(BF16).reshape(members, rows, width)
    residual, normed_all, up_all, down_all = phases[1](
        attn_part,
        tokens,
        gain_two,
        expert_up.reshape(-1, own_experts * ff),
        expert_down.reshape(-1, own_experts * ff),
    )
    normed_all = normed_all.reshape(span, width)
    up_all, down_all = up_all.reshape(width, -1), down_all.reshape(width, -1)

    mixture, grad_normed, *by_kind = experts(
        own_experts, capacity, route_all, normed_all, cot_all, gate_all, up_all, down_all
    )
    output = (residual + branch_scale * scatter(mixture, "expert")).astype(BF16)
    by_kind = [one.reshape(devices, -1, own_experts * ff) for one in by_kind]

    grad_residual, gain_two_part, grad_attn_out, sum_gate, sum_up = phases[2](
        grad_normed.reshape(members, rows, width),
        residual,
        cotangent,
        gain_two,
        by_kind[0],
        by_kind[1],
    )
    grad_attn_out = grad_attn_out.reshape(span, width)
    term_out = dot_tn(grad_attn_out, attended)
    grad_attended = dot(grad_attn_out, wo).astype(BF16)
    grad_heads = jnp.moveaxis(grad_attended.reshape(span, kv_heads, repeat, HEAD_SIZE), 1, 0)
    grad_q, grad_k, grad_v = jax.vmap(functools.partial(attend_backward, allowed=allowed))(
        q_heads, k_heads, v_heads, probs, grad_heads
    )
    grad_qk = jnp.concatenate(
        [
            jnp.moveaxis(grad_q, 0, 1).reshape(span, q_cols),
            jnp.moveaxis(grad_k, 0, 1).reshape(span, kv_cols),
        ],
        axis=1,
    )
    grad_qkv = jnp.concatenate(
        [
            rotate(grad_qk, cosine, sine, back=True).astype(BF16),
            jnp.moveaxis(grad_v, 0, 1).reshape(span, kv_cols).astype(BF16),
        ],
        axis=1,
    )
    grad_norm_part = dot_nt(grad_qkv, w_qkv)
    gain_one_part = jnp.sum(grad_norm_part * tokens_all * factor_one, axis=0)
    term_qkv = dot_tn(normed_attn, grad_qkv)
    packed_grads = jnp.concatenate(
        [
            term_qkv,
            term_out,
            gain_one_part[:, None],
            gain_two_part.reshape(-1, 1),
            jnp.zeros((width, 126), F32),
        ],
        axis=1,
    )
    grad_tokens, per_member, sum_down = phases[3](
        grad_norm_part.astype(BF16).reshape(members, rows, width),
        grad_residual,
        tokens,
        gain_one,
        packed_grads.astype(BF16).reshape(devices, -1, packed_grads.shape[1]),
        by_kind[2],
    )
    per_member = per_member.astype(F32)

    def columns(first, cols):
        part = per_member[:, :, first : first + cols]
        return jnp.moveaxis(part, 0, 1).reshape(part.shape[1], -1)

    gains = jnp.sum(per_member[:, :, qkv_cols + q_cols :], axis=0)
    return (
        output,
        grad_tokens,
        gains[:, 0],
        gains[:, 1],
        columns(0, q_cols),
        columns(q_cols, kv_cols),
        columns(q_cols + kv_cols, kv_cols),
        columns(qkv_cols, q_cols),
        sum_gate.reshape(-1, own_experts, ff),
        sum_up.reshape(-1, own_experts, ff),
        sum_down.reshape(-1, own_experts, ff),
    )


def shards_fast(
    tokens,
    cotangent,
    gain_attn,
    gain_ffn,
    w_query,
    key_weight,
    value_weight,
    w_out,
    expert_gate,
    expert_up,
    expert_down,
    expert_ids,
    gates,
    lengths,
    order,
):
    rows, width = tokens.shape
    members, devices = lax.axis_size("expert"), lax.axis_size("dp")
    span = rows * members
    own_experts, ff = expert_gate.shape[1], expert_gate.shape[2]
    capacity = rows * TOP // own_experts
    route = jnp.concatenate([expert_ids.astype(F32), gates], axis=1)
    segment, position = layout(lengths[0], order[0], span)
    lane = jnp.arange(LANES, dtype=jnp.int32) % HEAD_SIZE
    half = HEAD_SIZE // 2
    frequency = rope_base ** (-((lane % half).astype(F32) * (2.0 / HEAD_SIZE)))
    angles = position[:, None] * frequency[None, :]
    cosine, sine = jnp.cos(angles), jnp.where(lane < half, -1.0, 1.0) * jnp.sin(angles)
    (
        cot_all, route_all, pack_all, gate_all, up_all, down_all,
        normed_attn, qkv, kx, vx, probs, attended, residual, normed_all, gains,
    ) = forward_phase(
        members, tokens, cotangent, route, w_query, key_weight, value_weight, w_out,
        gain_attn[None], gain_ffn[None],
        expert_gate.reshape(-1, own_experts * ff),
        expert_up.reshape(-1, own_experts * ff),
        expert_down.reshape(-1, own_experts * ff),
        segment.astype(F32)[None], cosine, sine,
    )
    cot_all = cot_all.reshape(span, width)
    normed_all = normed_all.reshape(span, width)
    route_all = route_all.reshape(span, 2 * TOP)
    gate_all, up_all, down_all = (w.reshape(width, -1) for w in (gate_all, up_all, down_all))
    mixture, grad_normed, *by_kind = experts(
        own_experts, capacity, route_all, normed_all, cot_all, gate_all, up_all, down_all
    )
    by_kind = [one.reshape(devices, -1, own_experts * ff) for one in by_kind]

    output, grad_residual, gain_two_part, grad_attn_out, sum_gate, sum_up = third_phase(
        members, own_experts,
        grad_normed.reshape(members, rows, width),
        mixture.reshape(members, rows, width),
        residual,
        cotangent,
        gains,
        by_kind[0],
        by_kind[1],
    )
    (
        grad_tokens, grad_gains, d_query, d_key, d_value, d_out, d_down,
    ) = backward_phase(
        members, own_experts,
        grad_attn_out.reshape(span, width),
        grad_residual,
        gain_two_part,
        tokens,
        by_kind[2],
        gains,
        pack_all,
        normed_attn, qkv, kx, vx, probs, attended, cosine, sine,
    )
    return (
        output,
        grad_tokens,
        grad_gains[:, 0],
        grad_gains[:, 1],
        d_query,
        d_key,
        d_value,
        d_out,
        sum_gate.transpose(1, 0, 2),
        sum_up.transpose(1, 0, 2),
        d_down.transpose(1, 0, 2),
    )


def solution(mesh):
    both = P(("dp", "expert"), None)
    row, rows = P("dp"), P("dp", None)
    experts = P("dp", "expert", None)
    fast = mesh.shape["dp"] == 8 and mesh.shape["expert"] == 4
    return jax.shard_map(
        shards_fast if fast else shards_plain,
        mesh=mesh,
        in_specs=(both, both, row, row, rows, rows, rows, rows)
        + (experts, experts, experts, both, both, rows, rows),
        out_specs=(both, both, row, row, rows, rows, rows, rows, experts, experts, experts),
        check_vma=False,
    )
```

```python
import functools

import jax
import jax.numpy as jnp
from jax import lax
from jax.experimental import pallas as pl
from jax.experimental.pallas import tpu as pltpu
from jax.sharding import PartitionSpec as P

QUERY_HEADS = 24
KEY_VALUE_HEADS = 8
HEAD_SIZE = 64
TOP = 8

epsilon = 1e-06
rope_base = 10000.0
score_scale = 0.015625
branch_scale = 0.22
F32 = jnp.float32
BF16 = jnp.bfloat16
MESH = pl.DeviceIdType.MESH
LANES = 128
VMEM_LIMIT = 60 * 2**20


def layout(lengths_row, order_row, span):
    seqs = lengths_row.shape[0]
    slot_ids = jnp.arange(seqs, dtype=jnp.int32)
    picked = jnp.sum(
        jnp.where(order_row[:, None] == slot_ids[None, :], lengths_row[None, :], 0), axis=1
    )
    before = slot_ids[:, None] >= slot_ids[None, :]
    seq_ends = jnp.sum(jnp.where(before, picked[None, :], 0), axis=1)
    place = jnp.arange(span, dtype=jnp.int32)
    passed = place[:, None] >= seq_ends[None, :]
    segment = jnp.sum(passed.astype(jnp.int32), axis=1)
    start = jnp.sum(jnp.where(passed, picked[None, :], 0), axis=1)
    return segment, (place - start).astype(F32)


def rotation(position):
    half = HEAD_SIZE // 2
    frequency = rope_base ** (-(jnp.arange(half, dtype=F32) * (2.0 / HEAD_SIZE)))
    angles = position[:, None] * frequency[None, :]
    return jnp.cos(angles), jnp.sin(angles)


def rotate(rows, cosine, sine, back=False):
    t = rows.shape[0]
    heads = rows.reshape(t, -1, 2, HEAD_SIZE // 2)
    a, b = heads[:, :, 0], heads[:, :, 1]
    c, s = cosine[:, None, :], sine[:, None, :]
    if back:
        s = -s
    return jnp.stack([a * c - b * s, b * c + a * s], axis=2).reshape(t, -1)


def dot(a, b):
    return jnp.dot(a, b, preferred_element_type=F32)


def dot_nt(a, b):
    return jnp.einsum("tc,dc->td", a, b, preferred_element_type=F32)


def dot_tn(a, b):
    return jnp.einsum("td,tc->dc", a, b, preferred_element_type=F32)


def rms_factor(rows):
    return lax.rsqrt(jnp.mean(rows * rows, axis=-1, keepdims=True) + epsilon)


def norm_back(rows, factor, gain, grad):
    scaled = gain * grad
    return factor * scaled - rows * (factor * factor * factor) * jnp.mean(
        scaled * rows, axis=-1, keepdims=True
    )


def gather(x, axis):
    return lax.all_gather(x, axis, axis=0, tiled=True)


def scatter(x, axis):
    return lax.psum_scatter(x.astype(BF16), axis, scatter_dimension=0, tiled=True).astype(F32)


class Links:
    def __init__(self, send, recv, local, members):
        self.send, self.recv, self.local = send, recv, local
        self.remotes = self.locals = 0
        self.members = members
        self.d, self.z = lax.axis_index("dp"), lax.axis_index("expert")
        d = self.d
        core, x, y = d % 2, (d // 2) % 2, d // 4
        self.core = core
        self.sib = d + 1 - 2 * core
        self.x = d + 2 - 4 * x
        self.y = d + 4 - 8 * y
        self.diag = self.x + 4 - 8 * y
        self.waiting = []

    def other(self, d):
        return d + 1 - 2 * self.core

    def greet(self):
        barrier = pltpu.get_barrier_semaphore()
        last = self.members - 1

        def hello(d, z):
            pl.semaphore_signal(barrier, inc=1, device_id=(d, z), device_id_type=MESH)

        for d in (self.sib, self.x, self.y):
            hello(d, self.z)
        pl.when(self.z > 0)(lambda: hello(self.d, self.z - 1))
        pl.when(self.z < last)(lambda: hello(self.d, self.z + 1))
        ends = (self.z == 0).astype(jnp.int32) + (self.z == last).astype(jnp.int32)
        pl.semaphore_wait(barrier, 5 - ends)

    def remote(self, src, dst, to):
        k = self.remotes
        self.remotes += 1
        return pltpu.make_async_remote_copy(
            src_ref=src,
            dst_ref=dst,
            send_sem=self.send.at[k],
            recv_sem=self.recv.at[k],
            device_id=to,
            device_id_type=MESH,
        )

    def push(self, src, dst, d):
        copy = self.remote(src, dst, (d, self.z))
        copy.start()
        self.waiting.append(copy.wait_send)
        return copy

    def move(self, src, dst):
        k = self.locals
        self.locals += 1
        copy = pltpu.make_async_copy(src, dst, self.local.at[k])
        copy.start()
        return copy

    def finish(self):
        for wait in self.waiting:
            wait()


def run(order, **chains):
    for name in order:
        next(chains[name], None)
    chains = list(chains.values())
    while chains:
        for chain in list(chains):
            try:
                next(chain)
            except StopIteration:
                chains.remove(chain)


def line_gather(links, own, full):
    z, last = links.z, links.members - 1
    local = links.move(own, full.at[z])
    right, left = (links.d, z + 1), (links.d, z - 1)
    to_right, to_left = [], []
    for s in range(last):
        at_r, at_l = jnp.maximum(z - s, 0), jnp.minimum(z + s, last)
        to_right.append(links.remote(own if s == 0 else full.at[at_r], full.at[at_r], right))
        to_left.append(links.remote(own if s == 0 else full.at[at_l], full.at[at_l], left))
    for s in range(last):
        send_r, send_l = (z < last) & (z >= s), (z > 0) & (z + s <= last)
        pl.when(send_r)(to_right[s].start)
        pl.when(send_l)(to_left[s].start)
        yield
        pl.when((z > 0) & (z - 1 >= s))(to_right[s].wait_recv)
        pl.when((z < last) & (z + 1 + s <= last))(to_left[s].wait_recv)
    for s in range(last):
        send_r, send_l = (z < last) & (z >= s), (z > 0) & (z + s <= last)
        pl.when(send_r)(to_right[s].wait_send)
        pl.when(send_l)(to_left[s].wait_send)
    local.wait()


def add_rows(target, other, step=16):
    rows = target.shape[0]

    @pl.loop(0, rows // step)
    def _(i):
        at = pl.ds(pl.multiple_of(i * step, step), step)
        target[at] = (target[at].astype(F32) + other[at].astype(F32)).astype(target.dtype)


def line_sum(links, part, acc, from_left, from_right, finish, own=None, full=None, parts=2):
    z, last = links.z, links.members - 1
    rows = acc.shape[1] // parts
    spans = [pl.ds(h * rows, rows) for h in range(parts)]
    right, left = (links.d, z + 1), (links.d, z - 1)
    sum_r, sum_l, go_r, go_l, local = {}, {}, {}, {}, []
    for h, span in enumerate(spans):
        for o in range(last + 1):
            if o > 0:
                sum_r[h, o] = links.remote(acc.at[o, span], from_left.at[o, span], right)
            if o < last:
                sum_l[h, o] = links.remote(acc.at[o, span], from_right.at[o, span], left)
        for s in range(last if own is not None else 0):
            at_r, at_l = jnp.maximum(z - s, 0), jnp.minimum(z + s, last)
            here_r, here_l = full.at[at_r, span], full.at[at_l, span]
            go_r[h, s] = links.remote(own.at[span] if s == 0 else here_r, here_r, right)
            go_l[h, s] = links.remote(own.at[span] if s == 0 else here_l, here_l, left)

    def pass_right(h, o):
        @pl.when(z > 0)
        def _():
            sum_r[h, o].wait_recv()
            add_rows(acc.at[o, spans[h]], from_left.at[o, spans[h]])

        sum_r[h, o].start()

    def pass_left(h, o):
        @pl.when(z < last)
        def _():
            sum_l[h, o].wait_recv()
            add_rows(acc.at[o, spans[h]], from_right.at[o, spans[h]])

        sum_l[h, o].start()

    def send(h, s):
        pl.when((z < last) & (z >= s))(go_r[h, s].start)
        pl.when((z > 0) & (z + s <= last))(go_l[h, s].start)

    @pl.when(z == 0)
    def _():
        from_left[0] = jnp.zeros(from_left.shape[1:], from_left.dtype)

    @pl.when(z == last)
    def _():
        from_right[last] = jnp.zeros(from_right.shape[1:], from_right.dtype)

    made = set()
    for j in range(last):
        for o in (last - j, j):
            if o not in made:
                made.add(o)
                part(o)
        for h in range(parts):
            pl.when((z < last - j) & (2 * z < last))(functools.partial(pass_right, h, last - j))
            pl.when(z > j)(functools.partial(pass_left, h, j))
            pl.when((z < last - j) & (2 * z >= last))(functools.partial(pass_right, h, last - j))
            yield
    for h in range(parts):
        for o in range(last + 1):
            if o > 0:
                pl.when(z == o)(sum_r[h, o].wait_recv)
            if o < last:
                pl.when(z == o)(sum_l[h, o].wait_recv)
        finish(h * rows, rows)
        if own is None:
            continue
        send(h, 0)
        local.append(links.move(own.at[spans[h]], full.at[z, spans[h]]))
        yield
    for s in range(last if own is not None else 0):
        for h in range(parts):
            pl.when((z > 0) & (z - 1 >= s))(go_r[h, s].wait_recv)
            pl.when((z < last) & (z + 1 + s <= last))(go_l[h, s].wait_recv)
            if s + 1 < last:
                send(h, s + 1)
            yield
    for h in range(parts):
        for o in range(last + 1):
            if o > 0:
                pl.when(z < o)(sum_r[h, o].wait_send)
            if o < last:
                pl.when(z > o)(sum_l[h, o].wait_send)
        for s in range(last if own is not None else 0):
            pl.when((z < last) & (z >= s))(go_r[h, s].wait_send)
            pl.when((z > 0) & (z + s <= last))(go_l[h, s].wait_send)
    for copy in local:
        copy.wait()


def plane_gather(links, own, full):
    half = own.shape[0] // 2
    first, second = pl.ds(0, half), pl.ds(half, half)
    me = links.d
    local = links.move(own, full.at[me])
    by_x, by_y = {}, {}
    for by, d, h in ((by_y, links.y, first), (by_x, links.x, second), (by_x, links.x, first), (by_y, links.y, second)):
        by[h.start // half] = links.push(own.at[h], full.at[me, h], d)
    to_sib = [links.push(own, full.at[me], links.sib)]

    def share(d, h):
        to_sib.append(links.push(full.at[d, h], full.at[d, h], links.sib))

    yield
    by_y[0].wait_recv()
    over_x = links.push(full.at[links.y, first], full.at[links.y, first], links.x)
    share(links.y, first)
    by_x[1].wait_recv()
    over_y = links.push(full.at[links.x, second], full.at[links.x, second], links.y)
    share(links.x, second)
    yield
    by_x[0].wait_recv()
    share(links.x, first)
    by_y[1].wait_recv()
    share(links.y, second)
    yield
    over_x.wait_recv()
    share(links.diag, first)
    over_y.wait_recv()
    share(links.diag, second)
    yield
    for copy in to_sib:
        copy.wait_recv()
    local.wait()


def plane_scatter(links, part, mine, theirs, mid_x, mid_y, end_x, end_y):
    half = part.shape[1] // 2
    first, second = pl.ds(0, half), pl.ds(half, half)
    chips = (links.d, links.x, links.y, links.diag)
    from_sib, load = {}, {}
    held = [part.at[chip] if mine is None else mine.at[k] for k, chip in enumerate(chips)]
    for k in (3, 1, 2, 0):
        from_sib[k] = links.push(part.at[links.other(chips[k])], theirs.at[k], links.sib)
        if mine is not None:
            load[k] = links.move(part.at[chips[k]], held[k])
    yield
    for k in (3, 1, 2):
        if load:
            load[k].wait()
        from_sib[k].wait_recv()
        add_rows(held[k], theirs.at[k])
        if k == 3:
            to_mid_x = links.push(held[3].at[first], mid_x, links.x)
            to_mid_y = links.push(held[3].at[second], mid_y, links.y)
        if k == 1:
            to_end_x = links.push(held[1].at[first], end_x.at[first], links.x)
        if k == 2:
            to_end_y = links.push(held[2].at[second], end_y.at[second], links.y)
        if k != 1:
            yield
    to_mid_y.wait_recv()
    add_rows(held[1].at[second], mid_y)
    rest_x = links.push(held[1].at[second], end_x.at[second], links.x)
    to_mid_x.wait_recv()
    add_rows(held[2].at[first], mid_x)
    rest_y = links.push(held[2].at[first], end_y.at[first], links.y)
    yield
    if load:
        load[0].wait()
    from_sib[0].wait_recv()
    to_end_x.wait_recv()
    to_end_y.wait_recv()
    rest_x.wait_recv()
    rest_y.wait_recv()
    yield


def plane_scratch(rows, cols, mine=True):
    return [pltpu.VMEM((4, rows, cols), BF16)] * mine + [
        pltpu.VMEM((4, rows, cols), BF16),
        pltpu.VMEM((rows // 2, cols), BF16),
        pltpu.VMEM((rows // 2, cols), BF16),
        pltpu.VMEM((rows, cols), BF16),
        pltpu.VMEM((rows, cols), BF16),
    ]


def plane_result(mine, theirs, end_x, end_y, out, step=16):
    @pl.loop(0, out.shape[-2] // step)
    def _(i):
        at = pl.ds(pl.multiple_of(i * step, step), step)
        own = mine[at].astype(F32) + theirs[0, at].astype(F32)
        total = (own + end_x[at].astype(F32) + end_y[at].astype(F32)).astype(out.dtype)
        if len(out.shape) == 2:
            out[at] = total
        else:
            cols = out.shape[2]
            for e in range(out.shape[0]):
                out[e, at] = total[:, e * cols : (e + 1) * cols]


def line_result(z, acc, from_left, from_right, at):
    return (
        acc[z, at].astype(F32) + from_left[z, at].astype(F32) + from_right[z, at].astype(F32)
    )


ANY = pl.BlockSpec(memory_space=pl.ANY)
VMEM = pl.BlockSpec(memory_space=pltpu.VMEM)


def comm_call(kernel, name, number, members, remotes, locals_, in_specs, out_specs, out_shape, scratch):
    return pl.pallas_call(
        functools.partial(kernel, members),
        out_shape=out_shape,
        in_specs=in_specs,
        out_specs=out_specs,
        scratch_shapes=[
            pltpu.SemaphoreType.DMA((remotes,)),
            pltpu.SemaphoreType.DMA((remotes,)),
            pltpu.SemaphoreType.DMA((locals_,)),
            *scratch,
        ],
        compiler_params=pltpu.CompilerParams(
            collective_id=number, has_side_effects=True, vmem_limit_bytes=VMEM_LIMIT
        ),
        name=name,
    )


def sds(shape, dtype):
    return jax.ShapeDtypeStruct(shape, dtype)


def third_kernel(members, part, mixture, residual, cot, gain, gate, up, output, grad_residual, gain_part, out_all, gate_out, up_out, send, recv, local, acc, from_left, from_right, acc_m, left_m, right_m, grad_out, *rest):
    links = Links(send, recv, local, members)
    links.greet()
    for_gate, for_up = rest[:6], rest[6:]

    def finish(first, count):
        @pl.loop(0, count // 16)
        def _(i):
            at = pl.ds(pl.multiple_of(first + i * 16, 16), 16)
            grad = line_result(links.z, acc, from_left, from_right, at)
            here = residual[at]
            factor = rms_factor(here)
            gain_part[...] += jnp.sum(grad * here * factor, axis=0, keepdims=True)
            total = cot[at].astype(F32) + norm_back(here, factor, gain[1:2], grad)
            grad_residual[at] = total
            grad_out[at] = (branch_scale * total).astype(BF16)

    def chain():
        links.move(part, acc).wait()
        gain_part[...] = jnp.zeros(gain_part.shape, F32)
        yield from line_sum(
            links, lambda o: None, acc, from_left, from_right, finish, grad_out, out_all
        )

    def finish_mixture(first, count):
        @pl.loop(0, count // 16)
        def _(i):
            at = pl.ds(pl.multiple_of(first + i * 16, 16), 16)
            here = residual[at] + branch_scale * line_result(links.z, acc_m, left_m, right_m, at)
            output[at] = here.astype(BF16)

    def mixture_chain():
        links.move(mixture, acc_m).wait()
        yield from line_sum(links, lambda o: None, acc_m, left_m, right_m, finish_mixture)

    run(
        THIRD_ORDER,
        m=mixture_chain(),
        z=chain(),
        g=plane_scatter(links, gate, *for_gate),
        u=plane_scatter(links, up, *for_up),
    )
    plane_result(for_gate[0].at[0], for_gate[1], for_gate[4], for_gate[5], gate_out)
    plane_result(for_up[0].at[0], for_up[1], for_up[4], for_up[5], up_out)
    links.finish()


THIRD_ORDER = "uzuzzgugmmzzguzzzgzmzmzmmzmugguuzm"


def third_phase(members, own_experts, part, mixture, residual, cot, gain, gate, up):
    rows, width = cot.shape
    blocks = pltpu.VMEM((members, rows, width), BF16)
    return comm_call(
        third_kernel, "phase_three", 3, members, 80, 16,
        [ANY, ANY, VMEM, VMEM, VMEM, ANY, ANY], [VMEM, VMEM, VMEM, ANY, VMEM, VMEM],
        [
            sds((rows, width), BF16),
            sds((rows, width), F32),
            sds((1, width), F32),
            sds((members, rows, width), BF16),
            sds((own_experts, gate.shape[1], gate.shape[2] // own_experts), F32),
            sds((own_experts, up.shape[1], up.shape[2] // own_experts), F32),
        ],
        [blocks] * 6
        + [pltpu.VMEM((rows, width), BF16)]
        + plane_scratch(*gate.shape[1:])
        + plane_scratch(*up.shape[1:]),
    )(part, mixture, residual, cot, gain, gate, up)


def lane_ids(rows):
    return lax.broadcasted_iota(jnp.int32, (rows, LANES), 1)


def dims(a, b):
    return (((a,), (b,)), ((), ()))


def mm(a, b):
    return lax.dot_general(a, b, dims(1, 0), preferred_element_type=F32)


def mm_nt(a, b):
    return lax.dot_general(a, b, dims(1, 1), preferred_element_type=F32)


def mm_tn(a, b):
    return lax.dot_general(a, b, dims(0, 0), preferred_element_type=F32)


def first_lanes():
    same = lax.broadcasted_iota(jnp.int32, (16, LANES), 0) == lax.broadcasted_iota(jnp.int32, (16, LANES), 1)
    return same.astype(BF16)


def expert_kernel(capacity, own_experts, route, normed, cot, w_gate, w_up, w_down, mixture, grad_normed, d_gate, d_up, d_down, mix_sum, grad_sum, slot_cols, weight_cols, slot_rows):
    e = pl.program_id(0)
    span = normed.shape[0]

    @pl.when(e == 0)
    def _():
        mix_sum[...] = jnp.zeros(mix_sum.shape, F32)
        grad_sum[...] = jnp.zeros(grad_sum.shape, F32)
        lane = lane_ids(LANES)
        name = (lax.axis_index("expert") * own_experts + lane).astype(F32)
        name = jnp.where(lane < own_experts, name, -1.0)
        upto = (lane <= lax.broadcasted_iota(jnp.int32, (LANES, LANES), 0)).astype(BF16)
        before = jnp.zeros((1, LANES), F32)
        for b in range(span // LANES):
            at = pl.ds(b * LANES, LANES)
            chosen, weight = jnp.zeros((LANES, LANES), F32), jnp.zeros((LANES, LANES), F32)
            for k in range(TOP):
                named = route[at, k : k + 1] == name
                chosen = jnp.where(named, 1.0, chosen)
                weight = jnp.where(named, route[at, TOP + k : TOP + k + 1], weight)
            slot = mm(upto, chosen.astype(BF16)) + (before - 1.0)
            slot_cols[at] = jnp.where((chosen > 0.0) & (slot < capacity), slot, -1.0)
            weight_cols[at] = weight
            before = before + jnp.sum(chosen, axis=0, keepdims=True)
        slot_rows[...] = mm_nt(first_lanes(), slot_cols[...].astype(BF16))

    def column(values):
        return jnp.sum(jnp.where(lane_ids(span) == e, values[...], 0.0), axis=1, keepdims=True)

    slots = lax.broadcasted_iota(jnp.int32, (capacity, span), 0).astype(F32)
    pick = (slot_rows[pl.ds(e, 1)] == slots).astype(BF16)
    puts = column(slot_cols) == lax.broadcasted_iota(jnp.int32, (span, capacity), 1).astype(F32)
    put = puts.astype(BF16)
    gate_row = jnp.sum(jnp.where(puts, column(weight_cols), 0.0), axis=0, keepdims=True)
    same = lax.broadcasted_iota(jnp.int32, (capacity, capacity), 0) == lax.broadcasted_iota(jnp.int32, (capacity, capacity), 1)
    gate_col = jnp.sum(jnp.where(same, gate_row, 0.0), axis=1, keepdims=True)
    received = mm(pick, normed[...]).astype(BF16)
    pre_gate, pre_up = mm(received, w_gate[...]), mm(received, w_up[...])
    sig = 1.0 / (1.0 + jnp.exp(-pre_gate))
    silu = pre_gate * sig
    activ = (silu * pre_up).astype(BF16)
    produced = (gate_col * mm_nt(activ, w_down[...])).astype(BF16)
    mix_sum[...] += mm(put, produced)
    grad_out = (gate_col * (branch_scale * mm(pick, cot[...]))).astype(BF16)
    grad_activ = mm(grad_out, w_down[...])
    grad_gate = (grad_activ * pre_up * (sig * (1.0 + pre_gate * (1.0 - sig)))).astype(BF16)
    grad_up = (grad_activ * silu).astype(BF16)
    grad_pair = (mm_nt(grad_gate, w_gate[...]) + mm_nt(grad_up, w_up[...])).astype(BF16)
    grad_sum[...] += mm(put, grad_pair)
    d_gate[...] = mm_tn(received, grad_gate).astype(BF16)
    d_up[...] = mm_tn(received, grad_up).astype(BF16)
    d_down[...] = mm_tn(grad_out, activ).astype(BF16)

    @pl.when(e == pl.num_programs(0) - 1)
    def _():
        mixture[...] = mix_sum[...].astype(BF16)
        grad_normed[...] = grad_sum[...].astype(BF16)


def experts(own_experts, capacity, route, normed, cot, w_gate, w_up, w_down):
    span, width = normed.shape
    ff = w_gate.shape[1] // own_experts
    whole = pl.BlockSpec((span, width), lambda e: (0, 0))
    column = pl.BlockSpec((width, ff), lambda e: (0, e))
    grads = jax.ShapeDtypeStruct(w_gate.shape, BF16)
    rows = jax.ShapeDtypeStruct((span, width), BF16)
    return pl.pallas_call(
        functools.partial(expert_kernel, capacity, own_experts),
        grid=(own_experts,),
        in_specs=[pl.BlockSpec(route.shape, lambda e: (0, 0)), whole, whole, column, column, column],
        out_specs=[whole, whole, column, column, column],
        out_shape=[rows, rows, grads, grads, grads],
        scratch_shapes=[
            pltpu.VMEM((span, width), F32),
            pltpu.VMEM((span, width), F32),
            pltpu.VMEM((span, LANES), F32),
            pltpu.VMEM((span, LANES), F32),
            pltpu.VMEM((16, span), F32),
        ],
        compiler_params=pltpu.CompilerParams(vmem_limit_bytes=VMEM_LIMIT),
        name="experts",
    )(route, normed, cot, w_gate, w_up, w_down)


def turn(x, cosine, sine):
    half = HEAD_SIZE // 2
    ahead, behind = pltpu.roll(x, LANES - half, axis=1), pltpu.roll(x, half, axis=1)
    partner = jnp.where(lane_ids(x.shape[0]) % HEAD_SIZE < half, ahead, behind)
    return x * cosine + partner * sine


def spread(block, at, out):
    low = lane_ids(block.shape[0]) < HEAD_SIZE
    other = pltpu.roll(block, HEAD_SIZE, axis=1)
    zero = jnp.zeros_like(block)
    out[0, 0, at] = jnp.where(low, block, zero).astype(BF16)
    out[0, 1, at] = jnp.where(low, zero, other).astype(BF16)
    out[1, 0, at] = jnp.where(low, other, zero).astype(BF16)
    out[1, 1, at] = jnp.where(low, zero, block).astype(BF16)


def attention_setup(segment, bias):
    span = bias.shape[0]
    same = lax.broadcasted_iota(jnp.int32, (LANES, LANES), 0) == lane_ids(LANES)
    for b in range(span // LANES):
        at = pl.ds(b * LANES, LANES)
        row = b * LANES + lax.broadcasted_iota(jnp.int32, (LANES, span), 0)
        col = lax.broadcasted_iota(jnp.int32, (LANES, span), 1)
        here = segment[:, b * LANES : (b + 1) * LANES]
        here = jnp.sum(jnp.where(same, here, 0.0), axis=1, keepdims=True)
        ok = (here == segment) & (col <= row)
        bias[at] = jnp.where(ok, 0.0, -1e30)


def weight_columns(pack_all, first, cols):
    return pack_all[:, :, first : first + cols].reshape(-1, cols)


def gain_rows(pack_all, first):
    return mm_nt(first_lanes(), weight_columns(pack_all, first, LANES))


def attend_steps(qkv, kx, vx, bias, probs, attended):
    span, blocks = qkv.shape[0], attended.shape[1] // LANES
    repeat = QUERY_HEADS // KEY_VALUE_HEADS
    for j in range(blocks):
        for b in range(span // LANES):
            at, keys = pl.ds(b * LANES, LANES), (b + 1) * LANES
            q = qkv[at, j * LANES : (j + 1) * LANES]
            total = jnp.zeros((LANES, LANES), F32)
            for half in range(2):
                h = 2 * j + half
                kv = h // repeat
                scores = mm_nt(q, kx[kv, half, :keys]) + bias[at, :keys]
                peak = jnp.max(scores, axis=1, keepdims=True)
                exponent = jnp.exp(scores - peak)
                share = 1.0 / jnp.sum(exponent, axis=1, keepdims=True)
                low = (exponent * share).astype(BF16)
                probs[h, at, :keys] = low
                total += mm(low, vx[kv, half, :keys])
            attended[at, j * LANES : (j + 1) * LANES] = total.astype(BF16)
        yield


def forward_kernel(
    members, tokens, cot, ids, gates, w_query, w_key, w_value, w_out, small, gate, up, down, cosine, sine,
    cot_all, route_all, pack_all, gate_all, up_all, down_all, normed_attn, qkv, kx, vx, probs, attended, residual, normed_all, gains,
    send, recv, local, pack, route, flat, tokens_all, bias, acc, from_left, from_right, normed,
):
    links = Links(send, recv, local, members)
    count, _, cols = gate.shape
    loads = [
        [links.move(weight.at[e], flat.at[i, :, e * cols : (e + 1) * cols]) for e in range(count)]
        for i, weight in enumerate((gate, up, down))
    ]
    links.greet()
    route[...] = jnp.concatenate([ids[...].astype(F32), gates[...]], axis=0).T
    rows, width = tokens.shape
    span = rows * members
    q_cols = attended.shape[1]
    qkv_cols = qkv.shape[1]

    def pack_chain():
        loads, at = [], 0
        for weight in (w_query, w_key, w_value, w_out):
            cols = weight.shape[1] // members
            mine = pl.ds(pl.multiple_of(links.z * cols, LANES), cols)
            loads.append(links.move(weight.at[:, mine], pack.at[:, at : at + cols]))
            at += cols
        which = lax.broadcasted_iota(jnp.int32, (16, pack.shape[0]), 0)
        own = pack.shape[0]
        both = jnp.where(which == 0, small[1:2, :own], jnp.where(which == 1, small[2:3, :own], 0.0))
        pack[:, at:] = mm_tn(both.astype(BF16), first_lanes()).astype(BF16)
        for load in loads:
            load.wait()
        yield from plane_gather(links, pack, pack_all)

    def expert_chain(i, full):
        for load in loads[i]:
            load.wait()
        yield from plane_gather(links, flat.at[i], full)

    def produce(o):
        acc[o] = mm_nt(attended[o * rows : (o + 1) * rows], weight_columns(pack_all, qkv_cols, q_cols)).astype(BF16)

    def chain():
        attention_setup(small[0:1], bias)
        yield
        gains[...] = gain_rows(pack_all, qkv_cols + q_cols)

        @pl.loop(0, span // 16)
        def _(i):
            here = tokens_all[i // (rows // 16), pl.ds(pl.multiple_of(i % (rows // 16) * 16, 16), 16)].astype(F32)
            normed_attn[pl.ds(pl.multiple_of(i * 16, 16), 16)] = (here * rms_factor(here) * gains[0:1]).astype(BF16)

        @pl.loop(0, span // LANES)
        def _(i):
            at = pl.ds(pl.multiple_of(i * LANES, LANES), LANES)
            here = mm(normed_attn[at], weight_columns(pack_all, 0, qkv_cols))
            c, s = cosine[at], sine[at]
            for j in range(q_cols // LANES):
                lanes = slice(j * LANES, (j + 1) * LANES)
                qkv[at, lanes] = (turn(here[:, lanes], c, s).astype(BF16).astype(F32) * score_scale).astype(BF16)
            key = turn(here[:, q_cols : q_cols + LANES], c, s)
            value = here[:, q_cols + LANES :]
            qkv[at, q_cols : q_cols + LANES] = key.astype(BF16)
            qkv[at, q_cols + LANES :] = value.astype(BF16)
            spread(key, at, kx)
            spread(value, at, vx)

        yield
        yield from attend_steps(qkv, kx, vx, bias, probs, attended)

        def finish(first, count):
            @pl.loop(0, count // 16)
            def _(i):
                at = pl.ds(pl.multiple_of(first + i * 16, 16), 16)
                here = tokens[at].astype(F32) + branch_scale * line_result(links.z, acc, from_left, from_right, at)
                residual[at] = here
                normed[at] = (here * rms_factor(here) * gains[1:2]).astype(BF16)

        yield from line_sum(links, produce, acc, from_left, from_right, finish, normed, normed_all)

    run(
        FORWARD_ORDER,
        t=line_gather(links, tokens, tokens_all),
        r=line_gather(links, route, route_all),
        c=line_gather(links, cot, cot_all),
        p=pack_chain(),
        g=expert_chain(0, gate_all),
        u=expert_chain(1, up_all),
        d=expert_chain(2, down_all),
        a=chain(),
    )
    links.finish()


FORWARD_ORDER = "tptpdptpcaptgaaacdtrgatcaardaagdattpuparparadrpaarrd"


def forward_phase(members, tokens, cot, ids, gates, w_query, w_key, w_value, w_out, small, gate, up, down, cosine, sine):
    rows, width = tokens.shape
    q_cols = w_query.shape[1] // members
    qkv_cols = q_cols + 2 * w_key.shape[1] // members
    count, own, cols = gate.shape
    pack = (own, qkv_cols + q_cols + LANES)
    route, flat = (rows, 2 * ids.shape[0]), (own, count * cols)
    span = rows * members
    blocks = pltpu.VMEM((members, rows, width), BF16)
    heads = q_cols // HEAD_SIZE
    return comm_call(
        forward_kernel, "forward", 1, members, 120, 40,
        [VMEM, ANY, VMEM, VMEM, ANY, ANY, ANY, ANY, VMEM, ANY, ANY, ANY, VMEM, VMEM],
        [ANY, ANY, VMEM, ANY, ANY, ANY, VMEM, VMEM, VMEM, VMEM, VMEM, VMEM, VMEM, ANY, VMEM],
        [
            sds((members, rows, width), BF16),
            sds((members, *route), F32),
            sds((8, *pack), BF16),
            sds((8, *flat), BF16),
            sds((8, *flat), BF16),
            sds((8, *flat), BF16),
            sds((span, width), BF16),
            sds((span, qkv_cols), BF16),
            sds((2, 2, span, LANES), BF16),
            sds((2, 2, span, LANES), BF16),
            sds((heads, span, span), BF16),
            sds((span, q_cols), BF16),
            sds((rows, width), F32),
            sds((members, rows, width), BF16),
            sds((16, width), F32),
        ],
        [
            pltpu.VMEM(pack, BF16),
            pltpu.VMEM(route, F32),
            pltpu.VMEM((3, *flat), BF16),
            blocks,
            pltpu.VMEM((span, span), F32),
            blocks,
            blocks,
            blocks,
            pltpu.VMEM((rows, width), BF16),
        ],
    )(tokens, cot, ids, gates, w_query, w_key, w_value, w_out, small, gate, up, down, cosine, sine)


def attend_back_steps(qkv, kx, vx, probs, grad_attended, cosine, sine, grad_k, grad_v, grad_qkv):
    span = qkv.shape[0]
    blocks = grad_attended.shape[1] // LANES
    repeat = QUERY_HEADS // KEY_VALUE_HEADS
    grad_k[...] = jnp.zeros(grad_k.shape, F32)
    grad_v[...] = jnp.zeros(grad_v.shape, F32)
    for j in range(blocks):
        lanes = slice(j * LANES, (j + 1) * LANES)
        for b in range(span // LANES):
            at, keys = pl.ds(b * LANES, LANES), (b + 1) * LANES
            q, grad = qkv[at, lanes], grad_attended[at, lanes]
            total = jnp.zeros((LANES, LANES), F32)
            for half in range(2):
                h = 2 * j + half
                kv = h // repeat
                low = probs[h, at, :keys]
                share = low.astype(F32)
                grad_probs = mm_nt(grad, vx[kv, half, :keys])
                inner = jnp.sum(share * grad_probs, axis=1, keepdims=True)
                grad_scores = (share * (grad_probs - inner)).astype(BF16)
                total += mm(grad_scores, kx[kv, half, :keys])
                grad_k[kv, half, :keys] += mm_tn(grad_scores, q)
                grad_v[kv, half, :keys] += mm_tn(low, grad)
            grad_qkv[at, lanes] = turn(total * score_scale, cosine[at], -sine[at]).astype(BF16)
        yield
    first = blocks * LANES

    def fold(parts, at):
        low = lane_ids(LANES) < HEAD_SIZE
        same = jnp.where(low, parts[0, 0, at], parts[1, 1, at])
        crossed = jnp.where(low, parts[1, 0, at], parts[0, 1, at])
        return same + pltpu.roll(crossed, HEAD_SIZE, axis=1)

    for b in range(span // LANES):
        at = pl.ds(b * LANES, LANES)
        grad_qkv[at, first : first + LANES] = turn(fold(grad_k, at), cosine[at], -sine[at]).astype(BF16)
        grad_qkv[at, first + LANES :] = fold(grad_v, at).astype(BF16)


def backward_kernel(
    members, grad_out_all, grad_residual, gain_ffn_part, tokens, down, row_gains, pack_all, normed_attn, qkv, kx, vx, probs, attended, cosine, sine,
    grad_tokens, gains, d_query, d_key, d_value, d_out, d_down,
    send, recv, local, acc, from_left, from_right, grad_attended, grad_k, grad_v, grad_qkv, gain_part,
    for_w_out, for_w_query, for_rest, own_out, own_query, own_rest, all_out, all_query, all_rest, *rest,
):
    links = Links(send, recv, local, members)
    links.greet()
    rows, width = tokens.shape
    q_cols, qkv_cols = attended.shape[1], qkv.shape[1]
    kv_cols = (qkv_cols - q_cols) // 2
    with_out, with_query, with_rest, with_down = rest[:5], rest[5:10], rest[10:15], rest[15:]
    pairs = for_w_out.shape[0] // 2
    step = width // pairs

    def weight_term(rows_of, grads, out, cols):
        for i in range(pairs):
            term = mm_tn(rows_of[:, i * step : (i + 1) * step], grads)
            out[2 * i : 2 * i + 2, :, :cols] = term.astype(BF16).reshape(2, step // 2, cols)

    def weight_chain(fill, part, mine, full, scratch):
        fill()
        yield from plane_scatter(links, part, None, *scratch)
        plane_result(part.at[links.d], scratch[0], scratch[3], scratch[4], mine)
        yield from line_gather(links, mine, full)

    def fill_out():
        weight_term(grad_out_all, attended[...], for_w_out, q_cols)

    def fill_query():
        weight_term(normed_attn, grad_qkv[:, :q_cols], for_w_query, q_cols)

    def fill_rest():
        weight_term(normed_attn, grad_qkv[:, q_cols:], for_rest, 2 * kv_cols)
        which = lax.broadcasted_iota(jnp.int32, (16, width), 0)
        both = jnp.where(which == 0, gain_part[...] / row_gains[0:1], jnp.where(which == 1, gain_ffn_part[...], 0.0))
        columns = mm_tn(both.astype(BF16), first_lanes())
        for_rest[:, :, 2 * kv_cols :] = columns.astype(BF16).reshape(2 * pairs, step // 2, LANES)

    def produce(o):
        at = slice(o * rows, (o + 1) * rows)
        part = mm_nt(grad_qkv[at], weight_columns(pack_all, 0, qkv_cols))
        gain_part[...] += jnp.sum(part * normed_attn[at].astype(F32), axis=0, keepdims=True)
        acc[o] = part.astype(BF16)

    def chain():
        wo = weight_columns(pack_all, qkv_cols, q_cols)

        @pl.loop(0, grad_attended.shape[0] // LANES)
        def _(i):
            at = pl.ds(pl.multiple_of(i * LANES, LANES), LANES)
            grad_attended[at] = mm(grad_out_all[at], wo).astype(BF16)

        yield
        yield from attend_back_steps(qkv, kx, vx, probs, grad_attended, cosine, sine, grad_k, grad_v, grad_qkv)
        gain_part[...] = jnp.zeros(gain_part.shape, F32)
        yield

        def finish(first, count):
            @pl.loop(0, count // 16)
            def _(i):
                at = pl.ds(pl.multiple_of(first + i * 16, 16), 16)
                grad = line_result(links.z, acc, from_left, from_right, at)
                here = tokens[at].astype(F32)
                grad_tokens[at] = grad_residual[at] + norm_back(here, rms_factor(here), row_gains[0:1], grad)

        yield from line_sum(links, produce, acc, from_left, from_right, finish)

    run(
        BACKWARD_ORDER,
        d=plane_scatter(links, down, *with_down),
        o=weight_chain(fill_out, for_w_out, own_out, all_out, with_out),
        a=chain(),
        q=weight_chain(fill_query, for_w_query, own_query, all_query, with_query),
        r=weight_chain(fill_rest, for_rest, own_rest, all_rest, with_rest),
    )
    plane_result(with_down[0].at[0], with_down[1], with_down[4], with_down[5], d_down)
    for m in range(members):
        d_out[:, m * q_cols : (m + 1) * q_cols] = all_out[m].astype(F32)
        d_query[:, m * q_cols : (m + 1) * q_cols] = all_query[m].astype(F32)
        d_key[:, m * kv_cols : (m + 1) * kv_cols] = all_rest[m, :, :kv_cols].astype(F32)
        d_value[:, m * kv_cols : (m + 1) * kv_cols] = all_rest[m, :, kv_cols : 2 * kv_cols].astype(F32)
    gains[...] = sum(all_rest[m, :, 2 * kv_cols :].astype(F32) for m in range(members))
    links.finish()


BACKWARD_ORDER = "oadoaoaoaooqaqqdoaqdaqqarorarradrraqrqdaoodaaqdrddrr"


def backward_phase(members, own_experts, grad_out_all, grad_residual, gain_ffn_part, tokens, down, row_gains, pack_all, normed_attn, qkv, kx, vx, probs, attended, cosine, sine):
    rows, width = tokens.shape
    span, q_cols = attended.shape
    qkv_cols = qkv.shape[1]
    kv_cols = (qkv_cols - q_cols) // 2
    devices, own = down.shape[:2]
    line = [pltpu.VMEM((members, rows, width), BF16)] * 3
    three = (q_cols, q_cols, 2 * kv_cols + LANES)
    return comm_call(
        backward_kernel, "backward", 4, members, 100, 32,
        [VMEM, VMEM, VMEM, VMEM, ANY] + [VMEM] * 10,
        [VMEM] * 7,
        [
            sds((rows, width), F32),
            sds((own, LANES), F32),
            sds((own, members * q_cols), F32),
            sds((own, members * kv_cols), F32),
            sds((own, members * kv_cols), F32),
            sds((own, members * q_cols), F32),
            sds((own_experts, own, down.shape[2] // own_experts), F32),
        ],
        [
            *line,
            pltpu.VMEM((span, q_cols), BF16),
            pltpu.VMEM((2, 2, span, LANES), F32),
            pltpu.VMEM((2, 2, span, LANES), F32),
            pltpu.VMEM((span, qkv_cols), BF16),
            pltpu.VMEM((1, width), F32),
            *[pltpu.VMEM((devices, own, cols), BF16) for cols in three],
            *[pltpu.VMEM((own, cols), BF16) for cols in three],
            *[pltpu.VMEM((members, own, cols), BF16) for cols in three],
            *[one for cols in three for one in plane_scratch(own, cols, False)],
            *plane_scratch(*down.shape[1:]),
        ],
    )(grad_out_all, grad_residual, gain_ffn_part, tokens, down, row_gains, pack_all, normed_attn, qkv, kx, vx, probs, attended, cosine, sine)


def all_blocks(x, axis):
    return lax.all_gather(x, axis, axis=0)


def plain_first(members, tokens, cot, route, pack, gate):
    return (
        all_blocks(tokens, "expert"),
        all_blocks(cot, "expert"),
        all_blocks(route, "expert"),
        all_blocks(pack, "dp"),
        all_blocks(gate, "dp"),
    )


def line_total(part):
    return scatter(part.reshape(-1, part.shape[2]), "expert")


def plain_second(members, part, tokens, gain, up, down):
    residual = tokens.astype(F32) + branch_scale * line_total(part)
    normed = (residual * rms_factor(residual) * gain).astype(BF16)
    return residual, all_blocks(normed, "expert"), all_blocks(up, "dp"), all_blocks(down, "dp")


def plane_sum(part):
    return scatter(part.reshape(-1, part.shape[2]), "dp")


def plain_third(members, part, residual, cot, gain, gate, up):
    grad = line_total(part)
    factor = rms_factor(residual)
    gain_part = jnp.sum(grad * residual * factor, axis=0, keepdims=True)
    total = cot.astype(F32) + norm_back(residual, factor, gain, grad)
    out_all = all_blocks((branch_scale * total).astype(BF16), "expert")
    return total, gain_part, out_all, plane_sum(gate), plane_sum(up)


def plain_fourth(members, part, grad_residual, tokens, gain, pack, down):
    here = tokens.astype(F32)
    grad_tokens = grad_residual + norm_back(here, rms_factor(here), gain, line_total(part))
    return grad_tokens, all_blocks(plane_sum(pack).astype(BF16), "expert"), plane_sum(down)


def attend_forward(q, k, v, allowed):
    scores = jnp.einsum("irh,jh->rij", q, k, preferred_element_type=F32) * score_scale
    scores = jnp.where(allowed[None], scores, -1e30)
    peak = jnp.max(scores, axis=-1, keepdims=True)
    exponent = jnp.exp(scores - peak)
    total = jnp.sum(exponent, axis=-1, keepdims=True)
    probs = exponent / total
    return jnp.einsum("rij,jh->irh", probs.astype(BF16), v, preferred_element_type=F32), probs


def attend_backward(q, k, v, probs, grad, allowed):
    grad_probs = jnp.einsum("irh,jh->rij", grad, v, preferred_element_type=F32)
    inner = jnp.sum(probs * grad_probs, axis=-1, keepdims=True)
    grad_scores = (probs * (grad_probs - inner)).astype(BF16)
    grad_q = jnp.einsum("rij,jh->irh", grad_scores, k, preferred_element_type=F32) * score_scale
    grad_k = jnp.einsum("rij,irh->jh", grad_scores, q, preferred_element_type=F32) * score_scale
    grad_v = jnp.einsum("rij,irh->jh", probs.astype(BF16), grad, preferred_element_type=F32)
    return grad_q, grad_k, grad_v


def shards_plain(
    tokens,
    cotangent,
    gain_attn,
    gain_ffn,
    w_query,
    key_weight,
    value_weight,
    w_out,
    expert_gate,
    expert_up,
    expert_down,
    expert_ids,
    gates,
    lengths,
    order,
):
    rows, width = tokens.shape
    members = lax.axis_size("expert")
    member = lax.axis_index("expert")
    span = rows * members
    own_experts, ff = expert_gate.shape[1], expert_gate.shape[2]
    capacity = rows * TOP // own_experts
    q_cols = w_query.shape[1] // members
    kv_cols = key_weight.shape[1] // members
    kv_heads = kv_cols // HEAD_SIZE
    repeat = QUERY_HEADS // KEY_VALUE_HEADS

    def mine(weight, cols):
        return lax.dynamic_slice_in_dim(weight, member * cols, cols, axis=1)

    devices = lax.axis_size("dp")
    phases = [
        functools.partial(phase, members)
        for phase in (plain_first, plain_second, plain_third, plain_fourth)
    ]

    pack = jnp.concatenate(
        [
            mine(w_query, q_cols),
            mine(key_weight, kv_cols),
            mine(value_weight, kv_cols),
            mine(w_out, q_cols),
            gain_attn[:, None],
            gain_ffn[:, None],
            jnp.zeros((gain_attn.shape[0], 126), BF16),
        ],
        axis=1,
    )
    route = jnp.concatenate([expert_ids.astype(F32), gates], axis=1)
    tokens_all, cot_all, route_all, pack_all, gate_all = phases[0](
        tokens, cotangent, route, pack, expert_gate.reshape(-1, own_experts * ff)
    )
    tokens_all = tokens_all.reshape(span, width).astype(F32)
    cot_all = cot_all.reshape(span, width)
    route_all = route_all.reshape(span, 2 * TOP)
    pack_all = pack_all.reshape(width, -1)
    gate_all = gate_all.reshape(width, -1)
    qkv_cols = q_cols + 2 * kv_cols
    w_qkv = pack_all[:, :qkv_cols]
    wo = pack_all[:, qkv_cols : qkv_cols + q_cols]
    gain_one = pack_all[:, qkv_cols + q_cols].astype(F32)[None]
    gain_two = pack_all[:, qkv_cols + q_cols + 1].astype(F32)[None]

    segment, position = layout(lengths[0], order[0], span)
    cosine, sine = rotation(position)
    place = jnp.arange(span, dtype=jnp.int32)
    allowed = (segment[:, None] == segment[None, :]) & (place[None, :] <= place[:, None])
    factor_one = rms_factor(tokens_all)
    normed_attn = (tokens_all * factor_one * gain_one).astype(BF16)
    qkv = dot(normed_attn, w_qkv)
    qk = rotate(qkv[:, : q_cols + kv_cols], cosine, sine).astype(BF16)
    v = qkv[:, q_cols + kv_cols :].astype(BF16)
    q_heads = jnp.moveaxis(qk[:, :q_cols].reshape(span, kv_heads, repeat, HEAD_SIZE), 1, 0)
    k_heads = jnp.moveaxis(qk[:, q_cols:].reshape(span, kv_heads, HEAD_SIZE), 1, 0)
    v_heads = jnp.moveaxis(v.reshape(span, kv_heads, HEAD_SIZE), 1, 0)
    attended, probs = jax.vmap(functools.partial(attend_forward, allowed=allowed))(
        q_heads, k_heads, v_heads
    )
    attended = jnp.moveaxis(attended, 0, 1).reshape(span, q_cols).astype(BF16)
    attn_part = dot_nt(attended, wo).astype(BF16).reshape(members, rows, width)
    residual, normed_all, up_all, down_all = phases[1](
        attn_part,
        tokens,
        gain_two,
        expert_up.reshape(-1, own_experts * ff),
        expert_down.reshape(-1, own_experts * ff),
    )
    normed_all = normed_all.reshape(span, width)
    up_all, down_all = up_all.reshape(width, -1), down_all.reshape(width, -1)

    mixture, grad_normed, *by_kind = experts(
        own_experts, capacity, route_all, normed_all, cot_all, gate_all, up_all, down_all
    )
    output = (residual + branch_scale * scatter(mixture, "expert")).astype(BF16)
    by_kind = [one.reshape(devices, -1, own_experts * ff) for one in by_kind]

    grad_residual, gain_two_part, grad_attn_out, sum_gate, sum_up = phases[2](
        grad_normed.reshape(members, rows, width),
        residual,
        cotangent,
        gain_two,
        by_kind[0],
        by_kind[1],
    )
    grad_attn_out = grad_attn_out.reshape(span, width)
    term_out = dot_tn(grad_attn_out, attended)
    grad_attended = dot(grad_attn_out, wo).astype(BF16)
    grad_heads = jnp.moveaxis(grad_attended.reshape(span, kv_heads, repeat, HEAD_SIZE), 1, 0)
    grad_q, grad_k, grad_v = jax.vmap(functools.partial(attend_backward, allowed=allowed))(
        q_heads, k_heads, v_heads, probs, grad_heads
    )
    grad_qk = jnp.concatenate(
        [
            jnp.moveaxis(grad_q, 0, 1).reshape(span, q_cols),
            jnp.moveaxis(grad_k, 0, 1).reshape(span, kv_cols),
        ],
        axis=1,
    )
    grad_qkv = jnp.concatenate(
        [
            rotate(grad_qk, cosine, sine, back=True).astype(BF16),
            jnp.moveaxis(grad_v, 0, 1).reshape(span, kv_cols).astype(BF16),
        ],
        axis=1,
    )
    grad_norm_part = dot_nt(grad_qkv, w_qkv)
    gain_one_part = jnp.sum(grad_norm_part * tokens_all * factor_one, axis=0)
    term_qkv = dot_tn(normed_attn, grad_qkv)
    packed_grads = jnp.concatenate(
        [
            term_qkv,
            term_out,
            gain_one_part[:, None],
            gain_two_part.reshape(-1, 1),
            jnp.zeros((width, 126), F32),
        ],
        axis=1,
    )
    grad_tokens, per_member, sum_down = phases[3](
        grad_norm_part.astype(BF16).reshape(members, rows, width),
        grad_residual,
        tokens,
        gain_one,
        packed_grads.astype(BF16).reshape(devices, -1, packed_grads.shape[1]),
        by_kind[2],
    )
    per_member = per_member.astype(F32)

    def columns(first, cols):
        part = per_member[:, :, first : first + cols]
        return jnp.moveaxis(part, 0, 1).reshape(part.shape[1], -1)

    gains = jnp.sum(per_member[:, :, qkv_cols + q_cols :], axis=0)
    return (
        output,
        grad_tokens,
        gains[:, 0],
        gains[:, 1],
        columns(0, q_cols),
        columns(q_cols, kv_cols),
        columns(q_cols + kv_cols, kv_cols),
        columns(qkv_cols, q_cols),
        sum_gate.reshape(-1, own_experts, ff),
        sum_up.reshape(-1, own_experts, ff),
        sum_down.reshape(-1, own_experts, ff),
    )


def shards_fast(
    tokens,
    cotangent,
    gain_attn,
    gain_ffn,
    w_query,
    key_weight,
    value_weight,
    w_out,
    expert_gate,
    expert_up,
    expert_down,
    expert_ids,
    gates,
    lengths,
    order,
):
    rows, width = tokens.shape
    members, devices = lax.axis_size("expert"), lax.axis_size("dp")
    span = rows * members
    own_experts, ff = expert_gate.shape[1], expert_gate.shape[2]
    capacity = rows * TOP // own_experts
    segment, position = layout(lengths[0], order[0], span)
    lane = jnp.arange(LANES, dtype=jnp.int32) % HEAD_SIZE
    half = HEAD_SIZE // 2
    frequency = rope_base ** (-((lane % half).astype(F32) * (2.0 / HEAD_SIZE)))
    angles = position[:, None] * frequency[None, :]
    cosine, sine = jnp.cos(angles), jnp.where(lane < half, -1.0, 1.0) * jnp.sin(angles)
    spare = (0, span - gain_attn.shape[0])
    small = jnp.stack(
        [segment.astype(F32), jnp.pad(gain_attn.astype(F32), spare), jnp.pad(gain_ffn.astype(F32), spare)]
    )
    (
        cot_all, route_all, pack_all, gate_all, up_all, down_all,
        normed_attn, qkv, kx, vx, probs, attended, residual, normed_all, gains,
    ) = forward_phase(
        members, tokens, cotangent, expert_ids.T, gates.T, w_query, key_weight, value_weight, w_out,
        small, *(w.transpose(1, 0, 2) for w in (expert_gate, expert_up, expert_down)), cosine, sine,
    )
    cot_all = cot_all.reshape(span, width)
    normed_all = normed_all.reshape(span, width)
    route_all = route_all.reshape(span, 2 * TOP)
    gate_all, up_all, down_all = (w.reshape(width, -1) for w in (gate_all, up_all, down_all))
    mixture, grad_normed, *by_kind = experts(
        own_experts, capacity, route_all, normed_all, cot_all, gate_all, up_all, down_all
    )
    by_kind = [one.reshape(devices, -1, own_experts * ff) for one in by_kind]

    output, grad_residual, gain_two_part, grad_attn_out, sum_gate, sum_up = third_phase(
        members, own_experts,
        grad_normed.reshape(members, rows, width),
        mixture.reshape(members, rows, width),
        residual,
        cotangent,
        gains,
        by_kind[0],
        by_kind[1],
    )
    (
        grad_tokens, grad_gains, d_query, d_key, d_value, d_out, d_down,
    ) = backward_phase(
        members, own_experts,
        grad_attn_out.reshape(span, width),
        grad_residual,
        gain_two_part,
        tokens,
        by_kind[2],
        gains,
        pack_all,
        normed_attn, qkv, kx, vx, probs, attended, cosine, sine,
    )
    return (
        output,
        grad_tokens,
        grad_gains[:, 0],
        grad_gains[:, 1],
        d_query,
        d_key,
        d_value,
        d_out,
        sum_gate.transpose(1, 0, 2),
        sum_up.transpose(1, 0, 2),
        d_down.transpose(1, 0, 2),
    )


def solution(mesh):
    both = P(("dp", "expert"), None)
    row, rows = P("dp"), P("dp", None)
    experts = P("dp", "expert", None)
    fast = mesh.shape["dp"] == 8 and mesh.shape["expert"] == 4
    return jax.shard_map(
        shards_fast if fast else shards_plain,
        mesh=mesh,
        in_specs=(both, both, row, row, rows, rows, rows, rows)
        + (experts, experts, experts, both, both, rows, rows),
        out_specs=(both, both, row, row, rows, rows, rows, rows, experts, experts, experts),
        check_vma=False,
    )
```

```python
import functools

import jax
import jax.numpy as jnp
from jax import lax
from jax.experimental import pallas as pl
from jax.experimental.pallas import tpu as pltpu
from jax.sharding import PartitionSpec as P

QUERY_HEADS = 24
KEY_VALUE_HEADS = 8
HEAD_SIZE = 64
TOP = 8

epsilon = 1e-06
rope_base = 10000.0
score_scale = 0.015625
branch_scale = 0.22
F32 = jnp.float32
BF16 = jnp.bfloat16
MESH = pl.DeviceIdType.MESH
LANES = 128
VMEM_LIMIT = 60 * 2**20


def layout(lengths_row, order_row, span):
    seqs = lengths_row.shape[0]
    slot_ids = jnp.arange(seqs, dtype=jnp.int32)
    picked = jnp.sum(
        jnp.where(order_row[:, None] == slot_ids[None, :], lengths_row[None, :], 0), axis=1
    )
    before = slot_ids[:, None] >= slot_ids[None, :]
    seq_ends = jnp.sum(jnp.where(before, picked[None, :], 0), axis=1)
    place = jnp.arange(span, dtype=jnp.int32)
    passed = place[:, None] >= seq_ends[None, :]
    segment = jnp.sum(passed.astype(jnp.int32), axis=1)
    start = jnp.sum(jnp.where(passed, picked[None, :], 0), axis=1)
    return segment, (place - start).astype(F32)


def rotation(position):
    half = HEAD_SIZE // 2
    frequency = rope_base ** (-(jnp.arange(half, dtype=F32) * (2.0 / HEAD_SIZE)))
    angles = position[:, None] * frequency[None, :]
    return jnp.cos(angles), jnp.sin(angles)


def rotate(rows, cosine, sine, back=False):
    t = rows.shape[0]
    heads = rows.reshape(t, -1, 2, HEAD_SIZE // 2)
    a, b = heads[:, :, 0], heads[:, :, 1]
    c, s = cosine[:, None, :], sine[:, None, :]
    if back:
        s = -s
    return jnp.stack([a * c - b * s, b * c + a * s], axis=2).reshape(t, -1)


def dot(a, b):
    return jnp.dot(a, b, preferred_element_type=F32)


def dot_nt(a, b):
    return jnp.einsum("tc,dc->td", a, b, preferred_element_type=F32)


def dot_tn(a, b):
    return jnp.einsum("td,tc->dc", a, b, preferred_element_type=F32)


def rms_factor(rows):
    return lax.rsqrt(jnp.mean(rows * rows, axis=-1, keepdims=True) + epsilon)


def norm_back(rows, factor, gain, grad):
    scaled = gain * grad
    return factor * scaled - rows * (factor * factor * factor) * jnp.mean(
        scaled * rows, axis=-1, keepdims=True
    )


def gather(x, axis):
    return lax.all_gather(x, axis, axis=0, tiled=True)


def scatter(x, axis):
    return lax.psum_scatter(x.astype(BF16), axis, scatter_dimension=0, tiled=True).astype(F32)


class Links:
    def __init__(self, send, recv, local, members):
        self.send, self.recv, self.local = send, recv, local
        self.remotes = self.locals = 0
        self.members = members
        self.d, self.z = lax.axis_index("dp"), lax.axis_index("expert")
        d = self.d
        core, x, y = d % 2, (d // 2) % 2, d // 4
        self.core = core
        self.sib = d + 1 - 2 * core
        self.x = d + 2 - 4 * x
        self.y = d + 4 - 8 * y
        self.diag = self.x + 4 - 8 * y
        self.waiting = []

    def other(self, d):
        return d + 1 - 2 * self.core

    def greet(self):
        barrier = pltpu.get_barrier_semaphore()
        last = self.members - 1

        def hello(d, z):
            pl.semaphore_signal(barrier, inc=1, device_id=(d, z), device_id_type=MESH)

        for d in (self.sib, self.x, self.y):
            hello(d, self.z)
        pl.when(self.z > 0)(lambda: hello(self.d, self.z - 1))
        pl.when(self.z < last)(lambda: hello(self.d, self.z + 1))
        ends = (self.z == 0).astype(jnp.int32) + (self.z == last).astype(jnp.int32)
        pl.semaphore_wait(barrier, 5 - ends)

    def remote(self, src, dst, to):
        k = self.remotes
        self.remotes += 1
        return pltpu.make_async_remote_copy(
            src_ref=src,
            dst_ref=dst,
            send_sem=self.send.at[k],
            recv_sem=self.recv.at[k],
            device_id=to,
            device_id_type=MESH,
        )

    def push(self, src, dst, d):
        copy = self.remote(src, dst, (d, self.z))
        copy.start()
        self.waiting.append(copy.wait_send)
        return copy

    def move(self, src, dst):
        k = self.locals
        self.locals += 1
        copy = pltpu.make_async_copy(src, dst, self.local.at[k])
        copy.start()
        return copy

    def finish(self):
        for wait in self.waiting:
            wait()


def run(order, **chains):
    for name in order:
        next(chains[name], None)
    chains = list(chains.values())
    while chains:
        for chain in list(chains):
            try:
                next(chain)
            except StopIteration:
                chains.remove(chain)


def line_gather(links, own, full):
    z, last = links.z, links.members - 1
    local = links.move(own, full.at[z])
    right, left = (links.d, z + 1), (links.d, z - 1)
    to_right, to_left = [], []
    for s in range(last):
        at_r, at_l = jnp.maximum(z - s, 0), jnp.minimum(z + s, last)
        to_right.append(links.remote(own if s == 0 else full.at[at_r], full.at[at_r], right))
        to_left.append(links.remote(own if s == 0 else full.at[at_l], full.at[at_l], left))
    for s in range(last):
        send_r, send_l = (z < last) & (z >= s), (z > 0) & (z + s <= last)
        pl.when(send_r)(to_right[s].start)
        pl.when(send_l)(to_left[s].start)
        yield
        pl.when((z > 0) & (z - 1 >= s))(to_right[s].wait_recv)
        pl.when((z < last) & (z + 1 + s <= last))(to_left[s].wait_recv)
    for s in range(last):
        send_r, send_l = (z < last) & (z >= s), (z > 0) & (z + s <= last)
        pl.when(send_r)(to_right[s].wait_send)
        pl.when(send_l)(to_left[s].wait_send)
    local.wait()


def add_rows(target, other, step=16):
    rows = target.shape[0]

    @pl.loop(0, rows // step)
    def _(i):
        at = pl.ds(pl.multiple_of(i * step, step), step)
        target[at] = (target[at].astype(F32) + other[at].astype(F32)).astype(target.dtype)


def line_sum(links, part, acc, from_left, from_right, finish, own=None, full=None, parts=2):
    z, last = links.z, links.members - 1
    rows = acc.shape[1] // parts
    spans = [pl.ds(h * rows, rows) for h in range(parts)]
    right, left = (links.d, z + 1), (links.d, z - 1)
    sum_r, sum_l, go_r, go_l, local = {}, {}, {}, {}, []
    for h, span in enumerate(spans):
        for o in range(last + 1):
            if o > 0:
                sum_r[h, o] = links.remote(acc.at[o, span], from_left.at[o, span], right)
            if o < last:
                sum_l[h, o] = links.remote(acc.at[o, span], from_right.at[o, span], left)
        for s in range(last if own is not None else 0):
            at_r, at_l = jnp.maximum(z - s, 0), jnp.minimum(z + s, last)
            here_r, here_l = full.at[at_r, span], full.at[at_l, span]
            go_r[h, s] = links.remote(own.at[span] if s == 0 else here_r, here_r, right)
            go_l[h, s] = links.remote(own.at[span] if s == 0 else here_l, here_l, left)

    def pass_right(h, o):
        @pl.when(z > 0)
        def _():
            sum_r[h, o].wait_recv()
            add_rows(acc.at[o, spans[h]], from_left.at[o, spans[h]])

        sum_r[h, o].start()

    def pass_left(h, o):
        @pl.when(z < last)
        def _():
            sum_l[h, o].wait_recv()
            add_rows(acc.at[o, spans[h]], from_right.at[o, spans[h]])

        sum_l[h, o].start()

    def send(h, s):
        pl.when((z < last) & (z >= s))(go_r[h, s].start)
        pl.when((z > 0) & (z + s <= last))(go_l[h, s].start)

    @pl.when(z == 0)
    def _():
        from_left[0] = jnp.zeros(from_left.shape[1:], from_left.dtype)

    @pl.when(z == last)
    def _():
        from_right[last] = jnp.zeros(from_right.shape[1:], from_right.dtype)

    made = set()
    for j in range(last):
        for o in (last - j, j):
            if o not in made:
                made.add(o)
                part(o)
        for h in range(parts):
            pl.when((z < last - j) & (2 * z < last))(functools.partial(pass_right, h, last - j))
            pl.when(z > j)(functools.partial(pass_left, h, j))
            pl.when((z < last - j) & (2 * z >= last))(functools.partial(pass_right, h, last - j))
            yield
    for h in range(parts):
        for o in range(last + 1):
            if o > 0:
                pl.when(z == o)(sum_r[h, o].wait_recv)
            if o < last:
                pl.when(z == o)(sum_l[h, o].wait_recv)
        finish(h * rows, rows)
        if own is None:
            continue
        send(h, 0)
        local.append(links.move(own.at[spans[h]], full.at[z, spans[h]]))
        yield
    for s in range(last if own is not None else 0):
        for h in range(parts):
            pl.when((z > 0) & (z - 1 >= s))(go_r[h, s].wait_recv)
            pl.when((z < last) & (z + 1 + s <= last))(go_l[h, s].wait_recv)
            if s + 1 < last:
                send(h, s + 1)
            yield
    for h in range(parts):
        for o in range(last + 1):
            if o > 0:
                pl.when(z < o)(sum_r[h, o].wait_send)
            if o < last:
                pl.when(z > o)(sum_l[h, o].wait_send)
        for s in range(last if own is not None else 0):
            pl.when((z < last) & (z >= s))(go_r[h, s].wait_send)
            pl.when((z > 0) & (z + s <= last))(go_l[h, s].wait_send)
    for copy in local:
        copy.wait()


def plane_gather(links, own, full):
    half = own.shape[0] // 2
    first, second = pl.ds(0, half), pl.ds(half, half)
    me = links.d
    local = links.move(own, full.at[me])
    by_x, by_y = {}, {}
    for by, d, h in ((by_y, links.y, first), (by_x, links.x, second), (by_x, links.x, first), (by_y, links.y, second)):
        by[h.start // half] = links.push(own.at[h], full.at[me, h], d)
    to_sib = [links.push(own, full.at[me], links.sib)]

    def share(d, h):
        to_sib.append(links.push(full.at[d, h], full.at[d, h], links.sib))

    yield
    by_y[0].wait_recv()
    over_x = links.push(full.at[links.y, first], full.at[links.y, first], links.x)
    share(links.y, first)
    by_x[1].wait_recv()
    over_y = links.push(full.at[links.x, second], full.at[links.x, second], links.y)
    share(links.x, second)
    yield
    by_x[0].wait_recv()
    share(links.x, first)
    by_y[1].wait_recv()
    share(links.y, second)
    yield
    over_x.wait_recv()
    share(links.diag, first)
    over_y.wait_recv()
    share(links.diag, second)
    yield
    for copy in to_sib:
        copy.wait_recv()
    local.wait()


def plane_scatter(links, part, mine, theirs, mid_x, mid_y, end_x, end_y):
    half = part.shape[1] // 2
    first, second = pl.ds(0, half), pl.ds(half, half)
    chips = (links.d, links.x, links.y, links.diag)
    from_sib, load = {}, {}
    held = [part.at[chip] if mine is None else mine.at[k] for k, chip in enumerate(chips)]
    for k in (3, 1, 2, 0):
        from_sib[k] = links.push(part.at[links.other(chips[k])], theirs.at[k], links.sib)
        if mine is not None:
            load[k] = links.move(part.at[chips[k]], held[k])
    yield
    for k in (3, 1, 2):
        if load:
            load[k].wait()
        from_sib[k].wait_recv()
        add_rows(held[k], theirs.at[k])
        if k == 3:
            to_mid_x = links.push(held[3].at[first], mid_x, links.x)
            to_mid_y = links.push(held[3].at[second], mid_y, links.y)
        if k == 1:
            to_end_x = links.push(held[1].at[first], end_x.at[first], links.x)
        if k == 2:
            to_end_y = links.push(held[2].at[second], end_y.at[second], links.y)
        if k != 1:
            yield
    to_mid_y.wait_recv()
    add_rows(held[1].at[second], mid_y)
    rest_x = links.push(held[1].at[second], end_x.at[second], links.x)
    to_mid_x.wait_recv()
    add_rows(held[2].at[first], mid_x)
    rest_y = links.push(held[2].at[first], end_y.at[first], links.y)
    yield
    if load:
        load[0].wait()
    from_sib[0].wait_recv()
    to_end_x.wait_recv()
    to_end_y.wait_recv()
    rest_x.wait_recv()
    rest_y.wait_recv()
    yield


def plane_scratch(rows, cols, mine=True):
    return [pltpu.VMEM((4, rows, cols), BF16)] * mine + [
        pltpu.VMEM((4, rows, cols), BF16),
        pltpu.VMEM((rows // 2, cols), BF16),
        pltpu.VMEM((rows // 2, cols), BF16),
        pltpu.VMEM((rows, cols), BF16),
        pltpu.VMEM((rows, cols), BF16),
    ]


def plane_result(mine, theirs, end_x, end_y, out, step=16):
    @pl.loop(0, out.shape[-2] // step)
    def _(i):
        at = pl.ds(pl.multiple_of(i * step, step), step)
        own = mine[at].astype(F32) + theirs[0, at].astype(F32)
        total = (own + end_x[at].astype(F32) + end_y[at].astype(F32)).astype(out.dtype)
        if len(out.shape) == 2:
            out[at] = total
        else:
            cols = out.shape[2]
            for e in range(out.shape[0]):
                out[e, at] = total[:, e * cols : (e + 1) * cols]


def plane_total(links, part, scratch, total, out, stores):
    yield from plane_scatter(links, part, *scratch)
    plane_result(scratch[0].at[0], scratch[1], scratch[4], scratch[5], total)
    stores.append(links.move(total, out))


def line_result(z, acc, from_left, from_right, at):
    return (
        acc[z, at].astype(F32) + from_left[z, at].astype(F32) + from_right[z, at].astype(F32)
    )


ANY = pl.BlockSpec(memory_space=pl.ANY)
VMEM = pl.BlockSpec(memory_space=pltpu.VMEM)


def comm_call(kernel, name, number, members, remotes, locals_, in_specs, out_specs, out_shape, scratch):
    return pl.pallas_call(
        functools.partial(kernel, members),
        out_shape=out_shape,
        in_specs=in_specs,
        out_specs=out_specs,
        scratch_shapes=[
            pltpu.SemaphoreType.DMA((remotes,)),
            pltpu.SemaphoreType.DMA((remotes,)),
            pltpu.SemaphoreType.DMA((locals_,)),
            *scratch,
        ],
        compiler_params=pltpu.CompilerParams(
            collective_id=number, has_side_effects=True, vmem_limit_bytes=VMEM_LIMIT
        ),
        name=name,
    )


def sds(shape, dtype):
    return jax.ShapeDtypeStruct(shape, dtype)


def third_kernel(members, part, mixture, residual, cot, gain, gate, up, output, grad_residual, gain_part, out_all, gate_out, up_out, send, recv, local, acc, from_left, from_right, acc_m, left_m, right_m, grad_out, gate_sum, up_sum, *rest):
    links = Links(send, recv, local, members)
    links.greet()
    for_gate, for_up = rest[:6], rest[6:]
    stores = []

    def finish(first, count):
        @pl.loop(0, count // 16)
        def _(i):
            at = pl.ds(pl.multiple_of(first + i * 16, 16), 16)
            grad = line_result(links.z, acc, from_left, from_right, at)
            here = residual[at]
            factor = rms_factor(here)
            gain_part[...] += jnp.sum(grad * here * factor, axis=0, keepdims=True)
            total = cot[at].astype(F32) + norm_back(here, factor, gain[1:2], grad)
            grad_residual[at] = total
            grad_out[at] = (branch_scale * total).astype(BF16)

    def chain():
        links.move(part, acc).wait()
        gain_part[...] = jnp.zeros(gain_part.shape, F32)
        yield from line_sum(
            links, lambda o: None, acc, from_left, from_right, finish, grad_out, out_all
        )

    def finish_mixture(first, count):
        @pl.loop(0, count // 16)
        def _(i):
            at = pl.ds(pl.multiple_of(first + i * 16, 16), 16)
            here = residual[at] + branch_scale * line_result(links.z, acc_m, left_m, right_m, at)
            output[at] = here.astype(BF16)

    def mixture_chain():
        links.move(mixture, acc_m).wait()
        yield from line_sum(links, lambda o: None, acc_m, left_m, right_m, finish_mixture)

    run(
        THIRD_ORDER,
        m=mixture_chain(),
        z=chain(),
        g=plane_total(links, gate, for_gate, gate_sum, gate_out, stores),
        u=plane_total(links, up, for_up, up_sum, up_out, stores),
    )
    for store in stores:
        store.wait()
    links.finish()


THIRD_ORDER = "uzuzzgugmmzzguzzzgzmzmzmmzmugguuzm"


def third_phase(members, own_experts, part, mixture, residual, cot, gain, gate, up):
    rows, width = cot.shape
    blocks = pltpu.VMEM((members, rows, width), BF16)
    return comm_call(
        third_kernel, "phase_three", 3, members, 80, 24,
        [ANY, ANY, VMEM, VMEM, VMEM, ANY, ANY], [VMEM, VMEM, VMEM, ANY, ANY, ANY],
        [
            sds((rows, width), BF16),
            sds((rows, width), F32),
            sds((1, width), F32),
            sds((members, rows, width), BF16),
            sds((own_experts, gate.shape[1], gate.shape[2] // own_experts), F32),
            sds((own_experts, up.shape[1], up.shape[2] // own_experts), F32),
        ],
        [blocks] * 6
        + [pltpu.VMEM((rows, width), BF16)]
        + [pltpu.VMEM((own_experts, gate.shape[1], gate.shape[2] // own_experts), F32)] * 2
        + plane_scratch(*gate.shape[1:])
        + plane_scratch(*up.shape[1:]),
    )(part, mixture, residual, cot, gain, gate, up)


def lane_ids(rows):
    return lax.broadcasted_iota(jnp.int32, (rows, LANES), 1)


def dims(a, b):
    return (((a,), (b,)), ((), ()))


def mm(a, b):
    return lax.dot_general(a, b, dims(1, 0), preferred_element_type=F32)


def mm_nt(a, b):
    return lax.dot_general(a, b, dims(1, 1), preferred_element_type=F32)


def mm_tn(a, b):
    return lax.dot_general(a, b, dims(0, 0), preferred_element_type=F32)


def first_lanes():
    same = lax.broadcasted_iota(jnp.int32, (16, LANES), 0) == lax.broadcasted_iota(jnp.int32, (16, LANES), 1)
    return same.astype(BF16)


def expert_kernel(capacity, own_experts, route, normed, cot, w_gate, w_up, w_down, mixture, grad_normed, d_gate, d_up, d_down, mix_sum, grad_sum, slot_cols, weight_cols, slot_rows):
    e = pl.program_id(0)
    span = normed.shape[0]

    @pl.when(e == 0)
    def _():
        mix_sum[...] = jnp.zeros(mix_sum.shape, F32)
        grad_sum[...] = jnp.zeros(grad_sum.shape, F32)
        lane = lane_ids(LANES)
        name = (lax.axis_index("expert") * own_experts + lane).astype(F32)
        name = jnp.where(lane < own_experts, name, -1.0)
        upto = (lane <= lax.broadcasted_iota(jnp.int32, (LANES, LANES), 0)).astype(BF16)
        before = jnp.zeros((1, LANES), F32)
        for b in range(span // LANES):
            at = pl.ds(b * LANES, LANES)
            chosen, weight = jnp.zeros((LANES, LANES), F32), jnp.zeros((LANES, LANES), F32)
            for k in range(TOP):
                named = route[at, k : k + 1] == name
                chosen = jnp.where(named, 1.0, chosen)
                weight = jnp.where(named, route[at, TOP + k : TOP + k + 1], weight)
            slot = mm(upto, chosen.astype(BF16)) + (before - 1.0)
            slot_cols[at] = jnp.where((chosen > 0.0) & (slot < capacity), slot, -1.0)
            weight_cols[at] = weight
            before = before + jnp.sum(chosen, axis=0, keepdims=True)
        slot_rows[...] = mm_nt(first_lanes(), slot_cols[...].astype(BF16))

    def column(values):
        return jnp.sum(jnp.where(lane_ids(span) == e, values[...], 0.0), axis=1, keepdims=True)

    slots = lax.broadcasted_iota(jnp.int32, (capacity, span), 0).astype(F32)
    pick = (slot_rows[pl.ds(e, 1)] == slots).astype(BF16)
    puts = column(slot_cols) == lax.broadcasted_iota(jnp.int32, (span, capacity), 1).astype(F32)
    put = puts.astype(BF16)
    gate_row = jnp.sum(jnp.where(puts, column(weight_cols), 0.0), axis=0, keepdims=True)
    same = lax.broadcasted_iota(jnp.int32, (capacity, capacity), 0) == lax.broadcasted_iota(jnp.int32, (capacity, capacity), 1)
    gate_col = jnp.sum(jnp.where(same, gate_row, 0.0), axis=1, keepdims=True)
    received = mm(pick, normed[...]).astype(BF16)
    pre_gate, pre_up = mm(received, w_gate[...]), mm(received, w_up[...])
    sig = 1.0 / (1.0 + jnp.exp(-pre_gate))
    silu = pre_gate * sig
    activ = (silu * pre_up).astype(BF16)
    produced = (gate_col * mm_nt(activ, w_down[...])).astype(BF16)
    mix_sum[...] += mm(put, produced)
    grad_out = (gate_col * (branch_scale * mm(pick, cot[...]))).astype(BF16)
    grad_activ = mm(grad_out, w_down[...])
    grad_gate = (grad_activ * pre_up * (sig * (1.0 + pre_gate * (1.0 - sig)))).astype(BF16)
    grad_up = (grad_activ * silu).astype(BF16)
    grad_pair = (mm_nt(grad_gate, w_gate[...]) + mm_nt(grad_up, w_up[...])).astype(BF16)
    grad_sum[...] += mm(put, grad_pair)
    d_gate[...] = mm_tn(received, grad_gate).astype(BF16)
    d_up[...] = mm_tn(received, grad_up).astype(BF16)
    d_down[...] = mm_tn(grad_out, activ).astype(BF16)

    @pl.when(e == pl.num_programs(0) - 1)
    def _():
        mixture[...] = mix_sum[...].astype(BF16)
        grad_normed[...] = grad_sum[...].astype(BF16)


def experts(own_experts, capacity, route, normed, cot, w_gate, w_up, w_down):
    span, width = normed.shape
    ff = w_gate.shape[1] // own_experts
    whole = pl.BlockSpec((span, width), lambda e: (0, 0))
    column = pl.BlockSpec((width, ff), lambda e: (0, e))
    grads = jax.ShapeDtypeStruct(w_gate.shape, BF16)
    rows = jax.ShapeDtypeStruct((span, width), BF16)
    return pl.pallas_call(
        functools.partial(expert_kernel, capacity, own_experts),
        grid=(own_experts,),
        in_specs=[pl.BlockSpec(route.shape, lambda e: (0, 0)), whole, whole, column, column, column],
        out_specs=[whole, whole, column, column, column],
        out_shape=[rows, rows, grads, grads, grads],
        scratch_shapes=[
            pltpu.VMEM((span, width), F32),
            pltpu.VMEM((span, width), F32),
            pltpu.VMEM((span, LANES), F32),
            pltpu.VMEM((span, LANES), F32),
            pltpu.VMEM((16, span), F32),
        ],
        compiler_params=pltpu.CompilerParams(vmem_limit_bytes=VMEM_LIMIT),
        name="experts",
    )(route, normed, cot, w_gate, w_up, w_down)


def turn(x, cosine, sine):
    half = HEAD_SIZE // 2
    ahead, behind = pltpu.roll(x, LANES - half, axis=1), pltpu.roll(x, half, axis=1)
    partner = jnp.where(lane_ids(x.shape[0]) % HEAD_SIZE < half, ahead, behind)
    return x * cosine + partner * sine


def spread(block, at, out):
    low = lane_ids(block.shape[0]) < HEAD_SIZE
    other = pltpu.roll(block, HEAD_SIZE, axis=1)
    zero = jnp.zeros_like(block)
    out[0, 0, at] = jnp.where(low, block, zero).astype(BF16)
    out[0, 1, at] = jnp.where(low, zero, other).astype(BF16)
    out[1, 0, at] = jnp.where(low, other, zero).astype(BF16)
    out[1, 1, at] = jnp.where(low, zero, block).astype(BF16)


def attention_setup(segment, bias):
    span = bias.shape[0]
    same = lax.broadcasted_iota(jnp.int32, (LANES, LANES), 0) == lane_ids(LANES)
    for b in range(span // LANES):
        at = pl.ds(b * LANES, LANES)
        row = b * LANES + lax.broadcasted_iota(jnp.int32, (LANES, span), 0)
        col = lax.broadcasted_iota(jnp.int32, (LANES, span), 1)
        here = segment[:, b * LANES : (b + 1) * LANES]
        here = jnp.sum(jnp.where(same, here, 0.0), axis=1, keepdims=True)
        ok = (here == segment) & (col <= row)
        bias[at] = jnp.where(ok, 0.0, -1e30)


def weight_columns(pack_all, first, cols):
    return pack_all[:, :, first : first + cols].reshape(-1, cols)


def gain_rows(pack_all, first):
    return mm_nt(first_lanes(), weight_columns(pack_all, first, LANES))


def attend_steps(qkv, kx, vx, bias, probs, attended):
    span, blocks = qkv.shape[0], attended.shape[1] // LANES
    repeat = QUERY_HEADS // KEY_VALUE_HEADS
    for j in range(blocks):
        for b in range(span // LANES):
            at, keys = pl.ds(b * LANES, LANES), (b + 1) * LANES
            q = qkv[at, j * LANES : (j + 1) * LANES]
            total = jnp.zeros((LANES, LANES), F32)
            for half in range(2):
                h = 2 * j + half
                kv = h // repeat
                scores = mm_nt(q, kx[kv, half, :keys]) + bias[at, :keys]
                peak = jnp.max(scores, axis=1, keepdims=True)
                exponent = jnp.exp(scores - peak)
                share = 1.0 / jnp.sum(exponent, axis=1, keepdims=True)
                low = (exponent * share).astype(BF16)
                probs[h, at, :keys] = low
                total += mm(low, vx[kv, half, :keys])
            attended[at, j * LANES : (j + 1) * LANES] = total.astype(BF16)
        yield


def forward_kernel(
    members, tokens, cot, ids, gates, w_query, w_key, w_value, w_out, small, gate, up, down, cosine, sine,
    cot_all, route_all, pack_out, gate_all, up_all, down_all, normed_out, qkv_out, kx_out, vx_out, probs_out, attended_out, residual, normed_all, gains,
    send, recv, local, pack, route, flat, tokens_all, bias, acc, from_left, from_right, normed,
    pack_all, normed_attn, qkv, kx, vx, probs, attended,
):
    links = Links(send, recv, local, members)
    stores = []
    count, _, cols = gate.shape
    loads = [
        [links.move(weight.at[e], flat.at[i, :, e * cols : (e + 1) * cols]) for e in range(count)]
        for i, weight in enumerate((gate, up, down))
    ]
    links.greet()
    route[...] = jnp.concatenate([ids[...].astype(F32), gates[...]], axis=0).T
    rows, width = tokens.shape
    span = rows * members
    q_cols = attended.shape[1]
    qkv_cols = qkv.shape[1]

    def pack_chain():
        loads, at = [], 0
        for weight in (w_query, w_key, w_value, w_out):
            cols = weight.shape[1] // members
            mine = pl.ds(pl.multiple_of(links.z * cols, LANES), cols)
            loads.append(links.move(weight.at[:, mine], pack.at[:, at : at + cols]))
            at += cols
        which = lax.broadcasted_iota(jnp.int32, (16, pack.shape[0]), 0)
        own = pack.shape[0]
        both = jnp.where(which == 0, small[1:2, :own], jnp.where(which == 1, small[2:3, :own], 0.0))
        pack[:, at:] = mm_tn(both.astype(BF16), first_lanes()).astype(BF16)
        for load in loads:
            load.wait()
        yield from plane_gather(links, pack, pack_all)

    def expert_chain(i, full):
        for load in loads[i]:
            load.wait()
        yield from plane_gather(links, flat.at[i], full)

    def produce(o):
        acc[o] = mm_nt(attended[o * rows : (o + 1) * rows], weight_columns(pack_all, qkv_cols, q_cols)).astype(BF16)

    def chain():
        attention_setup(small[0:1], bias)
        yield
        gains[...] = gain_rows(pack_all, qkv_cols + q_cols)

        @pl.loop(0, span // 16)
        def _(i):
            here = tokens_all[i // (rows // 16), pl.ds(pl.multiple_of(i % (rows // 16) * 16, 16), 16)].astype(F32)
            normed_attn[pl.ds(pl.multiple_of(i * 16, 16), 16)] = (here * rms_factor(here) * gains[0:1]).astype(BF16)

        @pl.loop(0, span // LANES)
        def _(i):
            at = pl.ds(pl.multiple_of(i * LANES, LANES), LANES)
            here = mm(normed_attn[at], weight_columns(pack_all, 0, qkv_cols))
            c, s = cosine[at], sine[at]
            for j in range(q_cols // LANES):
                lanes = slice(j * LANES, (j + 1) * LANES)
                qkv[at, lanes] = (turn(here[:, lanes], c, s).astype(BF16).astype(F32) * score_scale).astype(BF16)
            key = turn(here[:, q_cols : q_cols + LANES], c, s)
            value = here[:, q_cols + LANES :]
            qkv[at, q_cols : q_cols + LANES] = key.astype(BF16)
            qkv[at, q_cols + LANES :] = value.astype(BF16)
            spread(key, at, kx)
            spread(value, at, vx)

        yield
        yield from attend_steps(qkv, kx, vx, bias, probs, attended)
        for kept, out in (
            (pack_all, pack_out), (normed_attn, normed_out), (qkv, qkv_out), (kx, kx_out),
            (vx, vx_out), (probs, probs_out), (attended, attended_out),
        ):
            stores.append(links.move(kept, out))

        def finish(first, count):
            @pl.loop(0, count // 16)
            def _(i):
                at = pl.ds(pl.multiple_of(first + i * 16, 16), 16)
                here = tokens[at].astype(F32) + branch_scale * line_result(links.z, acc, from_left, from_right, at)
                residual[at] = here
                normed[at] = (here * rms_factor(here) * gains[1:2]).astype(BF16)

        yield from line_sum(links, produce, acc, from_left, from_right, finish, normed, normed_all)

    run(
        FORWARD_ORDER,
        t=line_gather(links, tokens, tokens_all),
        r=line_gather(links, route, route_all),
        c=line_gather(links, cot, cot_all),
        p=pack_chain(),
        g=expert_chain(0, gate_all),
        u=expert_chain(1, up_all),
        d=expert_chain(2, down_all),
        a=chain(),
    )
    for store in stores:
        store.wait()
    links.finish()


FORWARD_ORDER = "tptpdptpcaptgaaacdtrgatcaardaagdattpuparparadrpaarrd"


def forward_phase(members, tokens, cot, ids, gates, w_query, w_key, w_value, w_out, small, gate, up, down, cosine, sine):
    rows, width = tokens.shape
    q_cols = w_query.shape[1] // members
    qkv_cols = q_cols + 2 * w_key.shape[1] // members
    count, own, cols = gate.shape
    pack = (own, qkv_cols + q_cols + LANES)
    route, flat = (rows, 2 * ids.shape[0]), (own, count * cols)
    span = rows * members
    blocks = pltpu.VMEM((members, rows, width), BF16)
    heads = q_cols // HEAD_SIZE
    return comm_call(
        forward_kernel, "forward", 1, members, 120, 40,
        [VMEM, ANY, VMEM, VMEM, ANY, ANY, ANY, ANY, VMEM, ANY, ANY, ANY, VMEM, VMEM],
        [ANY] * 12 + [VMEM, ANY, VMEM],
        [
            sds((members, rows, width), BF16),
            sds((members, *route), F32),
            sds((8, *pack), BF16),
            sds((8, *flat), BF16),
            sds((8, *flat), BF16),
            sds((8, *flat), BF16),
            sds((span, width), BF16),
            sds((span, qkv_cols), BF16),
            sds((2, 2, span, LANES), BF16),
            sds((2, 2, span, LANES), BF16),
            sds((heads, span, span), BF16),
            sds((span, q_cols), BF16),
            sds((rows, width), F32),
            sds((members, rows, width), BF16),
            sds((16, width), F32),
        ],
        [
            pltpu.VMEM(pack, BF16),
            pltpu.VMEM(route, F32),
            pltpu.VMEM((3, *flat), BF16),
            blocks,
            pltpu.VMEM((span, span), F32),
            blocks,
            blocks,
            blocks,
            pltpu.VMEM((rows, width), BF16),
            pltpu.VMEM((8, *pack), BF16),
            pltpu.VMEM((span, width), BF16),
            pltpu.VMEM((span, qkv_cols), BF16),
            pltpu.VMEM((2, 2, span, LANES), BF16),
            pltpu.VMEM((2, 2, span, LANES), BF16),
            pltpu.VMEM((heads, span, span), BF16),
            pltpu.VMEM((span, q_cols), BF16),
        ],
    )(tokens, cot, ids, gates, w_query, w_key, w_value, w_out, small, gate, up, down, cosine, sine)


def attend_back_steps(qkv, kx, vx, probs, grad_attended, cosine, sine, grad_k, grad_v, grad_qkv):
    span = qkv.shape[0]
    blocks = grad_attended.shape[1] // LANES
    repeat = QUERY_HEADS // KEY_VALUE_HEADS
    grad_k[...] = jnp.zeros(grad_k.shape, F32)
    grad_v[...] = jnp.zeros(grad_v.shape, F32)
    for j in range(blocks):
        lanes = slice(j * LANES, (j + 1) * LANES)
        for b in range(span // LANES):
            at, keys = pl.ds(b * LANES, LANES), (b + 1) * LANES
            q, grad = qkv[at, lanes], grad_attended[at, lanes]
            total = jnp.zeros((LANES, LANES), F32)
            for half in range(2):
                h = 2 * j + half
                kv = h // repeat
                low = probs[h, at, :keys]
                share = low.astype(F32)
                grad_probs = mm_nt(grad, vx[kv, half, :keys])
                inner = jnp.sum(share * grad_probs, axis=1, keepdims=True)
                grad_scores = (share * (grad_probs - inner)).astype(BF16)
                total += mm(grad_scores, kx[kv, half, :keys])
                grad_k[kv, half, :keys] += mm_tn(grad_scores, q)
                grad_v[kv, half, :keys] += mm_tn(low, grad)
            grad_qkv[at, lanes] = turn(total * score_scale, cosine[at], -sine[at]).astype(BF16)
        yield
    first = blocks * LANES

    def fold(parts, at):
        low = lane_ids(LANES) < HEAD_SIZE
        same = jnp.where(low, parts[0, 0, at], parts[1, 1, at])
        crossed = jnp.where(low, parts[1, 0, at], parts[0, 1, at])
        return same + pltpu.roll(crossed, HEAD_SIZE, axis=1)

    for b in range(span // LANES):
        at = pl.ds(b * LANES, LANES)
        grad_qkv[at, first : first + LANES] = turn(fold(grad_k, at), cosine[at], -sine[at]).astype(BF16)
        grad_qkv[at, first + LANES :] = fold(grad_v, at).astype(BF16)


def backward_kernel(
    members, grad_out_in, grad_residual, gain_ffn_part, tokens, down, row_gains, pack_in, normed_in, qkv_in, kx_in, vx_in, probs_in, attended_in, cosine, sine,
    grad_tokens, gains, d_query, d_key, d_value, d_out, down_out,
    send, recv, local, acc, from_left, from_right, grad_attended, grad_k, grad_v, grad_qkv, gain_part,
    for_w_out, for_w_query, for_rest, own_out, own_query, own_rest, all_out, all_query, all_rest,
    grad_out_all, pack_all, normed_attn, qkv, kx, vx, probs, attended, d_down, *rest,
):
    links = Links(send, recv, local, members)
    loads = {
        "attended": links.move(attended_in, attended),
        "grad": links.move(grad_out_in, grad_out_all),
        "pack": links.move(pack_in, pack_all),
        "qkv": links.move(qkv_in, qkv),
        "kx": links.move(kx_in, kx),
        "vx": links.move(vx_in, vx),
        "probs": links.move(probs_in, probs),
        "normed": links.move(normed_in, normed_attn),
    }
    stores = []

    def need(*names):
        for name in names:
            if name in loads:
                loads.pop(name).wait()

    links.greet()
    rows, width = tokens.shape
    q_cols, qkv_cols = attended.shape[1], qkv.shape[1]
    kv_cols = (qkv_cols - q_cols) // 2
    with_out, with_query, with_rest, with_down = rest[:5], rest[5:10], rest[10:15], rest[15:]
    pairs = for_w_out.shape[0] // 2
    step = width // pairs

    def weight_term(rows_of, grads, out, cols):
        for i in range(pairs):
            term = mm_tn(rows_of[:, i * step : (i + 1) * step], grads)
            out[2 * i : 2 * i + 2, :, :cols] = term.astype(BF16).reshape(2, step // 2, cols)

    def put_out():
        for m in range(members):
            d_out[:, m * q_cols : (m + 1) * q_cols] = all_out[m].astype(F32)

    def put_query():
        for m in range(members):
            d_query[:, m * q_cols : (m + 1) * q_cols] = all_query[m].astype(F32)

    def put_rest():
        for m in range(members):
            d_key[:, m * kv_cols : (m + 1) * kv_cols] = all_rest[m, :, :kv_cols].astype(F32)
            d_value[:, m * kv_cols : (m + 1) * kv_cols] = all_rest[m, :, kv_cols : 2 * kv_cols].astype(F32)
        gains[...] = sum(all_rest[m, :, 2 * kv_cols :].astype(F32) for m in range(members))

    def weight_chain(fill, part, mine, full, scratch, put):
        fill()
        yield from plane_scatter(links, part, None, *scratch)
        plane_result(part.at[links.d], scratch[0], scratch[3], scratch[4], mine)
        yield from line_gather(links, mine, full)
        put()

    def fill_out():
        need("grad", "attended")
        weight_term(grad_out_all, attended[...], for_w_out, q_cols)

    def fill_query():
        need("normed")
        weight_term(normed_attn, grad_qkv[:, :q_cols], for_w_query, q_cols)

    def fill_rest():
        weight_term(normed_attn, grad_qkv[:, q_cols:], for_rest, 2 * kv_cols)
        which = lax.broadcasted_iota(jnp.int32, (16, width), 0)
        both = jnp.where(which == 0, gain_part[...] / row_gains[0:1], jnp.where(which == 1, gain_ffn_part[...], 0.0))
        columns = mm_tn(both.astype(BF16), first_lanes())
        for_rest[:, :, 2 * kv_cols :] = columns.astype(BF16).reshape(2 * pairs, step // 2, LANES)

    def produce(o):
        at = slice(o * rows, (o + 1) * rows)
        part = mm_nt(grad_qkv[at], weight_columns(pack_all, 0, qkv_cols))
        gain_part[...] += jnp.sum(part * normed_attn[at].astype(F32), axis=0, keepdims=True)
        acc[o] = part.astype(BF16)

    def chain():
        need("grad", "pack")
        wo = weight_columns(pack_all, qkv_cols, q_cols)

        @pl.loop(0, grad_attended.shape[0] // LANES)
        def _(i):
            at = pl.ds(pl.multiple_of(i * LANES, LANES), LANES)
            grad_attended[at] = mm(grad_out_all[at], wo).astype(BF16)

        yield
        need("qkv", "kx", "vx", "probs")
        yield from attend_back_steps(qkv, kx, vx, probs, grad_attended, cosine, sine, grad_k, grad_v, grad_qkv)
        gain_part[...] = jnp.zeros(gain_part.shape, F32)
        need("normed")
        yield

        def finish(first, count):
            @pl.loop(0, count // 16)
            def _(i):
                at = pl.ds(pl.multiple_of(first + i * 16, 16), 16)
                grad = line_result(links.z, acc, from_left, from_right, at)
                here = tokens[at].astype(F32)
                grad_tokens[at] = grad_residual[at] + norm_back(here, rms_factor(here), row_gains[0:1], grad)

        yield from line_sum(links, produce, acc, from_left, from_right, finish)

    run(
        BACKWARD_ORDER,
        d=plane_total(links, down, with_down, d_down, down_out, stores),
        o=weight_chain(fill_out, for_w_out, own_out, all_out, with_out, put_out),
        a=chain(),
        q=weight_chain(fill_query, for_w_query, own_query, all_query, with_query, put_query),
        r=weight_chain(fill_rest, for_rest, own_rest, all_rest, with_rest, put_rest),
    )
    for store in stores:
        store.wait()
    links.finish()


BACKWARD_ORDER = "oadoaoaoaooqaqqdoaqdaqqarorarradrraqrqdaoodaaqdrddrr"


def backward_phase(members, own_experts, grad_out_all, grad_residual, gain_ffn_part, tokens, down, row_gains, pack_all, normed_attn, qkv, kx, vx, probs, attended, cosine, sine):
    rows, width = tokens.shape
    span, q_cols = attended.shape
    qkv_cols = qkv.shape[1]
    kv_cols = (qkv_cols - q_cols) // 2
    devices, own = down.shape[:2]
    line = [pltpu.VMEM((members, rows, width), BF16)] * 3
    three = (q_cols, q_cols, 2 * kv_cols + LANES)
    return comm_call(
        backward_kernel, "backward", 4, members, 100, 32,
        [ANY, VMEM, VMEM, VMEM, ANY, VMEM] + [ANY] * 7 + [VMEM] * 2,
        [VMEM] * 6 + [ANY],
        [
            sds((rows, width), F32),
            sds((own, LANES), F32),
            sds((own, members * q_cols), F32),
            sds((own, members * kv_cols), F32),
            sds((own, members * kv_cols), F32),
            sds((own, members * q_cols), F32),
            sds((own_experts, own, down.shape[2] // own_experts), F32),
        ],
        [
            *line,
            pltpu.VMEM((span, q_cols), BF16),
            pltpu.VMEM((2, 2, span, LANES), F32),
            pltpu.VMEM((2, 2, span, LANES), F32),
            pltpu.VMEM((span, qkv_cols), BF16),
            pltpu.VMEM((1, width), F32),
            *[pltpu.VMEM((devices, own, cols), BF16) for cols in three],
            *[pltpu.VMEM((own, cols), BF16) for cols in three],
            *[pltpu.VMEM((members, own, cols), BF16) for cols in three],
            *[pltpu.VMEM(a.shape, BF16) for a in (grad_out_all, pack_all, normed_attn, qkv, kx, vx, probs, attended)],
            pltpu.VMEM((own_experts, own, down.shape[2] // own_experts), F32),
            *[one for cols in three for one in plane_scratch(own, cols, False)],
            *plane_scratch(*down.shape[1:]),
        ],
    )(grad_out_all, grad_residual, gain_ffn_part, tokens, down, row_gains, pack_all, normed_attn, qkv, kx, vx, probs, attended, cosine, sine)


def all_blocks(x, axis):
    return lax.all_gather(x, axis, axis=0)


def plain_first(members, tokens, cot, route, pack, gate):
    return (
        all_blocks(tokens, "expert"),
        all_blocks(cot, "expert"),
        all_blocks(route, "expert"),
        all_blocks(pack, "dp"),
        all_blocks(gate, "dp"),
    )


def line_total(part):
    return scatter(part.reshape(-1, part.shape[2]), "expert")


def plain_second(members, part, tokens, gain, up, down):
    residual = tokens.astype(F32) + branch_scale * line_total(part)
    normed = (residual * rms_factor(residual) * gain).astype(BF16)
    return residual, all_blocks(normed, "expert"), all_blocks(up, "dp"), all_blocks(down, "dp")


def plane_sum(part):
    return scatter(part.reshape(-1, part.shape[2]), "dp")


def plain_third(members, part, residual, cot, gain, gate, up):
    grad = line_total(part)
    factor = rms_factor(residual)
    gain_part = jnp.sum(grad * residual * factor, axis=0, keepdims=True)
    total = cot.astype(F32) + norm_back(residual, factor, gain, grad)
    out_all = all_blocks((branch_scale * total).astype(BF16), "expert")
    return total, gain_part, out_all, plane_sum(gate), plane_sum(up)


def plain_fourth(members, part, grad_residual, tokens, gain, pack, down):
    here = tokens.astype(F32)
    grad_tokens = grad_residual + norm_back(here, rms_factor(here), gain, line_total(part))
    return grad_tokens, all_blocks(plane_sum(pack).astype(BF16), "expert"), plane_sum(down)


def attend_forward(q, k, v, allowed):
    scores = jnp.einsum("irh,jh->rij", q, k, preferred_element_type=F32) * score_scale
    scores = jnp.where(allowed[None], scores, -1e30)
    peak = jnp.max(scores, axis=-1, keepdims=True)
    exponent = jnp.exp(scores - peak)
    total = jnp.sum(exponent, axis=-1, keepdims=True)
    probs = exponent / total
    return jnp.einsum("rij,jh->irh", probs.astype(BF16), v, preferred_element_type=F32), probs


def attend_backward(q, k, v, probs, grad, allowed):
    grad_probs = jnp.einsum("irh,jh->rij", grad, v, preferred_element_type=F32)
    inner = jnp.sum(probs * grad_probs, axis=-1, keepdims=True)
    grad_scores = (probs * (grad_probs - inner)).astype(BF16)
    grad_q = jnp.einsum("rij,jh->irh", grad_scores, k, preferred_element_type=F32) * score_scale
    grad_k = jnp.einsum("rij,irh->jh", grad_scores, q, preferred_element_type=F32) * score_scale
    grad_v = jnp.einsum("rij,irh->jh", probs.astype(BF16), grad, preferred_element_type=F32)
    return grad_q, grad_k, grad_v


def shards_plain(
    tokens,
    cotangent,
    gain_attn,
    gain_ffn,
    w_query,
    key_weight,
    value_weight,
    w_out,
    expert_gate,
    expert_up,
    expert_down,
    expert_ids,
    gates,
    lengths,
    order,
):
    rows, width = tokens.shape
    members = lax.axis_size("expert")
    member = lax.axis_index("expert")
    span = rows * members
    own_experts, ff = expert_gate.shape[1], expert_gate.shape[2]
    capacity = rows * TOP // own_experts
    q_cols = w_query.shape[1] // members
    kv_cols = key_weight.shape[1] // members
    kv_heads = kv_cols // HEAD_SIZE
    repeat = QUERY_HEADS // KEY_VALUE_HEADS

    def mine(weight, cols):
        return lax.dynamic_slice_in_dim(weight, member * cols, cols, axis=1)

    devices = lax.axis_size("dp")
    phases = [
        functools.partial(phase, members)
        for phase in (plain_first, plain_second, plain_third, plain_fourth)
    ]

    pack = jnp.concatenate(
        [
            mine(w_query, q_cols),
            mine(key_weight, kv_cols),
            mine(value_weight, kv_cols),
            mine(w_out, q_cols),
            gain_attn[:, None],
            gain_ffn[:, None],
            jnp.zeros((gain_attn.shape[0], 126), BF16),
        ],
        axis=1,
    )
    route = jnp.concatenate([expert_ids.astype(F32), gates], axis=1)
    tokens_all, cot_all, route_all, pack_all, gate_all = phases[0](
        tokens, cotangent, route, pack, expert_gate.reshape(-1, own_experts * ff)
    )
    tokens_all = tokens_all.reshape(span, width).astype(F32)
    cot_all = cot_all.reshape(span, width)
    route_all = route_all.reshape(span, 2 * TOP)
    pack_all = pack_all.reshape(width, -1)
    gate_all = gate_all.reshape(width, -1)
    qkv_cols = q_cols + 2 * kv_cols
    w_qkv = pack_all[:, :qkv_cols]
    wo = pack_all[:, qkv_cols : qkv_cols + q_cols]
    gain_one = pack_all[:, qkv_cols + q_cols].astype(F32)[None]
    gain_two = pack_all[:, qkv_cols + q_cols + 1].astype(F32)[None]

    segment, position = layout(lengths[0], order[0], span)
    cosine, sine = rotation(position)
    place = jnp.arange(span, dtype=jnp.int32)
    allowed = (segment[:, None] == segment[None, :]) & (place[None, :] <= place[:, None])
    factor_one = rms_factor(tokens_all)
    normed_attn = (tokens_all * factor_one * gain_one).astype(BF16)
    qkv = dot(normed_attn, w_qkv)
    qk = rotate(qkv[:, : q_cols + kv_cols], cosine, sine).astype(BF16)
    v = qkv[:, q_cols + kv_cols :].astype(BF16)
    q_heads = jnp.moveaxis(qk[:, :q_cols].reshape(span, kv_heads, repeat, HEAD_SIZE), 1, 0)
    k_heads = jnp.moveaxis(qk[:, q_cols:].reshape(span, kv_heads, HEAD_SIZE), 1, 0)
    v_heads = jnp.moveaxis(v.reshape(span, kv_heads, HEAD_SIZE), 1, 0)
    attended, probs = jax.vmap(functools.partial(attend_forward, allowed=allowed))(
        q_heads, k_heads, v_heads
    )
    attended = jnp.moveaxis(attended, 0, 1).reshape(span, q_cols).astype(BF16)
    attn_part = dot_nt(attended, wo).astype(BF16).reshape(members, rows, width)
    residual, normed_all, up_all, down_all = phases[1](
        attn_part,
        tokens,
        gain_two,
        expert_up.reshape(-1, own_experts * ff),
        expert_down.reshape(-1, own_experts * ff),
    )
    normed_all = normed_all.reshape(span, width)
    up_all, down_all = up_all.reshape(width, -1), down_all.reshape(width, -1)

    mixture, grad_normed, *by_kind = experts(
        own_experts, capacity, route_all, normed_all, cot_all, gate_all, up_all, down_all
    )
    output = (residual + branch_scale * scatter(mixture, "expert")).astype(BF16)
    by_kind = [one.reshape(devices, -1, own_experts * ff) for one in by_kind]

    grad_residual, gain_two_part, grad_attn_out, sum_gate, sum_up = phases[2](
        grad_normed.reshape(members, rows, width),
        residual,
        cotangent,
        gain_two,
        by_kind[0],
        by_kind[1],
    )
    grad_attn_out = grad_attn_out.reshape(span, width)
    term_out = dot_tn(grad_attn_out, attended)
    grad_attended = dot(grad_attn_out, wo).astype(BF16)
    grad_heads = jnp.moveaxis(grad_attended.reshape(span, kv_heads, repeat, HEAD_SIZE), 1, 0)
    grad_q, grad_k, grad_v = jax.vmap(functools.partial(attend_backward, allowed=allowed))(
        q_heads, k_heads, v_heads, probs, grad_heads
    )
    grad_qk = jnp.concatenate(
        [
            jnp.moveaxis(grad_q, 0, 1).reshape(span, q_cols),
            jnp.moveaxis(grad_k, 0, 1).reshape(span, kv_cols),
        ],
        axis=1,
    )
    grad_qkv = jnp.concatenate(
        [
            rotate(grad_qk, cosine, sine, back=True).astype(BF16),
            jnp.moveaxis(grad_v, 0, 1).reshape(span, kv_cols).astype(BF16),
        ],
        axis=1,
    )
    grad_norm_part = dot_nt(grad_qkv, w_qkv)
    gain_one_part = jnp.sum(grad_norm_part * tokens_all * factor_one, axis=0)
    term_qkv = dot_tn(normed_attn, grad_qkv)
    packed_grads = jnp.concatenate(
        [
            term_qkv,
            term_out,
            gain_one_part[:, None],
            gain_two_part.reshape(-1, 1),
            jnp.zeros((width, 126), F32),
        ],
        axis=1,
    )
    grad_tokens, per_member, sum_down = phases[3](
        grad_norm_part.astype(BF16).reshape(members, rows, width),
        grad_residual,
        tokens,
        gain_one,
        packed_grads.astype(BF16).reshape(devices, -1, packed_grads.shape[1]),
        by_kind[2],
    )
    per_member = per_member.astype(F32)

    def columns(first, cols):
        part = per_member[:, :, first : first + cols]
        return jnp.moveaxis(part, 0, 1).reshape(part.shape[1], -1)

    gains = jnp.sum(per_member[:, :, qkv_cols + q_cols :], axis=0)
    return (
        output,
        grad_tokens,
        gains[:, 0],
        gains[:, 1],
        columns(0, q_cols),
        columns(q_cols, kv_cols),
        columns(q_cols + kv_cols, kv_cols),
        columns(qkv_cols, q_cols),
        sum_gate.reshape(-1, own_experts, ff),
        sum_up.reshape(-1, own_experts, ff),
        sum_down.reshape(-1, own_experts, ff),
    )


def shards_fast(
    tokens,
    cotangent,
    gain_attn,
    gain_ffn,
    w_query,
    key_weight,
    value_weight,
    w_out,
    expert_gate,
    expert_up,
    expert_down,
    expert_ids,
    gates,
    lengths,
    order,
):
    rows, width = tokens.shape
    members, devices = lax.axis_size("expert"), lax.axis_size("dp")
    span = rows * members
    own_experts, ff = expert_gate.shape[1], expert_gate.shape[2]
    capacity = rows * TOP // own_experts
    segment, position = layout(lengths[0], order[0], span)
    lane = jnp.arange(LANES, dtype=jnp.int32) % HEAD_SIZE
    half = HEAD_SIZE // 2
    frequency = rope_base ** (-((lane % half).astype(F32) * (2.0 / HEAD_SIZE)))
    angles = position[:, None] * frequency[None, :]
    cosine, sine = jnp.cos(angles), jnp.where(lane < half, -1.0, 1.0) * jnp.sin(angles)
    spare = (0, span - gain_attn.shape[0])
    small = jnp.stack(
        [segment.astype(F32), jnp.pad(gain_attn.astype(F32), spare), jnp.pad(gain_ffn.astype(F32), spare)]
    )
    (
        cot_all, route_all, pack_all, gate_all, up_all, down_all,
        normed_attn, qkv, kx, vx, probs, attended, residual, normed_all, gains,
    ) = forward_phase(
        members, tokens, cotangent, expert_ids.T, gates.T, w_query, key_weight, value_weight, w_out,
        small, *(w.transpose(1, 0, 2) for w in (expert_gate, expert_up, expert_down)), cosine, sine,
    )
    cot_all = cot_all.reshape(span, width)
    normed_all = normed_all.reshape(span, width)
    route_all = route_all.reshape(span, 2 * TOP)
    gate_all, up_all, down_all = (w.reshape(width, -1) for w in (gate_all, up_all, down_all))
    mixture, grad_normed, *by_kind = experts(
        own_experts, capacity, route_all, normed_all, cot_all, gate_all, up_all, down_all
    )
    by_kind = [one.reshape(devices, -1, own_experts * ff) for one in by_kind]

    output, grad_residual, gain_two_part, grad_attn_out, sum_gate, sum_up = third_phase(
        members, own_experts,
        grad_normed.reshape(members, rows, width),
        mixture.reshape(members, rows, width),
        residual,
        cotangent,
        gains,
        by_kind[0],
        by_kind[1],
    )
    (
        grad_tokens, grad_gains, d_query, d_key, d_value, d_out, d_down,
    ) = backward_phase(
        members, own_experts,
        grad_attn_out.reshape(span, width),
        grad_residual,
        gain_two_part,
        tokens,
        by_kind[2],
        gains,
        pack_all,
        normed_attn, qkv, kx, vx, probs, attended, cosine, sine,
    )
    return (
        output,
        grad_tokens,
        grad_gains[:, 0],
        grad_gains[:, 1],
        d_query,
        d_key,
        d_value,
        d_out,
        sum_gate.transpose(1, 0, 2),
        sum_up.transpose(1, 0, 2),
        d_down.transpose(1, 0, 2),
    )


def solution(mesh):
    both = P(("dp", "expert"), None)
    row, rows = P("dp"), P("dp", None)
    experts = P("dp", "expert", None)
    fast = mesh.shape["dp"] == 8 and mesh.shape["expert"] == 4
    return jax.shard_map(
        shards_fast if fast else shards_plain,
        mesh=mesh,
        in_specs=(both, both, row, row, rows, rows, rows, rows)
        + (experts, experts, experts, both, both, rows, rows),
        out_specs=(both, both, row, row, rows, rows, rows, rows, experts, experts, experts),
        check_vma=False,
    )
```

```python
import functools

import jax
import jax.numpy as jnp
from jax import lax
from jax.experimental import pallas as pl
from jax.experimental.pallas import tpu as pltpu
from jax.sharding import PartitionSpec as P

QUERY_HEADS = 24
KEY_VALUE_HEADS = 8
HEAD_SIZE = 64
TOP = 8

epsilon = 1e-06
rope_base = 10000.0
score_scale = 0.015625
branch_scale = 0.22
F32 = jnp.float32
BF16 = jnp.bfloat16
MESH = pl.DeviceIdType.MESH
LANES = 128
VMEM_LIMIT = 60 * 2**20


def layout(lengths_row, order_row, span):
    seqs = lengths_row.shape[0]
    slot_ids = jnp.arange(seqs, dtype=jnp.int32)
    picked = jnp.sum(
        jnp.where(order_row[:, None] == slot_ids[None, :], lengths_row[None, :], 0), axis=1
    )
    before = slot_ids[:, None] >= slot_ids[None, :]
    seq_ends = jnp.sum(jnp.where(before, picked[None, :], 0), axis=1)
    place = jnp.arange(span, dtype=jnp.int32)
    passed = place[:, None] >= seq_ends[None, :]
    segment = jnp.sum(passed.astype(jnp.int32), axis=1)
    start = jnp.sum(jnp.where(passed, picked[None, :], 0), axis=1)
    return segment, (place - start).astype(F32)


def rotation(position):
    half = HEAD_SIZE // 2
    frequency = rope_base ** (-(jnp.arange(half, dtype=F32) * (2.0 / HEAD_SIZE)))
    angles = position[:, None] * frequency[None, :]
    return jnp.cos(angles), jnp.sin(angles)


def rotate(rows, cosine, sine, back=False):
    t = rows.shape[0]
    heads = rows.reshape(t, -1, 2, HEAD_SIZE // 2)
    a, b = heads[:, :, 0], heads[:, :, 1]
    c, s = cosine[:, None, :], sine[:, None, :]
    if back:
        s = -s
    return jnp.stack([a * c - b * s, b * c + a * s], axis=2).reshape(t, -1)


def dot(a, b):
    return jnp.dot(a, b, preferred_element_type=F32)


def dot_nt(a, b):
    return jnp.einsum("tc,dc->td", a, b, preferred_element_type=F32)


def dot_tn(a, b):
    return jnp.einsum("td,tc->dc", a, b, preferred_element_type=F32)


def rms_factor(rows):
    return lax.rsqrt(jnp.mean(rows * rows, axis=-1, keepdims=True) + epsilon)


def norm_back(rows, factor, gain, grad):
    scaled = gain * grad
    return factor * scaled - rows * (factor * factor * factor) * jnp.mean(
        scaled * rows, axis=-1, keepdims=True
    )


def gather(x, axis):
    return lax.all_gather(x, axis, axis=0, tiled=True)


def scatter(x, axis):
    return lax.psum_scatter(x.astype(BF16), axis, scatter_dimension=0, tiled=True).astype(F32)


class Links:
    def __init__(self, send, recv, local, members):
        self.send, self.recv, self.local = send, recv, local
        self.remotes = self.locals = 0
        self.members = members
        self.d, self.z = lax.axis_index("dp"), lax.axis_index("expert")
        d = self.d
        core, x, y = d % 2, (d // 2) % 2, d // 4
        self.core = core
        self.sib = d + 1 - 2 * core
        self.x = d + 2 - 4 * x
        self.y = d + 4 - 8 * y
        self.diag = self.x + 4 - 8 * y
        self.waiting = []

    def other(self, d):
        return d + 1 - 2 * self.core

    def greet(self):
        barrier = pltpu.get_barrier_semaphore()
        last = self.members - 1

        def hello(d, z):
            pl.semaphore_signal(barrier, inc=1, device_id=(d, z), device_id_type=MESH)

        for d in (self.sib, self.x, self.y):
            hello(d, self.z)
        pl.when(self.z > 0)(lambda: hello(self.d, self.z - 1))
        pl.when(self.z < last)(lambda: hello(self.d, self.z + 1))
        ends = (self.z == 0).astype(jnp.int32) + (self.z == last).astype(jnp.int32)
        pl.semaphore_wait(barrier, 5 - ends)

    def remote(self, src, dst, to):
        k = self.remotes
        self.remotes += 1
        return pltpu.make_async_remote_copy(
            src_ref=src,
            dst_ref=dst,
            send_sem=self.send.at[k],
            recv_sem=self.recv.at[k],
            device_id=to,
            device_id_type=MESH,
        )

    def push(self, src, dst, d):
        copy = self.remote(src, dst, (d, self.z))
        copy.start()
        self.waiting.append(copy.wait_send)
        return copy

    def move(self, src, dst):
        k = self.locals
        self.locals += 1
        copy = pltpu.make_async_copy(src, dst, self.local.at[k])
        copy.start()
        return copy

    def finish(self):
        for wait in self.waiting:
            wait()


def run(order, **chains):
    for name in order:
        next(chains[name], None)
    chains = list(chains.values())
    while chains:
        for chain in list(chains):
            try:
                next(chain)
            except StopIteration:
                chains.remove(chain)


def line_gather(links, own, full):
    z, last = links.z, links.members - 1
    local = links.move(own, full.at[z])
    right, left = (links.d, z + 1), (links.d, z - 1)
    to_right, to_left = [], []
    for s in range(last):
        at_r, at_l = jnp.maximum(z - s, 0), jnp.minimum(z + s, last)
        to_right.append(links.remote(own if s == 0 else full.at[at_r], full.at[at_r], right))
        to_left.append(links.remote(own if s == 0 else full.at[at_l], full.at[at_l], left))
    for s in range(last):
        send_r, send_l = (z < last) & (z >= s), (z > 0) & (z + s <= last)
        pl.when(send_r)(to_right[s].start)
        pl.when(send_l)(to_left[s].start)
        yield
        pl.when((z > 0) & (z - 1 >= s))(to_right[s].wait_recv)
        pl.when((z < last) & (z + 1 + s <= last))(to_left[s].wait_recv)
    for s in range(last):
        send_r, send_l = (z < last) & (z >= s), (z > 0) & (z + s <= last)
        pl.when(send_r)(to_right[s].wait_send)
        pl.when(send_l)(to_left[s].wait_send)
    local.wait()


def add_rows(target, other, step=16):
    rows = target.shape[0]

    @pl.loop(0, rows // step)
    def _(i):
        at = pl.ds(pl.multiple_of(i * step, step), step)
        target[at] = (target[at].astype(F32) + other[at].astype(F32)).astype(target.dtype)


def line_sum(links, part, acc, from_left, from_right, finish, own=None, full=None, parts=2):
    z, last = links.z, links.members - 1
    rows = acc.shape[1] // parts
    spans = [pl.ds(h * rows, rows) for h in range(parts)]
    right, left = (links.d, z + 1), (links.d, z - 1)
    sum_r, sum_l, go_r, go_l, local = {}, {}, {}, {}, []
    for h, span in enumerate(spans):
        for o in range(last + 1):
            if o > 0:
                sum_r[h, o] = links.remote(acc.at[o, span], from_left.at[o, span], right)
            if o < last:
                sum_l[h, o] = links.remote(acc.at[o, span], from_right.at[o, span], left)
        for s in range(last if own is not None else 0):
            at_r, at_l = jnp.maximum(z - s, 0), jnp.minimum(z + s, last)
            here_r, here_l = full.at[at_r, span], full.at[at_l, span]
            go_r[h, s] = links.remote(own.at[span] if s == 0 else here_r, here_r, right)
            go_l[h, s] = links.remote(own.at[span] if s == 0 else here_l, here_l, left)

    def pass_right(h, o):
        @pl.when(z > 0)
        def _():
            sum_r[h, o].wait_recv()
            add_rows(acc.at[o, spans[h]], from_left.at[o, spans[h]])

        sum_r[h, o].start()

    def pass_left(h, o):
        @pl.when(z < last)
        def _():
            sum_l[h, o].wait_recv()
            add_rows(acc.at[o, spans[h]], from_right.at[o, spans[h]])

        sum_l[h, o].start()

    def send(h, s):
        pl.when((z < last) & (z >= s))(go_r[h, s].start)
        pl.when((z > 0) & (z + s <= last))(go_l[h, s].start)

    @pl.when(z == 0)
    def _():
        from_left[0] = jnp.zeros(from_left.shape[1:], from_left.dtype)

    @pl.when(z == last)
    def _():
        from_right[last] = jnp.zeros(from_right.shape[1:], from_right.dtype)

    made = set()
    for j in range(last):
        for o in (last - j, j):
            if o not in made:
                made.add(o)
                part(o)
        for h in range(parts):
            pl.when((z < last - j) & (2 * z < last))(functools.partial(pass_right, h, last - j))
            pl.when(z > j)(functools.partial(pass_left, h, j))
            pl.when((z < last - j) & (2 * z >= last))(functools.partial(pass_right, h, last - j))
            yield
    for h in range(parts):
        for o in range(last + 1):
            if o > 0:
                pl.when(z == o)(sum_r[h, o].wait_recv)
            if o < last:
                pl.when(z == o)(sum_l[h, o].wait_recv)
        finish(h * rows, rows)
        if own is None:
            continue
        send(h, 0)
        local.append(links.move(own.at[spans[h]], full.at[z, spans[h]]))
        yield
    for s in range(last if own is not None else 0):
        for h in range(parts):
            pl.when((z > 0) & (z - 1 >= s))(go_r[h, s].wait_recv)
            pl.when((z < last) & (z + 1 + s <= last))(go_l[h, s].wait_recv)
            if s + 1 < last:
                send(h, s + 1)
            yield
    for h in range(parts):
        for o in range(last + 1):
            if o > 0:
                pl.when(z < o)(sum_r[h, o].wait_send)
            if o < last:
                pl.when(z > o)(sum_l[h, o].wait_send)
        for s in range(last if own is not None else 0):
            pl.when((z < last) & (z >= s))(go_r[h, s].wait_send)
            pl.when((z > 0) & (z + s <= last))(go_l[h, s].wait_send)
    for copy in local:
        copy.wait()


def plane_gather(links, own, full):
    half = own.shape[0] // 2
    first, second = pl.ds(0, half), pl.ds(half, half)
    me = links.d
    local = links.move(own, full.at[me])
    by_x, by_y = {}, {}
    for by, d, h in ((by_y, links.y, first), (by_x, links.x, second), (by_x, links.x, first), (by_y, links.y, second)):
        by[h.start // half] = links.push(own.at[h], full.at[me, h], d)
    to_sib = [links.push(own, full.at[me], links.sib)]

    def share(d, h):
        to_sib.append(links.push(full.at[d, h], full.at[d, h], links.sib))

    yield
    by_y[0].wait_recv()
    over_x = links.push(full.at[links.y, first], full.at[links.y, first], links.x)
    share(links.y, first)
    by_x[1].wait_recv()
    over_y = links.push(full.at[links.x, second], full.at[links.x, second], links.y)
    share(links.x, second)
    yield
    by_x[0].wait_recv()
    share(links.x, first)
    by_y[1].wait_recv()
    share(links.y, second)
    yield
    over_x.wait_recv()
    share(links.diag, first)
    over_y.wait_recv()
    share(links.diag, second)
    yield
    for copy in to_sib:
        copy.wait_recv()
    local.wait()


def plane_scatter(links, part, mine, theirs, mid_x, mid_y, end_x, end_y):
    half = part.shape[1] // 2
    first, second = pl.ds(0, half), pl.ds(half, half)
    chips = (links.d, links.x, links.y, links.diag)
    from_sib, load = {}, {}
    held = [part.at[chip] if mine is None else mine.at[k] for k, chip in enumerate(chips)]
    for k in (3, 1, 2, 0):
        from_sib[k] = links.push(part.at[links.other(chips[k])], theirs.at[k], links.sib)
        if mine is not None:
            load[k] = links.move(part.at[chips[k]], held[k])
    yield
    for k in (3, 1, 2):
        if load:
            load[k].wait()
        from_sib[k].wait_recv()
        add_rows(held[k], theirs.at[k])
        if k == 3:
            to_mid_x = links.push(held[3].at[first], mid_x, links.x)
            to_mid_y = links.push(held[3].at[second], mid_y, links.y)
        if k == 1:
            to_end_x = links.push(held[1].at[first], end_x.at[first], links.x)
        if k == 2:
            to_end_y = links.push(held[2].at[second], end_y.at[second], links.y)
        if k != 1:
            yield
    to_mid_y.wait_recv()
    add_rows(held[1].at[second], mid_y)
    rest_x = links.push(held[1].at[second], end_x.at[second], links.x)
    to_mid_x.wait_recv()
    add_rows(held[2].at[first], mid_x)
    rest_y = links.push(held[2].at[first], end_y.at[first], links.y)
    yield
    if load:
        load[0].wait()
    from_sib[0].wait_recv()
    to_end_x.wait_recv()
    to_end_y.wait_recv()
    rest_x.wait_recv()
    rest_y.wait_recv()
    yield


def plane_scratch(rows, cols, mine=True):
    return [pltpu.VMEM((4, rows, cols), BF16)] * mine + [
        pltpu.VMEM((4, rows, cols), BF16),
        pltpu.VMEM((rows // 2, cols), BF16),
        pltpu.VMEM((rows // 2, cols), BF16),
        pltpu.VMEM((rows, cols), BF16),
        pltpu.VMEM((rows, cols), BF16),
    ]


def plane_result(mine, theirs, end_x, end_y, out, step=16):
    @pl.loop(0, out.shape[-2] // step)
    def _(i):
        at = pl.ds(pl.multiple_of(i * step, step), step)
        own = mine[at].astype(F32) + theirs[0, at].astype(F32)
        total = (own + end_x[at].astype(F32) + end_y[at].astype(F32)).astype(out.dtype)
        if len(out.shape) == 2:
            out[at] = total
        else:
            cols = out.shape[2]
            for e in range(out.shape[0]):
                out[e, at] = total[:, e * cols : (e + 1) * cols]


def plane_total(links, part, scratch, total, out, stores):
    yield from plane_scatter(links, part, *scratch)
    plane_result(scratch[0].at[0], scratch[1], scratch[4], scratch[5], total)
    stores.append(links.move(total, out))


def line_result(z, acc, from_left, from_right, at):
    return (
        acc[z, at].astype(F32) + from_left[z, at].astype(F32) + from_right[z, at].astype(F32)
    )


ANY = pl.BlockSpec(memory_space=pl.ANY)
VMEM = pl.BlockSpec(memory_space=pltpu.VMEM)


def comm_call(kernel, name, number, members, remotes, locals_, in_specs, out_specs, out_shape, scratch):
    return pl.pallas_call(
        functools.partial(kernel, members),
        out_shape=out_shape,
        in_specs=in_specs,
        out_specs=out_specs,
        scratch_shapes=[
            pltpu.SemaphoreType.DMA((remotes,)),
            pltpu.SemaphoreType.DMA((remotes,)),
            pltpu.SemaphoreType.DMA((locals_,)),
            *scratch,
        ],
        compiler_params=pltpu.CompilerParams(
            collective_id=number, has_side_effects=True, vmem_limit_bytes=VMEM_LIMIT
        ),
        name=name,
    )


def sds(shape, dtype):
    return jax.ShapeDtypeStruct(shape, dtype)


def third_kernel(members, part, mixture, residual, cot, gain, gate, up, output, grad_residual, gain_part, out_all, gate_out, up_out, send, recv, local, acc, from_left, from_right, acc_m, left_m, right_m, grad_out, gate_sum, up_sum, *rest):
    links = Links(send, recv, local, members)
    for_gate, for_up = rest[:6], rest[6:]
    stores = []

    def block_loads(source, into):
        loads = [links.move(source.at[o], into.at[o]) for o in range(members)]
        return lambda o: loads[o].wait()

    load_part, load_mixture = block_loads(part, acc), block_loads(mixture, acc_m)
    links.greet()

    def finish(first, count):
        @pl.loop(0, count // 16)
        def _(i):
            at = pl.ds(pl.multiple_of(first + i * 16, 16), 16)
            grad = line_result(links.z, acc, from_left, from_right, at)
            here = residual[at]
            factor = rms_factor(here)
            gain_part[...] += jnp.sum(grad * here * factor, axis=0, keepdims=True)
            total = cot[at].astype(F32) + norm_back(here, factor, gain[1:2], grad)
            grad_residual[at] = total
            grad_out[at] = (branch_scale * total).astype(BF16)

    def chain():
        gain_part[...] = jnp.zeros(gain_part.shape, F32)
        yield from line_sum(
            links, load_part, acc, from_left, from_right, finish, grad_out, out_all
        )

    def finish_mixture(first, count):
        @pl.loop(0, count // 16)
        def _(i):
            at = pl.ds(pl.multiple_of(first + i * 16, 16), 16)
            here = residual[at] + branch_scale * line_result(links.z, acc_m, left_m, right_m, at)
            output[at] = here.astype(BF16)

    def mixture_chain():
        yield from line_sum(links, load_mixture, acc_m, left_m, right_m, finish_mixture)

    run(
        THIRD_ORDER,
        m=mixture_chain(),
        z=chain(),
        g=plane_total(links, gate, for_gate, gate_sum, gate_out, stores),
        u=plane_total(links, up, for_up, up_sum, up_out, stores),
    )
    for store in stores:
        store.wait()
    links.finish()


THIRD_ORDER = "uzuzzgugmmzzguzzzgzmzmzmmzmugguuzm"


def third_phase(members, own_experts, part, mixture, residual, cot, gain, gate, up):
    rows, width = cot.shape
    blocks = pltpu.VMEM((members, rows, width), BF16)
    return comm_call(
        third_kernel, "phase_three", 3, members, 80, 24,
        [ANY, ANY, VMEM, VMEM, VMEM, ANY, ANY], [VMEM, VMEM, VMEM, ANY, ANY, ANY],
        [
            sds((rows, width), BF16),
            sds((rows, width), F32),
            sds((1, width), F32),
            sds((members, rows, width), BF16),
            sds((own_experts, gate.shape[1], gate.shape[2] // own_experts), F32),
            sds((own_experts, up.shape[1], up.shape[2] // own_experts), F32),
        ],
        [blocks] * 6
        + [pltpu.VMEM((rows, width), BF16)]
        + [pltpu.VMEM((own_experts, gate.shape[1], gate.shape[2] // own_experts), F32)] * 2
        + plane_scratch(*gate.shape[1:])
        + plane_scratch(*up.shape[1:]),
    )(part, mixture, residual, cot, gain, gate, up)


def lane_ids(rows):
    return lax.broadcasted_iota(jnp.int32, (rows, LANES), 1)


def dims(a, b):
    return (((a,), (b,)), ((), ()))


def mm(a, b):
    return lax.dot_general(a, b, dims(1, 0), preferred_element_type=F32)


def mm_nt(a, b):
    return lax.dot_general(a, b, dims(1, 1), preferred_element_type=F32)


def mm_tn(a, b):
    return lax.dot_general(a, b, dims(0, 0), preferred_element_type=F32)


def first_lanes():
    same = lax.broadcasted_iota(jnp.int32, (16, LANES), 0) == lax.broadcasted_iota(jnp.int32, (16, LANES), 1)
    return same.astype(BF16)


def expert_kernel(capacity, own_experts, route, normed, cot, w_gate, w_up, w_down, mixture, grad_normed, d_gate, d_up, d_down, mix_sum, grad_sum, slot_cols, weight_cols, slot_rows):
    e = pl.program_id(0)
    span = normed.shape[0]

    @pl.when(e == 0)
    def _():
        mix_sum[...] = jnp.zeros(mix_sum.shape, F32)
        grad_sum[...] = jnp.zeros(grad_sum.shape, F32)
        lane = lane_ids(LANES)
        name = (lax.axis_index("expert") * own_experts + lane).astype(F32)
        name = jnp.where(lane < own_experts, name, -1.0)
        upto = (lane <= lax.broadcasted_iota(jnp.int32, (LANES, LANES), 0)).astype(BF16)
        before = jnp.zeros((1, LANES), F32)
        for b in range(span // LANES):
            at = pl.ds(b * LANES, LANES)
            chosen, weight = jnp.zeros((LANES, LANES), F32), jnp.zeros((LANES, LANES), F32)
            for k in range(TOP):
                named = route[at, k : k + 1] == name
                chosen = jnp.where(named, 1.0, chosen)
                weight = jnp.where(named, route[at, TOP + k : TOP + k + 1], weight)
            slot = mm(upto, chosen.astype(BF16)) + (before - 1.0)
            slot_cols[at] = jnp.where((chosen > 0.0) & (slot < capacity), slot, -1.0)
            weight_cols[at] = weight
            before = before + jnp.sum(chosen, axis=0, keepdims=True)
        slot_rows[...] = mm_nt(first_lanes(), slot_cols[...].astype(BF16))

    def column(values):
        return jnp.sum(jnp.where(lane_ids(span) == e, values[...], 0.0), axis=1, keepdims=True)

    slots = lax.broadcasted_iota(jnp.int32, (capacity, span), 0).astype(F32)
    pick = (slot_rows[pl.ds(e, 1)] == slots).astype(BF16)
    puts = column(slot_cols) == lax.broadcasted_iota(jnp.int32, (span, capacity), 1).astype(F32)
    put = puts.astype(BF16)
    gate_row = jnp.sum(jnp.where(puts, column(weight_cols), 0.0), axis=0, keepdims=True)
    same = lax.broadcasted_iota(jnp.int32, (capacity, capacity), 0) == lax.broadcasted_iota(jnp.int32, (capacity, capacity), 1)
    gate_col = jnp.sum(jnp.where(same, gate_row, 0.0), axis=1, keepdims=True)
    received = mm(pick, normed[...]).astype(BF16)
    pre_gate, pre_up = mm(received, w_gate[...]), mm(received, w_up[...])
    sig = 1.0 / (1.0 + jnp.exp(-pre_gate))
    silu = pre_gate * sig
    activ = (silu * pre_up).astype(BF16)
    produced = (gate_col * mm_nt(activ, w_down[...])).astype(BF16)
    mix_sum[...] += mm(put, produced)
    grad_out = (gate_col * (branch_scale * mm(pick, cot[...]))).astype(BF16)
    grad_activ = mm(grad_out, w_down[...])
    grad_gate = (grad_activ * pre_up * (sig * (1.0 + pre_gate * (1.0 - sig)))).astype(BF16)
    grad_up = (grad_activ * silu).astype(BF16)
    grad_pair = (mm_nt(grad_gate, w_gate[...]) + mm_nt(grad_up, w_up[...])).astype(BF16)
    grad_sum[...] += mm(put, grad_pair)
    d_gate[...] = mm_tn(received, grad_gate).astype(BF16)
    d_up[...] = mm_tn(received, grad_up).astype(BF16)
    d_down[...] = mm_tn(grad_out, activ).astype(BF16)

    @pl.when(e == pl.num_programs(0) - 1)
    def _():
        mixture[...] = mix_sum[...].astype(BF16)
        grad_normed[...] = grad_sum[...].astype(BF16)


def experts(own_experts, capacity, route, normed, cot, w_gate, w_up, w_down):
    span, width = normed.shape
    ff = w_gate.shape[1] // own_experts
    whole = pl.BlockSpec((span, width), lambda e: (0, 0))
    column = pl.BlockSpec((width, ff), lambda e: (0, e))
    grads = jax.ShapeDtypeStruct(w_gate.shape, BF16)
    rows = jax.ShapeDtypeStruct((span, width), BF16)
    return pl.pallas_call(
        functools.partial(expert_kernel, capacity, own_experts),
        grid=(own_experts,),
        in_specs=[pl.BlockSpec(route.shape, lambda e: (0, 0)), whole, whole, column, column, column],
        out_specs=[whole, whole, column, column, column],
        out_shape=[rows, rows, grads, grads, grads],
        scratch_shapes=[
            pltpu.VMEM((span, width), F32),
            pltpu.VMEM((span, width), F32),
            pltpu.VMEM((span, LANES), F32),
            pltpu.VMEM((span, LANES), F32),
            pltpu.VMEM((16, span), F32),
        ],
        compiler_params=pltpu.CompilerParams(vmem_limit_bytes=VMEM_LIMIT),
        name="experts",
    )(route, normed, cot, w_gate, w_up, w_down)


def turn(x, cosine, sine):
    half = HEAD_SIZE // 2
    ahead, behind = pltpu.roll(x, LANES - half, axis=1), pltpu.roll(x, half, axis=1)
    partner = jnp.where(lane_ids(x.shape[0]) % HEAD_SIZE < half, ahead, behind)
    return x * cosine + partner * sine


def spread(block, at, out):
    low = lane_ids(block.shape[0]) < HEAD_SIZE
    other = pltpu.roll(block, HEAD_SIZE, axis=1)
    zero = jnp.zeros_like(block)
    out[0, 0, at] = jnp.where(low, block, zero).astype(BF16)
    out[0, 1, at] = jnp.where(low, zero, other).astype(BF16)
    out[1, 0, at] = jnp.where(low, other, zero).astype(BF16)
    out[1, 1, at] = jnp.where(low, zero, block).astype(BF16)


def attention_setup(segment, bias):
    span = bias.shape[0]
    same = lax.broadcasted_iota(jnp.int32, (LANES, LANES), 0) == lane_ids(LANES)
    for b in range(span // LANES):
        at = pl.ds(b * LANES, LANES)
        row = b * LANES + lax.broadcasted_iota(jnp.int32, (LANES, span), 0)
        col = lax.broadcasted_iota(jnp.int32, (LANES, span), 1)
        here = segment[:, b * LANES : (b + 1) * LANES]
        here = jnp.sum(jnp.where(same, here, 0.0), axis=1, keepdims=True)
        ok = (here == segment) & (col <= row)
        bias[at] = jnp.where(ok, 0.0, -1e30)


def weight_columns(pack_all, first, cols):
    return pack_all[:, :, first : first + cols].reshape(-1, cols)


def gain_rows(pack_all, first):
    return mm_nt(first_lanes(), weight_columns(pack_all, first, LANES))


def attend_steps(qkv, kx, vx, bias, probs, attended):
    span, blocks = qkv.shape[0], attended.shape[1] // LANES
    repeat = QUERY_HEADS // KEY_VALUE_HEADS
    for j in range(blocks):
        for b in range(span // LANES):
            at, keys = pl.ds(b * LANES, LANES), (b + 1) * LANES
            q = qkv[at, j * LANES : (j + 1) * LANES]
            total = jnp.zeros((LANES, LANES), F32)
            for half in range(2):
                h = 2 * j + half
                kv = h // repeat
                scores = mm_nt(q, kx[kv, half, :keys]) + bias[at, :keys]
                peak = jnp.max(scores, axis=1, keepdims=True)
                exponent = jnp.exp(scores - peak)
                share = 1.0 / jnp.sum(exponent, axis=1, keepdims=True)
                low = (exponent * share).astype(BF16)
                probs[h, at, :keys] = low
                total += mm(low, vx[kv, half, :keys])
            attended[at, j * LANES : (j + 1) * LANES] = total.astype(BF16)
        yield


def forward_kernel(
    members, tokens, cot, ids, gates, w_query, w_key, w_value, w_out, small, gate, up, down, cosine, sine,
    cot_all, route_all, pack_out, gate_all, up_all, down_all, normed_out, qkv_out, kx_out, vx_out, probs_out, attended_out, residual, normed_all, gains,
    send, recv, local, pack, route, flat, tokens_all, bias, acc, from_left, from_right, normed,
    pack_all, normed_attn, qkv, kx, vx, probs, attended,
):
    links = Links(send, recv, local, members)
    stores = []
    count, _, cols = gate.shape
    loads = [
        [links.move(weight.at[e], flat.at[i, :, e * cols : (e + 1) * cols]) for e in range(count)]
        for i, weight in enumerate((gate, up, down))
    ]
    links.greet()
    route[...] = jnp.concatenate([ids[...].astype(F32), gates[...]], axis=0).T
    rows, width = tokens.shape
    span = rows * members
    q_cols = attended.shape[1]
    qkv_cols = qkv.shape[1]

    def pack_chain():
        loads, at = [], 0
        for weight in (w_query, w_key, w_value, w_out):
            cols = weight.shape[1] // members
            mine = pl.ds(pl.multiple_of(links.z * cols, LANES), cols)
            loads.append(links.move(weight.at[:, mine], pack.at[:, at : at + cols]))
            at += cols
        which = lax.broadcasted_iota(jnp.int32, (16, pack.shape[0]), 0)
        own = pack.shape[0]
        both = jnp.where(which == 0, small[1:2, :own], jnp.where(which == 1, small[2:3, :own], 0.0))
        pack[:, at:] = mm_tn(both.astype(BF16), first_lanes()).astype(BF16)
        for load in loads:
            load.wait()
        yield from plane_gather(links, pack, pack_all)

    def expert_chain(i, full):
        for load in loads[i]:
            load.wait()
        yield from plane_gather(links, flat.at[i], full)

    def produce(o):
        acc[o] = mm_nt(attended[o * rows : (o + 1) * rows], weight_columns(pack_all, qkv_cols, q_cols)).astype(BF16)

    def chain():
        attention_setup(small[0:1], bias)
        yield
        gains[...] = gain_rows(pack_all, qkv_cols + q_cols)

        @pl.loop(0, span // 16)
        def _(i):
            here = tokens_all[i // (rows // 16), pl.ds(pl.multiple_of(i % (rows // 16) * 16, 16), 16)].astype(F32)
            normed_attn[pl.ds(pl.multiple_of(i * 16, 16), 16)] = (here * rms_factor(here) * gains[0:1]).astype(BF16)

        @pl.loop(0, span // LANES)
        def _(i):
            at = pl.ds(pl.multiple_of(i * LANES, LANES), LANES)
            here = mm(normed_attn[at], weight_columns(pack_all, 0, qkv_cols))
            c, s = cosine[at], sine[at]
            for j in range(q_cols // LANES):
                lanes = slice(j * LANES, (j + 1) * LANES)
                qkv[at, lanes] = (turn(here[:, lanes], c, s).astype(BF16).astype(F32) * score_scale).astype(BF16)
            key = turn(here[:, q_cols : q_cols + LANES], c, s)
            value = here[:, q_cols + LANES :]
            qkv[at, q_cols : q_cols + LANES] = key.astype(BF16)
            qkv[at, q_cols + LANES :] = value.astype(BF16)
            spread(key, at, kx)
            spread(value, at, vx)

        yield
        yield from attend_steps(qkv, kx, vx, bias, probs, attended)
        for kept, out in (
            (pack_all, pack_out), (normed_attn, normed_out), (qkv, qkv_out), (kx, kx_out),
            (vx, vx_out), (probs, probs_out), (attended, attended_out),
        ):
            stores.append(links.move(kept, out))

        def finish(first, count):
            @pl.loop(0, count // 16)
            def _(i):
                at = pl.ds(pl.multiple_of(first + i * 16, 16), 16)
                here = tokens[at].astype(F32) + branch_scale * line_result(links.z, acc, from_left, from_right, at)
                residual[at] = here
                normed[at] = (here * rms_factor(here) * gains[1:2]).astype(BF16)

        yield from line_sum(links, produce, acc, from_left, from_right, finish, normed, normed_all)

    run(
        FORWARD_ORDER,
        t=line_gather(links, tokens, tokens_all),
        r=line_gather(links, route, route_all),
        c=line_gather(links, cot, cot_all),
        p=pack_chain(),
        g=expert_chain(0, gate_all),
        u=expert_chain(1, up_all),
        d=expert_chain(2, down_all),
        a=chain(),
    )
    for store in stores:
        store.wait()
    links.finish()


FORWARD_ORDER = "tpptpadtcpgptpaatcargadctaatracauaacrtaagpgrrtaargtgdcrtp"


def forward_phase(members, tokens, cot, ids, gates, w_query, w_key, w_value, w_out, small, gate, up, down, cosine, sine):
    rows, width = tokens.shape
    q_cols = w_query.shape[1] // members
    qkv_cols = q_cols + 2 * w_key.shape[1] // members
    count, own, cols = gate.shape
    pack = (own, qkv_cols + q_cols + LANES)
    route, flat = (rows, 2 * ids.shape[0]), (own, count * cols)
    span = rows * members
    blocks = pltpu.VMEM((members, rows, width), BF16)
    heads = q_cols // HEAD_SIZE
    return comm_call(
        forward_kernel, "forward", 1, members, 120, 40,
        [VMEM, ANY, VMEM, VMEM, ANY, ANY, ANY, ANY, VMEM, ANY, ANY, ANY, VMEM, VMEM],
        [ANY] * 12 + [VMEM, ANY, VMEM],
        [
            sds((members, rows, width), BF16),
            sds((members, *route), F32),
            sds((8, *pack), BF16),
            sds((8, *flat), BF16),
            sds((8, *flat), BF16),
            sds((8, *flat), BF16),
            sds((span, width), BF16),
            sds((span, qkv_cols), BF16),
            sds((2, 2, span, LANES), BF16),
            sds((2, 2, span, LANES), BF16),
            sds((heads, span, span), BF16),
            sds((span, q_cols), BF16),
            sds((rows, width), F32),
            sds((members, rows, width), BF16),
            sds((16, width), F32),
        ],
        [
            pltpu.VMEM(pack, BF16),
            pltpu.VMEM(route, F32),
            pltpu.VMEM((3, *flat), BF16),
            blocks,
            pltpu.VMEM((span, span), F32),
            blocks,
            blocks,
            blocks,
            pltpu.VMEM((rows, width), BF16),
            pltpu.VMEM((8, *pack), BF16),
            pltpu.VMEM((span, width), BF16),
            pltpu.VMEM((span, qkv_cols), BF16),
            pltpu.VMEM((2, 2, span, LANES), BF16),
            pltpu.VMEM((2, 2, span, LANES), BF16),
            pltpu.VMEM((heads, span, span), BF16),
            pltpu.VMEM((span, q_cols), BF16),
        ],
    )(tokens, cot, ids, gates, w_query, w_key, w_value, w_out, small, gate, up, down, cosine, sine)


def attend_back_steps(qkv, kx, vx, probs, grad_attended, cosine, sine, grad_k, grad_v, grad_qkv):
    span = qkv.shape[0]
    blocks = grad_attended.shape[1] // LANES
    repeat = QUERY_HEADS // KEY_VALUE_HEADS
    grad_k[...] = jnp.zeros(grad_k.shape, F32)
    grad_v[...] = jnp.zeros(grad_v.shape, F32)
    for j in range(blocks):
        lanes = slice(j * LANES, (j + 1) * LANES)
        for b in range(span // LANES):
            at, keys = pl.ds(b * LANES, LANES), (b + 1) * LANES
            q, grad = qkv[at, lanes], grad_attended[at, lanes]
            total = jnp.zeros((LANES, LANES), F32)
            for half in range(2):
                h = 2 * j + half
                kv = h // repeat
                low = probs[h, at, :keys]
                share = low.astype(F32)
                grad_probs = mm_nt(grad, vx[kv, half, :keys])
                inner = jnp.sum(share * grad_probs, axis=1, keepdims=True)
                grad_scores = (share * (grad_probs - inner)).astype(BF16)
                total += mm(grad_scores, kx[kv, half, :keys])
                grad_k[kv, half, :keys] += mm_tn(grad_scores, q)
                grad_v[kv, half, :keys] += mm_tn(low, grad)
            grad_qkv[at, lanes] = turn(total * score_scale, cosine[at], -sine[at]).astype(BF16)
        yield
    first = blocks * LANES

    def fold(parts, at):
        low = lane_ids(LANES) < HEAD_SIZE
        same = jnp.where(low, parts[0, 0, at], parts[1, 1, at])
        crossed = jnp.where(low, parts[1, 0, at], parts[0, 1, at])
        return same + pltpu.roll(crossed, HEAD_SIZE, axis=1)

    for b in range(span // LANES):
        at = pl.ds(b * LANES, LANES)
        grad_qkv[at, first : first + LANES] = turn(fold(grad_k, at), cosine[at], -sine[at]).astype(BF16)
        grad_qkv[at, first + LANES :] = fold(grad_v, at).astype(BF16)


def backward_kernel(
    members, grad_out_in, grad_residual, gain_ffn_part, tokens, down, row_gains, pack_in, normed_in, qkv_in, kx_in, vx_in, probs_in, attended_in, cosine, sine,
    grad_tokens, gains, d_query, d_key, d_value, d_out, down_out,
    send, recv, local, acc, from_left, from_right, grad_attended, grad_k, grad_v, grad_qkv, gain_part,
    for_w_out, for_w_query, for_rest, own_out, own_query, own_rest, all_out, all_query, all_rest,
    grad_out_all, pack_all, normed_attn, qkv, kx, vx, probs, attended, d_down, *rest,
):
    links = Links(send, recv, local, members)
    loads = {
        "attended": links.move(attended_in, attended),
        "grad": links.move(grad_out_in, grad_out_all),
        "pack": links.move(pack_in, pack_all),
        "qkv": links.move(qkv_in, qkv),
        "kx": links.move(kx_in, kx),
        "vx": links.move(vx_in, vx),
        "probs": links.move(probs_in, probs),
        "normed": links.move(normed_in, normed_attn),
    }
    stores = []

    def need(*names):
        for name in names:
            if name in loads:
                loads.pop(name).wait()

    links.greet()
    rows, width = tokens.shape
    q_cols, qkv_cols = attended.shape[1], qkv.shape[1]
    kv_cols = (qkv_cols - q_cols) // 2
    with_out, with_query, with_rest, with_down = rest[:5], rest[5:10], rest[10:15], rest[15:]
    pairs = for_w_out.shape[0] // 2
    step = width // pairs

    def weight_term(rows_of, grads, out, cols):
        for i in range(pairs):
            term = mm_tn(rows_of[:, i * step : (i + 1) * step], grads)
            out[2 * i : 2 * i + 2, :, :cols] = term.astype(BF16).reshape(2, step // 2, cols)

    def put_out():
        for m in range(members):
            d_out[:, m * q_cols : (m + 1) * q_cols] = all_out[m].astype(F32)

    def put_query():
        for m in range(members):
            d_query[:, m * q_cols : (m + 1) * q_cols] = all_query[m].astype(F32)

    def put_rest():
        for m in range(members):
            d_key[:, m * kv_cols : (m + 1) * kv_cols] = all_rest[m, :, :kv_cols].astype(F32)
            d_value[:, m * kv_cols : (m + 1) * kv_cols] = all_rest[m, :, kv_cols : 2 * kv_cols].astype(F32)
        total = sum(all_rest[m, :, 2 * kv_cols :].astype(F32) for m in range(members))
        gains[...] = total.T[: gains.shape[0]]

    def weight_chain(fill, part, mine, full, scratch, put):
        fill()
        yield from plane_scatter(links, part, None, *scratch)
        plane_result(part.at[links.d], scratch[0], scratch[3], scratch[4], mine)
        yield from line_gather(links, mine, full)
        put()

    def fill_out():
        need("grad", "attended")
        weight_term(grad_out_all, attended[...], for_w_out, q_cols)

    def fill_query():
        need("normed")
        weight_term(normed_attn, grad_qkv[:, :q_cols], for_w_query, q_cols)

    def fill_rest():
        weight_term(normed_attn, grad_qkv[:, q_cols:], for_rest, 2 * kv_cols)
        which = lax.broadcasted_iota(jnp.int32, (16, width), 0)
        both = jnp.where(which == 0, gain_part[...] / row_gains[0:1], jnp.where(which == 1, gain_ffn_part[...], 0.0))
        columns = mm_tn(both.astype(BF16), first_lanes())
        for_rest[:, :, 2 * kv_cols :] = columns.astype(BF16).reshape(2 * pairs, step // 2, LANES)

    def produce(o):
        at = slice(o * rows, (o + 1) * rows)
        part = mm_nt(grad_qkv[at], weight_columns(pack_all, 0, qkv_cols))
        gain_part[...] += jnp.sum(part * normed_attn[at].astype(F32), axis=0, keepdims=True)
        acc[o] = part.astype(BF16)

    def chain():
        need("grad", "pack")
        wo = weight_columns(pack_all, qkv_cols, q_cols)

        @pl.loop(0, grad_attended.shape[0] // LANES)
        def _(i):
            at = pl.ds(pl.multiple_of(i * LANES, LANES), LANES)
            grad_attended[at] = mm(grad_out_all[at], wo).astype(BF16)

        yield
        need("qkv", "kx", "vx", "probs")
        yield from attend_back_steps(qkv, kx, vx, probs, grad_attended, cosine, sine, grad_k, grad_v, grad_qkv)
        gain_part[...] = jnp.zeros(gain_part.shape, F32)
        need("normed")
        yield

        def finish(first, count):
            @pl.loop(0, count // 16)
            def _(i):
                at = pl.ds(pl.multiple_of(first + i * 16, 16), 16)
                grad = line_result(links.z, acc, from_left, from_right, at)
                here = tokens[at].astype(F32)
                grad_tokens[at] = grad_residual[at] + norm_back(here, rms_factor(here), row_gains[0:1], grad)

        yield from line_sum(links, produce, acc, from_left, from_right, finish)

    run(
        BACKWARD_ORDER,
        d=plane_total(links, down, with_down, d_down, down_out, stores),
        o=weight_chain(fill_out, for_w_out, own_out, all_out, with_out, put_out),
        a=chain(),
        q=weight_chain(fill_query, for_w_query, own_query, all_query, with_query, put_query),
        r=weight_chain(fill_rest, for_rest, own_rest, all_rest, with_rest, put_rest),
    )
    for store in stores:
        store.wait()
    links.finish()


BACKWARD_ORDER = "oadoaoaoaooqaqqdoaqdaqqarorarradrraqrqdaoodaaqdrddrr"


def backward_phase(members, own_experts, grad_out_all, grad_residual, gain_ffn_part, tokens, down, row_gains, pack_all, normed_attn, qkv, kx, vx, probs, attended, cosine, sine):
    rows, width = tokens.shape
    span, q_cols = attended.shape
    qkv_cols = qkv.shape[1]
    kv_cols = (qkv_cols - q_cols) // 2
    devices, own = down.shape[:2]
    line = [pltpu.VMEM((members, rows, width), BF16)] * 3
    three = (q_cols, q_cols, 2 * kv_cols + LANES)
    return comm_call(
        backward_kernel, "backward", 4, members, 100, 32,
        [ANY, VMEM, VMEM, VMEM, ANY, VMEM] + [ANY] * 7 + [VMEM] * 2,
        [VMEM] * 6 + [ANY],
        [
            sds((rows, width), F32),
            sds((8, own), F32),
            sds((own, members * q_cols), F32),
            sds((own, members * kv_cols), F32),
            sds((own, members * kv_cols), F32),
            sds((own, members * q_cols), F32),
            sds((own_experts, own, down.shape[2] // own_experts), F32),
        ],
        [
            *line,
            pltpu.VMEM((span, q_cols), BF16),
            pltpu.VMEM((2, 2, span, LANES), F32),
            pltpu.VMEM((2, 2, span, LANES), F32),
            pltpu.VMEM((span, qkv_cols), BF16),
            pltpu.VMEM((1, width), F32),
            *[pltpu.VMEM((devices, own, cols), BF16) for cols in three],
            *[pltpu.VMEM((own, cols), BF16) for cols in three],
            *[pltpu.VMEM((members, own, cols), BF16) for cols in three],
            *[pltpu.VMEM(a.shape, BF16) for a in (grad_out_all, pack_all, normed_attn, qkv, kx, vx, probs, attended)],
            pltpu.VMEM((own_experts, own, down.shape[2] // own_experts), F32),
            *[one for cols in three for one in plane_scratch(own, cols, False)],
            *plane_scratch(*down.shape[1:]),
        ],
    )(grad_out_all, grad_residual, gain_ffn_part, tokens, down, row_gains, pack_all, normed_attn, qkv, kx, vx, probs, attended, cosine, sine)


def all_blocks(x, axis):
    return lax.all_gather(x, axis, axis=0)


def plain_first(members, tokens, cot, route, pack, gate):
    return (
        all_blocks(tokens, "expert"),
        all_blocks(cot, "expert"),
        all_blocks(route, "expert"),
        all_blocks(pack, "dp"),
        all_blocks(gate, "dp"),
    )


def line_total(part):
    return scatter(part.reshape(-1, part.shape[2]), "expert")


def plain_second(members, part, tokens, gain, up, down):
    residual = tokens.astype(F32) + branch_scale * line_total(part)
    normed = (residual * rms_factor(residual) * gain).astype(BF16)
    return residual, all_blocks(normed, "expert"), all_blocks(up, "dp"), all_blocks(down, "dp")


def plane_sum(part):
    return scatter(part.reshape(-1, part.shape[2]), "dp")


def plain_third(members, part, residual, cot, gain, gate, up):
    grad = line_total(part)
    factor = rms_factor(residual)
    gain_part = jnp.sum(grad * residual * factor, axis=0, keepdims=True)
    total = cot.astype(F32) + norm_back(residual, factor, gain, grad)
    out_all = all_blocks((branch_scale * total).astype(BF16), "expert")
    return total, gain_part, out_all, plane_sum(gate), plane_sum(up)


def plain_fourth(members, part, grad_residual, tokens, gain, pack, down):
    here = tokens.astype(F32)
    grad_tokens = grad_residual + norm_back(here, rms_factor(here), gain, line_total(part))
    return grad_tokens, all_blocks(plane_sum(pack).astype(BF16), "expert"), plane_sum(down)


def attend_forward(q, k, v, allowed):
    scores = jnp.einsum("irh,jh->rij", q, k, preferred_element_type=F32) * score_scale
    scores = jnp.where(allowed[None], scores, -1e30)
    peak = jnp.max(scores, axis=-1, keepdims=True)
    exponent = jnp.exp(scores - peak)
    total = jnp.sum(exponent, axis=-1, keepdims=True)
    probs = exponent / total
    return jnp.einsum("rij,jh->irh", probs.astype(BF16), v, preferred_element_type=F32), probs


def attend_backward(q, k, v, probs, grad, allowed):
    grad_probs = jnp.einsum("irh,jh->rij", grad, v, preferred_element_type=F32)
    inner = jnp.sum(probs * grad_probs, axis=-1, keepdims=True)
    grad_scores = (probs * (grad_probs - inner)).astype(BF16)
    grad_q = jnp.einsum("rij,jh->irh", grad_scores, k, preferred_element_type=F32) * score_scale
    grad_k = jnp.einsum("rij,irh->jh", grad_scores, q, preferred_element_type=F32) * score_scale
    grad_v = jnp.einsum("rij,irh->jh", probs.astype(BF16), grad, preferred_element_type=F32)
    return grad_q, grad_k, grad_v


def shards_plain(
    tokens,
    cotangent,
    gain_attn,
    gain_ffn,
    w_query,
    key_weight,
    value_weight,
    w_out,
    expert_gate,
    expert_up,
    expert_down,
    expert_ids,
    gates,
    lengths,
    order,
):
    rows, width = tokens.shape
    members = lax.axis_size("expert")
    member = lax.axis_index("expert")
    span = rows * members
    own_experts, ff = expert_gate.shape[1], expert_gate.shape[2]
    capacity = rows * TOP // own_experts
    q_cols = w_query.shape[1] // members
    kv_cols = key_weight.shape[1] // members
    kv_heads = kv_cols // HEAD_SIZE
    repeat = QUERY_HEADS // KEY_VALUE_HEADS

    def mine(weight, cols):
        return lax.dynamic_slice_in_dim(weight, member * cols, cols, axis=1)

    devices = lax.axis_size("dp")
    phases = [
        functools.partial(phase, members)
        for phase in (plain_first, plain_second, plain_third, plain_fourth)
    ]

    pack = jnp.concatenate(
        [
            mine(w_query, q_cols),
            mine(key_weight, kv_cols),
            mine(value_weight, kv_cols),
            mine(w_out, q_cols),
            gain_attn[:, None],
            gain_ffn[:, None],
            jnp.zeros((gain_attn.shape[0], 126), BF16),
        ],
        axis=1,
    )
    route = jnp.concatenate([expert_ids.astype(F32), gates], axis=1)
    tokens_all, cot_all, route_all, pack_all, gate_all = phases[0](
        tokens, cotangent, route, pack, expert_gate.reshape(-1, own_experts * ff)
    )
    tokens_all = tokens_all.reshape(span, width).astype(F32)
    cot_all = cot_all.reshape(span, width)
    route_all = route_all.reshape(span, 2 * TOP)
    pack_all = pack_all.reshape(width, -1)
    gate_all = gate_all.reshape(width, -1)
    qkv_cols = q_cols + 2 * kv_cols
    w_qkv = pack_all[:, :qkv_cols]
    wo = pack_all[:, qkv_cols : qkv_cols + q_cols]
    gain_one = pack_all[:, qkv_cols + q_cols].astype(F32)[None]
    gain_two = pack_all[:, qkv_cols + q_cols + 1].astype(F32)[None]

    segment, position = layout(lengths[0], order[0], span)
    cosine, sine = rotation(position)
    place = jnp.arange(span, dtype=jnp.int32)
    allowed = (segment[:, None] == segment[None, :]) & (place[None, :] <= place[:, None])
    factor_one = rms_factor(tokens_all)
    normed_attn = (tokens_all * factor_one * gain_one).astype(BF16)
    qkv = dot(normed_attn, w_qkv)
    qk = rotate(qkv[:, : q_cols + kv_cols], cosine, sine).astype(BF16)
    v = qkv[:, q_cols + kv_cols :].astype(BF16)
    q_heads = jnp.moveaxis(qk[:, :q_cols].reshape(span, kv_heads, repeat, HEAD_SIZE), 1, 0)
    k_heads = jnp.moveaxis(qk[:, q_cols:].reshape(span, kv_heads, HEAD_SIZE), 1, 0)
    v_heads = jnp.moveaxis(v.reshape(span, kv_heads, HEAD_SIZE), 1, 0)
    attended, probs = jax.vmap(functools.partial(attend_forward, allowed=allowed))(
        q_heads, k_heads, v_heads
    )
    attended = jnp.moveaxis(attended, 0, 1).reshape(span, q_cols).astype(BF16)
    attn_part = dot_nt(attended, wo).astype(BF16).reshape(members, rows, width)
    residual, normed_all, up_all, down_all = phases[1](
        attn_part,
        tokens,
        gain_two,
        expert_up.reshape(-1, own_experts * ff),
        expert_down.reshape(-1, own_experts * ff),
    )
    normed_all = normed_all.reshape(span, width)
    up_all, down_all = up_all.reshape(width, -1), down_all.reshape(width, -1)

    mixture, grad_normed, *by_kind = experts(
        own_experts, capacity, route_all, normed_all, cot_all, gate_all, up_all, down_all
    )
    output = (residual + branch_scale * scatter(mixture, "expert")).astype(BF16)
    by_kind = [one.reshape(devices, -1, own_experts * ff) for one in by_kind]

    grad_residual, gain_two_part, grad_attn_out, sum_gate, sum_up = phases[2](
        grad_normed.reshape(members, rows, width),
        residual,
        cotangent,
        gain_two,
        by_kind[0],
        by_kind[1],
    )
    grad_attn_out = grad_attn_out.reshape(span, width)
    term_out = dot_tn(grad_attn_out, attended)
    grad_attended = dot(grad_attn_out, wo).astype(BF16)
    grad_heads = jnp.moveaxis(grad_attended.reshape(span, kv_heads, repeat, HEAD_SIZE), 1, 0)
    grad_q, grad_k, grad_v = jax.vmap(functools.partial(attend_backward, allowed=allowed))(
        q_heads, k_heads, v_heads, probs, grad_heads
    )
    grad_qk = jnp.concatenate(
        [
            jnp.moveaxis(grad_q, 0, 1).reshape(span, q_cols),
            jnp.moveaxis(grad_k, 0, 1).reshape(span, kv_cols),
        ],
        axis=1,
    )
    grad_qkv = jnp.concatenate(
        [
            rotate(grad_qk, cosine, sine, back=True).astype(BF16),
            jnp.moveaxis(grad_v, 0, 1).reshape(span, kv_cols).astype(BF16),
        ],
        axis=1,
    )
    grad_norm_part = dot_nt(grad_qkv, w_qkv)
    gain_one_part = jnp.sum(grad_norm_part * tokens_all * factor_one, axis=0)
    term_qkv = dot_tn(normed_attn, grad_qkv)
    packed_grads = jnp.concatenate(
        [
            term_qkv,
            term_out,
            gain_one_part[:, None],
            gain_two_part.reshape(-1, 1),
            jnp.zeros((width, 126), F32),
        ],
        axis=1,
    )
    grad_tokens, per_member, sum_down = phases[3](
        grad_norm_part.astype(BF16).reshape(members, rows, width),
        grad_residual,
        tokens,
        gain_one,
        packed_grads.astype(BF16).reshape(devices, -1, packed_grads.shape[1]),
        by_kind[2],
    )
    per_member = per_member.astype(F32)

    def columns(first, cols):
        part = per_member[:, :, first : first + cols]
        return jnp.moveaxis(part, 0, 1).reshape(part.shape[1], -1)

    gains = jnp.sum(per_member[:, :, qkv_cols + q_cols :], axis=0)
    return (
        output,
        grad_tokens,
        gains[:, 0],
        gains[:, 1],
        columns(0, q_cols),
        columns(q_cols, kv_cols),
        columns(q_cols + kv_cols, kv_cols),
        columns(qkv_cols, q_cols),
        sum_gate.reshape(-1, own_experts, ff),
        sum_up.reshape(-1, own_experts, ff),
        sum_down.reshape(-1, own_experts, ff),
    )


def shards_fast(
    tokens,
    cotangent,
    gain_attn,
    gain_ffn,
    w_query,
    key_weight,
    value_weight,
    w_out,
    expert_gate,
    expert_up,
    expert_down,
    expert_ids,
    gates,
    lengths,
    order,
):
    rows, width = tokens.shape
    members, devices = lax.axis_size("expert"), lax.axis_size("dp")
    span = rows * members
    own_experts, ff = expert_gate.shape[1], expert_gate.shape[2]
    capacity = rows * TOP // own_experts
    segment, position = layout(lengths[0], order[0], span)
    lane = jnp.arange(LANES, dtype=jnp.int32) % HEAD_SIZE
    half = HEAD_SIZE // 2
    frequency = rope_base ** (-((lane % half).astype(F32) * (2.0 / HEAD_SIZE)))
    angles = position[:, None] * frequency[None, :]
    cosine, sine = jnp.cos(angles), jnp.where(lane < half, -1.0, 1.0) * jnp.sin(angles)
    spare = (0, span - gain_attn.shape[0])
    small = jnp.stack(
        [segment.astype(F32), jnp.pad(gain_attn.astype(F32), spare), jnp.pad(gain_ffn.astype(F32), spare)]
    )
    (
        cot_all, route_all, pack_all, gate_all, up_all, down_all,
        normed_attn, qkv, kx, vx, probs, attended, residual, normed_all, gains,
    ) = forward_phase(
        members, tokens, cotangent, expert_ids.T, gates.T, w_query, key_weight, value_weight, w_out,
        small, *(w.transpose(1, 0, 2) for w in (expert_gate, expert_up, expert_down)), cosine, sine,
    )
    cot_all = cot_all.reshape(span, width)
    normed_all = normed_all.reshape(span, width)
    route_all = route_all.reshape(span, 2 * TOP)
    gate_all, up_all, down_all = (w.reshape(width, -1) for w in (gate_all, up_all, down_all))
    mixture, grad_normed, *by_kind = experts(
        own_experts, capacity, route_all, normed_all, cot_all, gate_all, up_all, down_all
    )
    by_kind = [one.reshape(devices, -1, own_experts * ff) for one in by_kind]

    output, grad_residual, gain_two_part, grad_attn_out, sum_gate, sum_up = third_phase(
        members, own_experts,
        grad_normed.reshape(members, rows, width),
        mixture.reshape(members, rows, width),
        residual,
        cotangent,
        gains,
        by_kind[0],
        by_kind[1],
    )
    (
        grad_tokens, grad_gains, d_query, d_key, d_value, d_out, d_down,
    ) = backward_phase(
        members, own_experts,
        grad_attn_out.reshape(span, width),
        grad_residual,
        gain_two_part,
        tokens,
        by_kind[2],
        gains,
        pack_all,
        normed_attn, qkv, kx, vx, probs, attended, cosine, sine,
    )
    return (
        output,
        grad_tokens,
        grad_gains[0],
        grad_gains[1],
        d_query,
        d_key,
        d_value,
        d_out,
        sum_gate.transpose(1, 0, 2),
        sum_up.transpose(1, 0, 2),
        d_down.transpose(1, 0, 2),
    )


def solution(mesh):
    both = P(("dp", "expert"), None)
    row, rows = P("dp"), P("dp", None)
    experts = P("dp", "expert", None)
    fast = mesh.shape["dp"] == 8 and mesh.shape["expert"] == 4
    return jax.shard_map(
        shards_fast if fast else shards_plain,
        mesh=mesh,
        in_specs=(both, both, row, row, rows, rows, rows, rows)
        + (experts, experts, experts, both, both, rows, rows),
        out_specs=(both, both, row, row, rows, rows, rows, rows, experts, experts, experts),
        check_vma=False,
    )
```

```python
import functools

import jax
import jax.numpy as jnp
from jax import lax
from jax.experimental import pallas as pl
from jax.experimental.pallas import tpu as pltpu
from jax.sharding import PartitionSpec as P

QUERY_HEADS = 24
KEY_VALUE_HEADS = 8
HEAD_SIZE = 64
TOP = 8

epsilon = 1e-06
rope_base = 10000.0
score_scale = 0.015625
branch_scale = 0.22
F32 = jnp.float32
BF16 = jnp.bfloat16
MESH = pl.DeviceIdType.MESH
LANES = 128
VMEM_LIMIT = 60 * 2**20


def layout(lengths_row, order_row, span):
    seqs = lengths_row.shape[0]
    slot_ids = jnp.arange(seqs, dtype=jnp.int32)
    picked = jnp.sum(
        jnp.where(order_row[:, None] == slot_ids[None, :], lengths_row[None, :], 0), axis=1
    )
    before = slot_ids[:, None] >= slot_ids[None, :]
    seq_ends = jnp.sum(jnp.where(before, picked[None, :], 0), axis=1)
    place = jnp.arange(span, dtype=jnp.int32)
    passed = place[:, None] >= seq_ends[None, :]
    segment = jnp.sum(passed.astype(jnp.int32), axis=1)
    start = jnp.sum(jnp.where(passed, picked[None, :], 0), axis=1)
    return segment, (place - start).astype(F32)


def rotation(position):
    half = HEAD_SIZE // 2
    frequency = rope_base ** (-(jnp.arange(half, dtype=F32) * (2.0 / HEAD_SIZE)))
    angles = position[:, None] * frequency[None, :]
    return jnp.cos(angles), jnp.sin(angles)


def rotate(rows, cosine, sine, back=False):
    t = rows.shape[0]
    heads = rows.reshape(t, -1, 2, HEAD_SIZE // 2)
    a, b = heads[:, :, 0], heads[:, :, 1]
    c, s = cosine[:, None, :], sine[:, None, :]
    if back:
        s = -s
    return jnp.stack([a * c - b * s, b * c + a * s], axis=2).reshape(t, -1)


def dot(a, b):
    return jnp.dot(a, b, preferred_element_type=F32)


def dot_nt(a, b):
    return jnp.einsum("tc,dc->td", a, b, preferred_element_type=F32)


def dot_tn(a, b):
    return jnp.einsum("td,tc->dc", a, b, preferred_element_type=F32)


def rms_factor(rows):
    return lax.rsqrt(jnp.mean(rows * rows, axis=-1, keepdims=True) + epsilon)


def norm_back(rows, factor, gain, grad):
    scaled = gain * grad
    return factor * scaled - rows * (factor * factor * factor) * jnp.mean(
        scaled * rows, axis=-1, keepdims=True
    )


def gather(x, axis):
    return lax.all_gather(x, axis, axis=0, tiled=True)


def scatter(x, axis):
    return lax.psum_scatter(x.astype(BF16), axis, scatter_dimension=0, tiled=True).astype(F32)


class Links:
    def __init__(self, send, recv, local, members):
        self.send, self.recv, self.local = send, recv, local
        self.remotes = self.locals = 0
        self.members = members
        self.d, self.z = lax.axis_index("dp"), lax.axis_index("expert")
        d = self.d
        core, x, y = d % 2, (d // 2) % 2, d // 4
        self.core = core
        self.sib = d + 1 - 2 * core
        self.x = d + 2 - 4 * x
        self.y = d + 4 - 8 * y
        self.diag = self.x + 4 - 8 * y
        self.waiting = []

    def other(self, d):
        return d + 1 - 2 * self.core

    def greet(self):
        barrier = pltpu.get_barrier_semaphore()
        last = self.members - 1

        def hello(d, z):
            pl.semaphore_signal(barrier, inc=1, device_id=(d, z), device_id_type=MESH)

        for d in (self.sib, self.x, self.y):
            hello(d, self.z)
        pl.when(self.z > 0)(lambda: hello(self.d, self.z - 1))
        pl.when(self.z < last)(lambda: hello(self.d, self.z + 1))
        ends = (self.z == 0).astype(jnp.int32) + (self.z == last).astype(jnp.int32)
        pl.semaphore_wait(barrier, 5 - ends)

    def remote(self, src, dst, to):
        k = self.remotes
        self.remotes += 1
        return pltpu.make_async_remote_copy(
            src_ref=src,
            dst_ref=dst,
            send_sem=self.send.at[k],
            recv_sem=self.recv.at[k],
            device_id=to,
            device_id_type=MESH,
        )

    def push(self, src, dst, d):
        copy = self.remote(src, dst, (d, self.z))
        copy.start()
        self.waiting.append(copy.wait_send)
        return copy

    def move(self, src, dst):
        k = self.locals
        self.locals += 1
        copy = pltpu.make_async_copy(src, dst, self.local.at[k])
        copy.start()
        return copy

    def finish(self):
        for wait in self.waiting:
            wait()


def run(order, **chains):
    for name in order:
        next(chains[name], None)
    chains = list(chains.values())
    while chains:
        for chain in list(chains):
            try:
                next(chain)
            except StopIteration:
                chains.remove(chain)


def line_gather(links, own, full):
    z, last = links.z, links.members - 1
    local = links.move(own, full.at[z])
    right, left = (links.d, z + 1), (links.d, z - 1)
    to_right, to_left = [], []
    for s in range(last):
        at_r, at_l = jnp.maximum(z - s, 0), jnp.minimum(z + s, last)
        to_right.append(links.remote(own if s == 0 else full.at[at_r], full.at[at_r], right))
        to_left.append(links.remote(own if s == 0 else full.at[at_l], full.at[at_l], left))
    for s in range(last):
        send_r, send_l = (z < last) & (z >= s), (z > 0) & (z + s <= last)
        pl.when(send_r)(to_right[s].start)
        pl.when(send_l)(to_left[s].start)
        yield
        pl.when((z > 0) & (z - 1 >= s))(to_right[s].wait_recv)
        pl.when((z < last) & (z + 1 + s <= last))(to_left[s].wait_recv)
    for s in range(last):
        send_r, send_l = (z < last) & (z >= s), (z > 0) & (z + s <= last)
        pl.when(send_r)(to_right[s].wait_send)
        pl.when(send_l)(to_left[s].wait_send)
    local.wait()


def add_rows(target, other, step=16):
    rows = target.shape[0]

    @pl.loop(0, rows // step)
    def _(i):
        at = pl.ds(pl.multiple_of(i * step, step), step)
        target[at] = (target[at].astype(F32) + other[at].astype(F32)).astype(target.dtype)


def line_sum(links, part, acc, from_left, from_right, finish, own=None, full=None, parts=2):
    z, last = links.z, links.members - 1
    rows = acc.shape[1] // parts
    spans = [pl.ds(h * rows, rows) for h in range(parts)]
    right, left = (links.d, z + 1), (links.d, z - 1)
    sum_r, sum_l, go_r, go_l, local = {}, {}, {}, {}, []
    for h, span in enumerate(spans):
        for o in range(last + 1):
            if o > 0:
                sum_r[h, o] = links.remote(acc.at[o, span], from_left.at[o, span], right)
            if o < last:
                sum_l[h, o] = links.remote(acc.at[o, span], from_right.at[o, span], left)
        for s in range(last if own is not None else 0):
            at_r, at_l = jnp.maximum(z - s, 0), jnp.minimum(z + s, last)
            here_r, here_l = full.at[at_r, span], full.at[at_l, span]
            go_r[h, s] = links.remote(own.at[span] if s == 0 else here_r, here_r, right)
            go_l[h, s] = links.remote(own.at[span] if s == 0 else here_l, here_l, left)

    def pass_right(h, o):
        @pl.when(z > 0)
        def _():
            sum_r[h, o].wait_recv()
            add_rows(acc.at[o, spans[h]], from_left.at[o, spans[h]])

        sum_r[h, o].start()

    def pass_left(h, o):
        @pl.when(z < last)
        def _():
            sum_l[h, o].wait_recv()
            add_rows(acc.at[o, spans[h]], from_right.at[o, spans[h]])

        sum_l[h, o].start()

    def send(h, s):
        pl.when((z < last) & (z >= s))(go_r[h, s].start)
        pl.when((z > 0) & (z + s <= last))(go_l[h, s].start)

    @pl.when(z == 0)
    def _():
        from_left[0] = jnp.zeros(from_left.shape[1:], from_left.dtype)

    @pl.when(z == last)
    def _():
        from_right[last] = jnp.zeros(from_right.shape[1:], from_right.dtype)

    made = set()
    for j in range(last):
        for o in (last - j, j):
            if o not in made:
                made.add(o)
                part(o)
        for h in range(parts):
            pl.when((z < last - j) & (2 * z < last))(functools.partial(pass_right, h, last - j))
            pl.when(z > j)(functools.partial(pass_left, h, j))
            pl.when((z < last - j) & (2 * z >= last))(functools.partial(pass_right, h, last - j))
            yield
    for h in range(parts):
        for o in range(last + 1):
            if o > 0:
                pl.when(z == o)(sum_r[h, o].wait_recv)
            if o < last:
                pl.when(z == o)(sum_l[h, o].wait_recv)
        finish(h * rows, rows)
        if own is None:
            continue
        send(h, 0)
        local.append(links.move(own.at[spans[h]], full.at[z, spans[h]]))
        yield
    for s in range(last if own is not None else 0):
        for h in range(parts):
            pl.when((z > 0) & (z - 1 >= s))(go_r[h, s].wait_recv)
            pl.when((z < last) & (z + 1 + s <= last))(go_l[h, s].wait_recv)
            if s + 1 < last:
                send(h, s + 1)
            yield
    for h in range(parts):
        for o in range(last + 1):
            if o > 0:
                pl.when(z < o)(sum_r[h, o].wait_send)
            if o < last:
                pl.when(z > o)(sum_l[h, o].wait_send)
        for s in range(last if own is not None else 0):
            pl.when((z < last) & (z >= s))(go_r[h, s].wait_send)
            pl.when((z > 0) & (z + s <= last))(go_l[h, s].wait_send)
    for copy in local:
        copy.wait()


def plane_gather(links, own, full):
    half = own.shape[0] // 2
    first, second = pl.ds(0, half), pl.ds(half, half)
    me = links.d
    local = links.move(own, full.at[me])
    by_x, by_y = {}, {}
    for by, d, h in ((by_y, links.y, first), (by_x, links.x, second), (by_x, links.x, first), (by_y, links.y, second)):
        by[h.start // half] = links.push(own.at[h], full.at[me, h], d)
    to_sib = [links.push(own, full.at[me], links.sib)]

    def share(d, h):
        to_sib.append(links.push(full.at[d, h], full.at[d, h], links.sib))

    yield
    by_y[0].wait_recv()
    over_x = links.push(full.at[links.y, first], full.at[links.y, first], links.x)
    share(links.y, first)
    by_x[1].wait_recv()
    over_y = links.push(full.at[links.x, second], full.at[links.x, second], links.y)
    share(links.x, second)
    yield
    by_x[0].wait_recv()
    share(links.x, first)
    by_y[1].wait_recv()
    share(links.y, second)
    yield
    over_x.wait_recv()
    share(links.diag, first)
    over_y.wait_recv()
    share(links.diag, second)
    yield
    for copy in to_sib:
        copy.wait_recv()
    local.wait()


def plane_scatter(links, part, mine, theirs, mid_x, mid_y, end_x, end_y):
    half = part.shape[1] // 2
    first, second = pl.ds(0, half), pl.ds(half, half)
    chips = (links.d, links.x, links.y, links.diag)
    from_sib, load = {}, {}
    held = [part.at[chip] if mine is None else mine.at[k] for k, chip in enumerate(chips)]
    for k in (3, 1, 2, 0):
        from_sib[k] = links.push(part.at[links.other(chips[k])], theirs.at[k], links.sib)
        if mine is not None:
            load[k] = links.move(part.at[chips[k]], held[k])
    yield
    for k in (3, 1, 2):
        if load:
            load[k].wait()
        from_sib[k].wait_recv()
        add_rows(held[k], theirs.at[k])
        if k == 3:
            to_mid_x = links.push(held[3].at[first], mid_x, links.x)
            to_mid_y = links.push(held[3].at[second], mid_y, links.y)
        if k == 1:
            to_end_x = links.push(held[1].at[first], end_x.at[first], links.x)
        if k == 2:
            to_end_y = links.push(held[2].at[second], end_y.at[second], links.y)
        if k != 1:
            yield
    to_mid_y.wait_recv()
    add_rows(held[1].at[second], mid_y)
    rest_x = links.push(held[1].at[second], end_x.at[second], links.x)
    to_mid_x.wait_recv()
    add_rows(held[2].at[first], mid_x)
    rest_y = links.push(held[2].at[first], end_y.at[first], links.y)
    yield
    if load:
        load[0].wait()
    from_sib[0].wait_recv()
    to_end_x.wait_recv()
    to_end_y.wait_recv()
    rest_x.wait_recv()
    rest_y.wait_recv()
    yield


def plane_scratch(rows, cols, mine=True):
    return [pltpu.VMEM((4, rows, cols), BF16)] * mine + [
        pltpu.VMEM((4, rows, cols), BF16),
        pltpu.VMEM((rows // 2, cols), BF16),
        pltpu.VMEM((rows // 2, cols), BF16),
        pltpu.VMEM((rows, cols), BF16),
        pltpu.VMEM((rows, cols), BF16),
    ]


def plane_result(mine, theirs, end_x, end_y, out, step=16):
    @pl.loop(0, out.shape[-2] // step)
    def _(i):
        at = pl.ds(pl.multiple_of(i * step, step), step)
        own = mine[at].astype(F32) + theirs[0, at].astype(F32)
        total = (own + end_x[at].astype(F32) + end_y[at].astype(F32)).astype(out.dtype)
        if len(out.shape) == 2:
            out[at] = total
        else:
            cols = out.shape[2]
            for e in range(out.shape[0]):
                out[e, at] = total[:, e * cols : (e + 1) * cols]


def plane_total(links, part, scratch, total, out, stores):
    yield from plane_scatter(links, part, *scratch)
    plane_result(scratch[0].at[0], scratch[1], scratch[4], scratch[5], total)
    stores.append(links.move(total, out))


def line_result(z, acc, from_left, from_right, at):
    return (
        acc[z, at].astype(F32) + from_left[z, at].astype(F32) + from_right[z, at].astype(F32)
    )


ANY = pl.BlockSpec(memory_space=pl.ANY)
VMEM = pl.BlockSpec(memory_space=pltpu.VMEM)


def comm_call(kernel, name, number, members, remotes, locals_, in_specs, out_specs, out_shape, scratch):
    return pl.pallas_call(
        functools.partial(kernel, members),
        out_shape=out_shape,
        in_specs=in_specs,
        out_specs=out_specs,
        scratch_shapes=[
            pltpu.SemaphoreType.DMA((remotes,)),
            pltpu.SemaphoreType.DMA((remotes,)),
            pltpu.SemaphoreType.DMA((locals_,)),
            *scratch,
        ],
        compiler_params=pltpu.CompilerParams(
            collective_id=number, has_side_effects=True, vmem_limit_bytes=VMEM_LIMIT
        ),
        name=name,
    )


def sds(shape, dtype):
    return jax.ShapeDtypeStruct(shape, dtype)


def third_kernel(members, part, mixture, residual, cot, gain, gate, up, output, grad_residual, gain_part, out_all, gate_out, up_out, send, recv, local, acc, from_left, from_right, acc_m, left_m, right_m, grad_out, gate_sum, up_sum, *rest):
    links = Links(send, recv, local, members)
    for_gate, for_up = rest[:6], rest[6:]
    stores = []

    def block_loads(source, into):
        loads = [links.move(source.at[o], into.at[o]) for o in range(members)]
        return lambda o: loads[o].wait()

    load_part, load_mixture = block_loads(part, acc), block_loads(mixture, acc_m)
    links.greet()

    def finish(first, count):
        @pl.loop(0, count // 16)
        def _(i):
            at = pl.ds(pl.multiple_of(first + i * 16, 16), 16)
            grad = line_result(links.z, acc, from_left, from_right, at)
            here = residual[at]
            factor = rms_factor(here)
            gain_part[...] += jnp.sum(grad * here * factor, axis=0, keepdims=True)
            total = cot[at].astype(F32) + norm_back(here, factor, gain[1:2], grad)
            grad_residual[at] = total
            grad_out[at] = (branch_scale * total).astype(BF16)

    def chain():
        gain_part[...] = jnp.zeros(gain_part.shape, F32)
        yield from line_sum(
            links, load_part, acc, from_left, from_right, finish, grad_out, out_all
        )

    def finish_mixture(first, count):
        @pl.loop(0, count // 16)
        def _(i):
            at = pl.ds(pl.multiple_of(first + i * 16, 16), 16)
            here = residual[at] + branch_scale * line_result(links.z, acc_m, left_m, right_m, at)
            output[at] = here.astype(BF16)

    def mixture_chain():
        yield from line_sum(links, load_mixture, acc_m, left_m, right_m, finish_mixture)

    run(
        THIRD_ORDER,
        m=mixture_chain(),
        z=chain(),
        g=plane_total(links, gate, for_gate, gate_sum, gate_out, stores),
        u=plane_total(links, up, for_up, up_sum, up_out, stores),
    )
    for store in stores:
        store.wait()
    links.finish()


THIRD_ORDER = "uzuzzgugmmzzguzzzgzmzmzmmzmugguuzm"


def third_phase(members, own_experts, part, mixture, residual, cot, gain, gate, up):
    rows, width = cot.shape
    blocks = pltpu.VMEM((members, rows, width), BF16)
    return comm_call(
        third_kernel, "phase_three", 3, members, 80, 24,
        [ANY, ANY, VMEM, VMEM, VMEM, ANY, ANY], [VMEM, VMEM, VMEM, ANY, ANY, ANY],
        [
            sds((rows, width), BF16),
            sds((rows, width), F32),
            sds((1, width), F32),
            sds((members, rows, width), BF16),
            sds((own_experts, gate.shape[1], gate.shape[2] // own_experts), F32),
            sds((own_experts, up.shape[1], up.shape[2] // own_experts), F32),
        ],
        [blocks] * 6
        + [pltpu.VMEM((rows, width), BF16)]
        + [pltpu.VMEM((own_experts, gate.shape[1], gate.shape[2] // own_experts), F32)] * 2
        + plane_scratch(*gate.shape[1:])
        + plane_scratch(*up.shape[1:]),
    )(part, mixture, residual, cot, gain, gate, up)


def lane_ids(rows):
    return lax.broadcasted_iota(jnp.int32, (rows, LANES), 1)


def dims(a, b):
    return (((a,), (b,)), ((), ()))


def mm(a, b):
    return lax.dot_general(a, b, dims(1, 0), preferred_element_type=F32)


def mm_nt(a, b):
    return lax.dot_general(a, b, dims(1, 1), preferred_element_type=F32)


def mm_tn(a, b):
    return lax.dot_general(a, b, dims(0, 0), preferred_element_type=F32)


def first_lanes():
    same = lax.broadcasted_iota(jnp.int32, (16, LANES), 0) == lax.broadcasted_iota(jnp.int32, (16, LANES), 1)
    return same.astype(BF16)


def expert_kernel(capacity, own_experts, route, normed, cot, w_gate, w_up, w_down, mixture, grad_normed, d_gate, d_up, d_down, mix_sum, grad_sum, slot_cols, weight_cols, slot_rows):
    e = pl.program_id(0)
    span = normed.shape[0]

    @pl.when(e == 0)
    def _():
        mix_sum[...] = jnp.zeros(mix_sum.shape, F32)
        grad_sum[...] = jnp.zeros(grad_sum.shape, F32)
        lane = lane_ids(LANES)
        name = (lax.axis_index("expert") * own_experts + lane).astype(F32)
        name = jnp.where(lane < own_experts, name, -1.0)
        upto = (lane <= lax.broadcasted_iota(jnp.int32, (LANES, LANES), 0)).astype(BF16)
        before = jnp.zeros((1, LANES), F32)
        for b in range(span // LANES):
            at = pl.ds(b * LANES, LANES)
            chosen, weight = jnp.zeros((LANES, LANES), F32), jnp.zeros((LANES, LANES), F32)
            for k in range(TOP):
                named = route[at, k : k + 1] == name
                chosen = jnp.where(named, 1.0, chosen)
                weight = jnp.where(named, route[at, TOP + k : TOP + k + 1], weight)
            slot = mm(upto, chosen.astype(BF16)) + (before - 1.0)
            slot_cols[at] = jnp.where((chosen > 0.0) & (slot < capacity), slot, -1.0)
            weight_cols[at] = weight
            before = before + jnp.sum(chosen, axis=0, keepdims=True)
        slot_rows[...] = mm_nt(first_lanes(), slot_cols[...].astype(BF16))

    def column(values):
        return jnp.sum(jnp.where(lane_ids(span) == e, values[...], 0.0), axis=1, keepdims=True)

    slots = lax.broadcasted_iota(jnp.int32, (capacity, span), 0).astype(F32)
    pick = (slot_rows[pl.ds(e, 1)] == slots).astype(BF16)
    puts = column(slot_cols) == lax.broadcasted_iota(jnp.int32, (span, capacity), 1).astype(F32)
    put = puts.astype(BF16)
    gate_row = jnp.sum(jnp.where(puts, column(weight_cols), 0.0), axis=0, keepdims=True)
    same = lax.broadcasted_iota(jnp.int32, (capacity, capacity), 0) == lax.broadcasted_iota(jnp.int32, (capacity, capacity), 1)
    gate_col = jnp.sum(jnp.where(same, gate_row, 0.0), axis=1, keepdims=True)
    received = mm(pick, normed[...]).astype(BF16)
    pre_gate, pre_up = mm(received, w_gate[...]), mm(received, w_up[...])
    sig = 1.0 / (1.0 + jnp.exp(-pre_gate))
    silu = pre_gate * sig
    activ = (silu * pre_up).astype(BF16)
    produced = (gate_col * mm_nt(activ, w_down[...])).astype(BF16)
    mix_sum[...] += mm(put, produced)
    grad_out = (gate_col * (branch_scale * mm(pick, cot[...]))).astype(BF16)
    grad_activ = mm(grad_out, w_down[...])
    grad_gate = (grad_activ * pre_up * (sig * (1.0 + pre_gate * (1.0 - sig)))).astype(BF16)
    grad_up = (grad_activ * silu).astype(BF16)
    grad_pair = (mm_nt(grad_gate, w_gate[...]) + mm_nt(grad_up, w_up[...])).astype(BF16)
    grad_sum[...] += mm(put, grad_pair)
    d_gate[...] = mm_tn(received, grad_gate).astype(BF16)
    d_up[...] = mm_tn(received, grad_up).astype(BF16)
    d_down[...] = mm_tn(grad_out, activ).astype(BF16)

    @pl.when(e == pl.num_programs(0) - 1)
    def _():
        mixture[...] = mix_sum[...].astype(BF16)
        grad_normed[...] = grad_sum[...].astype(BF16)


def experts(own_experts, capacity, route, normed, cot, w_gate, w_up, w_down):
    span, width = normed.shape
    ff = w_gate.shape[1] // own_experts
    whole = pl.BlockSpec((span, width), lambda e: (0, 0))
    column = pl.BlockSpec((width, ff), lambda e: (0, e))
    grads = jax.ShapeDtypeStruct(w_gate.shape, BF16)
    rows = jax.ShapeDtypeStruct((span, width), BF16)
    return pl.pallas_call(
        functools.partial(expert_kernel, capacity, own_experts),
        grid=(own_experts,),
        in_specs=[pl.BlockSpec(route.shape, lambda e: (0, 0)), whole, whole, column, column, column],
        out_specs=[whole, whole, column, column, column],
        out_shape=[rows, rows, grads, grads, grads],
        scratch_shapes=[
            pltpu.VMEM((span, width), F32),
            pltpu.VMEM((span, width), F32),
            pltpu.VMEM((span, LANES), F32),
            pltpu.VMEM((span, LANES), F32),
            pltpu.VMEM((16, span), F32),
        ],
        compiler_params=pltpu.CompilerParams(vmem_limit_bytes=VMEM_LIMIT),
        name="experts",
    )(route, normed, cot, w_gate, w_up, w_down)


def turn(x, cosine, sine):
    half = HEAD_SIZE // 2
    ahead, behind = pltpu.roll(x, LANES - half, axis=1), pltpu.roll(x, half, axis=1)
    partner = jnp.where(lane_ids(x.shape[0]) % HEAD_SIZE < half, ahead, behind)
    return x * cosine + partner * sine


def spread(block, at, out):
    low = lane_ids(block.shape[0]) < HEAD_SIZE
    other = pltpu.roll(block, HEAD_SIZE, axis=1)
    zero = jnp.zeros_like(block)
    out[0, 0, at] = jnp.where(low, block, zero).astype(BF16)
    out[0, 1, at] = jnp.where(low, zero, other).astype(BF16)
    out[1, 0, at] = jnp.where(low, other, zero).astype(BF16)
    out[1, 1, at] = jnp.where(low, zero, block).astype(BF16)


def attention_setup(segment, bias):
    span = bias.shape[0]
    same = lax.broadcasted_iota(jnp.int32, (LANES, LANES), 0) == lane_ids(LANES)
    for b in range(span // LANES):
        at = pl.ds(b * LANES, LANES)
        row = b * LANES + lax.broadcasted_iota(jnp.int32, (LANES, span), 0)
        col = lax.broadcasted_iota(jnp.int32, (LANES, span), 1)
        here = segment[:, b * LANES : (b + 1) * LANES]
        here = jnp.sum(jnp.where(same, here, 0.0), axis=1, keepdims=True)
        ok = (here == segment) & (col <= row)
        bias[at] = jnp.where(ok, 0.0, -1e30)


def weight_columns(pack_all, first, cols):
    return pack_all[:, :, first : first + cols].reshape(-1, cols)


def gain_rows(pack_all, first):
    return mm_nt(first_lanes(), weight_columns(pack_all, first, LANES))


def attend_steps(qkv, kx, vx, bias, probs, attended):
    span, blocks = qkv.shape[0], attended.shape[1] // LANES
    repeat = QUERY_HEADS // KEY_VALUE_HEADS
    for j in range(blocks):
        for b in range(span // LANES):
            at, keys = pl.ds(b * LANES, LANES), (b + 1) * LANES
            q = qkv[at, j * LANES : (j + 1) * LANES]
            total = jnp.zeros((LANES, LANES), F32)
            for half in range(2):
                h = 2 * j + half
                kv = h // repeat
                scores = mm_nt(q, kx[kv, half, :keys]) + bias[at, :keys]
                peak = jnp.max(scores, axis=1, keepdims=True)
                exponent = jnp.exp(scores - peak)
                share = 1.0 / jnp.sum(exponent, axis=1, keepdims=True)
                low = (exponent * share).astype(BF16)
                probs[h, at, :keys] = low
                total += mm(low, vx[kv, half, :keys])
            attended[at, j * LANES : (j + 1) * LANES] = total.astype(BF16)
        yield


def forward_kernel(
    members, tokens, cot, ids, gates, w_query, w_key, w_value, w_out, small, gate, up, down, cosine, sine,
    cot_all, route_all, pack_out, gate_all, up_all, down_all, normed_out, qkv_out, kx_out, vx_out, probs_out, attended_out, residual, normed_all, gains,
    send, recv, local, pack, route, flat, tokens_all, bias, acc, from_left, from_right, normed,
    pack_all, normed_attn, qkv, kx, vx, probs, attended,
):
    links = Links(send, recv, local, members)
    stores = []
    count, _, cols = gate.shape
    loads = [
        [links.move(weight.at[e], flat.at[i, :, e * cols : (e + 1) * cols]) for e in range(count)]
        for i, weight in enumerate((gate, up, down))
    ]
    links.greet()
    route[...] = jnp.concatenate([ids[...].astype(F32), gates[...]], axis=0).T
    rows, width = tokens.shape
    span = rows * members
    q_cols = attended.shape[1]
    qkv_cols = qkv.shape[1]

    def pack_chain():
        loads, at = [], 0
        for weight in (w_query, w_key, w_value, w_out):
            cols = weight.shape[1] // members
            mine = pl.ds(pl.multiple_of(links.z * cols, LANES), cols)
            loads.append(links.move(weight.at[:, mine], pack.at[:, at : at + cols]))
            at += cols
        which = lax.broadcasted_iota(jnp.int32, (16, pack.shape[0]), 0)
        own = pack.shape[0]
        both = jnp.where(which == 0, small[1:2, :own], jnp.where(which == 1, small[2:3, :own], 0.0))
        pack[:, at:] = mm_tn(both.astype(BF16), first_lanes()).astype(BF16)
        for load in loads:
            load.wait()
        yield from plane_gather(links, pack, pack_all)

    def expert_chain(i, full):
        for load in loads[i]:
            load.wait()
        yield from plane_gather(links, flat.at[i], full)

    def produce(o):
        acc[o] = mm_nt(attended[o * rows : (o + 1) * rows], weight_columns(pack_all, qkv_cols, q_cols)).astype(BF16)

    def chain():
        attention_setup(small[0:1], bias)
        yield
        gains[...] = gain_rows(pack_all, qkv_cols + q_cols)

        @pl.loop(0, span // 16)
        def _(i):
            here = tokens_all[i // (rows // 16), pl.ds(pl.multiple_of(i % (rows // 16) * 16, 16), 16)].astype(F32)
            normed_attn[pl.ds(pl.multiple_of(i * 16, 16), 16)] = (here * rms_factor(here) * gains[0:1]).astype(BF16)

        @pl.loop(0, span // LANES)
        def _(i):
            at = pl.ds(pl.multiple_of(i * LANES, LANES), LANES)
            here = mm(normed_attn[at], weight_columns(pack_all, 0, qkv_cols))
            c, s = cosine[at], sine[at]
            for j in range(q_cols // LANES):
                lanes = slice(j * LANES, (j + 1) * LANES)
                qkv[at, lanes] = (turn(here[:, lanes], c, s).astype(BF16).astype(F32) * score_scale).astype(BF16)
            key = turn(here[:, q_cols : q_cols + LANES], c, s)
            value = here[:, q_cols + LANES :]
            qkv[at, q_cols : q_cols + LANES] = key.astype(BF16)
            qkv[at, q_cols + LANES :] = value.astype(BF16)
            spread(key, at, kx)
            spread(value, at, vx)

        yield
        yield from attend_steps(qkv, kx, vx, bias, probs, attended)
        for kept, out in (
            (pack_all, pack_out), (normed_attn, normed_out), (qkv, qkv_out), (kx, kx_out),
            (vx, vx_out), (probs, probs_out), (attended, attended_out),
        ):
            stores.append(links.move(kept, out))

        def finish(first, count):
            @pl.loop(0, count // 16)
            def _(i):
                at = pl.ds(pl.multiple_of(first + i * 16, 16), 16)
                here = tokens[at].astype(F32) + branch_scale * line_result(links.z, acc, from_left, from_right, at)
                residual[at] = here
                normed[at] = (here * rms_factor(here) * gains[1:2]).astype(BF16)

        yield from line_sum(links, produce, acc, from_left, from_right, finish, normed, normed_all)

    run(
        FORWARD_ORDER,
        t=line_gather(links, tokens, tokens_all),
        r=line_gather(links, route, route_all),
        c=line_gather(links, cot, cot_all),
        p=pack_chain(),
        g=expert_chain(0, gate_all),
        u=expert_chain(1, up_all),
        d=expert_chain(2, down_all),
        a=chain(),
    )
    for store in stores:
        store.wait()
    links.finish()


FORWARD_ORDER = "tpptpadtcpgptpaatcargadctaatracauaacrtaagpgrrtaargtgdcrtp"


def forward_phase(members, tokens, cot, ids, gates, w_query, w_key, w_value, w_out, small, gate, up, down, cosine, sine):
    rows, width = tokens.shape
    q_cols = w_query.shape[1] // members
    qkv_cols = q_cols + 2 * w_key.shape[1] // members
    count, own, cols = gate.shape
    pack = (own, qkv_cols + q_cols + LANES)
    route, flat = (rows, 2 * ids.shape[0]), (own, count * cols)
    span = rows * members
    blocks = pltpu.VMEM((members, rows, width), BF16)
    heads = q_cols // HEAD_SIZE
    return comm_call(
        forward_kernel, "forward", 1, members, 120, 40,
        [VMEM, ANY, VMEM, VMEM, ANY, ANY, ANY, ANY, VMEM, ANY, ANY, ANY, VMEM, VMEM],
        [ANY] * 12 + [VMEM, ANY, VMEM],
        [
            sds((members, rows, width), BF16),
            sds((members, *route), F32),
            sds((8, *pack), BF16),
            sds((8, *flat), BF16),
            sds((8, *flat), BF16),
            sds((8, *flat), BF16),
            sds((span, width), BF16),
            sds((span, qkv_cols), BF16),
            sds((2, 2, span, LANES), BF16),
            sds((2, 2, span, LANES), BF16),
            sds((heads, span, span), BF16),
            sds((span, q_cols), BF16),
            sds((rows, width), F32),
            sds((members, rows, width), BF16),
            sds((16, width), F32),
        ],
        [
            pltpu.VMEM(pack, BF16),
            pltpu.VMEM(route, F32),
            pltpu.VMEM((3, *flat), BF16),
            blocks,
            pltpu.VMEM((span, span), F32),
            blocks,
            blocks,
            blocks,
            pltpu.VMEM((rows, width), BF16),
            pltpu.VMEM((8, *pack), BF16),
            pltpu.VMEM((span, width), BF16),
            pltpu.VMEM((span, qkv_cols), BF16),
            pltpu.VMEM((2, 2, span, LANES), BF16),
            pltpu.VMEM((2, 2, span, LANES), BF16),
            pltpu.VMEM((heads, span, span), BF16),
            pltpu.VMEM((span, q_cols), BF16),
        ],
    )(tokens, cot, ids, gates, w_query, w_key, w_value, w_out, small, gate, up, down, cosine, sine)


def attend_back_steps(qkv, kx, vx, probs, grad_attended, cosine, sine, grad_k, grad_v, grad_qkv):
    span = qkv.shape[0]
    blocks = grad_attended.shape[1] // LANES
    repeat = QUERY_HEADS // KEY_VALUE_HEADS
    grad_k[...] = jnp.zeros(grad_k.shape, F32)
    grad_v[...] = jnp.zeros(grad_v.shape, F32)
    for j in range(blocks):
        lanes = slice(j * LANES, (j + 1) * LANES)
        for b in range(span // LANES):
            at, keys = pl.ds(b * LANES, LANES), (b + 1) * LANES
            q, grad = qkv[at, lanes], grad_attended[at, lanes]
            total = jnp.zeros((LANES, LANES), F32)
            for half in range(2):
                h = 2 * j + half
                kv = h // repeat
                low = probs[h, at, :keys]
                share = low.astype(F32)
                grad_probs = mm_nt(grad, vx[kv, half, :keys])
                inner = jnp.sum(share * grad_probs, axis=1, keepdims=True)
                grad_scores = (share * (grad_probs - inner)).astype(BF16)
                total += mm(grad_scores, kx[kv, half, :keys])
                grad_k[kv, half, :keys] += mm_tn(grad_scores, q)
                grad_v[kv, half, :keys] += mm_tn(low, grad)
            grad_qkv[at, lanes] = turn(total * score_scale, cosine[at], -sine[at]).astype(BF16)
        yield
    first = blocks * LANES

    def fold(parts, at):
        low = lane_ids(LANES) < HEAD_SIZE
        same = jnp.where(low, parts[0, 0, at], parts[1, 1, at])
        crossed = jnp.where(low, parts[1, 0, at], parts[0, 1, at])
        return same + pltpu.roll(crossed, HEAD_SIZE, axis=1)

    for b in range(span // LANES):
        at = pl.ds(b * LANES, LANES)
        grad_qkv[at, first : first + LANES] = turn(fold(grad_k, at), cosine[at], -sine[at]).astype(BF16)
        grad_qkv[at, first + LANES :] = fold(grad_v, at).astype(BF16)


def backward_kernel(
    members, grad_out_in, grad_residual, gain_ffn_part, tokens, down, row_gains, pack_in, normed_in, qkv_in, kx_in, vx_in, probs_in, attended_in, cosine, sine,
    grad_tokens, gains, d_query, d_key, d_value, d_out, down_out,
    send, recv, local, acc, from_left, from_right, grad_attended, grad_k, grad_v, grad_qkv, gain_part,
    for_w_out, for_w_query, for_rest, own_out, own_query, own_rest, all_out, all_query, all_rest,
    grad_out_all, pack_all, normed_attn, qkv, kx, vx, probs, attended, d_down, *rest,
):
    links = Links(send, recv, local, members)
    loads = {
        "attended": links.move(attended_in, attended),
        "grad": links.move(grad_out_in, grad_out_all),
        "pack": links.move(pack_in, pack_all),
        "qkv": links.move(qkv_in, qkv),
        "kx": links.move(kx_in, kx),
        "vx": links.move(vx_in, vx),
        "probs": links.move(probs_in, probs),
        "normed": links.move(normed_in, normed_attn),
    }
    stores = []

    def need(*names):
        for name in names:
            if name in loads:
                loads.pop(name).wait()

    links.greet()
    rows, width = tokens.shape
    q_cols, qkv_cols = attended.shape[1], qkv.shape[1]
    kv_cols = (qkv_cols - q_cols) // 2
    with_out, with_query, with_rest, with_down = rest[:5], rest[5:10], rest[10:15], rest[15:]
    pairs = for_w_out.shape[0] // 2
    step = width // pairs

    def weight_term(rows_of, grads, out, cols):
        for i in range(pairs):
            term = mm_tn(rows_of[:, i * step : (i + 1) * step], grads)
            out[2 * i : 2 * i + 2, :, :cols] = term.astype(BF16).reshape(2, step // 2, cols)

    def put_out():
        for m in range(members):
            d_out[:, m * q_cols : (m + 1) * q_cols] = all_out[m].astype(F32)

    def put_query():
        for m in range(members):
            d_query[:, m * q_cols : (m + 1) * q_cols] = all_query[m].astype(F32)

    def put_rest():
        for m in range(members):
            d_key[:, m * kv_cols : (m + 1) * kv_cols] = all_rest[m, :, :kv_cols].astype(F32)
            d_value[:, m * kv_cols : (m + 1) * kv_cols] = all_rest[m, :, kv_cols : 2 * kv_cols].astype(F32)
        total = sum(all_rest[m, :, 2 * kv_cols :].astype(F32) for m in range(members))
        gains[...] = total.T[: gains.shape[0]]

    def weight_chain(fill, part, mine, full, scratch, put):
        fill()
        yield from plane_scatter(links, part, None, *scratch)
        plane_result(part.at[links.d], scratch[0], scratch[3], scratch[4], mine)
        yield from line_gather(links, mine, full)
        put()

    def fill_out():
        need("grad", "attended")
        weight_term(grad_out_all, attended[...], for_w_out, q_cols)

    def fill_query():
        need("normed")
        weight_term(normed_attn, grad_qkv[:, :q_cols], for_w_query, q_cols)

    def fill_rest():
        weight_term(normed_attn, grad_qkv[:, q_cols:], for_rest, 2 * kv_cols)
        which = lax.broadcasted_iota(jnp.int32, (16, width), 0)
        both = jnp.where(which == 0, gain_part[...] / row_gains[0:1], jnp.where(which == 1, gain_ffn_part[...], 0.0))
        columns = mm_tn(both.astype(BF16), first_lanes())
        for_rest[:, :, 2 * kv_cols :] = columns.astype(BF16).reshape(2 * pairs, step // 2, LANES)

    def produce(o):
        at = slice(o * rows, (o + 1) * rows)
        part = mm_nt(grad_qkv[at], weight_columns(pack_all, 0, qkv_cols))
        gain_part[...] += jnp.sum(part * normed_attn[at].astype(F32), axis=0, keepdims=True)
        acc[o] = part.astype(BF16)

    def chain():
        need("grad", "pack")
        wo = weight_columns(pack_all, qkv_cols, q_cols)

        @pl.loop(0, grad_attended.shape[0] // LANES)
        def _(i):
            at = pl.ds(pl.multiple_of(i * LANES, LANES), LANES)
            grad_attended[at] = mm(grad_out_all[at], wo).astype(BF16)

        yield
        need("qkv", "kx", "vx", "probs")
        yield from attend_back_steps(qkv, kx, vx, probs, grad_attended, cosine, sine, grad_k, grad_v, grad_qkv)
        gain_part[...] = jnp.zeros(gain_part.shape, F32)
        need("normed")
        yield

        def finish(first, count):
            @pl.loop(0, count // 16)
            def _(i):
                at = pl.ds(pl.multiple_of(first + i * 16, 16), 16)
                grad = line_result(links.z, acc, from_left, from_right, at)
                here = tokens[at].astype(F32)
                grad_tokens[at] = grad_residual[at] + norm_back(here, rms_factor(here), row_gains[0:1], grad)

        yield from line_sum(links, produce, acc, from_left, from_right, finish)

    run(
        BACKWARD_ORDER,
        d=plane_total(links, down, with_down, d_down, down_out, stores),
        o=weight_chain(fill_out, for_w_out, own_out, all_out, with_out, put_out),
        a=chain(),
        q=weight_chain(fill_query, for_w_query, own_query, all_query, with_query, put_query),
        r=weight_chain(fill_rest, for_rest, own_rest, all_rest, with_rest, put_rest),
    )
    for store in stores:
        store.wait()
    links.finish()


BACKWARD_ORDER = "oadoaoaoaooqaqqdoaqdaqqarorarradrraqrqdaoodaaqdrddrr"


def backward_phase(members, own_experts, grad_out_all, grad_residual, gain_ffn_part, tokens, down, row_gains, pack_all, normed_attn, qkv, kx, vx, probs, attended, cosine, sine):
    rows, width = tokens.shape
    span, q_cols = attended.shape
    qkv_cols = qkv.shape[1]
    kv_cols = (qkv_cols - q_cols) // 2
    devices, own = down.shape[:2]
    line = [pltpu.VMEM((members, rows, width), BF16)] * 3
    three = (q_cols, q_cols, 2 * kv_cols + LANES)
    return comm_call(
        backward_kernel, "backward", 4, members, 100, 32,
        [ANY, VMEM, VMEM, VMEM, ANY, VMEM] + [ANY] * 7 + [VMEM] * 2,
        [VMEM] * 6 + [ANY],
        [
            sds((rows, width), F32),
            sds((8, own), F32),
            sds((own, members * q_cols), F32),
            sds((own, members * kv_cols), F32),
            sds((own, members * kv_cols), F32),
            sds((own, members * q_cols), F32),
            sds((own_experts, own, down.shape[2] // own_experts), F32),
        ],
        [
            *line,
            pltpu.VMEM((span, q_cols), BF16),
            pltpu.VMEM((2, 2, span, LANES), F32),
            pltpu.VMEM((2, 2, span, LANES), F32),
            pltpu.VMEM((span, qkv_cols), BF16),
            pltpu.VMEM((1, width), F32),
            *[pltpu.VMEM((devices, own, cols), BF16) for cols in three],
            *[pltpu.VMEM((own, cols), BF16) for cols in three],
            *[pltpu.VMEM((members, own, cols), BF16) for cols in three],
            *[pltpu.VMEM(a.shape, BF16) for a in (grad_out_all, pack_all, normed_attn, qkv, kx, vx, probs, attended)],
            pltpu.VMEM((own_experts, own, down.shape[2] // own_experts), F32),
            *[one for cols in three for one in plane_scratch(own, cols, False)],
            *plane_scratch(*down.shape[1:]),
        ],
    )(grad_out_all, grad_residual, gain_ffn_part, tokens, down, row_gains, pack_all, normed_attn, qkv, kx, vx, probs, attended, cosine, sine)


def results_kernel(count, *refs):
    sources, targets, held, came, went = refs[:count], refs[count : 2 * count], refs[2 * count : -2], refs[-2], refs[-1]
    moves = []
    for source, target, here in zip(sources, targets, held):
        pieces = source.shape[0] if len(source.shape) == 3 else 2
        step = source.shape[0] // pieces
        for i in range(pieces):
            at, k = pl.ds(i * step, step), len(moves)
            load = pltpu.make_async_copy(source.at[at], here.at[at], came.at[k])
            load.start()
            moves.append((load, pltpu.make_async_copy(here.at[at], target.at[at], went.at[k])))
    for load, store in moves:
        load.wait()
        store.start()
    for _, store in moves:
        store.wait()


def results(*arrays):
    return pl.pallas_call(
        functools.partial(results_kernel, len(arrays)),
        out_shape=[sds(a.shape, a.dtype) for a in arrays],
        in_specs=[ANY] * len(arrays),
        out_specs=[ANY] * len(arrays),
        scratch_shapes=[pltpu.VMEM(a.shape, a.dtype) for a in arrays] + [pltpu.SemaphoreType.DMA((64,))] * 2,
        compiler_params=pltpu.CompilerParams(vmem_limit_bytes=VMEM_LIMIT),
        name="results",
    )(*arrays)


def all_blocks(x, axis):
    return lax.all_gather(x, axis, axis=0)


def plain_first(members, tokens, cot, route, pack, gate):
    return (
        all_blocks(tokens, "expert"),
        all_blocks(cot, "expert"),
        all_blocks(route, "expert"),
        all_blocks(pack, "dp"),
        all_blocks(gate, "dp"),
    )


def line_total(part):
    return scatter(part.reshape(-1, part.shape[2]), "expert")


def plain_second(members, part, tokens, gain, up, down):
    residual = tokens.astype(F32) + branch_scale * line_total(part)
    normed = (residual * rms_factor(residual) * gain).astype(BF16)
    return residual, all_blocks(normed, "expert"), all_blocks(up, "dp"), all_blocks(down, "dp")


def plane_sum(part):
    return scatter(part.reshape(-1, part.shape[2]), "dp")


def plain_third(members, part, residual, cot, gain, gate, up):
    grad = line_total(part)
    factor = rms_factor(residual)
    gain_part = jnp.sum(grad * residual * factor, axis=0, keepdims=True)
    total = cot.astype(F32) + norm_back(residual, factor, gain, grad)
    out_all = all_blocks((branch_scale * total).astype(BF16), "expert")
    return total, gain_part, out_all, plane_sum(gate), plane_sum(up)


def plain_fourth(members, part, grad_residual, tokens, gain, pack, down):
    here = tokens.astype(F32)
    grad_tokens = grad_residual + norm_back(here, rms_factor(here), gain, line_total(part))
    return grad_tokens, all_blocks(plane_sum(pack).astype(BF16), "expert"), plane_sum(down)


def attend_forward(q, k, v, allowed):
    scores = jnp.einsum("irh,jh->rij", q, k, preferred_element_type=F32) * score_scale
    scores = jnp.where(allowed[None], scores, -1e30)
    peak = jnp.max(scores, axis=-1, keepdims=True)
    exponent = jnp.exp(scores - peak)
    total = jnp.sum(exponent, axis=-1, keepdims=True)
    probs = exponent / total
    return jnp.einsum("rij,jh->irh", probs.astype(BF16), v, preferred_element_type=F32), probs


def attend_backward(q, k, v, probs, grad, allowed):
    grad_probs = jnp.einsum("irh,jh->rij", grad, v, preferred_element_type=F32)
    inner = jnp.sum(probs * grad_probs, axis=-1, keepdims=True)
    grad_scores = (probs * (grad_probs - inner)).astype(BF16)
    grad_q = jnp.einsum("rij,jh->irh", grad_scores, k, preferred_element_type=F32) * score_scale
    grad_k = jnp.einsum("rij,irh->jh", grad_scores, q, preferred_element_type=F32) * score_scale
    grad_v = jnp.einsum("rij,irh->jh", probs.astype(BF16), grad, preferred_element_type=F32)
    return grad_q, grad_k, grad_v


def shards_plain(
    tokens,
    cotangent,
    gain_attn,
    gain_ffn,
    w_query,
    key_weight,
    value_weight,
    w_out,
    expert_gate,
    expert_up,
    expert_down,
    expert_ids,
    gates,
    lengths,
    order,
):
    rows, width = tokens.shape
    members = lax.axis_size("expert")
    member = lax.axis_index("expert")
    span = rows * members
    own_experts, ff = expert_gate.shape[1], expert_gate.shape[2]
    capacity = rows * TOP // own_experts
    q_cols = w_query.shape[1] // members
    kv_cols = key_weight.shape[1] // members
    kv_heads = kv_cols // HEAD_SIZE
    repeat = QUERY_HEADS // KEY_VALUE_HEADS

    def mine(weight, cols):
        return lax.dynamic_slice_in_dim(weight, member * cols, cols, axis=1)

    devices = lax.axis_size("dp")
    phases = [
        functools.partial(phase, members)
        for phase in (plain_first, plain_second, plain_third, plain_fourth)
    ]

    pack = jnp.concatenate(
        [
            mine(w_query, q_cols),
            mine(key_weight, kv_cols),
            mine(value_weight, kv_cols),
            mine(w_out, q_cols),
            gain_attn[:, None],
            gain_ffn[:, None],
            jnp.zeros((gain_attn.shape[0], 126), BF16),
        ],
        axis=1,
    )
    route = jnp.concatenate([expert_ids.astype(F32), gates], axis=1)
    tokens_all, cot_all, route_all, pack_all, gate_all = phases[0](
        tokens, cotangent, route, pack, expert_gate.reshape(-1, own_experts * ff)
    )
    tokens_all = tokens_all.reshape(span, width).astype(F32)
    cot_all = cot_all.reshape(span, width)
    route_all = route_all.reshape(span, 2 * TOP)
    pack_all = pack_all.reshape(width, -1)
    gate_all = gate_all.reshape(width, -1)
    qkv_cols = q_cols + 2 * kv_cols
    w_qkv = pack_all[:, :qkv_cols]
    wo = pack_all[:, qkv_cols : qkv_cols + q_cols]
    gain_one = pack_all[:, qkv_cols + q_cols].astype(F32)[None]
    gain_two = pack_all[:, qkv_cols + q_cols + 1].astype(F32)[None]

    segment, position = layout(lengths[0], order[0], span)
    cosine, sine = rotation(position)
    place = jnp.arange(span, dtype=jnp.int32)
    allowed = (segment[:, None] == segment[None, :]) & (place[None, :] <= place[:, None])
    factor_one = rms_factor(tokens_all)
    normed_attn = (tokens_all * factor_one * gain_one).astype(BF16)
    qkv = dot(normed_attn, w_qkv)
    qk = rotate(qkv[:, : q_cols + kv_cols], cosine, sine).astype(BF16)
    v = qkv[:, q_cols + kv_cols :].astype(BF16)
    q_heads = jnp.moveaxis(qk[:, :q_cols].reshape(span, kv_heads, repeat, HEAD_SIZE), 1, 0)
    k_heads = jnp.moveaxis(qk[:, q_cols:].reshape(span, kv_heads, HEAD_SIZE), 1, 0)
    v_heads = jnp.moveaxis(v.reshape(span, kv_heads, HEAD_SIZE), 1, 0)
    attended, probs = jax.vmap(functools.partial(attend_forward, allowed=allowed))(
        q_heads, k_heads, v_heads
    )
    attended = jnp.moveaxis(attended, 0, 1).reshape(span, q_cols).astype(BF16)
    attn_part = dot_nt(attended, wo).astype(BF16).reshape(members, rows, width)
    residual, normed_all, up_all, down_all = phases[1](
        attn_part,
        tokens,
        gain_two,
        expert_up.reshape(-1, own_experts * ff),
        expert_down.reshape(-1, own_experts * ff),
    )
    normed_all = normed_all.reshape(span, width)
    up_all, down_all = up_all.reshape(width, -1), down_all.reshape(width, -1)

    mixture, grad_normed, *by_kind = experts(
        own_experts, capacity, route_all, normed_all, cot_all, gate_all, up_all, down_all
    )
    output = (residual + branch_scale * scatter(mixture, "expert")).astype(BF16)
    by_kind = [one.reshape(devices, -1, own_experts * ff) for one in by_kind]

    grad_residual, gain_two_part, grad_attn_out, sum_gate, sum_up = phases[2](
        grad_normed.reshape(members, rows, width),
        residual,
        cotangent,
        gain_two,
        by_kind[0],
        by_kind[1],
    )
    grad_attn_out = grad_attn_out.reshape(span, width)
    term_out = dot_tn(grad_attn_out, attended)
    grad_attended = dot(grad_attn_out, wo).astype(BF16)
    grad_heads = jnp.moveaxis(grad_attended.reshape(span, kv_heads, repeat, HEAD_SIZE), 1, 0)
    grad_q, grad_k, grad_v = jax.vmap(functools.partial(attend_backward, allowed=allowed))(
        q_heads, k_heads, v_heads, probs, grad_heads
    )
    grad_qk = jnp.concatenate(
        [
            jnp.moveaxis(grad_q, 0, 1).reshape(span, q_cols),
            jnp.moveaxis(grad_k, 0, 1).reshape(span, kv_cols),
        ],
        axis=1,
    )
    grad_qkv = jnp.concatenate(
        [
            rotate(grad_qk, cosine, sine, back=True).astype(BF16),
            jnp.moveaxis(grad_v, 0, 1).reshape(span, kv_cols).astype(BF16),
        ],
        axis=1,
    )
    grad_norm_part = dot_nt(grad_qkv, w_qkv)
    gain_one_part = jnp.sum(grad_norm_part * tokens_all * factor_one, axis=0)
    term_qkv = dot_tn(normed_attn, grad_qkv)
    packed_grads = jnp.concatenate(
        [
            term_qkv,
            term_out,
            gain_one_part[:, None],
            gain_two_part.reshape(-1, 1),
            jnp.zeros((width, 126), F32),
        ],
        axis=1,
    )
    grad_tokens, per_member, sum_down = phases[3](
        grad_norm_part.astype(BF16).reshape(members, rows, width),
        grad_residual,
        tokens,
        gain_one,
        packed_grads.astype(BF16).reshape(devices, -1, packed_grads.shape[1]),
        by_kind[2],
    )
    per_member = per_member.astype(F32)

    def columns(first, cols):
        part = per_member[:, :, first : first + cols]
        return jnp.moveaxis(part, 0, 1).reshape(part.shape[1], -1)

    gains = jnp.sum(per_member[:, :, qkv_cols + q_cols :], axis=0)
    return (
        output,
        grad_tokens,
        gains[:, 0],
        gains[:, 1],
        columns(0, q_cols),
        columns(q_cols, kv_cols),
        columns(q_cols + kv_cols, kv_cols),
        columns(qkv_cols, q_cols),
        sum_gate.reshape(-1, own_experts, ff),
        sum_up.reshape(-1, own_experts, ff),
        sum_down.reshape(-1, own_experts, ff),
    )


def shards_fast(
    tokens,
    cotangent,
    gain_attn,
    gain_ffn,
    w_query,
    key_weight,
    value_weight,
    w_out,
    expert_gate,
    expert_up,
    expert_down,
    expert_ids,
    gates,
    lengths,
    order,
):
    rows, width = tokens.shape
    members, devices = lax.axis_size("expert"), lax.axis_size("dp")
    span = rows * members
    own_experts, ff = expert_gate.shape[1], expert_gate.shape[2]
    capacity = rows * TOP // own_experts
    segment, position = layout(lengths[0], order[0], span)
    lane = jnp.arange(LANES, dtype=jnp.int32) % HEAD_SIZE
    half = HEAD_SIZE // 2
    frequency = rope_base ** (-((lane % half).astype(F32) * (2.0 / HEAD_SIZE)))
    angles = position[:, None] * frequency[None, :]
    cosine, sine = jnp.cos(angles), jnp.where(lane < half, -1.0, 1.0) * jnp.sin(angles)
    spare = (0, span - gain_attn.shape[0])
    small = jnp.stack(
        [segment.astype(F32), jnp.pad(gain_attn.astype(F32), spare), jnp.pad(gain_ffn.astype(F32), spare)]
    )
    (
        cot_all, route_all, pack_all, gate_all, up_all, down_all,
        normed_attn, qkv, kx, vx, probs, attended, residual, normed_all, gains,
    ) = forward_phase(
        members, tokens, cotangent, expert_ids.T, gates.T, w_query, key_weight, value_weight, w_out,
        small, *(w.transpose(1, 0, 2) for w in (expert_gate, expert_up, expert_down)), cosine, sine,
    )
    cot_all = cot_all.reshape(span, width)
    normed_all = normed_all.reshape(span, width)
    route_all = route_all.reshape(span, 2 * TOP)
    gate_all, up_all, down_all = (w.reshape(width, -1) for w in (gate_all, up_all, down_all))
    mixture, grad_normed, *by_kind = experts(
        own_experts, capacity, route_all, normed_all, cot_all, gate_all, up_all, down_all
    )
    by_kind = [one.reshape(devices, -1, own_experts * ff) for one in by_kind]

    output, grad_residual, gain_two_part, grad_attn_out, sum_gate, sum_up = third_phase(
        members, own_experts,
        grad_normed.reshape(members, rows, width),
        mixture.reshape(members, rows, width),
        residual,
        cotangent,
        gains,
        by_kind[0],
        by_kind[1],
    )
    (
        grad_tokens, grad_gains, d_query, d_key, d_value, d_out, d_down,
    ) = backward_phase(
        members, own_experts,
        grad_attn_out.reshape(span, width),
        grad_residual,
        gain_two_part,
        tokens,
        by_kind[2],
        gains,
        pack_all,
        normed_attn, qkv, kx, vx, probs, attended, cosine, sine,
    )
    output, grad_tokens, d_query, d_key, d_value, d_out, sum_gate, sum_up, d_down = results(
        output, grad_tokens, d_query, d_key, d_value, d_out, sum_gate, sum_up, d_down
    )
    return (
        output,
        grad_tokens,
        grad_gains[0],
        grad_gains[1],
        d_query,
        d_key,
        d_value,
        d_out,
        sum_gate.transpose(1, 0, 2),
        sum_up.transpose(1, 0, 2),
        d_down.transpose(1, 0, 2),
    )


def solution(mesh):
    both = P(("dp", "expert"), None)
    row, rows = P("dp"), P("dp", None)
    experts = P("dp", "expert", None)
    fast = mesh.shape["dp"] == 8 and mesh.shape["expert"] == 4
    return jax.shard_map(
        shards_fast if fast else shards_plain,
        mesh=mesh,
        in_specs=(both, both, row, row, rows, rows, rows, rows)
        + (experts, experts, experts, both, both, rows, rows),
        out_specs=(both, both, row, row, rows, rows, rows, rows, experts, experts, experts),
        check_vma=False,
    )
```

```python
import functools

import jax
import jax.numpy as jnp
from jax import lax
from jax.experimental import pallas as pl
from jax.experimental.pallas import tpu as pltpu
from jax.sharding import PartitionSpec as P

QUERY_HEADS = 24
KEY_VALUE_HEADS = 8
HEAD_SIZE = 64
TOP = 8

epsilon = 1e-06
rope_base = 10000.0
score_scale = 0.015625
branch_scale = 0.22
F32 = jnp.float32
BF16 = jnp.bfloat16
MESH = pl.DeviceIdType.MESH
LANES = 128
VMEM_LIMIT = 60 * 2**20


def layout(lengths_row, order_row, span):
    seqs = lengths_row.shape[0]
    slot_ids = jnp.arange(seqs, dtype=jnp.int32)
    picked = jnp.sum(
        jnp.where(order_row[:, None] == slot_ids[None, :], lengths_row[None, :], 0), axis=1
    )
    before = slot_ids[:, None] >= slot_ids[None, :]
    seq_ends = jnp.sum(jnp.where(before, picked[None, :], 0), axis=1)
    place = jnp.arange(span, dtype=jnp.int32)
    passed = place[:, None] >= seq_ends[None, :]
    segment = jnp.sum(passed.astype(jnp.int32), axis=1)
    start = jnp.sum(jnp.where(passed, picked[None, :], 0), axis=1)
    return segment, (place - start).astype(F32)


def rotation(position):
    half = HEAD_SIZE // 2
    frequency = rope_base ** (-(jnp.arange(half, dtype=F32) * (2.0 / HEAD_SIZE)))
    angles = position[:, None] * frequency[None, :]
    return jnp.cos(angles), jnp.sin(angles)


def rotate(rows, cosine, sine, back=False):
    t = rows.shape[0]
    heads = rows.reshape(t, -1, 2, HEAD_SIZE // 2)
    a, b = heads[:, :, 0], heads[:, :, 1]
    c, s = cosine[:, None, :], sine[:, None, :]
    if back:
        s = -s
    return jnp.stack([a * c - b * s, b * c + a * s], axis=2).reshape(t, -1)


def dot(a, b):
    return jnp.dot(a, b, preferred_element_type=F32)


def dot_nt(a, b):
    return jnp.einsum("tc,dc->td", a, b, preferred_element_type=F32)


def dot_tn(a, b):
    return jnp.einsum("td,tc->dc", a, b, preferred_element_type=F32)


def rms_factor(rows):
    return lax.rsqrt(jnp.mean(rows * rows, axis=-1, keepdims=True) + epsilon)


def norm_back(rows, factor, gain, grad):
    scaled = gain * grad
    return factor * scaled - rows * (factor * factor * factor) * jnp.mean(
        scaled * rows, axis=-1, keepdims=True
    )


def gather(x, axis):
    return lax.all_gather(x, axis, axis=0, tiled=True)


def scatter(x, axis):
    return lax.psum_scatter(x.astype(BF16), axis, scatter_dimension=0, tiled=True).astype(F32)


class Links:
    def __init__(self, send, recv, local, members):
        self.send, self.recv, self.local = send, recv, local
        self.remotes = self.locals = 0
        self.members = members
        self.d, self.z = lax.axis_index("dp"), lax.axis_index("expert")
        d = self.d
        core, x, y = d % 2, (d // 2) % 2, d // 4
        self.core = core
        self.sib = d + 1 - 2 * core
        self.x = d + 2 - 4 * x
        self.y = d + 4 - 8 * y
        self.diag = self.x + 4 - 8 * y
        self.waiting = []

    def other(self, d):
        return d + 1 - 2 * self.core

    def greet(self):
        barrier = pltpu.get_barrier_semaphore()
        last = self.members - 1

        def hello(d, z):
            pl.semaphore_signal(barrier, inc=1, device_id=(d, z), device_id_type=MESH)

        for d in (self.sib, self.x, self.y):
            hello(d, self.z)
        pl.when(self.z > 0)(lambda: hello(self.d, self.z - 1))
        pl.when(self.z < last)(lambda: hello(self.d, self.z + 1))
        ends = (self.z == 0).astype(jnp.int32) + (self.z == last).astype(jnp.int32)
        pl.semaphore_wait(barrier, 5 - ends)

    def remote(self, src, dst, to):
        k = self.remotes
        self.remotes += 1
        return pltpu.make_async_remote_copy(
            src_ref=src,
            dst_ref=dst,
            send_sem=self.send.at[k],
            recv_sem=self.recv.at[k],
            device_id=to,
            device_id_type=MESH,
        )

    def push(self, src, dst, d):
        copy = self.remote(src, dst, (d, self.z))
        copy.start()
        self.waiting.append(copy.wait_send)
        return copy

    def move(self, src, dst):
        k = self.locals
        self.locals += 1
        copy = pltpu.make_async_copy(src, dst, self.local.at[k])
        copy.start()
        return copy

    def finish(self):
        for wait in self.waiting:
            wait()


def run(order, **chains):
    for name in order:
        next(chains[name], None)
    chains = list(chains.values())
    while chains:
        for chain in list(chains):
            try:
                next(chain)
            except StopIteration:
                chains.remove(chain)


def line_gather(links, own, full):
    z, last = links.z, links.members - 1
    local = links.move(own, full.at[z])
    right, left = (links.d, z + 1), (links.d, z - 1)
    to_right, to_left = [], []
    for s in range(last):
        at_r, at_l = jnp.maximum(z - s, 0), jnp.minimum(z + s, last)
        to_right.append(links.remote(own if s == 0 else full.at[at_r], full.at[at_r], right))
        to_left.append(links.remote(own if s == 0 else full.at[at_l], full.at[at_l], left))
    for s in range(last):
        send_r, send_l = (z < last) & (z >= s), (z > 0) & (z + s <= last)
        pl.when(send_r)(to_right[s].start)
        pl.when(send_l)(to_left[s].start)
        yield
        pl.when((z > 0) & (z - 1 >= s))(to_right[s].wait_recv)
        pl.when((z < last) & (z + 1 + s <= last))(to_left[s].wait_recv)
    for s in range(last):
        send_r, send_l = (z < last) & (z >= s), (z > 0) & (z + s <= last)
        pl.when(send_r)(to_right[s].wait_send)
        pl.when(send_l)(to_left[s].wait_send)
    local.wait()


def add_rows(target, other, step=16):
    rows = target.shape[0]

    @pl.loop(0, rows // step)
    def _(i):
        at = pl.ds(pl.multiple_of(i * step, step), step)
        target[at] = (target[at].astype(F32) + other[at].astype(F32)).astype(target.dtype)


def line_sum(links, part, acc, from_left, from_right, finish, own=None, full=None, parts=2):
    z, last = links.z, links.members - 1
    rows = acc.shape[1] // parts
    spans = [pl.ds(h * rows, rows) for h in range(parts)]
    right, left = (links.d, z + 1), (links.d, z - 1)
    sum_r, sum_l, go_r, go_l, local = {}, {}, {}, {}, []
    for h, span in enumerate(spans):
        for o in range(last + 1):
            if o > 0:
                sum_r[h, o] = links.remote(acc.at[o, span], from_left.at[o, span], right)
            if o < last:
                sum_l[h, o] = links.remote(acc.at[o, span], from_right.at[o, span], left)
        for s in range(last if own is not None else 0):
            at_r, at_l = jnp.maximum(z - s, 0), jnp.minimum(z + s, last)
            here_r, here_l = full.at[at_r, span], full.at[at_l, span]
            go_r[h, s] = links.remote(own.at[span] if s == 0 else here_r, here_r, right)
            go_l[h, s] = links.remote(own.at[span] if s == 0 else here_l, here_l, left)

    def pass_right(h, o):
        @pl.when(z > 0)
        def _():
            sum_r[h, o].wait_recv()
            add_rows(acc.at[o, spans[h]], from_left.at[o, spans[h]])

        sum_r[h, o].start()

    def pass_left(h, o):
        @pl.when(z < last)
        def _():
            sum_l[h, o].wait_recv()
            add_rows(acc.at[o, spans[h]], from_right.at[o, spans[h]])

        sum_l[h, o].start()

    def send(h, s):
        pl.when((z < last) & (z >= s))(go_r[h, s].start)
        pl.when((z > 0) & (z + s <= last))(go_l[h, s].start)

    @pl.when(z == 0)
    def _():
        from_left[0] = jnp.zeros(from_left.shape[1:], from_left.dtype)

    @pl.when(z == last)
    def _():
        from_right[last] = jnp.zeros(from_right.shape[1:], from_right.dtype)

    made = set()
    for j in range(last):
        for o in (last - j, j):
            if o not in made:
                made.add(o)
                part(o)
        for h in range(parts):
            pl.when((z < last - j) & (2 * z < last))(functools.partial(pass_right, h, last - j))
            pl.when(z > j)(functools.partial(pass_left, h, j))
            pl.when((z < last - j) & (2 * z >= last))(functools.partial(pass_right, h, last - j))
            yield
    for h in range(parts):
        for o in range(last + 1):
            if o > 0:
                pl.when(z == o)(sum_r[h, o].wait_recv)
            if o < last:
                pl.when(z == o)(sum_l[h, o].wait_recv)
        finish(h * rows, rows)
        if own is None:
            continue
        send(h, 0)
        local.append(links.move(own.at[spans[h]], full.at[z, spans[h]]))
        yield
    for s in range(last if own is not None else 0):
        for h in range(parts):
            pl.when((z > 0) & (z - 1 >= s))(go_r[h, s].wait_recv)
            pl.when((z < last) & (z + 1 + s <= last))(go_l[h, s].wait_recv)
            if s + 1 < last:
                send(h, s + 1)
            yield
    for h in range(parts):
        for o in range(last + 1):
            if o > 0:
                pl.when(z < o)(sum_r[h, o].wait_send)
            if o < last:
                pl.when(z > o)(sum_l[h, o].wait_send)
        for s in range(last if own is not None else 0):
            pl.when((z < last) & (z >= s))(go_r[h, s].wait_send)
            pl.when((z > 0) & (z + s <= last))(go_l[h, s].wait_send)
    for copy in local:
        copy.wait()


def plane_gather(links, own, full):
    half = own.shape[0] // 2
    first, second = pl.ds(0, half), pl.ds(half, half)
    me = links.d
    local = links.move(own, full.at[me])
    by_x, by_y = {}, {}
    for by, d, h in ((by_y, links.y, first), (by_x, links.x, second), (by_x, links.x, first), (by_y, links.y, second)):
        by[h.start // half] = links.push(own.at[h], full.at[me, h], d)
    to_sib = [links.push(own, full.at[me], links.sib)]

    def share(d, h):
        to_sib.append(links.push(full.at[d, h], full.at[d, h], links.sib))

    yield
    by_y[0].wait_recv()
    over_x = links.push(full.at[links.y, first], full.at[links.y, first], links.x)
    share(links.y, first)
    by_x[1].wait_recv()
    over_y = links.push(full.at[links.x, second], full.at[links.x, second], links.y)
    share(links.x, second)
    yield
    by_x[0].wait_recv()
    share(links.x, first)
    by_y[1].wait_recv()
    share(links.y, second)
    yield
    over_x.wait_recv()
    share(links.diag, first)
    over_y.wait_recv()
    share(links.diag, second)
    yield
    for copy in to_sib:
        copy.wait_recv()
    local.wait()


def plane_scatter(links, part, mine, theirs, mid_x, mid_y, end_x, end_y):
    half = part.shape[1] // 2
    first, second = pl.ds(0, half), pl.ds(half, half)
    chips = (links.d, links.x, links.y, links.diag)
    from_sib, load = {}, {}
    held = [part.at[chip] if mine is None else mine.at[k] for k, chip in enumerate(chips)]
    for k in (3, 1, 2, 0):
        from_sib[k] = links.push(part.at[links.other(chips[k])], theirs.at[k], links.sib)
        if mine is not None:
            load[k] = links.move(part.at[chips[k]], held[k])
    yield
    for k in (3, 1, 2):
        if load:
            load[k].wait()
        from_sib[k].wait_recv()
        add_rows(held[k], theirs.at[k])
        if k == 3:
            to_mid_x = links.push(held[3].at[first], mid_x, links.x)
            to_mid_y = links.push(held[3].at[second], mid_y, links.y)
        if k == 1:
            to_end_x = links.push(held[1].at[first], end_x.at[first], links.x)
        if k == 2:
            to_end_y = links.push(held[2].at[second], end_y.at[second], links.y)
        if k != 1:
            yield
    to_mid_y.wait_recv()
    add_rows(held[1].at[second], mid_y)
    rest_x = links.push(held[1].at[second], end_x.at[second], links.x)
    to_mid_x.wait_recv()
    add_rows(held[2].at[first], mid_x)
    rest_y = links.push(held[2].at[first], end_y.at[first], links.y)
    yield
    if load:
        load[0].wait()
    from_sib[0].wait_recv()
    to_end_x.wait_recv()
    to_end_y.wait_recv()
    rest_x.wait_recv()
    rest_y.wait_recv()
    yield


def plane_scratch(rows, cols, mine=True):
    return [pltpu.VMEM((4, rows, cols), BF16)] * mine + [
        pltpu.VMEM((4, rows, cols), BF16),
        pltpu.VMEM((rows // 2, cols), BF16),
        pltpu.VMEM((rows // 2, cols), BF16),
        pltpu.VMEM((rows, cols), BF16),
        pltpu.VMEM((rows, cols), BF16),
    ]


def plane_result(mine, theirs, end_x, end_y, out, step=16):
    @pl.loop(0, out.shape[-2] // step)
    def _(i):
        at = pl.ds(pl.multiple_of(i * step, step), step)
        own = mine[at].astype(F32) + theirs[0, at].astype(F32)
        total = (own + end_x[at].astype(F32) + end_y[at].astype(F32)).astype(out.dtype)
        if len(out.shape) == 2:
            out[at] = total
        else:
            cols = out.shape[2]
            for e in range(out.shape[0]):
                out[e, at] = total[:, e * cols : (e + 1) * cols]


def plane_total(links, part, scratch, total, out, stores):
    yield from plane_scatter(links, part, *scratch)
    plane_result(scratch[0].at[0], scratch[1], scratch[4], scratch[5], total)
    stores.append(links.move(total, out))


def line_result(z, acc, from_left, from_right, at):
    return (
        acc[z, at].astype(F32) + from_left[z, at].astype(F32) + from_right[z, at].astype(F32)
    )


ANY = pl.BlockSpec(memory_space=pl.ANY)
VMEM = pl.BlockSpec(memory_space=pltpu.VMEM)


def comm_call(kernel, name, number, members, remotes, locals_, in_specs, out_specs, out_shape, scratch):
    return pl.pallas_call(
        functools.partial(kernel, members),
        out_shape=out_shape,
        in_specs=in_specs,
        out_specs=out_specs,
        scratch_shapes=[
            pltpu.SemaphoreType.DMA((remotes,)),
            pltpu.SemaphoreType.DMA((remotes,)),
            pltpu.SemaphoreType.DMA((locals_,)),
            *scratch,
        ],
        compiler_params=pltpu.CompilerParams(
            collective_id=number, has_side_effects=True, vmem_limit_bytes=VMEM_LIMIT
        ),
        name=name,
    )


def sds(shape, dtype):
    return jax.ShapeDtypeStruct(shape, dtype)


def third_kernel(members, part, mixture, residual, cot, gain, gate, up, output, grad_residual, gain_part, out_all, gate_out, up_out, send, recv, local, acc, from_left, from_right, acc_m, left_m, right_m, grad_out, gate_sum, up_sum, *rest):
    links = Links(send, recv, local, members)
    for_gate, for_up = rest[:6], rest[6:]
    stores = []

    def block_loads(source, into):
        loads = [links.move(source.at[o], into.at[o]) for o in range(members)]
        return lambda o: loads[o].wait()

    load_part, load_mixture = block_loads(part, acc), block_loads(mixture, acc_m)
    links.greet()

    def finish(first, count):
        @pl.loop(0, count // 16)
        def _(i):
            at = pl.ds(pl.multiple_of(first + i * 16, 16), 16)
            grad = line_result(links.z, acc, from_left, from_right, at)
            here = residual[at]
            factor = rms_factor(here)
            gain_part[...] += jnp.sum(grad * here * factor, axis=0, keepdims=True)
            total = cot[at].astype(F32) + norm_back(here, factor, gain[1:2], grad)
            grad_residual[at] = total
            grad_out[at] = (branch_scale * total).astype(BF16)

    def chain():
        gain_part[...] = jnp.zeros(gain_part.shape, F32)
        yield from line_sum(
            links, load_part, acc, from_left, from_right, finish, grad_out, out_all
        )

    def finish_mixture(first, count):
        @pl.loop(0, count // 16)
        def _(i):
            at = pl.ds(pl.multiple_of(first + i * 16, 16), 16)
            here = residual[at] + branch_scale * line_result(links.z, acc_m, left_m, right_m, at)
            output[at] = here.astype(BF16)

    def mixture_chain():
        yield from line_sum(links, load_mixture, acc_m, left_m, right_m, finish_mixture)

    run(
        THIRD_ORDER,
        m=mixture_chain(),
        z=chain(),
        g=plane_total(links, gate, for_gate, gate_sum, gate_out, stores),
        u=plane_total(links, up, for_up, up_sum, up_out, stores),
    )
    for store in stores:
        store.wait()
    links.finish()


THIRD_ORDER = "uzuzzgugmmzzguzzzgzmzmzmmzmugguuzm"


def third_phase(members, own_experts, part, mixture, residual, cot, gain, gate, up):
    rows, width = cot.shape
    blocks = pltpu.VMEM((members, rows, width), BF16)
    return comm_call(
        third_kernel, "phase_three", 3, members, 80, 24,
        [ANY, ANY, VMEM, VMEM, VMEM, ANY, ANY], [VMEM, VMEM, VMEM, ANY, ANY, ANY],
        [
            sds((rows, width), BF16),
            sds((rows, width), F32),
            sds((1, width), F32),
            sds((members, rows, width), BF16),
            sds((own_experts, gate.shape[1], gate.shape[2] // own_experts), F32),
            sds((own_experts, up.shape[1], up.shape[2] // own_experts), F32),
        ],
        [blocks] * 6
        + [pltpu.VMEM((rows, width), BF16)]
        + [pltpu.VMEM((own_experts, gate.shape[1], gate.shape[2] // own_experts), F32)] * 2
        + plane_scratch(*gate.shape[1:])
        + plane_scratch(*up.shape[1:]),
    )(part, mixture, residual, cot, gain, gate, up)


def lane_ids(rows):
    return lax.broadcasted_iota(jnp.int32, (rows, LANES), 1)


def dims(a, b):
    return (((a,), (b,)), ((), ()))


def mm(a, b):
    return lax.dot_general(a, b, dims(1, 0), preferred_element_type=F32)


def mm_nt(a, b):
    return lax.dot_general(a, b, dims(1, 1), preferred_element_type=F32)


def mm_tn(a, b):
    return lax.dot_general(a, b, dims(0, 0), preferred_element_type=F32)


def first_lanes():
    same = lax.broadcasted_iota(jnp.int32, (16, LANES), 0) == lax.broadcasted_iota(jnp.int32, (16, LANES), 1)
    return same.astype(BF16)


def expert_kernel(capacity, own_experts, route, normed, cot, w_gate, w_up, w_down, mixture, grad_normed, d_gate, d_up, d_down, mix_sum, grad_sum, slot_cols, weight_cols, slot_rows):
    e = pl.program_id(0)
    span = normed.shape[0]

    @pl.when(e == 0)
    def _():
        lane = lane_ids(LANES)
        name = (lax.axis_index("expert") * own_experts + lane).astype(F32)
        name = jnp.where(lane < own_experts, name, -1.0)
        upto = (lane <= lax.broadcasted_iota(jnp.int32, (LANES, LANES), 0)).astype(BF16)
        before = jnp.zeros((1, LANES), F32)
        for b in range(span // LANES):
            at = pl.ds(b * LANES, LANES)
            chosen, weight = jnp.zeros((LANES, LANES), F32), jnp.zeros((LANES, LANES), F32)
            for k in range(TOP):
                named = route[at, k : k + 1] == name
                chosen = jnp.where(named, 1.0, chosen)
                weight = jnp.where(named, route[at, TOP + k : TOP + k + 1], weight)
            slot = mm(upto, chosen.astype(BF16)) + (before - 1.0)
            slot_cols[at] = jnp.where((chosen > 0.0) & (slot < capacity), slot, -1.0)
            weight_cols[at] = weight
            before = before + jnp.sum(chosen, axis=0, keepdims=True)
        slot_rows[...] = mm_nt(first_lanes(), slot_cols[...].astype(BF16))

    def add_to(total, term):
        total[...] = jnp.where(e == 0, 0.0, total[...]) + term

    def column(values):
        return jnp.sum(jnp.where(lane_ids(span) == e, values[...], 0.0), axis=1, keepdims=True)

    slots = lax.broadcasted_iota(jnp.int32, (capacity, span), 0).astype(F32)
    pick = (slot_rows[pl.ds(e, 1)] == slots).astype(BF16)
    puts = column(slot_cols) == lax.broadcasted_iota(jnp.int32, (span, capacity), 1).astype(F32)
    put = puts.astype(BF16)
    gate_row = jnp.sum(jnp.where(puts, column(weight_cols), 0.0), axis=0, keepdims=True)
    same = lax.broadcasted_iota(jnp.int32, (capacity, capacity), 0) == lax.broadcasted_iota(jnp.int32, (capacity, capacity), 1)
    gate_col = jnp.sum(jnp.where(same, gate_row, 0.0), axis=1, keepdims=True)
    received = mm(pick, normed[...]).astype(BF16)
    pre_gate, pre_up = mm(received, w_gate[...]), mm(received, w_up[...])
    sig = 1.0 / (1.0 + jnp.exp(-pre_gate))
    silu = pre_gate * sig
    activ = (silu * pre_up).astype(BF16)
    produced = (gate_col * mm_nt(activ, w_down[...])).astype(BF16)
    add_to(mix_sum, mm(put, produced))
    grad_out = (gate_col * (branch_scale * mm(pick, cot[...]))).astype(BF16)
    grad_activ = mm(grad_out, w_down[...])
    grad_gate = (grad_activ * pre_up * (sig * (1.0 + pre_gate * (1.0 - sig)))).astype(BF16)
    grad_up = (grad_activ * silu).astype(BF16)
    grad_pair = (mm_nt(grad_gate, w_gate[...]) + mm_nt(grad_up, w_up[...])).astype(BF16)
    add_to(grad_sum, mm(put, grad_pair))
    d_gate[...] = mm_tn(received, grad_gate).astype(BF16)
    d_up[...] = mm_tn(received, grad_up).astype(BF16)
    d_down[...] = mm_tn(grad_out, activ).astype(BF16)

    @pl.when(e == pl.num_programs(0) - 1)
    def _():
        mixture[...] = mix_sum[...].astype(BF16)
        grad_normed[...] = grad_sum[...].astype(BF16)


def experts(own_experts, capacity, route, normed, cot, w_gate, w_up, w_down):
    span, width = normed.shape
    ff = w_gate.shape[1] // own_experts
    whole = pl.BlockSpec((span, width), lambda e: (0, 0))
    column = pl.BlockSpec((width, ff), lambda e: (0, e))
    grads = jax.ShapeDtypeStruct(w_gate.shape, BF16)
    rows = jax.ShapeDtypeStruct((span, width), BF16)
    return pl.pallas_call(
        functools.partial(expert_kernel, capacity, own_experts),
        grid=(own_experts,),
        in_specs=[pl.BlockSpec(route.shape, lambda e: (0, 0)), whole, whole, column, column, column],
        out_specs=[whole, whole, column, column, column],
        out_shape=[rows, rows, grads, grads, grads],
        scratch_shapes=[
            pltpu.VMEM((span, width), F32),
            pltpu.VMEM((span, width), F32),
            pltpu.VMEM((span, LANES), F32),
            pltpu.VMEM((span, LANES), F32),
            pltpu.VMEM((16, span), F32),
        ],
        compiler_params=pltpu.CompilerParams(vmem_limit_bytes=VMEM_LIMIT),
        name="experts",
    )(route, normed, cot, w_gate, w_up, w_down)


def turn(x, cosine, sine):
    half = HEAD_SIZE // 2
    ahead, behind = pltpu.roll(x, LANES - half, axis=1), pltpu.roll(x, half, axis=1)
    partner = jnp.where(lane_ids(x.shape[0]) % HEAD_SIZE < half, ahead, behind)
    return x * cosine + partner * sine


def spread(block, at, out):
    low = lane_ids(block.shape[0]) < HEAD_SIZE
    other = pltpu.roll(block, HEAD_SIZE, axis=1)
    zero = jnp.zeros_like(block)
    out[0, 0, at] = jnp.where(low, block, zero).astype(BF16)
    out[0, 1, at] = jnp.where(low, zero, other).astype(BF16)
    out[1, 0, at] = jnp.where(low, other, zero).astype(BF16)
    out[1, 1, at] = jnp.where(low, zero, block).astype(BF16)


def attention_setup(segment, bias):
    span = bias.shape[0]
    same = lax.broadcasted_iota(jnp.int32, (LANES, LANES), 0) == lane_ids(LANES)
    for b in range(span // LANES):
        at = pl.ds(b * LANES, LANES)
        row = b * LANES + lax.broadcasted_iota(jnp.int32, (LANES, span), 0)
        col = lax.broadcasted_iota(jnp.int32, (LANES, span), 1)
        here = segment[:, b * LANES : (b + 1) * LANES]
        here = jnp.sum(jnp.where(same, here, 0.0), axis=1, keepdims=True)
        ok = (here == segment) & (col <= row)
        bias[at] = jnp.where(ok, 0.0, -1e30)


def weight_columns(pack_all, first, cols):
    return pack_all[:, :, first : first + cols].reshape(-1, cols)


def gain_rows(pack_all, first):
    return mm_nt(first_lanes(), weight_columns(pack_all, first, LANES))


def attend_steps(qkv, kx, vx, bias, probs, attended):
    span, blocks = qkv.shape[0], attended.shape[1] // LANES
    repeat = QUERY_HEADS // KEY_VALUE_HEADS
    for j in range(blocks):
        for b in range(span // LANES):
            at, keys = pl.ds(b * LANES, LANES), (b + 1) * LANES
            q = qkv[at, j * LANES : (j + 1) * LANES]
            total = jnp.zeros((LANES, LANES), F32)
            for half in range(2):
                h = 2 * j + half
                kv = h // repeat
                scores = mm_nt(q, kx[kv, half, :keys]) + bias[at, :keys]
                peak = jnp.max(scores, axis=1, keepdims=True)
                exponent = jnp.exp(scores - peak)
                share = 1.0 / jnp.sum(exponent, axis=1, keepdims=True)
                low = (exponent * share).astype(BF16)
                probs[h, at, :keys] = low
                total += mm(low, vx[kv, half, :keys])
            attended[at, j * LANES : (j + 1) * LANES] = total.astype(BF16)
        yield


def forward_kernel(
    members, tokens, cot, ids, gates, w_query, w_key, w_value, w_out, small, gate, up, down, cosine, sine,
    cot_all, route_all, pack_out, gate_all, up_all, down_all, normed_out, qkv_out, kx_out, vx_out, probs_out, attended_out, residual, normed_all, gains,
    send, recv, local, pack, route, flat, tokens_all, bias, acc, from_left, from_right, normed,
    pack_all, normed_attn, qkv, kx, vx, probs, attended,
):
    links = Links(send, recv, local, members)
    stores = []
    count, _, cols = gate.shape
    loads = [
        [links.move(weight.at[e], flat.at[i, :, e * cols : (e + 1) * cols]) for e in range(count)]
        for i, weight in enumerate((gate, up, down))
    ]
    links.greet()
    route[...] = jnp.concatenate([ids[...].astype(F32), gates[...]], axis=0).T
    rows, width = tokens.shape
    span = rows * members
    q_cols = attended.shape[1]
    qkv_cols = qkv.shape[1]

    def pack_chain():
        loads, at = [], 0
        for weight in (w_query, w_key, w_value, w_out):
            cols = weight.shape[1] // members
            mine = pl.ds(pl.multiple_of(links.z * cols, LANES), cols)
            loads.append(links.move(weight.at[:, mine], pack.at[:, at : at + cols]))
            at += cols
        which = lax.broadcasted_iota(jnp.int32, (16, pack.shape[0]), 0)
        own = pack.shape[0]
        both = jnp.where(which == 0, small[1:2, :own], jnp.where(which == 1, small[2:3, :own], 0.0))
        pack[:, at:] = mm_tn(both.astype(BF16), first_lanes()).astype(BF16)
        for load in loads:
            load.wait()
        yield from plane_gather(links, pack, pack_all)

    def expert_chain(i, full):
        for load in loads[i]:
            load.wait()
        yield from plane_gather(links, flat.at[i], full)

    def produce(o):
        acc[o] = mm_nt(attended[o * rows : (o + 1) * rows], weight_columns(pack_all, qkv_cols, q_cols)).astype(BF16)

    def chain():
        attention_setup(small[0:1], bias)
        yield
        gains[...] = gain_rows(pack_all, qkv_cols + q_cols)

        @pl.loop(0, span // 16)
        def _(i):
            here = tokens_all[i // (rows // 16), pl.ds(pl.multiple_of(i % (rows // 16) * 16, 16), 16)].astype(F32)
            normed_attn[pl.ds(pl.multiple_of(i * 16, 16), 16)] = (here * rms_factor(here) * gains[0:1]).astype(BF16)

        @pl.loop(0, span // LANES)
        def _(i):
            at = pl.ds(pl.multiple_of(i * LANES, LANES), LANES)
            here = mm(normed_attn[at], weight_columns(pack_all, 0, qkv_cols))
            c, s = cosine[at], sine[at]
            for j in range(q_cols // LANES):
                lanes = slice(j * LANES, (j + 1) * LANES)
                qkv[at, lanes] = (turn(here[:, lanes], c, s).astype(BF16).astype(F32) * score_scale).astype(BF16)
            key = turn(here[:, q_cols : q_cols + LANES], c, s)
            value = here[:, q_cols + LANES :]
            qkv[at, q_cols : q_cols + LANES] = key.astype(BF16)
            qkv[at, q_cols + LANES :] = value.astype(BF16)
            spread(key, at, kx)
            spread(value, at, vx)

        yield
        yield from attend_steps(qkv, kx, vx, bias, probs, attended)
        for kept, out in (
            (pack_all, pack_out), (normed_attn, normed_out), (qkv, qkv_out), (kx, kx_out),
            (vx, vx_out), (probs, probs_out), (attended, attended_out),
        ):
            stores.append(links.move(kept, out))

        def finish(first, count):
            @pl.loop(0, count // 16)
            def _(i):
                at = pl.ds(pl.multiple_of(first + i * 16, 16), 16)
                here = tokens[at].astype(F32) + branch_scale * line_result(links.z, acc, from_left, from_right, at)
                residual[at] = here
                normed[at] = (here * rms_factor(here) * gains[1:2]).astype(BF16)

        yield from line_sum(links, produce, acc, from_left, from_right, finish, normed, normed_all)

    run(
        FORWARD_ORDER,
        t=line_gather(links, tokens, tokens_all),
        r=line_gather(links, route, route_all),
        c=line_gather(links, cot, cot_all),
        p=pack_chain(),
        g=expert_chain(0, gate_all),
        u=expert_chain(1, up_all),
        d=expert_chain(2, down_all),
        a=chain(),
    )
    for store in stores:
        store.wait()
    links.finish()


FORWARD_ORDER = "tpptpadtcpgptpaatcargadctaatracauaacrtaagpgrrtaargtgdcrtp"


def forward_phase(members, tokens, cot, ids, gates, w_query, w_key, w_value, w_out, small, gate, up, down, cosine, sine):
    rows, width = tokens.shape
    q_cols = w_query.shape[1] // members
    qkv_cols = q_cols + 2 * w_key.shape[1] // members
    count, own, cols = gate.shape
    pack = (own, qkv_cols + q_cols + LANES)
    route, flat = (rows, 2 * ids.shape[0]), (own, count * cols)
    span = rows * members
    blocks = pltpu.VMEM((members, rows, width), BF16)
    heads = q_cols // HEAD_SIZE
    return comm_call(
        forward_kernel, "forward", 1, members, 120, 40,
        [VMEM, ANY, VMEM, VMEM, ANY, ANY, ANY, ANY, VMEM, ANY, ANY, ANY, VMEM, VMEM],
        [ANY] * 12 + [VMEM, ANY, VMEM],
        [
            sds((members, rows, width), BF16),
            sds((members, *route), F32),
            sds((8, *pack), BF16),
            sds((8, *flat), BF16),
            sds((8, *flat), BF16),
            sds((8, *flat), BF16),
            sds((span, width), BF16),
            sds((span, qkv_cols), BF16),
            sds((2, 2, span, LANES), BF16),
            sds((2, 2, span, LANES), BF16),
            sds((heads, span, span), BF16),
            sds((span, q_cols), BF16),
            sds((rows, width), F32),
            sds((members, rows, width), BF16),
            sds((16, width), F32),
        ],
        [
            pltpu.VMEM(pack, BF16),
            pltpu.VMEM(route, F32),
            pltpu.VMEM((3, *flat), BF16),
            blocks,
            pltpu.VMEM((span, span), F32),
            blocks,
            blocks,
            blocks,
            pltpu.VMEM((rows, width), BF16),
            pltpu.VMEM((8, *pack), BF16),
            pltpu.VMEM((span, width), BF16),
            pltpu.VMEM((span, qkv_cols), BF16),
            pltpu.VMEM((2, 2, span, LANES), BF16),
            pltpu.VMEM((2, 2, span, LANES), BF16),
            pltpu.VMEM((heads, span, span), BF16),
            pltpu.VMEM((span, q_cols), BF16),
        ],
    )(tokens, cot, ids, gates, w_query, w_key, w_value, w_out, small, gate, up, down, cosine, sine)


def attend_back_steps(qkv, kx, vx, probs, grad_attended, cosine, sine, grad_k, grad_v, grad_qkv):
    span = qkv.shape[0]
    blocks = grad_attended.shape[1] // LANES
    repeat = QUERY_HEADS // KEY_VALUE_HEADS
    grad_k[...] = jnp.zeros(grad_k.shape, F32)
    grad_v[...] = jnp.zeros(grad_v.shape, F32)
    for j in range(blocks):
        lanes = slice(j * LANES, (j + 1) * LANES)
        for b in range(span // LANES):
            at, keys = pl.ds(b * LANES, LANES), (b + 1) * LANES
            q, grad = qkv[at, lanes], grad_attended[at, lanes]
            total = jnp.zeros((LANES, LANES), F32)
            for half in range(2):
                h = 2 * j + half
                kv = h // repeat
                low = probs[h, at, :keys]
                share = low.astype(F32)
                grad_probs = mm_nt(grad, vx[kv, half, :keys])
                inner = jnp.sum(share * grad_probs, axis=1, keepdims=True)
                grad_scores = (share * (grad_probs - inner)).astype(BF16)
                total += mm(grad_scores, kx[kv, half, :keys])
                grad_k[kv, half, :keys] += mm_tn(grad_scores, q)
                grad_v[kv, half, :keys] += mm_tn(low, grad)
            grad_qkv[at, lanes] = turn(total * score_scale, cosine[at], -sine[at]).astype(BF16)
        yield
    first = blocks * LANES

    def fold(parts, at):
        low = lane_ids(LANES) < HEAD_SIZE
        same = jnp.where(low, parts[0, 0, at], parts[1, 1, at])
        crossed = jnp.where(low, parts[1, 0, at], parts[0, 1, at])
        return same + pltpu.roll(crossed, HEAD_SIZE, axis=1)

    for b in range(span // LANES):
        at = pl.ds(b * LANES, LANES)
        grad_qkv[at, first : first + LANES] = turn(fold(grad_k, at), cosine[at], -sine[at]).astype(BF16)
        grad_qkv[at, first + LANES :] = fold(grad_v, at).astype(BF16)


def backward_kernel(
    members, grad_out_in, grad_residual, gain_ffn_part, tokens, down, row_gains, pack_in, normed_in, qkv_in, kx_in, vx_in, probs_in, attended_in, cosine, sine,
    grad_tokens, gains, d_query, d_key, d_value, d_out, down_out,
    send, recv, local, acc, from_left, from_right, grad_attended, grad_k, grad_v, grad_qkv, gain_part,
    for_w_out, for_w_query, for_rest, own_out, own_query, own_rest, all_out, all_query, all_rest,
    grad_out_all, pack_all, normed_attn, qkv, kx, vx, probs, attended, d_down, *rest,
):
    links = Links(send, recv, local, members)
    loads = {
        "attended": links.move(attended_in, attended),
        "grad": links.move(grad_out_in, grad_out_all),
        "pack": links.move(pack_in, pack_all),
        "qkv": links.move(qkv_in, qkv),
        "kx": links.move(kx_in, kx),
        "vx": links.move(vx_in, vx),
        "probs": links.move(probs_in, probs),
        "normed": links.move(normed_in, normed_attn),
    }
    stores = []

    def need(*names):
        for name in names:
            if name in loads:
                loads.pop(name).wait()

    links.greet()
    rows, width = tokens.shape
    q_cols, qkv_cols = attended.shape[1], qkv.shape[1]
    kv_cols = (qkv_cols - q_cols) // 2
    with_out, with_query, with_rest, with_down = rest[:5], rest[5:10], rest[10:15], rest[15:]
    pairs = for_w_out.shape[0] // 2
    step = width // pairs

    def weight_term(rows_of, grads, out, cols):
        for i in range(pairs):
            term = mm_tn(rows_of[:, i * step : (i + 1) * step], grads)
            out[2 * i : 2 * i + 2, :, :cols] = term.astype(BF16).reshape(2, step // 2, cols)

    def put_out():
        for m in range(members):
            d_out[:, m * q_cols : (m + 1) * q_cols] = all_out[m].astype(F32)

    def put_query():
        for m in range(members):
            d_query[:, m * q_cols : (m + 1) * q_cols] = all_query[m].astype(F32)

    def put_rest():
        for m in range(members):
            d_key[:, m * kv_cols : (m + 1) * kv_cols] = all_rest[m, :, :kv_cols].astype(F32)
            d_value[:, m * kv_cols : (m + 1) * kv_cols] = all_rest[m, :, kv_cols : 2 * kv_cols].astype(F32)
        total = sum(all_rest[m, :, 2 * kv_cols :].astype(F32) for m in range(members))
        gains[...] = total.T[: gains.shape[0]]

    def weight_chain(fill, part, mine, full, scratch, put):
        fill()
        yield from plane_scatter(links, part, None, *scratch)
        plane_result(part.at[links.d], scratch[0], scratch[3], scratch[4], mine)
        yield from line_gather(links, mine, full)
        put()

    def fill_out():
        need("grad", "attended")
        weight_term(grad_out_all, attended[...], for_w_out, q_cols)

    def fill_query():
        need("normed")
        weight_term(normed_attn, grad_qkv[:, :q_cols], for_w_query, q_cols)

    def fill_rest():
        weight_term(normed_attn, grad_qkv[:, q_cols:], for_rest, 2 * kv_cols)
        which = lax.broadcasted_iota(jnp.int32, (16, width), 0)
        both = jnp.where(which == 0, gain_part[...] / row_gains[0:1], jnp.where(which == 1, gain_ffn_part[...], 0.0))
        columns = mm_tn(both.astype(BF16), first_lanes())
        for_rest[:, :, 2 * kv_cols :] = columns.astype(BF16).reshape(2 * pairs, step // 2, LANES)

    def produce(o):
        at = slice(o * rows, (o + 1) * rows)
        part = mm_nt(grad_qkv[at], weight_columns(pack_all, 0, qkv_cols))
        gain_part[...] += jnp.sum(part * normed_attn[at].astype(F32), axis=0, keepdims=True)
        acc[o] = part.astype(BF16)

    def chain():
        need("grad", "pack")
        wo = weight_columns(pack_all, qkv_cols, q_cols)

        @pl.loop(0, grad_attended.shape[0] // LANES)
        def _(i):
            at = pl.ds(pl.multiple_of(i * LANES, LANES), LANES)
            grad_attended[at] = mm(grad_out_all[at], wo).astype(BF16)

        yield
        need("qkv", "kx", "vx", "probs")
        yield from attend_back_steps(qkv, kx, vx, probs, grad_attended, cosine, sine, grad_k, grad_v, grad_qkv)
        gain_part[...] = jnp.zeros(gain_part.shape, F32)
        need("normed")
        yield

        def finish(first, count):
            @pl.loop(0, count // 16)
            def _(i):
                at = pl.ds(pl.multiple_of(first + i * 16, 16), 16)
                grad = line_result(links.z, acc, from_left, from_right, at)
                here = tokens[at].astype(F32)
                grad_tokens[at] = grad_residual[at] + norm_back(here, rms_factor(here), row_gains[0:1], grad)

        yield from line_sum(links, produce, acc, from_left, from_right, finish)

    run(
        BACKWARD_ORDER,
        d=plane_total(links, down, with_down, d_down, down_out, stores),
        o=weight_chain(fill_out, for_w_out, own_out, all_out, with_out, put_out),
        a=chain(),
        q=weight_chain(fill_query, for_w_query, own_query, all_query, with_query, put_query),
        r=weight_chain(fill_rest, for_rest, own_rest, all_rest, with_rest, put_rest),
    )
    for store in stores:
        store.wait()
    links.finish()


BACKWARD_ORDER = "oadoaoaoaooqaqqdoaqdaqqarorarradrraqrqdaoodaaqdrddrr"


def backward_phase(members, own_experts, grad_out_all, grad_residual, gain_ffn_part, tokens, down, row_gains, pack_all, normed_attn, qkv, kx, vx, probs, attended, cosine, sine):
    rows, width = tokens.shape
    span, q_cols = attended.shape
    qkv_cols = qkv.shape[1]
    kv_cols = (qkv_cols - q_cols) // 2
    devices, own = down.shape[:2]
    line = [pltpu.VMEM((members, rows, width), BF16)] * 3
    three = (q_cols, q_cols, 2 * kv_cols + LANES)
    return comm_call(
        backward_kernel, "backward", 4, members, 100, 32,
        [ANY, VMEM, VMEM, VMEM, ANY, VMEM] + [ANY] * 7 + [VMEM] * 2,
        [VMEM] * 6 + [ANY],
        [
            sds((rows, width), F32),
            sds((8, own), F32),
            sds((own, members * q_cols), F32),
            sds((own, members * kv_cols), F32),
            sds((own, members * kv_cols), F32),
            sds((own, members * q_cols), F32),
            sds((own_experts, own, down.shape[2] // own_experts), F32),
        ],
        [
            *line,
            pltpu.VMEM((span, q_cols), BF16),
            pltpu.VMEM((2, 2, span, LANES), F32),
            pltpu.VMEM((2, 2, span, LANES), F32),
            pltpu.VMEM((span, qkv_cols), BF16),
            pltpu.VMEM((1, width), F32),
            *[pltpu.VMEM((devices, own, cols), BF16) for cols in three],
            *[pltpu.VMEM((own, cols), BF16) for cols in three],
            *[pltpu.VMEM((members, own, cols), BF16) for cols in three],
            *[pltpu.VMEM(a.shape, BF16) for a in (grad_out_all, pack_all, normed_attn, qkv, kx, vx, probs, attended)],
            pltpu.VMEM((own_experts, own, down.shape[2] // own_experts), F32),
            *[one for cols in three for one in plane_scratch(own, cols, False)],
            *plane_scratch(*down.shape[1:]),
        ],
    )(grad_out_all, grad_residual, gain_ffn_part, tokens, down, row_gains, pack_all, normed_attn, qkv, kx, vx, probs, attended, cosine, sine)


def results_kernel(count, *refs):
    sources, targets, held, came, went = refs[:count], refs[count : 2 * count], refs[2 * count : -2], refs[-2], refs[-1]
    moves = []
    for source, target, here in zip(sources, targets, held):
        pieces = source.shape[0] if len(source.shape) == 3 else 2
        step = source.shape[0] // pieces
        for i in range(pieces):
            at, k = pl.ds(i * step, step), len(moves)
            load = pltpu.make_async_copy(source.at[at], here.at[at], came.at[k])
            load.start()
            moves.append((load, pltpu.make_async_copy(here.at[at], target.at[at], went.at[k])))
    for load, store in moves:
        load.wait()
        store.start()
    for _, store in moves:
        store.wait()


def results(*arrays):
    return pl.pallas_call(
        functools.partial(results_kernel, len(arrays)),
        out_shape=[sds(a.shape, a.dtype) for a in arrays],
        in_specs=[ANY] * len(arrays),
        out_specs=[ANY] * len(arrays),
        scratch_shapes=[pltpu.VMEM(a.shape, a.dtype) for a in arrays] + [pltpu.SemaphoreType.DMA((64,))] * 2,
        compiler_params=pltpu.CompilerParams(vmem_limit_bytes=VMEM_LIMIT),
        name="results",
    )(*arrays)


def all_blocks(x, axis):
    return lax.all_gather(x, axis, axis=0)


def plain_first(members, tokens, cot, route, pack, gate):
    return (
        all_blocks(tokens, "expert"),
        all_blocks(cot, "expert"),
        all_blocks(route, "expert"),
        all_blocks(pack, "dp"),
        all_blocks(gate, "dp"),
    )


def line_total(part):
    return scatter(part.reshape(-1, part.shape[2]), "expert")


def plain_second(members, part, tokens, gain, up, down):
    residual = tokens.astype(F32) + branch_scale * line_total(part)
    normed = (residual * rms_factor(residual) * gain).astype(BF16)
    return residual, all_blocks(normed, "expert"), all_blocks(up, "dp"), all_blocks(down, "dp")


def plane_sum(part):
    return scatter(part.reshape(-1, part.shape[2]), "dp")


def plain_third(members, part, residual, cot, gain, gate, up):
    grad = line_total(part)
    factor = rms_factor(residual)
    gain_part = jnp.sum(grad * residual * factor, axis=0, keepdims=True)
    total = cot.astype(F32) + norm_back(residual, factor, gain, grad)
    out_all = all_blocks((branch_scale * total).astype(BF16), "expert")
    return total, gain_part, out_all, plane_sum(gate), plane_sum(up)


def plain_fourth(members, part, grad_residual, tokens, gain, pack, down):
    here = tokens.astype(F32)
    grad_tokens = grad_residual + norm_back(here, rms_factor(here), gain, line_total(part))
    return grad_tokens, all_blocks(plane_sum(pack).astype(BF16), "expert"), plane_sum(down)


def attend_forward(q, k, v, allowed):
    scores = jnp.einsum("irh,jh->rij", q, k, preferred_element_type=F32) * score_scale
    scores = jnp.where(allowed[None], scores, -1e30)
    peak = jnp.max(scores, axis=-1, keepdims=True)
    exponent = jnp.exp(scores - peak)
    total = jnp.sum(exponent, axis=-1, keepdims=True)
    probs = exponent / total
    return jnp.einsum("rij,jh->irh", probs.astype(BF16), v, preferred_element_type=F32), probs


def attend_backward(q, k, v, probs, grad, allowed):
    grad_probs = jnp.einsum("irh,jh->rij", grad, v, preferred_element_type=F32)
    inner = jnp.sum(probs * grad_probs, axis=-1, keepdims=True)
    grad_scores = (probs * (grad_probs - inner)).astype(BF16)
    grad_q = jnp.einsum("rij,jh->irh", grad_scores, k, preferred_element_type=F32) * score_scale
    grad_k = jnp.einsum("rij,irh->jh", grad_scores, q, preferred_element_type=F32) * score_scale
    grad_v = jnp.einsum("rij,irh->jh", probs.astype(BF16), grad, preferred_element_type=F32)
    return grad_q, grad_k, grad_v


def shards_plain(
    tokens,
    cotangent,
    gain_attn,
    gain_ffn,
    w_query,
    key_weight,
    value_weight,
    w_out,
    expert_gate,
    expert_up,
    expert_down,
    expert_ids,
    gates,
    lengths,
    order,
):
    rows, width = tokens.shape
    members = lax.axis_size("expert")
    member = lax.axis_index("expert")
    span = rows * members
    own_experts, ff = expert_gate.shape[1], expert_gate.shape[2]
    capacity = rows * TOP // own_experts
    q_cols = w_query.shape[1] // members
    kv_cols = key_weight.shape[1] // members
    kv_heads = kv_cols // HEAD_SIZE
    repeat = QUERY_HEADS // KEY_VALUE_HEADS

    def mine(weight, cols):
        return lax.dynamic_slice_in_dim(weight, member * cols, cols, axis=1)

    devices = lax.axis_size("dp")
    phases = [
        functools.partial(phase, members)
        for phase in (plain_first, plain_second, plain_third, plain_fourth)
    ]

    pack = jnp.concatenate(
        [
            mine(w_query, q_cols),
            mine(key_weight, kv_cols),
            mine(value_weight, kv_cols),
            mine(w_out, q_cols),
            gain_attn[:, None],
            gain_ffn[:, None],
            jnp.zeros((gain_attn.shape[0], 126), BF16),
        ],
        axis=1,
    )
    route = jnp.concatenate([expert_ids.astype(F32), gates], axis=1)
    tokens_all, cot_all, route_all, pack_all, gate_all = phases[0](
        tokens, cotangent, route, pack, expert_gate.reshape(-1, own_experts * ff)
    )
    tokens_all = tokens_all.reshape(span, width).astype(F32)
    cot_all = cot_all.reshape(span, width)
    route_all = route_all.reshape(span, 2 * TOP)
    pack_all = pack_all.reshape(width, -1)
    gate_all = gate_all.reshape(width, -1)
    qkv_cols = q_cols + 2 * kv_cols
    w_qkv = pack_all[:, :qkv_cols]
    wo = pack_all[:, qkv_cols : qkv_cols + q_cols]
    gain_one = pack_all[:, qkv_cols + q_cols].astype(F32)[None]
    gain_two = pack_all[:, qkv_cols + q_cols + 1].astype(F32)[None]

    segment, position = layout(lengths[0], order[0], span)
    cosine, sine = rotation(position)
    place = jnp.arange(span, dtype=jnp.int32)
    allowed = (segment[:, None] == segment[None, :]) & (place[None, :] <= place[:, None])
    factor_one = rms_factor(tokens_all)
    normed_attn = (tokens_all * factor_one * gain_one).astype(BF16)
    qkv = dot(normed_attn, w_qkv)
    qk = rotate(qkv[:, : q_cols + kv_cols], cosine, sine).astype(BF16)
    v = qkv[:, q_cols + kv_cols :].astype(BF16)
    q_heads = jnp.moveaxis(qk[:, :q_cols].reshape(span, kv_heads, repeat, HEAD_SIZE), 1, 0)
    k_heads = jnp.moveaxis(qk[:, q_cols:].reshape(span, kv_heads, HEAD_SIZE), 1, 0)
    v_heads = jnp.moveaxis(v.reshape(span, kv_heads, HEAD_SIZE), 1, 0)
    attended, probs = jax.vmap(functools.partial(attend_forward, allowed=allowed))(
        q_heads, k_heads, v_heads
    )
    attended = jnp.moveaxis(attended, 0, 1).reshape(span, q_cols).astype(BF16)
    attn_part = dot_nt(attended, wo).astype(BF16).reshape(members, rows, width)
    residual, normed_all, up_all, down_all = phases[1](
        attn_part,
        tokens,
        gain_two,
        expert_up.reshape(-1, own_experts * ff),
        expert_down.reshape(-1, own_experts * ff),
    )
    normed_all = normed_all.reshape(span, width)
    up_all, down_all = up_all.reshape(width, -1), down_all.reshape(width, -1)

    mixture, grad_normed, *by_kind = experts(
        own_experts, capacity, route_all, normed_all, cot_all, gate_all, up_all, down_all
    )
    output = (residual + branch_scale * scatter(mixture, "expert")).astype(BF16)
    by_kind = [one.reshape(devices, -1, own_experts * ff) for one in by_kind]

    grad_residual, gain_two_part, grad_attn_out, sum_gate, sum_up = phases[2](
        grad_normed.reshape(members, rows, width),
        residual,
        cotangent,
        gain_two,
        by_kind[0],
        by_kind[1],
    )
    grad_attn_out = grad_attn_out.reshape(span, width)
    term_out = dot_tn(grad_attn_out, attended)
    grad_attended = dot(grad_attn_out, wo).astype(BF16)
    grad_heads = jnp.moveaxis(grad_attended.reshape(span, kv_heads, repeat, HEAD_SIZE), 1, 0)
    grad_q, grad_k, grad_v = jax.vmap(functools.partial(attend_backward, allowed=allowed))(
        q_heads, k_heads, v_heads, probs, grad_heads
    )
    grad_qk = jnp.concatenate(
        [
            jnp.moveaxis(grad_q, 0, 1).reshape(span, q_cols),
            jnp.moveaxis(grad_k, 0, 1).reshape(span, kv_cols),
        ],
        axis=1,
    )
    grad_qkv = jnp.concatenate(
        [
            rotate(grad_qk, cosine, sine, back=True).astype(BF16),
            jnp.moveaxis(grad_v, 0, 1).reshape(span, kv_cols).astype(BF16),
        ],
        axis=1,
    )
    grad_norm_part = dot_nt(grad_qkv, w_qkv)
    gain_one_part = jnp.sum(grad_norm_part * tokens_all * factor_one, axis=0)
    term_qkv = dot_tn(normed_attn, grad_qkv)
    packed_grads = jnp.concatenate(
        [
            term_qkv,
            term_out,
            gain_one_part[:, None],
            gain_two_part.reshape(-1, 1),
            jnp.zeros((width, 126), F32),
        ],
        axis=1,
    )
    grad_tokens, per_member, sum_down = phases[3](
        grad_norm_part.astype(BF16).reshape(members, rows, width),
        grad_residual,
        tokens,
        gain_one,
        packed_grads.astype(BF16).reshape(devices, -1, packed_grads.shape[1]),
        by_kind[2],
    )
    per_member = per_member.astype(F32)

    def columns(first, cols):
        part = per_member[:, :, first : first + cols]
        return jnp.moveaxis(part, 0, 1).reshape(part.shape[1], -1)

    gains = jnp.sum(per_member[:, :, qkv_cols + q_cols :], axis=0)
    return (
        output,
        grad_tokens,
        gains[:, 0],
        gains[:, 1],
        columns(0, q_cols),
        columns(q_cols, kv_cols),
        columns(q_cols + kv_cols, kv_cols),
        columns(qkv_cols, q_cols),
        sum_gate.reshape(-1, own_experts, ff),
        sum_up.reshape(-1, own_experts, ff),
        sum_down.reshape(-1, own_experts, ff),
    )


def shards_fast(
    tokens,
    cotangent,
    gain_attn,
    gain_ffn,
    w_query,
    key_weight,
    value_weight,
    w_out,
    expert_gate,
    expert_up,
    expert_down,
    expert_ids,
    gates,
    lengths,
    order,
):
    rows, width = tokens.shape
    members, devices = lax.axis_size("expert"), lax.axis_size("dp")
    span = rows * members
    own_experts, ff = expert_gate.shape[1], expert_gate.shape[2]
    capacity = rows * TOP // own_experts
    segment, position = layout(lengths[0], order[0], span)
    lane = jnp.arange(LANES, dtype=jnp.int32) % HEAD_SIZE
    half = HEAD_SIZE // 2
    frequency = rope_base ** (-((lane % half).astype(F32) * (2.0 / HEAD_SIZE)))
    angles = position[:, None] * frequency[None, :]
    cosine, sine = jnp.cos(angles), jnp.where(lane < half, -1.0, 1.0) * jnp.sin(angles)
    spare = (0, span - gain_attn.shape[0])
    small = jnp.stack(
        [segment.astype(F32), jnp.pad(gain_attn.astype(F32), spare), jnp.pad(gain_ffn.astype(F32), spare)]
    )
    (
        cot_all, route_all, pack_all, gate_all, up_all, down_all,
        normed_attn, qkv, kx, vx, probs, attended, residual, normed_all, gains,
    ) = forward_phase(
        members, tokens, cotangent, expert_ids.T, gates.T, w_query, key_weight, value_weight, w_out,
        small, *(w.transpose(1, 0, 2) for w in (expert_gate, expert_up, expert_down)), cosine, sine,
    )
    cot_all = cot_all.reshape(span, width)
    normed_all = normed_all.reshape(span, width)
    route_all = route_all.reshape(span, 2 * TOP)
    gate_all, up_all, down_all = (w.reshape(width, -1) for w in (gate_all, up_all, down_all))
    mixture, grad_normed, *by_kind = experts(
        own_experts, capacity, route_all, normed_all, cot_all, gate_all, up_all, down_all
    )
    by_kind = [one.reshape(devices, -1, own_experts * ff) for one in by_kind]

    output, grad_residual, gain_two_part, grad_attn_out, sum_gate, sum_up = third_phase(
        members, own_experts,
        grad_normed.reshape(members, rows, width),
        mixture.reshape(members, rows, width),
        residual,
        cotangent,
        gains,
        by_kind[0],
        by_kind[1],
    )
    (
        grad_tokens, grad_gains, d_query, d_key, d_value, d_out, d_down,
    ) = backward_phase(
        members, own_experts,
        grad_attn_out.reshape(span, width),
        grad_residual,
        gain_two_part,
        tokens,
        by_kind[2],
        gains,
        pack_all,
        normed_attn, qkv, kx, vx, probs, attended, cosine, sine,
    )
    sum_gate, sum_up, d_down, d_query, d_out, grad_tokens, output, d_key, d_value = results(
        sum_gate, sum_up, d_down, d_query, d_out, grad_tokens, output, d_key, d_value
    )
    return (
        output,
        grad_tokens,
        grad_gains[0],
        grad_gains[1],
        d_query,
        d_key,
        d_value,
        d_out,
        sum_gate.transpose(1, 0, 2),
        sum_up.transpose(1, 0, 2),
        d_down.transpose(1, 0, 2),
    )


def solution(mesh):
    both = P(("dp", "expert"), None)
    row, rows = P("dp"), P("dp", None)
    experts = P("dp", "expert", None)
    fast = mesh.shape["dp"] == 8 and mesh.shape["expert"] == 4
    return jax.shard_map(
        shards_fast if fast else shards_plain,
        mesh=mesh,
        in_specs=(both, both, row, row, rows, rows, rows, rows)
        + (experts, experts, experts, both, both, rows, rows),
        out_specs=(both, both, row, row, rows, rows, rows, rows, experts, experts, experts),
        check_vma=False,
    )
```
